32 devices in a mesh: dp: 4 (over y, x), fsdp: 8 (over z, core).
Axes of the slice: x: 2, y: 2, z: 4, core: 2. Of those that a mesh axis runs over, the one named last changes fastest.
Arguments:
- tokens: bfloat16 [32, 1024, 768], P(('dp', 'fsdp')), may hold values from -6 to 6
- ln1_gain: bfloat16 [768], P(('dp', 'fsdp')), may hold values from 0.5 to 1.5
- ln1_bias: bfloat16 [768], P(('dp', 'fsdp')), may hold values from -1.75 to 1.75
- qkv_weight: bfloat16 [768, 2304], P(('dp', 'fsdp')), may hold values from -0.21875 to 0.21875
- qv_bias: bfloat16 [1536], P(('dp', 'fsdp')), may hold values from -3 to 3
- out_weight: bfloat16 [768, 768], P(('dp', 'fsdp')), may hold values from -1.75 to 1.75
- out_bias: bfloat16 [768], P(('dp', 'fsdp')), may hold values from -1.75 to 1.75
- ln2_gain: bfloat16 [768], P(('dp', 'fsdp')), may hold values from 0.5 to 1.5
- ln2_bias: bfloat16 [768], P(('dp', 'fsdp')), may hold values from -1.75 to 1.75
- fc_weight: bfloat16 [768, 3072], P(('dp', 'fsdp')), may hold values from -0.21875 to 0.21875
- fc_bias: bfloat16 [3072], P(('dp', 'fsdp')), may hold values from -1.75 to 1.75
- proj_weight: bfloat16 [3072, 768], P(('dp', 'fsdp')), may hold values from -0.109375 to 0.109375
- proj_bias: bfloat16 [768], P(('dp', 'fsdp')), may hold values from -1.75 to 1.75
- cotangent: bfloat16 [32, 1024, 768], P(('dp', 'fsdp')), may hold values from -6 to 6
- thought_slots: int32 [32, 2], P(('dp', 'fsdp')), may hold values from 257 to 383, as said below
- thought_count: int32 [32], P(('dp', 'fsdp')), may hold values from 1 to 2
- answer_start: int32 [32], P(('dp', 'fsdp')), may hold values from 260 to 449, as said below
Outputs:
- output: bfloat16 [32, 1024, 768], P(('dp', 'fsdp'))
- input_grad: float32 [32, 1024, 768], P(('dp', 'fsdp'))
- ln1_gain_grad: float32 [768], P(('dp', 'fsdp'))
- ln1_bias_grad: float32 [768], P(('dp', 'fsdp'))
- qkv_weight_grad: float32 [768, 2304], P(('dp', 'fsdp'))
- qv_bias_grad: float32 [1536], P(('dp', 'fsdp'))
- out_weight_grad: float32 [768, 768], P(('dp', 'fsdp'))
- out_bias_grad: float32 [768], P(('dp', 'fsdp'))
- ln2_gain_grad: float32 [768], P(('dp', 'fsdp'))
- ln2_bias_grad: float32 [768], P(('dp', 'fsdp'))
- fc_weight_grad: float32 [768, 3072], P(('dp', 'fsdp'))
- fc_bias_grad: float32 [3072], P(('dp', 'fsdp'))
- proj_weight_grad: float32 [3072, 768], P(('dp', 'fsdp'))
- proj_bias_grad: float32 [768], P(('dp', 'fsdp'))
The draws below stay inside these ranges and needn't reach their ends.
Inputs may be any that keep to these rules, and one draw needn't show every extreme that they name: `thought_slots`: the 2 slots of a sequence are consecutive positions after its question; the position before the first slot holds the start marker. `answer_start`: A sequence's answer starts after its last thought slot and one end marker.
All inputs are finite; a program needn't handle non-finite values.
Results may differ from the reference program's by a relative error of at most 0.019.
Values may be sent and summed in bfloat16 or wider, within the bound.
No kernel may reach another device: no remote copies, remote signals or barrier semaphores. Data moves between devices by JAX's collectives and lax.ppermute only.
A program may use at most 256 MiB of HBM per device.

```python
import jax
import jax.numpy as jnp
from jax import lax

D = 768
H = 12
HD = 64
FF = 3072
SEQ = 1024
QUESTION = 256
THOUGHTS = 2
PREFIX = 384
ROWS = 32


def thought_layout(key):
    key_one, key_two, key_three, key_four = jax.random.split(key, 4)
    first_slot = jax.random.randint(key_one, (ROWS,), QUESTION + 1, PREFIX - THOUGHTS + 1)
    extra_gap = jax.random.randint(key_two, (ROWS,), 0, SEQ // 16 + 1)
    high_row = jax.random.randint(key_three, (), 0, ROWS)
    low_row = (high_row + 1 + jax.random.randint(key_four, (), 0, ROWS - 1)) % ROWS
    row_index = lax.iota(jnp.int32, ROWS)
    first_slot = jnp.where(row_index == high_row, PREFIX - THOUGHTS, jnp.where(row_index == low_row, QUESTION + 1, first_slot))
    extra_gap = jnp.where(row_index == high_row, SEQ // 16, jnp.where(row_index == low_row, 0, extra_gap))
    return (first_slot.astype(jnp.int32), extra_gap.astype(jnp.int32))


def draw_thought_slots(key, part):
    layout = thought_layout(jax.random.fold_in(key, 11))
    return (layout[0][:, None] + lax.iota(jnp.int32, THOUGHTS)[None, :]).astype(jnp.int32)


def draw_answer_start(key, part):
    layout = thought_layout(jax.random.fold_in(key, 11))
    return (layout[0] + THOUGHTS + 1 + layout[1]).astype(jnp.int32)


def plant(drawn, own_key, least, top_value):
    index_at = [jax.random.randint(jax.random.fold_in(own_key, axis), (), 0, length) for axis, length in enumerate(drawn.shape)]
    widest = drawn.shape.index(max(drawn.shape))
    neighbour = index_at[:widest] + [(index_at[widest] + 1) % drawn.shape[widest]] + index_at[widest + 1:]
    return drawn.at[tuple(index_at)].set(least).at[tuple(neighbour)].set(top_value)


def shard_levels(key, extent, shards, low, top_value):
    loudness, own = 1.0, jax.random.fold_in(key, 6)
    for axis_at, blocks in shards:
        steps = jnp.exp(jax.random.uniform(jax.random.fold_in(own, axis_at), (blocks,), jnp.float32, low / len(shards), top_value / len(shards)))
        loudness = loudness * jnp.repeat(steps, extent[axis_at] // blocks).reshape([-1 if axis == axis_at else 1 for axis in range(len(extent))])
    return loudness


def normal_values(own_key, dims, scale, reach, shards=(), kind=jnp.bfloat16):
    level = shard_levels(own_key, dims, shards, -0.22, 0.18) if shards else 1.0
    array = jax.random.normal(own_key, dims, jnp.float32) * scale * level
    return jnp.minimum(jnp.maximum(array, -reach), reach).astype(kind)


def setup_inputs(seed: int = 0) -> dict:
    splits = jax.random.split(jax.random.key(seed), 18)
    tokens = normal_values(splits[0], (ROWS, SEQ, D), 1.0, 6.0, ((0, 32),))
    ln1_gain = jnp.clip(1.0 + 0.1 * jax.random.normal(splits[1], (D,), jnp.float32), 0.5, 1.5).astype(jnp.bfloat16)
    ln1_bias = normal_values(splits[2], (D,), 0.3, 1.75, ((0, 32),))
    qkv_weight = normal_values(splits[3], (D, 3 * D), D ** -0.5, 0.21875, ((0, 32),))
    qv_bias = normal_values(splits[4], (2 * D,), 0.5, 3.0, ((0, 32),))
    out_weight = normal_values(splits[5], (D, D), (D * 16 // SEQ) ** -0.5, 1.75, ((0, 32),))
    out_bias = normal_values(splits[6], (D,), 0.3, 1.75, ((0, 32),))
    ln2_gain = jnp.clip(1.0 + 0.1 * jax.random.normal(splits[7], (D,), jnp.float32), 0.5, 1.5).astype(jnp.bfloat16)
    ln2_bias = normal_values(splits[8], (D,), 0.3, 1.75, ((0, 32),))
    fc_weight = normal_values(splits[9], (D, FF), D ** -0.5, 0.21875, ((0, 32),))
    fc_bias = normal_values(splits[10], (FF,), 0.3, 1.75, ((0, 32),))
    proj_weight = normal_values(splits[11], (FF, D), FF ** -0.5, 0.109375, ((0, 32),))
    proj_bias = normal_values(splits[12], (D,), 0.3, 1.75, ((0, 32),))
    cotangent = normal_values(splits[13], (ROWS, SEQ, D), 1.0, 6.0, ((0, 32),))
    thought_slots = draw_thought_slots(jax.random.fold_in(splits[17], 71), 0)
    thought_count = plant(jax.random.randint(splits[15], (ROWS,), 1, THOUGHTS + 1), jax.random.fold_in(splits[15], 1), 1, THOUGHTS).astype(jnp.int32)
    answer_start = draw_answer_start(jax.random.fold_in(splits[17], 71), 0)
    return {"tokens": tokens, "ln1_gain": ln1_gain, "ln1_bias": ln1_bias, "qkv_weight": qkv_weight, "qv_bias": qv_bias, "out_weight": out_weight, "out_bias": out_bias, "ln2_gain": ln2_gain, "ln2_bias": ln2_bias, "fc_weight": fc_weight, "fc_bias": fc_bias, "proj_weight": proj_weight, "proj_bias": proj_bias, "cotangent": cotangent, "thought_slots": thought_slots, "thought_count": thought_count, "answer_start": answer_start}


EXACT = lax.Precision.HIGHEST
SCALE = 0.125

@jax.custom_vjp
def low(v):
    return lax.optimization_barrier(v.astype(jnp.bfloat16)).astype(jnp.float32)

@jax.custom_vjp
def low_back(v):
    return v

def low_keep(v):
    return (low(v), None)

def low_pass(kept, grad):
    return (grad,)

def back_keep(v):
    return (v, None)

def back_low(kept, grad):
    return (low(grad),)
low.defvjp(low_keep, low_pass)
low_back.defvjp(back_keep, back_low)

def layer_norm(hidden, gain, bias):
    row_mean = lax.optimization_barrier(jnp.mean(hidden, axis=-1, keepdims=True))
    centred = hidden - row_mean
    variance = lax.optimization_barrier(jnp.mean(centred * centred, axis=-1, keepdims=True))
    return centred * lax.rsqrt(variance + 1e-05) * gain + bias

def apply_layer(hidden, params):
    ln1_gain, ln1_bias, qkv_weight, qv_bias, out_weight, out_bias, ln2_gain, ln2_bias, fc_weight, fc_bias, proj_weight, proj_bias = params
    n_rows = hidden.shape[0]
    first_low = low(layer_norm(hidden, ln1_gain, ln1_bias))
    bias_full = jnp.concatenate([qv_bias[:D], jnp.zeros((D,), jnp.float32), qv_bias[D:]])
    qkv_rows = low(low_back(jnp.dot(first_low, qkv_weight, precision=EXACT) + bias_full))
    queries = qkv_rows[:, :D].reshape(n_rows, H, HD)
    key_rows = qkv_rows[:, D:2 * D].reshape(n_rows, H, HD)
    value_rows = qkv_rows[:, 2 * D:].reshape(n_rows, H, HD)
    scores = low_back(jnp.einsum('qhd,khd->hqk', queries, key_rows, precision=EXACT) * SCALE)
    positions = lax.iota(jnp.int32, n_rows)
    causal = positions[:, None] >= positions[None, :]
    scores = jnp.where(causal[None, :, :], scores, -1e+30)
    soft_rows = low(jax.nn.softmax(scores, axis=-1))
    mixed_rows = jnp.einsum('hqk,khd->qhd', soft_rows, value_rows, precision=EXACT).reshape(n_rows, D)
    mixed_low = low(low_back(mixed_rows))
    resid = hidden + low_back(jnp.dot(mixed_low, out_weight, precision=EXACT) + out_bias)
    second_low = low(layer_norm(resid, ln2_gain, ln2_bias))
    pre_act = low_back(jnp.dot(second_low, fc_weight, precision=EXACT) + fc_bias)
    act_low = low(jax.nn.gelu(pre_act, approximate=True))
    return resid + low_back(jnp.dot(act_low, proj_weight, precision=EXACT) + proj_bias)

def reference(tokens, ln1_gain, ln1_bias, qkv_weight, qv_bias, out_weight, out_bias, ln2_gain, ln2_bias, fc_weight, fc_bias, proj_weight, proj_bias, cotangent, thought_slots, thought_count, answer_start):
    params = tuple((weight_arg.astype(jnp.float32) for weight_arg in (ln1_gain, ln1_bias, qkv_weight, qv_bias, out_weight, out_bias, ln2_gain, ln2_bias, fc_weight, fc_bias, proj_weight, proj_bias)))
    positions = lax.iota(jnp.int32, SEQ)

    def row_forward(row_in, slots, count, weights):
        hidden = row_in
        for slot_index in range(THOUGHTS):
            early_out = apply_layer(hidden[:PREFIX], weights)
            slot_row = slots[slot_index]
            fed_row = lax.dynamic_index_in_dim(early_out, slot_row - 1, 0, keepdims=False)
            chosen = (positions == slot_row) & (slot_index < count)
            hidden = jnp.where(chosen[:, None], fed_row[None, :], hidden)
        return apply_layer(hidden, weights)

    def row_step(running, row_data):
        row_tokens, row_cot, slots, count, begin_row = row_data

        def forward(row_in, *weights):
            return row_forward(row_in, slots, count, weights)
        final_out, pullback = jax.vjp(forward, row_tokens.astype(jnp.float32), *params)
        answer_cot = jnp.where((positions >= begin_row)[:, None], row_cot.astype(jnp.float32), 0.0)
        gradients = pullback(answer_cot)
        running = tuple((total_part + new_part for total_part, new_part in zip(running, gradients[1:])))
        return (running, (final_out.astype(jnp.bfloat16), gradients[0]))
    initial = tuple((jnp.zeros(weight_arg.shape, jnp.float32) for weight_arg in params))
    totals, (output, input_grad) = lax.scan(row_step, initial, (tokens, cotangent, thought_slots, thought_count, answer_start))
    return (output, input_grad, totals[0], totals[1], totals[2], totals[3], totals[4], totals[5], totals[6], totals[7], totals[8], totals[9], totals[10], totals[11])
```

```python
import math

import jax
import jax.numpy as jnp
from jax import lax
from jax.experimental import pallas as pl
from jax.experimental.pallas import tpu as pltpu
from jax.sharding import PartitionSpec as P

HD = 64
THOUGHTS = 2
PREFIX = 384
QUESTION = 256
SCALE = 0.125
EPSILON = 1e-05
BLOCK = 256
PAIR = 2 * HD
NEG = -1e30

F32 = jnp.float32
BF16 = jnp.bfloat16
VMEM_LIMIT = 56 * 1024 * 1024


def dot(a, b):
    return lax.dot_general(a, b, (((1,), (0,)), ((), ())), preferred_element_type=F32)


def dot_nt(a, b):
    return lax.dot_general(a, b, (((1,), (1,)), ((), ())), preferred_element_type=F32)


def dot_tn(a, b):
    return lax.dot_general(a, b, (((0,), (0,)), ((), ())), preferred_element_type=F32)


def bits_of(size):
    return [1 << i for i in reversed(range(int(math.log2(size))))]


class Links:
    def __init__(self, sizes):
        self.sizes = sizes
        self.canon = [("dp", b) for b in bits_of(sizes["dp"])] + [
            ("fsdp", b) for b in bits_of(sizes["fsdp"])
        ]
        dp_bits = [("dp", b) for b in bits_of(sizes["dp"])]
        f_bits = [("fsdp", b) for b in bits_of(sizes["fsdp"])]
        self.groups = {"x": dp_bits[-1:], "y": dp_bits[:-1], "z": f_bits[:-1], "c": f_bits[-1:]}

    def order(self, text):
        out = []
        for letter in text:
            out += self.groups[letter]
        return out

    def swap(self, value, stage):
        axis, bit = stage
        return lax.ppermute(value, axis, [(i, i ^ bit) for i in range(self.sizes[axis])])

    def mine(self, stage):
        axis, bit = stage
        return (lax.axis_index(axis) & bit) != 0

    def gather(self, shard, text):
        done = []
        buf = shard
        for stage in self.order(text):
            got = self.swap(buf, stage)
            place = sum(1 for d in done if self.canon.index(d) < self.canon.index(stage))
            high = self.mine(stage)
            buf = jnp.stack([jnp.where(high, got, buf), jnp.where(high, buf, got)], axis=place)
            done.append(stage)
        return buf.reshape((-1,) + shard.shape)

    def scatter(self, value, text):
        tail = value.shape[1:]
        left = list(self.canon)
        buf = value.reshape((2,) * len(left) + tail)
        for stage in self.order(text):
            place = left.index(stage)
            high = self.mine(stage).astype(jnp.int32)
            keep = lax.dynamic_index_in_dim(buf, high, place, keepdims=False)
            send = lax.dynamic_index_in_dim(buf, 1 - high, place, keepdims=False)
            got = self.swap(send, stage)
            buf = keep.astype(F32) + got.astype(F32)
            left.remove(stage)
            if left:
                buf = buf.astype(BF16)
        return buf


def attend_kernel(q_ref, k_ref, v_ref, o_ref, lse_ref):
    seq_len = q_ref.shape[0]
    keys = k_ref[...]
    values_t = v_ref[...].T
    lane = lax.broadcasted_iota(jnp.int32, (BLOCK, PAIR), 1)
    sub = lax.broadcasted_iota(jnp.int32, (PAIR, BLOCK), 0)
    key_pos = lax.broadcasted_iota(jnp.int32, (BLOCK, BLOCK), 0)
    row_pos = lax.broadcasted_iota(jnp.int32, (BLOCK, BLOCK), 1)
    causal = key_pos <= row_pos
    for begin in range(0, seq_len, BLOCK):
        end = begin + BLOCK
        queries = q_ref[begin:end, :] * jnp.asarray(SCALE, BF16)
        parts = []
        for head in range(2):
            own = jnp.where((lane >= HD) == bool(head), queries, jnp.zeros_like(queries))
            last = jnp.where(causal, dot_nt(keys[begin:end], own), NEG)
            peak = jnp.max(last, axis=0, keepdims=True)
            if begin:
                before = dot_nt(keys[:begin], own)
                peak = jnp.maximum(peak, jnp.max(before, axis=0, keepdims=True))
            expo = jnp.exp(last - peak)
            total = jnp.sum(expo, axis=0, keepdims=True)
            mixed = dot(values_t[:, begin:end], expo.astype(BF16))
            if begin:
                expo = jnp.exp(before - peak)
                total = total + jnp.sum(expo, axis=0, keepdims=True)
                mixed = mixed + dot(values_t[:, :begin], expo.astype(BF16))
            parts.append(mixed / total)
            lse_ref[0, head : head + 1, begin:end] = peak + jnp.log(total)
        o_ref[begin:end, :] = jnp.where(sub < HD, parts[0], parts[1]).T.astype(BF16)


def attend(qkv):
    seq_len, triple = qkv.shape
    width = triple // 3
    pairs = width // PAIR
    return pl.pallas_call(
        attend_kernel,
        grid=(pairs,),
        in_specs=[
            pl.BlockSpec((seq_len, PAIR), lambda g: (0, g)),
            pl.BlockSpec((seq_len, PAIR), lambda g: (0, g + pairs)),
            pl.BlockSpec((seq_len, PAIR), lambda g: (0, g + 2 * pairs)),
        ],
        out_specs=[
            pl.BlockSpec((seq_len, PAIR), lambda g: (0, g)),
            pl.BlockSpec((1, 2, seq_len), lambda g: (g, 0, 0)),
        ],
        out_shape=[
            jax.ShapeDtypeStruct((seq_len, width), BF16),
            jax.ShapeDtypeStruct((pairs, 2, seq_len), F32),
        ],
        compiler_params=pltpu.CompilerParams(vmem_limit_bytes=VMEM_LIMIT),
        name="attention_forward",
    )(qkv, qkv, qkv)


def attend_back_kernel(q_ref, k_ref, v_ref, o_ref, lse_ref, g_ref, dq_ref, dk_ref, dv_ref):
    seq_len = q_ref.shape[0]
    first_row = seq_len - g_ref.shape[0]
    keys = k_ref[...]
    values = v_ref[...]
    keys_t = keys.T
    lane = lax.broadcasted_iota(jnp.int32, (BLOCK, PAIR), 1)
    sub = lax.broadcasted_iota(jnp.int32, (PAIR, BLOCK), 0)
    key_pos = lax.broadcasted_iota(jnp.int32, (BLOCK, BLOCK), 0)
    row_pos = lax.broadcasted_iota(jnp.int32, (BLOCK, BLOCK), 1)
    causal = key_pos <= row_pos
    dk_ref[...] = jnp.zeros_like(dk_ref)
    dv_ref[...] = jnp.zeros_like(dv_ref)
    for begin in range(first_row, seq_len, BLOCK):
        end = begin + BLOCK
        local = begin - first_row
        queries = q_ref[begin:end, :] * jnp.asarray(SCALE, BF16)
        grads = g_ref[local : local + BLOCK, :]
        product_t = (grads.astype(F32) * o_ref[begin:end, :].astype(F32)).T
        parts = []
        for head in range(2):
            chosen = (lane >= HD) == bool(head)
            own = jnp.where(chosen, queries, jnp.zeros_like(queries))
            own_grad = jnp.where(chosen, grads, jnp.zeros_like(grads))
            delta = jnp.sum(product_t[head * HD : (head + 1) * HD], axis=0, keepdims=True)
            lse = lse_ref[0, head : head + 1, begin:end]
            total = None
            for low, high in ((0, begin), (begin, end)):
                scores = dot_nt(keys[low:high], own)
                if high == end:
                    scores = jnp.where(causal, scores, NEG)
                probs = jnp.exp(scores - lse)
                prob_grad = dot_nt(values[low:high], own_grad)
                score_grad = (probs * (prob_grad - delta)).astype(BF16)
                dv_ref[low:high, :] += dot(probs.astype(BF16), own_grad)
                dk_ref[low:high, :] += dot(score_grad, own)
                part = dot(keys_t[:, low:high], score_grad)
                total = part if total is None else total + part
            parts.append(total)
        dq_ref[local : local + BLOCK, :] = jnp.where(sub < HD, parts[0], parts[1]).T * SCALE


def attend_back(qkv, mixed_low, lse, mixed_grad):
    seq_len, triple = qkv.shape
    width = triple // 3
    pairs = width // PAIR
    rows = mixed_grad.shape[0]
    return pl.pallas_call(
        attend_back_kernel,
        grid=(pairs,),
        in_specs=[
            pl.BlockSpec((seq_len, PAIR), lambda g: (0, g)),
            pl.BlockSpec((seq_len, PAIR), lambda g: (0, g + pairs)),
            pl.BlockSpec((seq_len, PAIR), lambda g: (0, g + 2 * pairs)),
            pl.BlockSpec((seq_len, PAIR), lambda g: (0, g)),
            pl.BlockSpec((1, 2, seq_len), lambda g: (g, 0, 0)),
            pl.BlockSpec((rows, PAIR), lambda g: (0, g)),
        ],
        out_specs=[
            pl.BlockSpec((rows, PAIR), lambda g: (0, g)),
            pl.BlockSpec((seq_len, PAIR), lambda g: (0, g)),
            pl.BlockSpec((seq_len, PAIR), lambda g: (0, g)),
        ],
        out_shape=[
            jax.ShapeDtypeStruct((rows, width), F32),
            jax.ShapeDtypeStruct((seq_len, width), F32),
            jax.ShapeDtypeStruct((seq_len, width), F32),
        ],
        compiler_params=pltpu.CompilerParams(vmem_limit_bytes=VMEM_LIMIT),
        name="attention_backward",
    )(qkv, qkv, qkv, mixed_low, lse, mixed_grad)


def row_norm(row, gain, bias):
    mean = jnp.mean(row, axis=-1, keepdims=True)
    centred = row - mean
    inverse = lax.rsqrt(jnp.mean(centred * centred, axis=-1, keepdims=True) + EPSILON)
    normed = centred * inverse
    return normed * gain + bias, normed, inverse


def row_norm_back(incoming, normed, inverse, gain):
    scaled = incoming * gain
    inner = (
        scaled
        - jnp.mean(scaled, axis=-1, keepdims=True)
        - normed * jnp.mean(scaled * normed, axis=-1, keepdims=True)
    )
    return inner * inverse


GELU_A = 0.7978845608028654
GELU_B = 0.044715


def gelu(pre):
    return 0.5 * pre * (1.0 + jnp.tanh(GELU_A * (pre + GELU_B * pre * pre * pre)))


def gelu_slope(pre):
    square = pre * pre
    curve = jnp.tanh(GELU_A * pre * (1.0 + GELU_B * square))
    return 0.5 * (1.0 + curve) + 0.5 * pre * (1.0 - curve * curve) * GELU_A * (
        1.0 + 3.0 * GELU_B * square
    )


def widen(row):
    return jnp.broadcast_to(row, (8, row.shape[1])).astype(BF16)


def pick(block, index):
    rows = lax.broadcasted_iota(jnp.int32, block.shape, 0)
    return jnp.sum(jnp.where(rows == index, block.astype(F32), 0.0), axis=0, keepdims=True)


def put(block, index, row):
    rows = lax.broadcasted_iota(jnp.int32, block.shape, 0)
    return jnp.where(rows == index, row.astype(block.dtype), block)


def by_head(row, heads):
    shape = (heads, row.shape[1])
    lane_head = lax.broadcasted_iota(jnp.int32, shape, 1) // HD
    return jnp.where(lane_head == lax.broadcasted_iota(jnp.int32, shape, 0), row, 0.0)


def heads_only(block):
    lane_head = lax.broadcasted_iota(jnp.int32, block.shape, 1) // HD
    own = lane_head == lax.broadcasted_iota(jnp.int32, block.shape, 0)
    return jnp.sum(jnp.where(own, block, 0.0), axis=0, keepdims=True)


HEAD_ROWS = 16


def thoughts_kernel(
    info_ref,
    tok_ref,
    qkv_ref,
    wqkv_ref,
    wout_ref,
    wfc_ref,
    wproj_ref,
    vec_ref,
    fcb_ref,
    qkvb_ref,
    hid_ref,
    qkvm_ref,
    pre_ref,
    prob_ref,
    res_ref,
):
    width = tok_ref.shape[1]
    ln1_gain, ln1_bias, out_bias, ln2_gain, ln2_bias, proj_bias = (
        vec_ref[i : i + 1, :] for i in range(6)
    )
    slot = info_ref[0]
    count = info_ref[1]
    hid_ref[...] = tok_ref[...].astype(F32)
    qkvm_ref[...] = qkv_ref[QUESTION:PREFIX, :]
    hidden_row = pick(hid_ref[...], slot - 1 - QUESTION)
    qkv_row = pick(qkvm_ref[...], slot - 1 - QUESTION)
    for step in range(THOUGHTS):
        at = slot - 1 + step
        query = by_head(qkv_row[:, :width] * SCALE, HEAD_ROWS).astype(BF16)
        scores = jnp.concatenate(
            [
                dot_nt(query, qkv_ref[:QUESTION, width : 2 * width]),
                dot_nt(query, qkvm_ref[:, width : 2 * width]),
            ],
            axis=1,
        )
        key_pos = lax.broadcasted_iota(jnp.int32, scores.shape, 1)
        scores = jnp.where(key_pos <= at, scores, NEG)
        expo = jnp.exp(scores - jnp.max(scores, axis=1, keepdims=True))
        probs = expo / jnp.sum(expo, axis=1, keepdims=True)
        prob_ref[step * HEAD_ROWS : (step + 1) * HEAD_ROWS, :] = probs
        low = probs.astype(BF16)
        mixed = heads_only(
            dot(low[:, :QUESTION], qkv_ref[:QUESTION, 2 * width :])
            + dot(low[:, QUESTION:], qkvm_ref[:, 2 * width :])
        )
        resid = hidden_row + dot(widen(mixed), wout_ref[...])[0:1] + out_bias
        res_ref[step : step + 1, :] = resid
        second, _, _ = row_norm(resid, ln2_gain, ln2_bias)
        pre = dot(widen(second), wfc_ref[...])[0:1] + fcb_ref[0:1, :]
        pre_ref[step : step + 1, :] = pre
        fed = resid + dot(widen(gelu(pre)), wproj_ref[...])[0:1] + proj_bias
        first, _, _ = row_norm(fed, ln1_gain, ln1_bias)
        qkv_row = dot(widen(first), wqkv_ref[...])[0:1] + qkvb_ref[0:1, :]
        qkv_row = qkv_row.astype(BF16).astype(F32)
        hidden_row = fed
        spot = jnp.where(step < count, slot + step - QUESTION, -1)
        hid_ref[...] = put(hid_ref[...], spot, fed)
        qkvm_ref[...] = put(qkvm_ref[...], spot, qkv_row)


def whole(array):
    zeros = (0,) * array.ndim
    return pl.BlockSpec(array.shape, lambda i, zeros=zeros: zeros)


def thoughts_forward(info, tokens, qkv, weights, vec, fc_bias, qkv_bias):
    width = tokens.shape[1]
    wqkv, wout, wfc, wproj = weights
    middle = PREFIX - QUESTION
    out_shape = [
        jax.ShapeDtypeStruct((middle, width), F32),
        jax.ShapeDtypeStruct((middle, 3 * width), BF16),
        jax.ShapeDtypeStruct((8, wfc.shape[1]), F32),
        jax.ShapeDtypeStruct((THOUGHTS * HEAD_ROWS, PREFIX), F32),
        jax.ShapeDtypeStruct((8, width), F32),
    ]
    return pl.pallas_call(
        thoughts_kernel,
        grid=(1,),
        in_specs=[
            pl.BlockSpec(memory_space=pltpu.SMEM),
            pl.BlockSpec((middle, width), lambda i: (QUESTION // middle, 0)),
            pl.BlockSpec((PREFIX, 3 * width), lambda i: (0, 0)),
            whole(wqkv),
            whole(wout),
            whole(wfc),
            whole(wproj),
            whole(vec),
            whole(fc_bias),
            whole(qkv_bias),
        ],
        out_specs=[whole(s) for s in out_shape],
        out_shape=out_shape,
        compiler_params=pltpu.CompilerParams(vmem_limit_bytes=VMEM_LIMIT),
        name="thought_rows_forward",
    )(info, tokens, qkv, wqkv, wout, wfc, wproj, vec, fc_bias, qkv_bias)


def thoughts_back_kernel(
    info_ref,
    hid_ref,
    qkv_ref,
    dk_in_ref,
    dv_in_ref,
    pre_ref,
    prob_ref,
    res_ref,
    wqkv_ref,
    wout_ref,
    wfc_ref,
    wproj_ref,
    vec_ref,
    dk_ref,
    dv_ref,
    dq_ref,
    up_ref,
    pg_ref,
    sg_ref,
    rg_ref,
):
    width = hid_ref.shape[1]
    ln1_gain, ln1_bias, _, ln2_gain, ln2_bias, _ = (vec_ref[i : i + 1, :] for i in range(6))
    slot = info_ref[0]
    count = info_ref[1]
    dk_ref[...] = dk_in_ref[...]
    dv_ref[...] = dv_in_ref[...]

    def through_first(at, query_grad):
        grad_row = jnp.concatenate(
            [query_grad, dk_ref[pl.ds(at, 1), :], dv_ref[pl.ds(at, 1), :]], axis=1
        )
        first_grad = dot_nt(widen(grad_row), wqkv_ref[...])[0:1]
        _, normed, inverse = row_norm(hid_ref[pl.ds(at - QUESTION, 1), :], ln1_gain, ln1_bias)
        return row_norm_back(first_grad, normed, inverse, ln1_gain)

    carried = through_first(slot + 1, jnp.zeros((1, width), F32))
    for step in reversed(range(THOUGHTS)):
        at = slot - 1 + step
        upstream = jnp.where(step < count, carried, 0.0)
        up_ref[step : step + 1, :] = upstream
        act_grad = dot_nt(widen(upstream), wproj_ref[...])[0:1]
        pre_grad = act_grad * gelu_slope(pre_ref[step : step + 1, :])
        pg_ref[step : step + 1, :] = pre_grad
        second_grad = dot_nt(widen(pre_grad), wfc_ref[...])[0:1]
        sg_ref[step : step + 1, :] = second_grad
        _, normed, inverse = row_norm(res_ref[step : step + 1, :], ln2_gain, ln2_bias)
        resid_grad = upstream + row_norm_back(second_grad, normed, inverse, ln2_gain)
        rg_ref[step : step + 1, :] = resid_grad
        mixed_grad = dot_nt(widen(resid_grad), wout_ref[...])[0:1]
        own_grad = by_head(mixed_grad, HEAD_ROWS).astype(BF16)
        query = by_head(pick(qkv_ref[QUESTION:PREFIX, :width], at - QUESTION) * SCALE, HEAD_ROWS)
        query = query.astype(BF16)
        probs = prob_ref[step * HEAD_ROWS : (step + 1) * HEAD_ROWS, :]
        prob_grad = dot_nt(own_grad, qkv_ref[:, 2 * width :])
        delta = jnp.sum(prob_grad * probs, axis=1, keepdims=True)
        score_grad = (probs * (prob_grad - delta)).astype(BF16)
        query_grad = heads_only(dot(score_grad, qkv_ref[:, width : 2 * width])) * SCALE
        dq_ref[step : step + 1, :] = query_grad
        dk_ref[...] += dot_tn(score_grad, query)
        dv_ref[...] += dot_tn(probs.astype(BF16), own_grad)
        if step:
            carried = resid_grad + through_first(at, query_grad)


def thoughts_back(info, hidden_mid, qkv, dk, dv, pre, probs, resid, weights, vec):
    width = hidden_mid.shape[1]
    wqkv, wout, wfc, wproj = weights
    out_shape = [
        jax.ShapeDtypeStruct((PREFIX, width), F32),
        jax.ShapeDtypeStruct((PREFIX, width), F32),
        jax.ShapeDtypeStruct((8, width), F32),
        jax.ShapeDtypeStruct((8, width), F32),
        jax.ShapeDtypeStruct((8, wfc.shape[1]), F32),
        jax.ShapeDtypeStruct((8, width), F32),
        jax.ShapeDtypeStruct((8, width), F32),
    ]
    return pl.pallas_call(
        thoughts_back_kernel,
        grid=(1,),
        in_specs=[
            pl.BlockSpec(memory_space=pltpu.SMEM),
            whole(hidden_mid),
            pl.BlockSpec((PREFIX, 3 * width), lambda i: (0, 0)),
            pl.BlockSpec((PREFIX, width), lambda i: (0, 0)),
            pl.BlockSpec((PREFIX, width), lambda i: (0, 0)),
            whole(pre),
            whole(probs),
            whole(resid),
            whole(wqkv),
            whole(wout),
            whole(wfc),
            whole(wproj),
            whole(vec),
        ],
        out_specs=[whole(s) for s in out_shape],
        out_shape=out_shape,
        compiler_params=pltpu.CompilerParams(vmem_limit_bytes=VMEM_LIMIT),
        name="thought_rows_backward",
    )(info, hidden_mid, qkv, dk, dv, pre, probs, resid, wqkv, wout, wfc, wproj, vec)


def norm_parts(hidden):
    mean = jnp.mean(hidden, axis=-1, keepdims=True)
    centred = hidden - mean
    inverse = lax.rsqrt(jnp.mean(centred * centred, axis=-1, keepdims=True) + EPSILON)
    return centred * inverse, inverse


def step_on_sequence(weights, small, tokens, cotangent, slots, count, answer_start):
    wqkv, wout, wfc, wproj = weights
    seq_len, width = tokens.shape
    vecs = {name: value.astype(F32) for name, value in small.items()}
    qkv_bias = jnp.concatenate(
        [vecs["qv_bias"][:width], jnp.zeros((width,), F32), vecs["qv_bias"][width:]]
    )
    names = ("ln1_gain", "ln1_bias", "out_bias", "ln2_gain", "ln2_bias", "proj_bias")
    vec = jnp.stack([vecs[n] for n in names] + [jnp.zeros((width,), F32)] * 2)
    info = jnp.stack([slots[0], count])

    tokens32 = tokens.astype(F32)
    normed, _ = norm_parts(tokens32)
    first_low = (normed * vecs["ln1_gain"] + vecs["ln1_bias"]).astype(BF16)
    qkv_first = (dot(first_low, wqkv) + qkv_bias).astype(BF16)
    hidden_mid, qkv_mid, pre_rows, prob_rows, res_rows = thoughts_forward(
        info, tokens, qkv_first, weights, vec, vecs["fc_bias"][None], qkv_bias[None]
    )
    qkv = lax.dynamic_update_slice(qkv_first, qkv_mid, (QUESTION, 0))
    hidden = lax.dynamic_update_slice(tokens32, hidden_mid, (QUESTION, 0))
    mixed_low, lse = attend(qkv)
    resid = hidden + dot(mixed_low, wout) + vecs["out_bias"]
    normed_two, inverse_two = norm_parts(resid)
    second_low = (normed_two * vecs["ln2_gain"] + vecs["ln2_bias"]).astype(BF16)
    pre = dot(second_low, wfc) + vecs["fc_bias"]
    act_low = gelu(pre).astype(BF16)
    final = resid + dot(act_low, wproj) + vecs["proj_bias"]
    output = final.astype(BF16)

    rows = seq_len - QUESTION
    late = QUESTION + lax.iota(jnp.int32, rows)
    upstream_low = jnp.where(
        (late >= answer_start)[:, None], cotangent[QUESTION:], jnp.zeros((), BF16)
    )
    act_grad = dot_nt(upstream_low, wproj)
    pre_grad = (act_grad * gelu_slope(pre[QUESTION:])).astype(BF16)
    second_grad = dot_nt(pre_grad, wfc)
    normed_late = normed_two[QUESTION:]
    resid_grad = upstream_low.astype(F32) + row_norm_back(
        second_grad, normed_late, inverse_two[QUESTION:], vecs["ln2_gain"]
    )
    mixed_grad = dot_nt(resid_grad.astype(BF16), wout).astype(BF16)
    query_grad, key_grad, value_grad = attend_back(qkv, mixed_low, lse, mixed_grad)
    key_early, value_early, dq_rows, up_rows, pg_rows, sg_rows, rg_rows = thoughts_back(
        info, hidden_mid, qkv, key_grad, value_grad, pre_rows, prob_rows, res_rows, weights, vec
    )
    spot = (slots[0] - 1 - QUESTION, 0)

    def insert(block, extra):
        return lax.dynamic_update_slice(block, extra[:THOUGHTS].astype(block.dtype), spot)

    upstream_low = insert(upstream_low, up_rows)
    pre_grad = insert(pre_grad, pg_rows)
    second_grad = insert(second_grad, sg_rows)
    resid_grad = insert(resid_grad, rg_rows)
    attn_grad = resid_grad.astype(BF16)
    query_grad = insert(query_grad, dq_rows)

    proj_grad = dot_tn(act_low[QUESTION:], upstream_low)
    fc_grad = dot_tn(second_low[QUESTION:], pre_grad)
    out_grad = dot_tn(mixed_low[QUESTION:], attn_grad)
    key_grad = lax.dynamic_update_slice(key_grad, key_early, (0, 0))
    value_grad = lax.dynamic_update_slice(value_grad, value_early, (0, 0))
    qkv_grad = jnp.concatenate(
        [jnp.pad(query_grad, ((QUESTION, 0), (0, 0))), key_grad, value_grad], axis=1
    ).astype(BF16)
    normed_one, inverse_one = norm_parts(hidden)
    first_low = (normed_one * vecs["ln1_gain"] + vecs["ln1_bias"]).astype(BF16)
    qkv_weight_grad = dot_tn(first_low, qkv_grad)
    first_grad = dot_nt(qkv_grad, wqkv)
    hidden_part = row_norm_back(first_grad, normed_one, inverse_one, vecs["ln1_gain"])
    positions = lax.iota(jnp.int32, seq_len)
    replaced = jnp.zeros((seq_len,), jnp.bool_)
    for step in range(THOUGHTS):
        replaced = replaced | ((positions == slots[0] + step) & (step < count))
    input_grad = jnp.where(
        replaced[:, None], 0.0, jnp.pad(resid_grad, ((QUESTION, 0), (0, 0))) + hidden_part
    )
    column_sums = jnp.sum(qkv_grad.astype(F32), axis=0)
    small_grads = {
        "ln1_gain": jnp.sum(first_grad * normed_one, axis=0),
        "ln1_bias": jnp.sum(first_grad, axis=0),
        "qv_bias": jnp.concatenate([column_sums[:width], column_sums[2 * width :]]),
        "out_bias": jnp.sum(attn_grad.astype(F32), axis=0),
        "ln2_gain": jnp.sum(second_grad * normed_late, axis=0),
        "ln2_bias": jnp.sum(second_grad, axis=0),
        "fc_bias": jnp.sum(pre_grad.astype(F32), axis=0),
        "proj_bias": jnp.sum(upstream_low.astype(F32), axis=0),
    }
    return output, input_grad, (qkv_weight_grad, out_grad, fc_grad, proj_grad), small_grads


SMALL = ("ln1_gain", "ln1_bias", "qv_bias", "out_bias", "ln2_gain", "ln2_bias", "fc_bias", "proj_bias")


def on_device(
    links,
    tokens,
    ln1_gain,
    ln1_bias,
    qkv_weight,
    qv_bias,
    out_weight,
    out_bias,
    ln2_gain,
    ln2_bias,
    fc_weight,
    fc_bias,
    proj_weight,
    proj_bias,
    cotangent,
    thought_slots,
    thought_count,
    answer_start,
):
    devices = links.sizes["dp"] * links.sizes["fsdp"]
    small_shards = dict(
        ln1_gain=ln1_gain,
        ln1_bias=ln1_bias,
        qv_bias=qv_bias,
        out_bias=out_bias,
        ln2_gain=ln2_gain,
        ln2_bias=ln2_bias,
        fc_bias=fc_bias,
        proj_bias=proj_bias,
    )
    packed = jnp.concatenate([small_shards[n] for n in SMALL])[None]
    gathered = links.gather(packed, "zxyc")[:, 0]
    small = {}
    begin = 0
    for name in SMALL:
        size = small_shards[name].shape[0]
        small[name] = gathered[:, begin : begin + size].reshape(-1)
        begin += size

    def columns(shard, orders):
        step = shard.shape[1] // len(orders)
        parts = [
            links.gather(shard[:, i * step : (i + 1) * step], text)
            for i, text in enumerate(orders)
        ]
        return jnp.concatenate(parts, axis=2).reshape(-1, shard.shape[1])

    weights = (
        columns(qkv_weight, ("zxyc", "zyxc")),
        columns(out_weight, ("xzyc",)),
        columns(fc_weight, ("zxyc", "zyxc")),
        columns(proj_weight, ("zxyc", "zyxc")),
    )
    output, input_grad, grads, small_grads = step_on_sequence(
        weights,
        small,
        tokens[0],
        cotangent[0],
        thought_slots[0],
        thought_count[0],
        answer_start[0],
    )

    def spread(grad, orders):
        rows = grad.shape[0] // devices
        step = grad.shape[1] // len(orders)
        low = grad.astype(BF16).reshape(devices, rows, grad.shape[1])
        return jnp.concatenate(
            [
                links.scatter(low[:, :, i * step : (i + 1) * step], text)
                for i, text in enumerate(orders)
            ],
            axis=1,
        )

    qkv_g, out_g, fc_g, proj_g = grads
    proj_g = spread(proj_g, ("cyxz", "cxyz"))
    fc_g = spread(fc_g, ("cyxz", "cxyz"))
    out_g = spread(out_g, ("cyzx",))
    qkv_g = spread(qkv_g, ("cyxz", "cxyz"))
    low = jnp.concatenate(
        [small_grads[n].reshape(devices, 1, -1) for n in SMALL], axis=2
    ).astype(BF16)
    flat = links.scatter(low, "cyxz")[0]
    owned = {}
    begin = 0
    for name in SMALL:
        size = small_shards[name].shape[0]
        owned[name] = flat[begin : begin + size]
        begin += size
    return (
        output[None],
        input_grad[None],
        owned["ln1_gain"],
        owned["ln1_bias"],
        qkv_g,
        owned["qv_bias"],
        out_g,
        owned["out_bias"],
        owned["ln2_gain"],
        owned["ln2_bias"],
        fc_g,
        owned["fc_bias"],
        proj_g,
        owned["proj_bias"],
    )


def solution(mesh):
    links = Links({name: mesh.shape[name] for name in ("dp", "fsdp")})
    both = ("dp", "fsdp")
    cube, matrix, vector = P(both, None, None), P(both, None), P(both)
    weight_specs = (
        vector,
        vector,
        matrix,
        vector,
        matrix,
        vector,
        vector,
        vector,
        matrix,
        vector,
        matrix,
        vector,
    )

    def per_device(*args):
        return on_device(links, *args)

    return jax.shard_map(
        per_device,
        mesh=mesh,
        in_specs=(cube,) + weight_specs + (cube, matrix, vector, vector),
        out_specs=(cube, cube) + weight_specs,
        check_vma=False,
    )
```

```python
import functools
import math

import jax
import jax.numpy as jnp
from jax import lax
from jax.experimental import pallas as pl
from jax.experimental.pallas import tpu as pltpu
from jax.sharding import PartitionSpec as P

HD = 64
THOUGHTS = 2
PREFIX = 384
QUESTION = 256
SCALE = 0.125
EPSILON = 1e-05
BLOCK = 256
HEAD_ROWS = 16
WINDOW = 32
LANES = 128
PAIR = 2 * HD
NEG = -1e30

F32 = jnp.float32
BF16 = jnp.bfloat16
VMEM_LIMIT = 56 * 1024 * 1024


def cost(microseconds):
    return pl.CostEstimate(
        flops=int(microseconds * 1.15e9),
        bytes_accessed=int(microseconds * 3.6e6),
        transcendentals=0,
    )


def dot(a, b):
    return lax.dot_general(a, b, (((1,), (0,)), ((), ())), preferred_element_type=F32)


def dot_nt(a, b):
    return lax.dot_general(a, b, (((1,), (1,)), ((), ())), preferred_element_type=F32)


def dot_tn(a, b):
    return lax.dot_general(a, b, (((0,), (0,)), ((), ())), preferred_element_type=F32)


def bits_of(size):
    return [1 << i for i in reversed(range(int(math.log2(size))))]


class Links:
    def __init__(self, sizes):
        self.sizes = sizes
        self.canon = [("dp", b) for b in bits_of(sizes["dp"])] + [
            ("fsdp", b) for b in bits_of(sizes["fsdp"])
        ]
        dp_bits = [("dp", b) for b in bits_of(sizes["dp"])]
        f_bits = [("fsdp", b) for b in bits_of(sizes["fsdp"])]
        self.groups = {"x": dp_bits[-1:], "y": dp_bits[:-1], "z": f_bits[:-1], "c": f_bits[-1:]}

    def order(self, text):
        out = []
        for letter in text:
            out += self.groups[letter]
        return out

    def swap(self, value, stage):
        axis, bit = stage
        return lax.ppermute(value, axis, [(i, i ^ bit) for i in range(self.sizes[axis])])

    def mine(self, stage):
        axis, bit = stage
        return (lax.axis_index(axis) & bit) != 0

    def gather(self, shard, text, axis=0):
        return Gather(self, shard, text, axis).finish()

    def scatter(self, value, text):
        return Scatter(self, value, text)


class Gather:
    def __init__(self, links, shard, text, axis=0):
        self.links = links
        self.shape = shard.shape
        self.axis = axis
        self.todo = links.order(text)
        self.done = []
        self.buf = shard
        self.got = None

    def go(self):
        self.add()
        self.stage = self.todo.pop(0)
        self.got = self.links.swap(self.buf, self.stage)
        return self.buf

    def add(self):
        if self.got is not None:
            canon = self.links.canon
            place = sum(1 for d in self.done if canon.index(d) < canon.index(self.stage))
            high = self.links.mine(self.stage)
            pair = [jnp.where(high, self.got, self.buf), jnp.where(high, self.buf, self.got)]
            self.buf = jnp.stack(pair, axis=self.axis + place)
            self.done.append(self.stage)
            self.got = None
        return self.buf

    def finish(self):
        while self.todo:
            self.go()
        self.add()
        shape = self.shape
        return self.buf.reshape(shape[: self.axis] + (-1,) + shape[self.axis + 1 :])


class Scatter:
    def __init__(self, links, value, text):
        self.links = links
        self.left = list(links.canon)
        self.todo = list(reversed(links.order(text)))
        self.buf = value.reshape((2,) * len(self.left) + value.shape[1:])
        self.got = None

    def go(self):
        self.add()
        stage = self.todo.pop(0)
        place = self.left.index(stage)
        self.left.remove(stage)
        high = self.links.mine(stage).astype(jnp.int32)
        self.keep = lax.dynamic_index_in_dim(self.buf, high, place, keepdims=False)
        sent = lax.dynamic_index_in_dim(self.buf, 1 - high, place, keepdims=False)
        self.got = self.links.swap(sent, stage)
        return sent

    def add(self):
        if self.got is None:
            return self.buf
        self.buf = self.keep.astype(F32) + self.got.astype(F32)
        if self.left:
            self.buf = self.buf.astype(BF16)
        self.got = None
        return self.buf

    def finish(self):
        while self.todo:
            self.go()
            self.add()
        return self.buf


def join_after(swaps, *deps):
    for swap in swaps:
        swap.got = after(swap.got, *deps)
        swap.add()


def go_after(swaps, *deps):
    for swap in swaps:
        swap.buf = after(swap.buf, *deps)
    return tuple(swap.go() for swap in swaps)


def after(value, *deps):
    return lax.optimization_barrier((value, deps))[0]


def attend_kernel(info_ref, q_ref, k_ref, v_ref, o_ref, lse_ref):
    seq_len = q_ref.shape[0]
    slot = info_ref[0]
    keys = k_ref[...]
    values_t = v_ref[...].T
    lane = lax.broadcasted_iota(jnp.int32, (BLOCK, PAIR), 1)
    sub = lax.broadcasted_iota(jnp.int32, (PAIR, BLOCK), 0)
    key_pos = lax.broadcasted_iota(jnp.int32, (BLOCK, BLOCK), 0)
    row_pos = lax.broadcasted_iota(jnp.int32, (BLOCK, BLOCK), 1)
    causal = key_pos <= row_pos
    middle_pos = QUESTION + lax.broadcasted_iota(jnp.int32, (PREFIX - QUESTION, BLOCK), 0)
    is_slot = (middle_pos >= slot) & (middle_pos < slot + THOUGHTS)

    def hide(scores):
        if scores.shape[0] <= QUESTION:
            return scores
        middle = jnp.where(is_slot, NEG, scores[QUESTION:PREFIX])
        return jnp.concatenate([scores[:QUESTION], middle, scores[PREFIX:]], axis=0)

    for begin in range(0, seq_len, BLOCK):
        end = begin + BLOCK
        queries = q_ref[begin:end, :] * jnp.asarray(SCALE, BF16)
        parts = []
        for head in range(2):
            own = jnp.where((lane >= HD) == bool(head), queries, jnp.zeros_like(queries))
            scores = dot_nt(keys[:end], own)
            last = jnp.where(causal, scores[begin:], NEG)
            if begin:
                last = jnp.concatenate([scores[:begin], last], axis=0)
            scores = hide(last)
            peak = jnp.max(scores, axis=0, keepdims=True)
            expo = jnp.exp(scores - peak)
            total = jnp.sum(expo, axis=0, keepdims=True)
            mixed = dot(values_t[:, :end], expo.astype(BF16))
            parts.append(mixed / total)
            lse_ref[pl.ds(2 * pl.program_id(0) + head, 1), begin:end] = peak + jnp.log(total)
        o_ref[begin:end, :] = jnp.where(sub < HD, parts[0], parts[1]).T.astype(BF16)


def attend(info, qkv):
    _, seq_len, width = qkv.shape
    pairs = width // PAIR

    def columns(i):
        return pl.BlockSpec((None, seq_len, PAIR), lambda g, i=i: (i, 0, g))

    return pl.pallas_call(
        attend_kernel,
        grid=(pairs,),
        in_specs=[
            pl.BlockSpec(memory_space=pltpu.SMEM),
            *(columns(i) for i in range(3)),
        ],
        out_specs=[
            pl.BlockSpec((seq_len, PAIR), lambda g: (0, g)),
            pl.BlockSpec((HEAD_ROWS, seq_len), lambda g: (0, 0)),
        ],
        out_shape=[
            jax.ShapeDtypeStruct((seq_len, width), BF16),
            jax.ShapeDtypeStruct((HEAD_ROWS, seq_len), F32),
        ],
        compiler_params=pltpu.CompilerParams(vmem_limit_bytes=VMEM_LIMIT),
        cost_estimate=cost(12),
        name="attention_forward",
    )(info, qkv, qkv, qkv)


def attend_back_kernel(
    q_ref, k_ref, v_ref, o_ref, lse_ref, g_ref, out_ref, dk_acc, dv_acc
):
    seq_len = q_ref.shape[0]
    pair = pl.program_id(0)
    first_row = seq_len - g_ref.shape[0]
    keys = k_ref[...]
    values = v_ref[...]
    keys_t = keys.T
    lane = lax.broadcasted_iota(jnp.int32, (BLOCK, PAIR), 1)
    sub = lax.broadcasted_iota(jnp.int32, (PAIR, BLOCK), 0)
    key_pos = lax.broadcasted_iota(jnp.int32, (BLOCK, BLOCK), 0)
    row_pos = lax.broadcasted_iota(jnp.int32, (BLOCK, BLOCK), 1)
    causal = key_pos <= row_pos
    dk_acc[...] = jnp.zeros_like(dk_acc)
    dv_acc[...] = jnp.zeros_like(dv_acc)
    for begin in range(first_row, seq_len, BLOCK):
        end = begin + BLOCK
        local = begin - first_row
        queries = q_ref[begin:end, :] * jnp.asarray(SCALE, BF16)
        grads = g_ref[local : local + BLOCK, :]
        product_t = (grads.astype(F32) * o_ref[begin:end, :].astype(F32)).T
        parts = []
        for head in range(2):
            chosen = (lane >= HD) == bool(head)
            own = jnp.where(chosen, queries, jnp.zeros_like(queries))
            own_grad = jnp.where(chosen, grads, jnp.zeros_like(grads))
            delta = jnp.sum(product_t[head * HD : (head + 1) * HD], axis=0, keepdims=True)
            lse = lse_ref[pl.ds(2 * pair + head, 1), begin:end]
            total = None
            for low, high in ((0, begin), (begin, end)):
                scores = dot_nt(keys[low:high], own)
                if high == end:
                    scores = jnp.where(causal, scores, NEG)
                probs = jnp.exp(scores - lse)
                prob_grad = dot_nt(values[low:high], own_grad)
                score_grad = (probs * (prob_grad - delta)).astype(BF16)
                dv_acc[low:high, :] += dot(probs.astype(BF16), own_grad)
                dk_acc[low:high, :] += dot(score_grad, own)
                part = dot(keys_t[:, low:high], score_grad)
                total = part if total is None else total + part
            parts.append(total)
        mine = jnp.where(sub < HD, parts[0], parts[1]).T * SCALE
        out_ref[0, begin:end, :] = mine.astype(BF16)
    out_ref[0, :first_row, :] = jnp.zeros((first_row, PAIR), BF16)
    out_ref[1] = dk_acc[...].astype(BF16)
    out_ref[2] = dv_acc[...].astype(BF16)


def attend_back(qkv, mixed_low, lse, mixed_grad):
    _, seq_len, width = qkv.shape
    rows = mixed_grad.shape[0]

    def columns(i):
        return pl.BlockSpec((None, seq_len, PAIR), lambda g, i=i: (i, 0, g))

    late = pl.BlockSpec((rows, PAIR), lambda g: (0, g))
    return pl.pallas_call(
        attend_back_kernel,
        grid=(width // PAIR,),
        in_specs=[
            *(columns(i) for i in range(3)),
            pl.BlockSpec((seq_len, PAIR), lambda g: (0, g)),
            pl.BlockSpec((HEAD_ROWS, seq_len), lambda g: (0, 0)),
            late,
        ],
        out_specs=pl.BlockSpec((3, seq_len, PAIR), lambda g: (0, 0, g)),
        out_shape=jax.ShapeDtypeStruct((3, seq_len, width), BF16),
        scratch_shapes=[pltpu.VMEM((seq_len, PAIR), F32), pltpu.VMEM((seq_len, PAIR), F32)],
        compiler_params=pltpu.CompilerParams(vmem_limit_bytes=VMEM_LIMIT),
        cost_estimate=cost(13),
        name="attention_backward",
    )(qkv, qkv, qkv, mixed_low, lse, mixed_grad)


def add_slots_kernel(
    info_ref, q_ref, qkv_ref, o_ref, lse_ref, rows_ref, row_lse_ref, mixed_ref, out_lse_ref
):
    seq_len, width = o_ref.shape
    rows = seq_len - QUESTION
    slot = info_ref[0]
    row_pos = QUESTION + lax.broadcasted_iota(jnp.int32, (HEAD_ROWS, rows), 1)
    late_q = q_ref[QUESTION:, :]
    lse = lse_ref[:, QUESTION:]
    scores = []
    values = []
    top = lse
    for j in range(THOUGHTS):
        local = slot + j - QUESTION
        key = by_head(pick(qkv_ref[1, QUESTION:PREFIX, :], local) * SCALE, HEAD_ROWS)
        values.append(pick(qkv_ref[2, QUESTION:PREFIX, :], local))
        score = jnp.where(row_pos >= slot + j, dot_nt(key.astype(BF16), late_q), NEG)
        scores.append(score)
        top = jnp.maximum(top, score)
    whole_sum = jnp.exp(lse - top)
    for score in scores:
        whole_sum = whole_sum + jnp.exp(score - top)
    new_lse = top + jnp.log(whole_sum)
    ones = by_head(jnp.ones((1, width), F32), HEAD_ROWS).astype(BF16)
    share = jnp.exp(lse - new_lse)
    high = share.astype(BF16)
    mixed = o_ref[QUESTION:, :].astype(F32) * (
        dot_tn(high, ones) + dot_tn((share - high.astype(F32)).astype(BF16), ones)
    )
    for score, value in zip(scores, values):
        mixed = mixed + dot_tn(jnp.exp(score - new_lse).astype(BF16), ones) * value
    mixed_ref[:QUESTION, :] = o_ref[:QUESTION, :]
    mixed_ref[PREFIX:, :] = mixed[PREFIX - QUESTION :].astype(BF16)
    out_lse_ref[:, :QUESTION] = lse_ref[:, :QUESTION]
    column = lax.broadcasted_iota(jnp.int32, (HEAD_ROWS, PREFIX - QUESTION), 1)
    middle = new_lse[:, : PREFIX - QUESTION]
    block = mixed[: PREFIX - QUESTION].astype(BF16)
    for j in range(THOUGHTS):
        local = slot + j - QUESTION
        block = put(block, local, rows_ref[1 + j : 2 + j, :])
        middle = jnp.where(column == local, row_lse_ref[:, 1 + j : 2 + j], middle)
    mixed_ref[QUESTION:PREFIX, :] = block
    out_lse_ref[:, QUESTION:PREFIX] = middle
    out_lse_ref[:, PREFIX:] = new_lse[:, PREFIX - QUESTION :]


def add_slots(info, qkv, mixed_low, lse, slot_rows, slot_lse):
    seq_len, width = mixed_low.shape
    return pl.pallas_call(
        add_slots_kernel,
        grid=(1,),
        in_specs=[
            pl.BlockSpec(memory_space=pltpu.SMEM),
            pl.BlockSpec((None, seq_len, width), lambda i: (0, 0, 0)),
            pl.BlockSpec((3, PREFIX, width), lambda i: (0, 0, 0)),
            whole(mixed_low),
            whole(lse),
            whole(slot_rows),
            whole(slot_lse),
        ],
        out_specs=[whole(mixed_low), whole(lse)],
        out_shape=[
            jax.ShapeDtypeStruct(mixed_low.shape, BF16),
            jax.ShapeDtypeStruct(lse.shape, F32),
        ],
        compiler_params=pltpu.CompilerParams(vmem_limit_bytes=VMEM_LIMIT),
        cost_estimate=cost(3),
        name="attention_add_slots",
    )(info, qkv, qkv, mixed_low, lse, slot_rows, slot_lse)


def row_norm(row, gain, bias):
    mean = jnp.mean(row, axis=-1, keepdims=True)
    centred = row - mean
    inverse = lax.rsqrt(jnp.mean(centred * centred, axis=-1, keepdims=True) + EPSILON)
    normed = centred * inverse
    return normed * gain + bias, normed, inverse


def row_norm_back(incoming, normed, inverse, gain):
    scaled = incoming * gain
    inner = (
        scaled
        - jnp.mean(scaled, axis=-1, keepdims=True)
        - normed * jnp.mean(scaled * normed, axis=-1, keepdims=True)
    )
    return inner * inverse


GELU_A = 0.7978845608028654
GELU_B = 0.044715


def gelu(pre):
    return 0.5 * pre * (1.0 + jnp.tanh(GELU_A * (pre + GELU_B * pre * pre * pre)))


def gelu_slope(pre):
    square = pre * pre
    curve = jnp.tanh(GELU_A * pre * (1.0 + GELU_B * square))
    return 0.5 * (1.0 + curve) + 0.5 * pre * (1.0 - curve * curve) * GELU_A * (
        1.0 + 3.0 * GELU_B * square
    )


def widen(row):
    return jnp.broadcast_to(row, (8, row.shape[1])).astype(BF16)


def pick(block, index):
    rows = lax.broadcasted_iota(jnp.int32, block.shape, 0)
    return jnp.sum(jnp.where(rows == index, block.astype(F32), 0.0), axis=0, keepdims=True)


def put(block, index, row):
    rows = lax.broadcasted_iota(jnp.int32, block.shape, 0)
    return jnp.where(rows == index, row.astype(block.dtype), block)


def by_head(row, heads):
    shape = (heads, row.shape[1])
    lane_head = lax.broadcasted_iota(jnp.int32, shape, 1) // HD
    return jnp.where(lane_head == lax.broadcasted_iota(jnp.int32, shape, 0), row, 0.0)


def heads_only(block):
    lane_head = lax.broadcasted_iota(jnp.int32, block.shape, 1) // HD
    own = lane_head == lax.broadcasted_iota(jnp.int32, block.shape, 0)
    return jnp.sum(jnp.where(own, block, 0.0), axis=0, keepdims=True)


def through_blocks(row, ref):
    wide = widen(row)
    return jnp.concatenate([dot(wide, ref[j])[0:1] for j in range(ref.shape[0])], axis=1)


def thoughts_kernel(
    info_ref,
    tok_ref,
    qkv_ref,
    wqk_ref,
    wvo_ref,
    wfc_ref,
    wproj_ref,
    vec_ref,
    fcb_ref,
    qkvb_ref,
    hid_ref,
    qkvm_ref,
    pre_ref,
    prob_ref,
    res_ref,
    rows_ref,
    row_lse_ref,
):
    width = tok_ref.shape[1]
    blocks = wfc_ref.shape[0]
    ln1_gain, ln1_bias, out_bias, ln2_gain, ln2_bias, proj_bias = (
        vec_ref[i : i + 1, :] for i in range(6)
    )
    slot = info_ref[0]
    count = info_ref[1]
    hid_ref[...] = tok_ref[...].astype(F32)
    qkvm_ref[...] = qkv_ref[:, QUESTION:PREFIX, :]
    rows_ref[...] = jnp.zeros_like(rows_ref)
    column = lax.broadcasted_iota(jnp.int32, row_lse_ref.shape, 1)
    row_lse_ref[...] = jnp.zeros_like(row_lse_ref)
    hidden_row = pick(hid_ref[...], slot - 1 - QUESTION)
    for step in range(THOUGHTS + 1):
        at = slot - 1 + step
        qkv_row = pick(qkvm_ref[0], at - QUESTION)
        query = by_head(qkv_row * SCALE, HEAD_ROWS).astype(BF16)
        scores = jnp.concatenate(
            [
                dot_nt(query, qkv_ref[1, :QUESTION, :]),
                dot_nt(query, qkvm_ref[1]),
            ],
            axis=1,
        )
        key_pos = lax.broadcasted_iota(jnp.int32, scores.shape, 1)
        scores = jnp.where(key_pos <= at, scores, NEG)
        peak = jnp.max(scores, axis=1, keepdims=True)
        expo = jnp.exp(scores - peak)
        total = jnp.sum(expo, axis=1, keepdims=True)
        probs = expo / total
        low = probs.astype(BF16)
        mixed = heads_only(
            dot(low[:, :QUESTION], qkv_ref[2, :QUESTION, :])
            + dot(low[:, QUESTION:], qkvm_ref[2])
        )
        rows_ref[step : step + 1, :] = mixed
        row_lse_ref[...] = jnp.where(column == step, peak + jnp.log(total), row_lse_ref[...])
        if step == THOUGHTS:
            break
        prob_ref[step * HEAD_ROWS : (step + 1) * HEAD_ROWS, :] = probs
        resid = hidden_row + dot(widen(mixed), wvo_ref[1])[0:1] + out_bias
        res_ref[step : step + 1, :] = resid
        second, _, _ = row_norm(resid, ln2_gain, ln2_bias)
        pre = through_blocks(second, wfc_ref) + fcb_ref[0:1, :]
        pre_ref[step : step + 1, :] = pre
        act = gelu(pre)
        fed = resid + proj_bias
        for j in range(blocks):
            fed = fed + dot(widen(act[:, j * width : (j + 1) * width]), wproj_ref[j])[0:1]
        first, _, _ = row_norm(fed, ln1_gain, ln1_bias)
        first = widen(first)
        hidden_row = fed
        spot = jnp.where(step < count, slot + step - QUESTION, -1)
        hid_ref[...] = put(hid_ref[...], spot, fed)
        for i in range(3):
            span = slice(i * width, (i + 1) * width)
            weight = wqk_ref[i] if i < 2 else wvo_ref[0]
            new_row = dot(first, weight)[0:1] + qkvb_ref[0:1, span]
            qkvm_ref[i] = put(qkvm_ref[i], spot, new_row)


def whole(array):
    zeros = (0,) * array.ndim
    return pl.BlockSpec(array.shape, lambda i, zeros=zeros: zeros)


def weight_specs(blocks, width):
    near = pl.BlockSpec((2, width, width), lambda i: (0, 0, 0))
    return [
        near,
        near,
        pl.BlockSpec((blocks, width, width), lambda i: (0, 0, 0)),
        pl.BlockSpec((blocks, width, width), lambda i: (1, 0, 0)),
    ]


def weight_operands(weights):
    query_key, value_out, far = weights
    return query_key, value_out, far, far


def thoughts_forward(info, tokens, qkv, weights, vec, fc_bias, qkv_bias):
    width = tokens.shape[1]
    middle = PREFIX - QUESTION
    out_shape = [
        jax.ShapeDtypeStruct((middle, width), F32),
        jax.ShapeDtypeStruct((3, middle, width), BF16),
        jax.ShapeDtypeStruct((8, fc_bias.shape[1]), F32),
        jax.ShapeDtypeStruct((THOUGHTS * HEAD_ROWS, PREFIX), F32),
        jax.ShapeDtypeStruct((8, width), F32),
        jax.ShapeDtypeStruct((8, width), F32),
        jax.ShapeDtypeStruct((HEAD_ROWS, LANES), F32),
    ]
    return pl.pallas_call(
        thoughts_kernel,
        grid=(1,),
        in_specs=[
            pl.BlockSpec(memory_space=pltpu.SMEM),
            pl.BlockSpec((middle, width), lambda i: (QUESTION // middle, 0)),
            pl.BlockSpec((3, PREFIX, width), lambda i: (0, 0, 0)),
            *weight_specs(fc_bias.shape[1] // width, width),
            whole(vec),
            whole(fc_bias),
            whole(qkv_bias),
        ],
        out_specs=[whole(s) for s in out_shape],
        out_shape=out_shape,
        compiler_params=pltpu.CompilerParams(vmem_limit_bytes=VMEM_LIMIT),
        cost_estimate=cost(7),
        name="thought_rows_forward",
    )(info, tokens, qkv, *weight_operands(weights), vec, fc_bias, qkv_bias)


def thoughts_back_kernel(
    info_ref,
    hid_ref,
    qkv_ref,
    late_q_ref,
    mixed_ref,
    lse_ref,
    pre_ref,
    prob_ref,
    res_ref,
    wqk_ref,
    wvo_ref,
    wfc_ref,
    wproj_ref,
    vec_ref,
    mg_in,
    rg_in,
    sum_ref,
    fac_ref,
    mg_out,
    rg_out,
    mg_ref,
    rg_win,
    sems,
):
    width = hid_ref.shape[1]
    blocks = wfc_ref.shape[0]
    units = blocks * width
    rows = mg_ref.shape[0]
    ln1_gain, ln1_bias, _, ln2_gain, ln2_bias, _ = (vec_ref[i : i + 1, :] for i in range(6))
    slot = info_ref[0]
    count = info_ref[1]
    base = pl.multiple_of(((slot - 1 - QUESTION) // 16) * 16, 16)

    def window(ref):
        return ref.at[pl.ds(base, WINDOW)]

    loads = [
        pltpu.make_async_copy(mg_in, mg_ref, sems.at[0]),
        pltpu.make_async_copy(window(rg_in), rg_win, sems.at[1]),
    ]
    for copy in loads:
        copy.start()
    for copy in loads:
        copy.wait()

    late_q = late_q_ref[QUESTION:, :]
    mixed_grad = mg_ref[...]
    product = mixed_grad.astype(F32) * mixed_ref[QUESTION:, :].astype(F32)
    high = product.astype(BF16)
    ones = by_head(jnp.ones((1, width), F32), HEAD_ROWS).astype(BF16)
    delta = dot_nt(ones, high) + dot_nt(ones, (product - high.astype(F32)).astype(BF16))
    row_pos = QUESTION + lax.broadcasted_iota(jnp.int32, (HEAD_ROWS, rows), 1)
    lse = lse_ref[:, QUESTION:]

    def at_slot(at):
        local = at - QUESTION
        key = by_head(pick(qkv_ref[1, QUESTION:PREFIX, :], local) * SCALE, HEAD_ROWS)
        value = by_head(pick(qkv_ref[2, QUESTION:PREFIX, :], local), HEAD_ROWS)
        scores = dot_nt(key.astype(BF16), late_q)
        probs = jnp.where(row_pos >= at, jnp.exp(jnp.minimum(scores - lse, 0.0)), 0.0)
        prob_grad = dot_nt(value.astype(BF16), mixed_grad)
        score_grad = (probs * (prob_grad - delta)).astype(BF16)
        return (
            heads_only(dot(score_grad, late_q)) * SCALE,
            heads_only(dot(probs.astype(BF16), mixed_grad)),
        )

    def through_first(at, query_grad, key_grad, value_grad):
        first_grad = (
            dot_nt(widen(query_grad), wqk_ref[0])
            + dot_nt(widen(key_grad), wqk_ref[1])
            + dot_nt(widen(value_grad), wvo_ref[0])
        )[0:1]
        _, normed, inverse = row_norm(hid_ref[pl.ds(at - QUESTION, 1), :], ln1_gain, ln1_bias)
        return row_norm_back(first_grad, normed, inverse, ln1_gain)

    sum_ref[...] = jnp.zeros_like(sum_ref)
    fac_ref[...] = jnp.zeros_like(fac_ref)
    carried = through_first(slot + 1, jnp.zeros((1, width), F32), *at_slot(slot + 1))
    for step in reversed(range(THOUGHTS)):
        at = slot - 1 + step
        upstream = jnp.where(step < count, carried, 0.0)
        low = widen(upstream)
        act_grad = jnp.concatenate([dot_nt(low, wproj_ref[j])[0:1] for j in range(blocks)], axis=1)
        pre = pre_ref[step : step + 1, :]
        pre_grad = (act_grad * gelu_slope(pre)).astype(BF16).astype(F32)
        second_grad = jnp.zeros((1, width), F32)
        for j in range(blocks):
            piece = pre_grad[:, j * width : (j + 1) * width]
            second_grad = second_grad + dot_nt(widen(piece), wfc_ref[j])[0:1]
        second, normed, inverse = row_norm(res_ref[step : step + 1, :], ln2_gain, ln2_bias)
        resid_grad = upstream + row_norm_back(second_grad, normed, inverse, ln2_gain)
        mixed_row = dot_nt(widen(resid_grad), wvo_ref[1])[0:1]
        local = at - QUESTION
        rg_win[...] = put(rg_win[...], local - base, resid_grad)
        mg_ref[: PREFIX - QUESTION, :] = put(mg_ref[: PREFIX - QUESTION, :], local, mixed_row)
        up_low = upstream.astype(BF16).astype(F32)
        sum_ref[0:1, :units] += pre_grad
        sum_ref[1:2, :width] += second_grad * normed
        sum_ref[2:3, :width] += second_grad
        sum_ref[3:4, :width] += up_low
        sum_ref[4:5, :width] += resid_grad.astype(BF16).astype(F32)
        fac_ref[step : step + 1, :units] = gelu(pre)
        fac_ref[step : step + 1, units : units + width] = up_low
        fac_ref[step : step + 1, units + width : units + 2 * width] = second
        fac_ref[step : step + 1, units + 2 * width :] = pre_grad
        if step:
            own_grad = by_head(mixed_row, HEAD_ROWS).astype(BF16)
            query = by_head(pick(qkv_ref[0, QUESTION:PREFIX, :], local) * SCALE, HEAD_ROWS)
            query = query.astype(BF16)
            probs = prob_ref[step * HEAD_ROWS : (step + 1) * HEAD_ROWS, :]
            prob_grad = dot_nt(own_grad, qkv_ref[2])
            own_delta = jnp.sum(prob_grad * probs, axis=1, keepdims=True)
            score_grad = (probs * (prob_grad - own_delta)).astype(BF16)
            query_grad = heads_only(dot(score_grad, qkv_ref[1])) * SCALE
            key_grad, value_grad = at_slot(at)
            own = lax.broadcasted_iota(jnp.int32, probs.shape, 1) == at
            score_own = jnp.sum(jnp.where(own, score_grad.astype(F32), 0.0), axis=1, keepdims=True)
            prob_own = jnp.sum(jnp.where(own, probs, 0.0), axis=1, keepdims=True)
            key_grad += jnp.sum(score_own * query.astype(F32), axis=0, keepdims=True)
            value_grad += jnp.sum(prob_own * own_grad.astype(F32), axis=0, keepdims=True)
            carried = resid_grad + through_first(at, query_grad, key_grad, value_grad)
    stores = [
        pltpu.make_async_copy(mg_ref, mg_out, sems.at[0]),
        pltpu.make_async_copy(rg_win, window(rg_out), sems.at[1]),
    ]
    for copy in stores:
        copy.start()
    for copy in stores:
        copy.wait()


SUM_ROWS = ("fc_bias", "ln2_gain", "ln2_bias", "proj_bias", "out_bias")


def thoughts_back(info, hidden_mid, qkv, mixed_low, lse, saved, weights, vec, mixed_grad, resid_grad):
    width = hidden_mid.shape[1]
    blocks = weights[2].shape[0] // 2
    units = blocks * width
    seq_len = qkv.shape[1]
    anywhere = pl.BlockSpec(memory_space=pl.ANY)
    out_shape = [
        jax.ShapeDtypeStruct((8, units), F32),
        jax.ShapeDtypeStruct((8, 2 * units + 2 * width), F32),
        jax.ShapeDtypeStruct(mixed_grad.shape, BF16),
        jax.ShapeDtypeStruct(resid_grad.shape, F32),
    ]
    return pl.pallas_call(
        thoughts_back_kernel,
        grid=(1,),
        in_specs=[
            pl.BlockSpec(memory_space=pltpu.SMEM),
            whole(hidden_mid),
            pl.BlockSpec((3, PREFIX, width), lambda i: (0, 0, 0)),
            pl.BlockSpec((None, seq_len, width), lambda i: (0, 0, 0)),
            whole(mixed_low),
            whole(lse),
            *(whole(x) for x in saved),
            *weight_specs(blocks, width),
            whole(vec),
            anywhere,
            anywhere,
        ],
        out_specs=[whole(out_shape[0]), whole(out_shape[1]), anywhere, anywhere],
        out_shape=out_shape,
        input_output_aliases={14: 2, 15: 3},
        scratch_shapes=[
            pltpu.VMEM(mixed_grad.shape, BF16),
            pltpu.VMEM((WINDOW, width), F32),
            pltpu.SemaphoreType.DMA((2,)),
        ],
        compiler_params=pltpu.CompilerParams(vmem_limit_bytes=VMEM_LIMIT),
        cost_estimate=cost(12),
        name="thought_rows_backward",
    )(
        info,
        hidden_mid,
        qkv,
        qkv,
        mixed_low,
        lse,
        *saved,
        *weight_operands(weights),
        vec,
        mixed_grad,
        resid_grad,
    )


def forward_kernel(
    hid_ref, mixed_ref, wvo_ref, wfc_ref, wproj_ref, vec_ref, fcb_ref, out_ref, second_ref,
    act_ref, slope_ref, normed_ref, inverse_ref,
):
    width = hid_ref.shape[1]
    out_bias, ln2_gain, ln2_bias, proj_bias = (vec_ref[i : i + 1, :] for i in range(2, 6))
    resid = hid_ref[...] + dot(mixed_ref[...], wvo_ref[0]) + out_bias
    second, normed, inverse = row_norm(resid, ln2_gain, ln2_bias)
    low = second.astype(BF16)
    second_ref[...] = low
    normed_ref[...] = normed
    inverse_ref[...] = jnp.broadcast_to(inverse, inverse_ref.shape)
    total = resid + proj_bias
    for j in range(wfc_ref.shape[0]):
        span = slice(j * width, (j + 1) * width)
        pre = dot(low, wfc_ref[j]) + fcb_ref[:, span]
        square = pre * pre
        curve = jnp.tanh(GELU_A * pre * (1.0 + GELU_B * square))
        half = 0.5 + 0.5 * curve
        act = (pre * half).astype(BF16)
        rise = 0.5 * GELU_A + (1.5 * GELU_A * GELU_B) * square
        slope_ref[:, span] = (half + pre * rise * (1.0 - curve * curve)).astype(BF16)
        act_ref[:, span] = act
        total = total + dot(act, wproj_ref[j])
    out_ref[...] = total.astype(BF16)


def feed_forward(hidden, mixed_low, weights, vec, fc_bias):
    _, value_out, far, _ = weight_operands(weights)
    seq_len, width = hidden.shape
    units = fc_bias.shape[1]

    def rows(columns):
        return pl.BlockSpec((BLOCK, columns), lambda i: (i, 0))

    return pl.pallas_call(
        forward_kernel,
        grid=(seq_len // BLOCK,),
        in_specs=[
            rows(width),
            rows(width),
            pl.BlockSpec((1, width, width), lambda i: (1, 0, 0)),
            *weight_specs(units // width, width)[2:],
            whole(vec),
            whole(fc_bias),
        ],
        out_specs=[rows(width), rows(width), rows(units), rows(units), rows(width), rows(LANES)],
        out_shape=[
            jax.ShapeDtypeStruct((seq_len, width), BF16),
            jax.ShapeDtypeStruct((seq_len, width), BF16),
            jax.ShapeDtypeStruct((seq_len, units), BF16),
            jax.ShapeDtypeStruct((seq_len, units), BF16),
            jax.ShapeDtypeStruct((seq_len, width), F32),
            jax.ShapeDtypeStruct((seq_len, LANES), F32),
        ],
        compiler_params=pltpu.CompilerParams(vmem_limit_bytes=VMEM_LIMIT),
        cost_estimate=cost(12),
        name="feed_forward",
    )(hidden, mixed_low, value_out, far, far, vec, fc_bias)


def back_kernel(
    up_ref, slope_ref, normed_ref, inverse_ref, wvo_ref, wfc_ref, wproj_ref, vec_ref, pg_ref,
    rg_ref, mg_ref, sum_ref,
):
    width = up_ref.shape[1]
    blocks = wfc_ref.shape[0]
    units = blocks * width
    ln2_gain = vec_ref[3:4, :]

    @pl.when(pl.program_id(0) == 0)
    def _():
        sum_ref[...] = jnp.zeros_like(sum_ref)

    up = up_ref[...]
    second_grad = jnp.zeros(up.shape, F32)
    for j in range(blocks):
        span = slice(j * width, (j + 1) * width)
        pre_grad = (dot_nt(up, wproj_ref[j]) * slope_ref[:, span].astype(F32)).astype(BF16)
        pg_ref[:, span] = pre_grad
        sum_ref[0:1, span] += jnp.sum(pre_grad.astype(F32), axis=0, keepdims=True)
        second_grad = second_grad + dot_nt(pre_grad, wfc_ref[j])
    normed = normed_ref[...]
    up32 = up.astype(F32)
    resid_grad = up32 + row_norm_back(second_grad, normed, inverse_ref[:, :1], ln2_gain)
    attn_grad = resid_grad.astype(BF16)
    rg_ref[...] = resid_grad
    mg_ref[...] = dot_nt(attn_grad, wvo_ref[0]).astype(BF16)
    sum_ref[1:2, :width] += jnp.sum(second_grad * normed, axis=0, keepdims=True)
    sum_ref[2:3, :width] += jnp.sum(second_grad, axis=0, keepdims=True)
    sum_ref[3:4, :width] += jnp.sum(up32, axis=0, keepdims=True)
    sum_ref[4:5, :width] += jnp.sum(attn_grad.astype(F32), axis=0, keepdims=True)


def feed_back(upstream_low, slope, normed, inverse, weights, vec):
    _, value_out, far, _ = weight_operands(weights)
    count, width = upstream_low.shape
    units = slope.shape[1]
    skip = QUESTION // BLOCK

    def rows(columns, begin=0):
        return pl.BlockSpec((BLOCK, columns), lambda i, begin=begin: (i + begin, 0))

    sums = jax.ShapeDtypeStruct((8, units), F32)
    return pl.pallas_call(
        back_kernel,
        grid=(count // BLOCK,),
        in_specs=[
            rows(width),
            rows(units, skip),
            rows(width, skip),
            rows(LANES, skip),
            pl.BlockSpec((1, width, width), lambda i: (1, 0, 0)),
            *weight_specs(units // width, width)[2:],
            whole(vec),
        ],
        out_specs=[rows(units), rows(width), rows(width), whole(sums)],
        out_shape=[
            jax.ShapeDtypeStruct((count, units), BF16),
            jax.ShapeDtypeStruct((count, width), F32),
            jax.ShapeDtypeStruct((count, width), BF16),
            sums,
        ],
        compiler_params=pltpu.CompilerParams(vmem_limit_bytes=VMEM_LIMIT),
        cost_estimate=cost(9),
        name="feed_backward",
    )(upstream_low, slope, normed, inverse, value_out, far, far, vec)


def first_back_kernel(
    info_ref, hid_ref, grad_ref, rg_ref, wqk_ref, wvo_ref, vec_ref, in_ref, first_ref, sum_ref
):
    rows, width = hid_ref.shape
    step = pl.program_id(0)
    slot = info_ref[0]
    count = info_ref[1]

    @pl.when(step == 0)
    def _():
        sum_ref[...] = jnp.zeros_like(sum_ref)

    gain = vec_ref[0:1, :]
    first, normed, inverse = row_norm(hid_ref[...], gain, vec_ref[1:2, :])
    first_ref[...] = first.astype(BF16)
    first_grad = jnp.zeros((rows, width), F32)
    for i in range(3):
        weight = wqk_ref[i] if i < 2 else wvo_ref[0]
        first_grad = first_grad + dot_nt(grad_ref[i], weight)
        if i != 1:
            at = 2 + i // 2
            columns = jnp.sum(grad_ref[i].astype(F32), axis=0, keepdims=True)
            sum_ref[at : at + 1, :] += columns
    sum_ref[0:1, :] += jnp.sum(first_grad * normed, axis=0, keepdims=True)
    sum_ref[1:2, :] += jnp.sum(first_grad, axis=0, keepdims=True)
    late = (step >= QUESTION // BLOCK).astype(F32)
    grad = row_norm_back(first_grad, normed, inverse, gain) + late * rg_ref[...]
    position = step * rows + lax.broadcasted_iota(jnp.int32, (rows, 1), 0)
    replaced = (position >= slot) & (position < slot + jnp.minimum(count, THOUGHTS))
    in_ref[...] = jnp.where(replaced, 0.0, grad)


def first_back(info, hidden, qkv_grad, resid_grad, weights, vec):
    seq_len, width = hidden.shape
    skip = QUESTION // BLOCK
    sums = jax.ShapeDtypeStruct((8, width), F32)
    rows = pl.BlockSpec((BLOCK, width), lambda i: (i, 0))
    return pl.pallas_call(
        first_back_kernel,
        grid=(seq_len // BLOCK,),
        in_specs=[
            pl.BlockSpec(memory_space=pltpu.SMEM),
            rows,
            pl.BlockSpec((3, BLOCK, width), lambda i: (0, i, 0)),
            pl.BlockSpec((BLOCK, width), lambda i: (jnp.maximum(i - skip, 0), 0)),
            pl.BlockSpec((2, width, width), lambda i: (0, 0, 0)),
            pl.BlockSpec((1, width, width), lambda i: (0, 0, 0)),
            whole(vec),
        ],
        out_specs=[rows, rows, whole(sums)],
        out_shape=[
            jax.ShapeDtypeStruct((seq_len, width), F32),
            jax.ShapeDtypeStruct((seq_len, width), BF16),
            sums,
        ],
        compiler_params=pltpu.CompilerParams(vmem_limit_bytes=VMEM_LIMIT),
        cost_estimate=cost(5),
        name="first_norm_backward",
    )(info, hidden, qkv_grad, resid_grad, weights[0], weights[1], vec)


def first_kernel(tok_ref, wqk_ref, wvo_ref, vec_ref, qkvb_ref, qkv_ref):
    width = tok_ref.shape[1]
    first, _, _ = row_norm(tok_ref[...].astype(F32), vec_ref[0:1, :], vec_ref[1:2, :])
    first = first.astype(BF16)
    for i in range(3):
        weight = wqk_ref[i] if i < 2 else wvo_ref[0]
        span = slice(i * width, (i + 1) * width)
        qkv_ref[i] = (dot(first, weight) + qkvb_ref[:, span]).astype(BF16)


def first_forward(tokens, query_key, value_out, vec, qkv_bias):
    seq_len, width = tokens.shape
    return pl.pallas_call(
        first_kernel,
        grid=(seq_len // BLOCK,),
        in_specs=[
            pl.BlockSpec((BLOCK, width), lambda i: (i, 0)),
            pl.BlockSpec((2, width, width), lambda i: (0, 0, 0)),
            pl.BlockSpec((1, width, width), lambda i: (0, 0, 0)),
            whole(vec),
            whole(qkv_bias),
        ],
        out_specs=pl.BlockSpec((3, BLOCK, width), lambda i: (0, i, 0)),
        out_shape=jax.ShapeDtypeStruct((3, seq_len, width), BF16),
        compiler_params=pltpu.CompilerParams(vmem_limit_bytes=VMEM_LIMIT),
        cost_estimate=cost(4),
        name="first_norm_forward",
    )(tokens, query_key, value_out, vec, qkv_bias)


def group_of(blocks, own):
    each = blocks * own
    group = LANES // math.gcd(LANES, each)
    size = group * each
    row = lax.broadcasted_iota(jnp.int32, (size, size), 0)
    column = lax.broadcasted_iota(jnp.int32, (size, size), 1)
    device, block, i = row // each, row % each // own, row % own
    return group, column == block * (group * own) + device * own + i


def split_units_kernel(blocks, fc_ref, out_ref):
    own = fc_ref.shape[0]
    width = out_ref.shape[2]
    group, swap = group_of(blocks, own)
    swap = swap.astype(BF16)
    size = group * blocks * own
    span = group * own
    for g in range(width // span):
        part = dot(fc_ref[:, g * size : (g + 1) * size], swap)
        for j in range(blocks):
            piece = part[:, j * span : (j + 1) * span]
            out_ref[j, :, g * span : (g + 1) * span] = piece.astype(BF16)


def split_units(fc_shard, blocks):
    own, units = fc_shard.shape
    return pl.pallas_call(
        functools.partial(split_units_kernel, blocks),
        out_shape=jax.ShapeDtypeStruct((blocks, own, units // blocks), BF16),
        compiler_params=pltpu.CompilerParams(vmem_limit_bytes=VMEM_LIMIT),
        name="units_split",
    )(fc_shard)


def row_terms_kernel(index_ref, fac_ref, proj_ref, fc_ref, proj_out, fc_out):
    blocks, own, width = proj_ref.shape
    units = blocks * width
    shape = (width, own)
    mine = lax.broadcasted_iota(jnp.int32, shape, 0) - index_ref[0] * own
    select = (mine == lax.broadcasted_iota(jnp.int32, shape, 1)).astype(BF16)
    upstream = fac_ref[:, units : units + width]
    terms = []
    second = dot(fac_ref[:, units + width : units + 2 * width], select).astype(BF16)
    for j in range(blocks):
        act = dot(fac_ref[:, j * width : (j + 1) * width], select).astype(BF16)
        proj_out[j] = proj_ref[j] + dot_tn(act, upstream)
        begin = units + 2 * width + j * width
        terms.append(fc_ref[j] + dot_tn(second, fac_ref[:, begin : begin + width]))
    group, swap = group_of(blocks, own)
    swap = swap.astype(BF16)
    size = group * blocks * own
    span = group * own
    for g in range(width // span):
        part = jnp.concatenate([t[:, g * span : (g + 1) * span] for t in terms], axis=1)
        total = jnp.zeros_like(part)
        for _ in range(3):
            piece = part.astype(BF16)
            part = part - piece.astype(F32)
            total = total + dot_nt(piece, swap)
        fc_out[:, g * size : (g + 1) * size] = total


def row_terms(index, factors, proj_sum, fc_sum):
    blocks, own, width = fc_sum.shape
    out_shape = [
        jax.ShapeDtypeStruct(proj_sum.shape, F32),
        jax.ShapeDtypeStruct((own, blocks * width), F32),
    ]
    return pl.pallas_call(
        row_terms_kernel,
        grid=(1,),
        in_specs=[
            pl.BlockSpec(memory_space=pltpu.SMEM),
            whole(factors),
            whole(proj_sum),
            whole(fc_sum),
        ],
        out_specs=[whole(x) for x in out_shape],
        out_shape=out_shape,
        compiler_params=pltpu.CompilerParams(vmem_limit_bytes=VMEM_LIMIT),
        cost_estimate=cost(2),
        name="thought_rows_terms",
    )(index, factors, proj_sum, fc_sum)


def spread_matrix(shard, count):
    shape = (shard, shard * count)
    column = lax.broadcasted_iota(jnp.int32, shape, 1) % shard
    return (column == lax.broadcasted_iota(jnp.int32, shape, 0)).astype(BF16)


def owner_mask(shard, count):
    shape = (count, shard * count)
    owner = lax.broadcasted_iota(jnp.int32, shape, 1) // shard
    return owner == lax.broadcasted_iota(jnp.int32, shape, 0)


VECTOR_ROWS = ("ln1_gain", "ln1_bias", "out_bias", "ln2_gain", "ln2_bias", "proj_bias")


def unpack_kernel(sizes, devices, packed_ref, vec_ref, fcb_ref, qkvb_ref):
    vec_ref[...] = jnp.zeros_like(vec_ref)
    width = vec_ref.shape[1]
    for at, (name, size) in enumerate(sizes):
        if name == "fc_bias":
            own = width // devices
            for j in range(size // own):
                spread = dot(packed_ref[at][:, j * own : (j + 1) * own], spread_matrix(own, devices))
                spread = jnp.where(owner_mask(own, devices), spread, 0.0)
                span = slice(j * width, (j + 1) * width)
                fcb_ref[:, span] = jnp.sum(spread, axis=0, keepdims=True)
            continue
        block = packed_ref[at][:, :size]
        spread = dot(block, spread_matrix(size, devices))
        full = jnp.sum(jnp.where(owner_mask(size, devices), spread, 0.0), axis=0, keepdims=True)
        if name == "qv_bias":
            qkvb_ref[:, :width] = full[:, :width]
            qkvb_ref[:, width : 2 * width] = jnp.zeros((1, width), F32)
            qkvb_ref[:, 2 * width :] = full[:, width:]
        else:
            at = VECTOR_ROWS.index(name)
            vec_ref[at : at + 1, :] = full


def unpack(packed, sizes):
    devices = packed.shape[1]
    size = dict(sizes)
    width = size["ln1_gain"] * devices
    return pl.pallas_call(
        functools.partial(unpack_kernel, sizes, devices),
        out_shape=[
            jax.ShapeDtypeStruct((8, width), F32),
            jax.ShapeDtypeStruct((1, size["fc_bias"] * devices), F32),
            jax.ShapeDtypeStruct((1, 3 * width), F32),
        ],
        compiler_params=pltpu.CompilerParams(vmem_limit_bytes=VMEM_LIMIT),
        name="vectors_unpack",
    )(packed)


def pack_kernel(sizes, devices, *refs):
    out_ref = refs[-1]
    out_ref[...] = jnp.zeros_like(out_ref)
    width = refs[0].shape[1]
    for at, ((name, size), ref) in enumerate(zip(sizes, refs)):
        if name == "fc_bias":
            own = width // devices
            for j in range(size // own):
                row = jnp.broadcast_to(ref[:, j * width : (j + 1) * width], (devices, width))
                row = jnp.where(owner_mask(own, devices), row, 0.0).astype(BF16)
                piece = dot_nt(row, spread_matrix(own, devices))
                out_ref[at, :, j * own : (j + 1) * own] = piece.astype(BF16)
            continue
        row = jnp.broadcast_to(ref[...], (devices, ref.shape[1]))
        own = jnp.where(owner_mask(size, devices), row, 0.0).astype(BF16)
        out_ref[at, :, :size] = dot_nt(own, spread_matrix(size, devices)).astype(BF16)


def pack(rows, sizes, devices):
    return pl.pallas_call(
        functools.partial(pack_kernel, sizes, devices),
        out_shape=jax.ShapeDtypeStruct((len(sizes), devices, LANES), BF16),
        compiler_params=pltpu.CompilerParams(vmem_limit_bytes=VMEM_LIMIT),
        name="vectors_pack",
    )(*[rows[name] for name, _ in sizes])


def join_kernel(*refs):
    out_ref = refs[-1]
    out_ref[...] = jnp.zeros_like(out_ref)
    for at, ref in enumerate(refs[:-1]):
        out_ref[at : at + 1, : ref.shape[0]] = ref[...].astype(F32).reshape(1, ref.shape[0])


def join(vectors):
    return pl.pallas_call(
        join_kernel,
        out_shape=jax.ShapeDtypeStruct((len(vectors), LANES), F32),
        name="vectors_join",
    )(*vectors)


def part_kernel(joined_ref, *refs):
    for at, ref in enumerate(refs):
        ref[...] = joined_ref[at, : ref.shape[0]]


def part(joined, sizes):
    return pl.pallas_call(
        part_kernel,
        out_shape=[jax.ShapeDtypeStruct((size,), F32) for _, size in sizes],
        name="vectors_part",
    )(joined)


def norm_parts(hidden):
    mean = jnp.mean(hidden, axis=-1, keepdims=True)
    centred = hidden - mean
    inverse = lax.rsqrt(jnp.mean(centred * centred, axis=-1, keepdims=True) + EPSILON)
    return centred * inverse, inverse


def step_on_sequence(
    near, far, vectors, tokens, cotangent, slots, count, answer_start, devices, sizes, comm
):
    query_key, value_out = near
    vec, fc_bias, qkv_bias = vectors
    seq_len, width = tokens.shape
    info = jnp.stack([slots[0], count])

    qkv_first = first_forward(tokens, query_key, value_out, vec, qkv_bias)
    mixed_hidden, lse_hidden = attend(info, qkv_first)
    late = QUESTION + lax.iota(jnp.int32, seq_len - QUESTION)
    upstream_low = jnp.where(
        (late >= answer_start)[:, None], cotangent[QUESTION:], jnp.zeros((), BF16)
    )
    tokens32 = tokens.astype(F32)
    weights = (query_key, value_out, after(far, mixed_hidden, upstream_low, tokens32))
    hidden_mid, qkv_mid, *saved, slot_rows, slot_lse = thoughts_forward(
        info, tokens, qkv_first, weights, vec, fc_bias, qkv_bias
    )
    qkv = lax.dynamic_update_slice(qkv_first, qkv_mid, (0, QUESTION, 0))
    hidden = lax.dynamic_update_slice(tokens32, hidden_mid, (QUESTION, 0))
    mixed_low, lse = add_slots(info, qkv, mixed_hidden, lse_hidden, slot_rows, slot_lse)
    output, second_low, act_low, slope, normed_two, inverse_two = feed_forward(
        hidden, mixed_low, weights, vec, fc_bias
    )

    proj_grad = comm.order(dot_tn(act_low[QUESTION:], upstream_low).astype(BF16))
    proj_half = comm.early(proj_grad)
    pre_grad, resid_grad, mixed_grad, sums = feed_back(
        after(upstream_low, proj_grad), slope, normed_two, inverse_two, weights, vec
    )
    fc_grad = dot_tn(second_low[QUESTION:], pre_grad).astype(BF16)
    units = fc_grad.shape[1]
    fc_going = comm.scatter(
        [fc_grad[:, j * width : (j + 1) * width] for j in range(units // width)], "zyxc"
    )
    sent = fc_going.go()
    row_sums, factors, mixed_grad, resid_grad = thoughts_back(
        info,
        hidden_mid,
        qkv,
        mixed_low,
        after(lse, sent),
        saved,
        weights,
        vec,
        mixed_grad,
        resid_grad,
    )
    join_after([fc_going], row_sums)
    out_grad = dot_tn(mixed_low[QUESTION:], resid_grad.astype(BF16)).astype(BF16)
    spread = comm.factors(factors[:THOUGHTS].astype(BF16))
    sent = go_after([fc_going, spread], out_grad)
    proj_half = after(proj_half, out_grad)
    proj_going = comm.early_end(proj_half)
    lse, back_grad = after((lse, mixed_grad), sent, proj_half)
    qkv_grad = attend_back(qkv, mixed_low, lse, back_grad)
    join_after([fc_going, spread], qkv_grad)
    sent = go_after([fc_going, spread], qkv_grad)
    input_grad, first_low, first_sums = first_back(
        info, hidden, after(qkv_grad, sent), resid_grad, weights, vec
    )
    sums = sums + row_sums
    small = {name: sums[i : i + 1, :width] for i, name in enumerate(SUM_ROWS)}
    small["fc_bias"] = sums[0:1]
    small["ln1_gain"] = first_sums[0:1]
    small["ln1_bias"] = first_sums[1:2]
    small["qv_bias"] = jnp.concatenate([first_sums[2:3], first_sums[3:4]], axis=1)
    packed = pack(small, sizes, devices)
    join_after([spread], packed)
    first_low = after(first_low, go_after([spread], packed))
    qkv_weight_grad = [dot_tn(first_low, qkv_grad[i]).astype(BF16) for i in range(3)]
    join_after([fc_going, spread], *qkv_weight_grad)
    return (
        output,
        input_grad,
        (proj_going, fc_going, spread, out_grad, qkv_weight_grad, packed),
    )


SMALL = ("ln1_gain", "ln1_bias", "qv_bias", "out_bias", "ln2_gain", "ln2_bias", "fc_bias", "proj_bias")


def on_device(
    links,
    tokens,
    ln1_gain,
    ln1_bias,
    qkv_weight,
    qv_bias,
    out_weight,
    out_bias,
    ln2_gain,
    ln2_bias,
    fc_weight,
    fc_bias,
    proj_weight,
    proj_bias,
    cotangent,
    thought_slots,
    thought_count,
    answer_start,
):
    devices = links.sizes["dp"] * links.sizes["fsdp"]
    small_shards = dict(
        ln1_gain=ln1_gain,
        ln1_bias=ln1_bias,
        qv_bias=qv_bias,
        out_bias=out_bias,
        ln2_gain=ln2_gain,
        ln2_bias=ln2_bias,
        fc_bias=fc_bias,
        proj_bias=proj_bias,
    )
    sizes = tuple((n, small_shards[n].shape[0]) for n in SMALL)
    own, width = out_weight.shape
    blocks = proj_weight.shape[0] // own
    both = ("dp", "fsdp")

    far_shard = jnp.concatenate(
        [split_units(fc_weight, blocks), proj_weight.reshape(blocks, own, width)], axis=0
    )
    far = lax.all_gather(far_shard, both, axis=1, tiled=True)

    packed = join([small_shards[n] for n in SMALL]).astype(BF16)
    small = links.gather(packed, "zxyc", axis=0).reshape(devices, len(sizes), LANES)
    parts = [qkv_weight[:, i * width : (i + 1) * width] for i in range(3)] + [out_weight]
    query_key = links.gather(jnp.stack(parts[:2]), "zxyc", axis=1).reshape(2, -1, width)
    value_out = links.gather(jnp.stack(parts[2:]), "zyxc", axis=1).reshape(2, -1, width)

    class Comm:
        @staticmethod
        def order(grad):
            value = grad.reshape(blocks, links.sizes["dp"], links.sizes["fsdp"], own, width)
            return value.transpose(2, 1, 0, 3, 4).reshape(-1, width)

        @staticmethod
        def early(value):
            return lax.psum_scatter(value, "fsdp", scatter_dimension=0, tiled=True)

        @staticmethod
        def early_end(value):
            value = lax.psum_scatter(value, "dp", scatter_dimension=0, tiled=True)
            return value.reshape(blocks, own, width)

        @staticmethod
        def scatter(grads, text):
            cut = [g.reshape(devices, g.shape[0] // devices, g.shape[1]) for g in grads]
            return links.scatter(jnp.stack(cut, axis=1), text)

        @staticmethod
        def factors(rows):
            return Gather(links, rows, "zxyc")

    output, input_grad, late = step_on_sequence(
        (query_key, value_out),
        far,
        unpack(small.transpose(1, 0, 2), sizes),
        tokens[0],
        cotangent[0],
        thought_slots[0],
        thought_count[0],
        answer_start[0],
        devices,
        sizes,
        Comm,
    )
    proj_going, fc_going, spread, out_grad, qkv_grads, packed = late
    cut = [g.reshape(devices, own, width) for g in qkv_grads[:2]]
    cut.append(jnp.pad(packed.transpose(1, 0, 2), ((0, 0), (0, 0), (0, width - LANES))))
    first = links.scatter(jnp.concatenate(cut, axis=1), "zxyc")
    rest = Comm.scatter([qkv_grads[2], out_grad], "zyxc")
    swaps = [first, rest, fc_going, spread]
    terms_left = True
    done = ()
    while any(swap.todo for swap in swaps) or terms_left:
        group = [swap for swap in swaps if swap.todo]
        sent = go_after(group, *done)
        if terms_left and fc_going not in group and spread not in group:
            terms_left = False
            index = lax.axis_index(both)[None].astype(jnp.int32)
            factors = after(spread.finish(), sent).reshape(devices * THOUGHTS, -1)
            proj_g, fc_g = row_terms(index, factors, proj_going.astype(F32), fc_going.buf)
            done = (proj_g, fc_g)
        join_after(group, *done)
        done = tuple(swap.buf for swap in group)
    first, small_sum = first.buf[: 2 * own].reshape(2, own, width), first.buf[2 * own :, :LANES]
    rest = rest.buf
    proj_g = proj_g.reshape(blocks * own, width)
    qkv_g = jnp.concatenate([first[0], first[1], rest[0]], axis=1)
    out_g = rest[1]
    owned = dict(zip(SMALL, part(small_sum, sizes)))
    return (
        output[None],
        input_grad[None],
        owned["ln1_gain"],
        owned["ln1_bias"],
        qkv_g,
        owned["qv_bias"],
        out_g,
        owned["out_bias"],
        owned["ln2_gain"],
        owned["ln2_bias"],
        fc_g,
        owned["fc_bias"],
        proj_g,
        owned["proj_bias"],
    )


def solution(mesh):
    links = Links({name: mesh.shape[name] for name in ("dp", "fsdp")})
    both = ("dp", "fsdp")
    cube, matrix, vector = P(both, None, None), P(both, None), P(both)
    weight_specs = (
        vector,
        vector,
        matrix,
        vector,
        matrix,
        vector,
        vector,
        vector,
        matrix,
        vector,
        matrix,
        vector,
    )

    def per_device(*args):
        return on_device(links, *args)

    return jax.shard_map(
        per_device,
        mesh=mesh,
        in_specs=(cube,) + weight_specs + (cube, matrix, vector, vector),
        out_specs=(cube, cube) + weight_specs,
        check_vma=False,
    )
```

```python
import functools
import math

import jax
import jax.numpy as jnp
import numpy as np
from jax import lax
from jax.experimental import pallas as pl
from jax.experimental.pallas import tpu as pltpu
from jax.sharding import PartitionSpec as P

HD = 64
THOUGHTS = 2
PREFIX = 384
QUESTION = 256
SCALE = 0.125
EPSILON = 1e-05
BLOCK = 256
HEAD_ROWS = 16
WINDOW = 32
LANES = 128
PAIR = 2 * HD
NEG = -1e30

F32 = jnp.float32
BF16 = jnp.bfloat16
VMEM_LIMIT = 56 * 1024 * 1024


def cost(microseconds):
    return pl.CostEstimate(
        flops=int(microseconds * 1.15e9),
        bytes_accessed=int(microseconds * 3.6e6),
        transcendentals=0,
    )


def dot(a, b):
    return lax.dot_general(a, b, (((1,), (0,)), ((), ())), preferred_element_type=F32)


def dot_nt(a, b):
    return lax.dot_general(a, b, (((1,), (1,)), ((), ())), preferred_element_type=F32)


def dot_tn(a, b):
    return lax.dot_general(a, b, (((0,), (0,)), ((), ())), preferred_element_type=F32)


def bits_of(size):
    return [1 << i for i in reversed(range(int(math.log2(size))))]


class Links:
    def __init__(self, sizes):
        self.sizes = sizes
        self.canon = [("dp", b) for b in bits_of(sizes["dp"])] + [
            ("fsdp", b) for b in bits_of(sizes["fsdp"])
        ]
        dp_bits = [("dp", b) for b in bits_of(sizes["dp"])]
        f_bits = [("fsdp", b) for b in bits_of(sizes["fsdp"])]
        self.groups = {"x": dp_bits[-1:], "y": dp_bits[:-1], "z": f_bits[:-1], "c": f_bits[-1:]}

    def order(self, text):
        out = []
        for letter in text:
            out += self.groups[letter]
        return out

    def swap(self, value, stage):
        axis, bit = stage
        return lax.ppermute(value, axis, [(i, i ^ bit) for i in range(self.sizes[axis])])

    def mine(self, stage):
        axis, bit = stage
        return (lax.axis_index(axis) & bit) != 0

    def gather(self, shard, text, axis=0):
        return Gather(self, shard, text, axis).finish()

    def chips(self, text):
        stages = list(reversed(self.order(text)))[1:]
        rest = [c for c in self.canon if c in stages]
        order = []
        for spot in range(1 << len(stages)):
            chip = 0
            for at, stage in enumerate(stages):
                if spot & (1 << (len(stages) - 1 - at)):
                    chip |= 1 << (len(rest) - 1 - rest.index(stage))
            order.append(chip)
        return order

    def scatter(self, value, text):
        return Scatter(self, value, text)


class Gather:
    def __init__(self, links, shard, text, axis=0):
        self.links = links
        self.shape = shard.shape
        self.axis = axis
        self.todo = links.order(text)
        self.done = []
        self.buf = shard
        self.got = None

    def go(self):
        self.add()
        self.stage = self.todo.pop(0)
        self.got = self.links.swap(self.buf, self.stage)
        return self.buf

    def add(self):
        if self.got is not None:
            canon = self.links.canon
            place = sum(1 for d in self.done if canon.index(d) < canon.index(self.stage))
            high = self.links.mine(self.stage)
            pair = [jnp.where(high, self.got, self.buf), jnp.where(high, self.buf, self.got)]
            self.buf = jnp.stack(pair, axis=self.axis + place)
            self.done.append(self.stage)
            self.got = None
        return self.buf

    def last(self):
        while self.todo:
            self.go()
        shape = self.shape
        shape = shape[: self.axis] + (-1,) + shape[self.axis :]
        return [self.buf.reshape(shape), self.got.reshape(shape)]

    def finish(self):
        while self.todo:
            self.go()
        self.add()
        shape = self.shape
        return self.buf.reshape(shape[: self.axis] + (-1,) + shape[self.axis + 1 :])


class Scatter:
    def __init__(self, links, value, text):
        self.links = links
        self.left = list(links.canon)
        self.todo = list(reversed(links.order(text)))
        self.got = None
        self.split = False
        if isinstance(value, tuple):
            self.split = True
            self.left = self.todo[1:]
            shape = (2,) * len(self.left) + value[0].shape[1:]
            self.keep, self.buf = (v.reshape(shape) for v in value)
        else:
            self.buf = value.reshape((2,) * len(self.left) + value.shape[1:])

    def go(self):
        self.add()
        stage = self.todo.pop(0)
        if self.split:
            self.split = False
            self.got = self.links.swap(self.buf, stage)
            return self.buf
        place = self.left.index(stage)
        self.left.remove(stage)
        high = self.links.mine(stage).astype(jnp.int32)
        self.keep = lax.dynamic_index_in_dim(self.buf, high, place, keepdims=False)
        sent = lax.dynamic_index_in_dim(self.buf, 1 - high, place, keepdims=False)
        self.got = self.links.swap(sent, stage)
        return sent

    def add(self):
        if self.got is None:
            return self.buf
        self.buf = self.keep.astype(F32) + self.got.astype(F32)
        if self.left:
            self.buf = self.buf.astype(BF16)
        self.got = None
        return self.buf

    def finish(self):
        while self.todo:
            self.go()
            self.add()
        return self.buf


def join_after(swaps, *deps):
    for swap in swaps:
        swap.got = after(swap.got, *deps)
        swap.add()


def go_after(swaps, *deps):
    for swap in swaps:
        swap.buf = after(swap.buf, *deps)
    return tuple(swap.go() for swap in swaps)


def after(value, *deps):
    return lax.optimization_barrier((value, deps))[0]


def attend_kernel(info_ref, q_ref, k_ref, v_ref, o_ref, lse_ref):
    seq_len = q_ref.shape[0]
    slot = info_ref[0]
    keys = k_ref[...]
    values_t = v_ref[...].T
    lane = lax.broadcasted_iota(jnp.int32, (BLOCK, PAIR), 1)
    sub = lax.broadcasted_iota(jnp.int32, (PAIR, BLOCK), 0)
    key_pos = lax.broadcasted_iota(jnp.int32, (BLOCK, BLOCK), 0)
    row_pos = lax.broadcasted_iota(jnp.int32, (BLOCK, BLOCK), 1)
    causal = key_pos <= row_pos
    middle_pos = QUESTION + lax.broadcasted_iota(jnp.int32, (PREFIX - QUESTION, BLOCK), 0)
    is_slot = (middle_pos >= slot) & (middle_pos < slot + THOUGHTS)

    def hide(scores):
        if scores.shape[0] <= QUESTION:
            return scores
        middle = jnp.where(is_slot, NEG, scores[QUESTION:PREFIX])
        return jnp.concatenate([scores[:QUESTION], middle, scores[PREFIX:]], axis=0)

    for begin in range(0, seq_len, BLOCK):
        end = begin + BLOCK
        queries = q_ref[begin:end, :] * jnp.asarray(SCALE, BF16)
        parts = []
        for head in range(2):
            own = jnp.where((lane >= HD) == bool(head), queries, jnp.zeros_like(queries))
            scores = dot_nt(keys[:end], own)
            last = jnp.where(causal, scores[begin:], NEG)
            if begin:
                last = jnp.concatenate([scores[:begin], last], axis=0)
            scores = hide(last)
            peak = jnp.max(scores, axis=0, keepdims=True)
            expo = jnp.exp(scores - peak)
            total = jnp.sum(expo, axis=0, keepdims=True)
            mixed = dot(values_t[:, :end], expo.astype(BF16))
            parts.append(mixed / total)
            lse_ref[pl.ds(2 * pl.program_id(0) + head, 1), begin:end] = peak + jnp.log(total)
        o_ref[begin:end, :] = jnp.where(sub < HD, parts[0], parts[1]).T.astype(BF16)


def attend(info, qkv):
    _, seq_len, width = qkv.shape
    pairs = width // PAIR

    def columns(i):
        return pl.BlockSpec((None, seq_len, PAIR), lambda g, i=i: (i, 0, g))

    return pl.pallas_call(
        attend_kernel,
        grid=(pairs,),
        in_specs=[
            pl.BlockSpec(memory_space=pltpu.SMEM),
            *(columns(i) for i in range(3)),
        ],
        out_specs=[
            pl.BlockSpec((seq_len, PAIR), lambda g: (0, g)),
            pl.BlockSpec((HEAD_ROWS, seq_len), lambda g: (0, 0)),
        ],
        out_shape=[
            jax.ShapeDtypeStruct((seq_len, width), BF16),
            jax.ShapeDtypeStruct((HEAD_ROWS, seq_len), F32),
        ],
        compiler_params=pltpu.CompilerParams(vmem_limit_bytes=VMEM_LIMIT),
        cost_estimate=cost(2.0),
        name="attention_forward",
    )(info, qkv, qkv, qkv)


def attend_back_kernel(
    q_ref, k_ref, v_ref, o_ref, lse_ref, g_ref, out_ref, dk_acc, dv_acc
):
    seq_len = q_ref.shape[0]
    pair = pl.program_id(0)
    first_row = seq_len - g_ref.shape[0]
    keys = k_ref[...]
    values = v_ref[...]
    keys_t = keys.T
    lane = lax.broadcasted_iota(jnp.int32, (BLOCK, PAIR), 1)
    sub = lax.broadcasted_iota(jnp.int32, (PAIR, BLOCK), 0)
    key_pos = lax.broadcasted_iota(jnp.int32, (BLOCK, BLOCK), 0)
    row_pos = lax.broadcasted_iota(jnp.int32, (BLOCK, BLOCK), 1)
    causal = key_pos <= row_pos
    dk_acc[...] = jnp.zeros_like(dk_acc)
    dv_acc[...] = jnp.zeros_like(dv_acc)
    for begin in range(first_row, seq_len, BLOCK):
        end = begin + BLOCK
        local = begin - first_row
        queries = q_ref[begin:end, :] * jnp.asarray(SCALE, BF16)
        grads = g_ref[local : local + BLOCK, :]
        product_t = (grads.astype(F32) * o_ref[begin:end, :].astype(F32)).T
        parts = []
        for head in range(2):
            chosen = (lane >= HD) == bool(head)
            own = jnp.where(chosen, queries, jnp.zeros_like(queries))
            own_grad = jnp.where(chosen, grads, jnp.zeros_like(grads))
            delta = jnp.sum(product_t[head * HD : (head + 1) * HD], axis=0, keepdims=True)
            lse = lse_ref[pl.ds(2 * pair + head, 1), begin:end]
            total = None
            for low, high in ((0, begin), (begin, end)):
                scores = dot_nt(keys[low:high], own)
                if high == end:
                    scores = jnp.where(causal, scores, NEG)
                probs = jnp.exp(scores - lse)
                prob_grad = dot_nt(values[low:high], own_grad)
                score_grad = (probs * (prob_grad - delta)).astype(BF16)
                dv_acc[low:high, :] += dot(probs.astype(BF16), own_grad)
                dk_acc[low:high, :] += dot(score_grad, own)
                part = dot(keys_t[:, low:high], score_grad)
                total = part if total is None else total + part
            parts.append(total)
        mine = jnp.where(sub < HD, parts[0], parts[1]).T * SCALE
        out_ref[0, begin:end, :] = mine.astype(BF16)
    out_ref[0, :first_row, :] = jnp.zeros((first_row, PAIR), BF16)
    out_ref[1] = dk_acc[...].astype(BF16)
    out_ref[2] = dv_acc[...].astype(BF16)


def attend_back(qkv, mixed_low, lse, mixed_grad):
    _, seq_len, width = qkv.shape
    rows = mixed_grad.shape[0]

    def columns(i):
        return pl.BlockSpec((None, seq_len, PAIR), lambda g, i=i: (i, 0, g))

    late = pl.BlockSpec((rows, PAIR), lambda g: (0, g))
    return pl.pallas_call(
        attend_back_kernel,
        grid=(width // PAIR,),
        in_specs=[
            *(columns(i) for i in range(3)),
            pl.BlockSpec((seq_len, PAIR), lambda g: (0, g)),
            pl.BlockSpec((HEAD_ROWS, seq_len), lambda g: (0, 0)),
            late,
        ],
        out_specs=pl.BlockSpec((3, seq_len, PAIR), lambda g: (0, 0, g)),
        out_shape=jax.ShapeDtypeStruct((3, seq_len, width), BF16),
        scratch_shapes=[pltpu.VMEM((seq_len, PAIR), F32), pltpu.VMEM((seq_len, PAIR), F32)],
        compiler_params=pltpu.CompilerParams(vmem_limit_bytes=VMEM_LIMIT),
        cost_estimate=cost(2.17),
        name="attention_backward",
    )(qkv, qkv, qkv, mixed_low, lse, mixed_grad)


def row_norm(row, gain, bias):
    mean = jnp.mean(row, axis=-1, keepdims=True)
    centred = row - mean
    inverse = lax.rsqrt(jnp.mean(centred * centred, axis=-1, keepdims=True) + EPSILON)
    normed = centred * inverse
    return normed * gain + bias, normed, inverse


def row_norm_back(incoming, normed, inverse, gain):
    scaled = incoming * gain
    inner = (
        scaled
        - jnp.mean(scaled, axis=-1, keepdims=True)
        - normed * jnp.mean(scaled * normed, axis=-1, keepdims=True)
    )
    return inner * inverse


GELU_A = 0.7978845608028654
GELU_B = 0.044715


def gelu(pre):
    return 0.5 * pre * (1.0 + jnp.tanh(GELU_A * (pre + GELU_B * pre * pre * pre)))


def gelu_slope(pre):
    square = pre * pre
    curve = jnp.tanh(GELU_A * pre * (1.0 + GELU_B * square))
    return 0.5 * (1.0 + curve) + 0.5 * pre * (1.0 - curve * curve) * GELU_A * (
        1.0 + 3.0 * GELU_B * square
    )


def widen(row):
    return jnp.broadcast_to(row, (8, row.shape[1])).astype(BF16)


def pick(block, index):
    rows = lax.broadcasted_iota(jnp.int32, block.shape, 0)
    return jnp.sum(jnp.where(rows == index, block.astype(F32), 0.0), axis=0, keepdims=True)


def put(block, index, row):
    rows = lax.broadcasted_iota(jnp.int32, block.shape, 0)
    return jnp.where(rows == index, row.astype(block.dtype), block)


def by_head(row, heads):
    shape = (heads, row.shape[1])
    lane_head = lax.broadcasted_iota(jnp.int32, shape, 1) // HD
    return jnp.where(lane_head == lax.broadcasted_iota(jnp.int32, shape, 0), row, 0.0)


def heads_only(block):
    lane_head = lax.broadcasted_iota(jnp.int32, block.shape, 1) // HD
    own = lane_head == lax.broadcasted_iota(jnp.int32, block.shape, 0)
    return jnp.sum(jnp.where(own, block, 0.0), axis=0, keepdims=True)


def thoughts_kernel(
    info_ref,
    tok_ref,
    lse_in_ref,
    vec_ref,
    fcb_ref,
    qkvb_ref,
    near_in,
    far_in,
    qkv_in,
    mixed_in,
    hid_in,
    lse_ref,
    pre_ref,
    prob_ref,
    res_ref,
    qkv_out,
    mixed_out,
    hid_out,
    kv_ref,
    late_q_ref,
    mixed_ref,
    hid_ref,
    near_ref,
    far_ref,
    sems,
):
    width = tok_ref.shape[1]
    blocks = (far_ref.shape[0] - 1) // 2
    rows = late_q_ref.shape[0]
    ln1_gain, ln1_bias, out_bias, ln2_gain, ln2_bias, proj_bias = (
        vec_ref[i : i + 1, :] for i in range(6)
    )
    slot = info_ref[0]
    count = info_ref[1]

    loads = [
        (qkv_in.at[:, pl.ds(0, PREFIX)], kv_ref),
        (far_in.at[pl.ds(2 * blocks, 1)], far_ref.at[pl.ds(2 * blocks, 1)]),
        (far_in.at[pl.ds(0, blocks)], far_ref.at[pl.ds(0, blocks)]),
        (far_in.at[pl.ds(blocks, blocks)], far_ref.at[pl.ds(blocks, blocks)]),
        (near_in, near_ref),
        (qkv_in.at[0, pl.ds(QUESTION, rows)], late_q_ref),
        (mixed_in.at[pl.ds(QUESTION, rows)], mixed_ref),
    ]
    loads = [pltpu.make_async_copy(a, b, sems.at[i]) for i, (a, b) in enumerate(loads)]
    for copy in loads:
        copy.start()
    hid_ref[...] = tok_ref[...].astype(F32)
    hidden_row = pick(hid_ref[...], slot - 1 - QUESTION)
    loads[0].wait()
    slot_rows = []
    slot_lse = []
    for step in range(THOUGHTS + 1):
        at = slot - 1 + step
        qkv_row = pick(kv_ref[0, QUESTION:, :], at - QUESTION)
        query = by_head(qkv_row * SCALE, HEAD_ROWS).astype(BF16)
        scores = dot_nt(query, kv_ref[1])
        key_pos = lax.broadcasted_iota(jnp.int32, scores.shape, 1)
        scores = jnp.where(key_pos <= at, scores, NEG)
        peak = jnp.max(scores, axis=1, keepdims=True)
        expo = jnp.exp(scores - peak)
        total = jnp.sum(expo, axis=1, keepdims=True)
        probs = expo / total
        mixed = heads_only(dot(probs.astype(BF16), kv_ref[2]))
        if step:
            slot_rows.append(mixed)
            slot_lse.append(peak + jnp.log(total))
        if step == THOUGHTS:
            break
        prob_ref[step * HEAD_ROWS : (step + 1) * HEAD_ROWS, :] = probs
        if not step:
            loads[1].wait()
        resid = hidden_row + dot(widen(mixed), far_ref[2 * blocks])[0:1] + out_bias
        res_ref[step : step + 1, :] = resid
        second, _, _ = row_norm(resid, ln2_gain, ln2_bias)
        second = widen(second)
        if not step:
            loads[2].wait()
        acts = []
        for j in range(blocks):
            span = slice(j * width, (j + 1) * width)
            pre = dot(second, far_ref[j])[0:1] + fcb_ref[0:1, span]
            pre_ref[step : step + 1, span] = pre
            acts.append(widen(gelu(pre)))
        if not step:
            loads[3].wait()
        fed = resid + proj_bias
        for j in range(blocks):
            fed = fed + dot(acts[j], far_ref[blocks + j])[0:1]
        first, _, _ = row_norm(fed, ln1_gain, ln1_bias)
        first = widen(first)
        hidden_row = fed
        spot = jnp.where(step < count, slot + step - QUESTION, -1)
        hid_ref[...] = put(hid_ref[...], spot, fed)
        if not step:
            loads[4].wait()
        for i in range(3):
            span = slice(i * width, (i + 1) * width)
            new_row = dot(first, near_ref[i])[0:1] + qkvb_ref[0:1, span]
            kv_ref[i, QUESTION:, :] = put(kv_ref[i, QUESTION:, :], spot, new_row)
    loads[5].wait()
    loads[6].wait()
    stores = [
        pltpu.make_async_copy(
            kv_ref.at[:, pl.ds(QUESTION, PREFIX - QUESTION)],
            qkv_out.at[:, pl.ds(QUESTION, PREFIX - QUESTION)],
            sems.at[0],
        ),
        pltpu.make_async_copy(
            hid_ref, hid_out.at[pl.ds(QUESTION, PREFIX - QUESTION)], sems.at[1]
        ),
    ]
    for copy in stores:
        copy.start()

    row_pos = QUESTION + lax.broadcasted_iota(jnp.int32, (HEAD_ROWS, rows), 1)
    late_q = late_q_ref[...]
    lse = lse_in_ref[:, QUESTION:]
    scores = []
    values = []
    top = lse
    for j in range(THOUGHTS):
        local = slot + j - QUESTION
        key = by_head(pick(kv_ref[1, QUESTION:, :], local) * SCALE, HEAD_ROWS)
        values.append(pick(kv_ref[2, QUESTION:, :], local))
        score = jnp.where(row_pos >= slot + j, dot_nt(key.astype(BF16), late_q), NEG)
        scores.append(score)
        top = jnp.maximum(top, score)
    whole_sum = jnp.exp(lse - top)
    for score in scores:
        whole_sum = whole_sum + jnp.exp(score - top)
    new_lse = top + jnp.log(whole_sum)
    ones = by_head(jnp.ones((1, width), F32), HEAD_ROWS).astype(BF16)
    share = jnp.exp(lse - new_lse)
    high = share.astype(BF16)
    low = (share - high.astype(F32)).astype(BF16)
    weights = [jnp.exp(score - new_lse).astype(BF16) for score in scores]
    step_rows = PREFIX - QUESTION
    for begin in range(0, rows, step_rows):
        span = slice(begin, begin + step_rows)
        part = mixed_ref[span, :].astype(F32) * (
            dot_tn(high[:, span], ones) + dot_tn(low[:, span], ones)
        )
        for weight, value in zip(weights, values):
            part = part + dot_tn(weight[:, span], ones) * value
        if not begin:
            for j in range(THOUGHTS):
                part = put(part, slot + j - QUESTION, slot_rows[j])
        mixed_ref[span, :] = part.astype(BF16)
    stores.append(
        pltpu.make_async_copy(mixed_ref, mixed_out.at[pl.ds(QUESTION, rows)], sems.at[2])
    )
    stores[-1].start()
    lse_ref[:, :QUESTION] = lse_in_ref[:, :QUESTION]
    column = lax.broadcasted_iota(jnp.int32, (HEAD_ROWS, step_rows), 1)
    middle = new_lse[:, :step_rows]
    for j in range(THOUGHTS):
        middle = jnp.where(column == slot + j - QUESTION, slot_lse[j], middle)
    lse_ref[:, QUESTION:PREFIX] = middle
    lse_ref[:, PREFIX:] = new_lse[:, step_rows:]
    for copy in stores:
        copy.wait()


def whole(array):
    zeros = (0,) * array.ndim
    return pl.BlockSpec(array.shape, lambda i, zeros=zeros: zeros)


def fc_spec(far):
    return pl.BlockSpec((far.shape[0] // 2,) + far.shape[1:], lambda i: (0, 0, 0))


def proj_spec(far):
    return pl.BlockSpec((far.shape[0] // 2,) + far.shape[1:], lambda i: (1, 0, 0))


def out_spec(far):
    last = far.shape[0] - 1
    return pl.BlockSpec((1,) + far.shape[1:], lambda i: (last, 0, 0))


def thoughts_forward(info, tokens, tokens32, qkv, mixed_low, lse, weights, vec, fc_bias, qkv_bias):
    near, far = weights
    seq_len, width = tokens.shape
    rows = seq_len - QUESTION
    middle = PREFIX - QUESTION
    anywhere = pl.BlockSpec(memory_space=pl.ANY)
    out_shape = [
        jax.ShapeDtypeStruct(lse.shape, F32),
        jax.ShapeDtypeStruct((8, fc_bias.shape[1]), F32),
        jax.ShapeDtypeStruct((THOUGHTS * HEAD_ROWS, PREFIX), F32),
        jax.ShapeDtypeStruct((8, width), F32),
        jax.ShapeDtypeStruct(qkv.shape, BF16),
        jax.ShapeDtypeStruct(mixed_low.shape, BF16),
        jax.ShapeDtypeStruct(tokens32.shape, F32),
    ]
    return pl.pallas_call(
        thoughts_kernel,
        grid=(1,),
        in_specs=[
            pl.BlockSpec(memory_space=pltpu.SMEM),
            pl.BlockSpec((middle, width), lambda i: (QUESTION // middle, 0)),
            whole(lse),
            whole(vec),
            whole(fc_bias),
            whole(qkv_bias),
            *[anywhere] * 5,
        ],
        out_specs=[*(whole(x) for x in out_shape[:4]), *[anywhere] * 3],
        out_shape=out_shape,
        input_output_aliases={8: 4, 9: 5, 10: 6},
        scratch_shapes=[
            pltpu.VMEM((3, PREFIX, width), BF16),
            pltpu.VMEM((rows, width), BF16),
            pltpu.VMEM((rows, width), BF16),
            pltpu.VMEM((middle, width), F32),
            pltpu.VMEM(near.shape, BF16),
            pltpu.VMEM(far.shape, BF16),
            pltpu.SemaphoreType.DMA((7,)),
        ],
        compiler_params=pltpu.CompilerParams(vmem_limit_bytes=VMEM_LIMIT),
        cost_estimate=cost(2),
        name="thought_rows_forward",
    )(info, tokens, lse, vec, fc_bias, qkv_bias, near, far, qkv, mixed_low, tokens32)


def thoughts_back_kernel(
    info_ref,
    hid_ref,
    qkv_ref,
    lse_ref,
    pre_ref,
    prob_ref,
    res_ref,
    vec_ref,
    near_in,
    far_in,
    qkv_in,
    mixed_in,
    mg_in,
    rg_in,
    sum_ref,
    fac_ref,
    mg_out,
    rg_out,
    mg_ref,
    rg_win,
    late_q_ref,
    mixed_ref,
    near_ref,
    far_ref,
    sems,
):
    width = hid_ref.shape[1]
    blocks = (far_ref.shape[0] - 1) // 2
    units = blocks * width
    rows = mg_ref.shape[0]
    ln1_gain, ln1_bias, _, ln2_gain, ln2_bias, _ = (vec_ref[i : i + 1, :] for i in range(6))
    slot = info_ref[0]
    count = info_ref[1]
    base = pl.multiple_of(((slot - 1 - QUESTION) // 16) * 16, 16)

    def window(ref):
        return ref.at[pl.ds(base, WINDOW)]

    loads = [
        (mg_in, mg_ref),
        (mixed_in.at[pl.ds(QUESTION, rows)], mixed_ref),
        (qkv_in.at[0, pl.ds(QUESTION, rows)], late_q_ref),
        (window(rg_in), rg_win),
        (near_in, near_ref),
        (far_in.at[pl.ds(blocks, blocks)], far_ref.at[pl.ds(blocks, blocks)]),
        (far_in.at[pl.ds(0, blocks)], far_ref.at[pl.ds(0, blocks)]),
        (far_in.at[pl.ds(2 * blocks, 1)], far_ref.at[pl.ds(2 * blocks, 1)]),
    ]
    loads = [pltpu.make_async_copy(a, b, sems.at[i]) for i, (a, b) in enumerate(loads)]
    for copy in loads:
        copy.start()
    for copy in loads[:4]:
        copy.wait()

    late_q = late_q_ref[...]
    mixed_grad = mg_ref[...]
    product = mixed_grad.astype(F32) * mixed_ref[...].astype(F32)
    high = product.astype(BF16)
    ones = by_head(jnp.ones((1, width), F32), HEAD_ROWS).astype(BF16)
    delta = dot_nt(ones, high) + dot_nt(ones, (product - high.astype(F32)).astype(BF16))
    row_pos = QUESTION + lax.broadcasted_iota(jnp.int32, (HEAD_ROWS, rows), 1)
    lse = lse_ref[:, QUESTION:]

    def at_slot(at):
        local = at - QUESTION
        key = by_head(pick(qkv_ref[1, QUESTION:PREFIX, :], local) * SCALE, HEAD_ROWS)
        value = by_head(pick(qkv_ref[2, QUESTION:PREFIX, :], local), HEAD_ROWS)
        scores = dot_nt(key.astype(BF16), late_q)
        probs = jnp.where(row_pos >= at, jnp.exp(jnp.minimum(scores - lse, 0.0)), 0.0)
        prob_grad = dot_nt(value.astype(BF16), mixed_grad)
        score_grad = (probs * (prob_grad - delta)).astype(BF16)
        return (
            heads_only(dot(score_grad, late_q)) * SCALE,
            heads_only(dot(probs.astype(BF16), mixed_grad)),
        )

    def through_first(at, query_grad, key_grad, value_grad):
        first_grad = (
            dot_nt(widen(query_grad), near_ref[0])
            + dot_nt(widen(key_grad), near_ref[1])
            + dot_nt(widen(value_grad), near_ref[2])
        )[0:1]
        _, normed, inverse = row_norm(hid_ref[pl.ds(at - QUESTION, 1), :], ln1_gain, ln1_bias)
        return row_norm_back(first_grad, normed, inverse, ln1_gain)

    sum_ref[...] = jnp.zeros_like(sum_ref)
    fac_ref[...] = jnp.zeros_like(fac_ref)
    slot_grads = at_slot(slot + 1)
    loads[4].wait()
    carried = through_first(slot + 1, jnp.zeros((1, width), F32), *slot_grads)
    for copy in loads[5:]:
        copy.wait()
    for step in reversed(range(THOUGHTS)):
        at = slot - 1 + step
        upstream = jnp.where(step < count, carried, 0.0)
        low = widen(upstream)
        act_grad = jnp.concatenate([dot_nt(low, far_ref[blocks + j])[0:1] for j in range(blocks)], axis=1)
        pre = pre_ref[step : step + 1, :]
        pre_grad = (act_grad * gelu_slope(pre)).astype(BF16).astype(F32)
        second_grad = jnp.zeros((1, width), F32)
        for j in range(blocks):
            piece = pre_grad[:, j * width : (j + 1) * width]
            second_grad = second_grad + dot_nt(widen(piece), far_ref[j])[0:1]
        second, normed, inverse = row_norm(res_ref[step : step + 1, :], ln2_gain, ln2_bias)
        resid_grad = upstream + row_norm_back(second_grad, normed, inverse, ln2_gain)
        mixed_row = dot_nt(widen(resid_grad), far_ref[2 * blocks])[0:1]
        local = at - QUESTION
        rg_win[...] = put(rg_win[...], local - base, resid_grad)
        mg_ref[: PREFIX - QUESTION, :] = put(mg_ref[: PREFIX - QUESTION, :], local, mixed_row)
        up_low = upstream.astype(BF16).astype(F32)
        sum_ref[0:1, :units] += pre_grad
        sum_ref[1:2, :width] += second_grad * normed
        sum_ref[2:3, :width] += second_grad
        sum_ref[3:4, :width] += up_low
        sum_ref[4:5, :width] += resid_grad.astype(BF16).astype(F32)
        fac_ref[step : step + 1, :units] = gelu(pre)
        fac_ref[step : step + 1, units : units + width] = up_low
        fac_ref[step : step + 1, units + width : units + 2 * width] = second
        fac_ref[step : step + 1, units + 2 * width :] = pre_grad
        if step:
            own_grad = by_head(mixed_row, HEAD_ROWS).astype(BF16)
            query = by_head(pick(qkv_ref[0, QUESTION:PREFIX, :], local) * SCALE, HEAD_ROWS)
            query = query.astype(BF16)
            probs = prob_ref[step * HEAD_ROWS : (step + 1) * HEAD_ROWS, :]
            prob_grad = dot_nt(own_grad, qkv_ref[2])
            own_delta = jnp.sum(prob_grad * probs, axis=1, keepdims=True)
            score_grad = (probs * (prob_grad - own_delta)).astype(BF16)
            query_grad = heads_only(dot(score_grad, qkv_ref[1])) * SCALE
            key_grad, value_grad = at_slot(at)
            own = lax.broadcasted_iota(jnp.int32, probs.shape, 1) == at
            score_own = jnp.sum(jnp.where(own, score_grad.astype(F32), 0.0), axis=1, keepdims=True)
            prob_own = jnp.sum(jnp.where(own, probs, 0.0), axis=1, keepdims=True)
            key_grad += jnp.sum(score_own * query.astype(F32), axis=0, keepdims=True)
            value_grad += jnp.sum(prob_own * own_grad.astype(F32), axis=0, keepdims=True)
            carried = resid_grad + through_first(at, query_grad, key_grad, value_grad)
    stores = [
        pltpu.make_async_copy(mg_ref, mg_out, sems.at[0]),
        pltpu.make_async_copy(rg_win, window(rg_out), sems.at[1]),
    ]
    for copy in stores:
        copy.start()
    for copy in stores:
        copy.wait()


SUM_ROWS = ("fc_bias", "ln2_gain", "ln2_bias", "proj_bias", "out_bias")


def thoughts_back(info, hidden, qkv, mixed_low, lse, saved, weights, vec, mixed_grad, resid_grad):
    near, far = weights
    width = hidden.shape[1]
    units = far.shape[0] // 2 * width
    middle = PREFIX - QUESTION
    anywhere = pl.BlockSpec(memory_space=pl.ANY)
    out_shape = [
        jax.ShapeDtypeStruct((8, units), F32),
        jax.ShapeDtypeStruct((8, 2 * units + 2 * width), F32),
        jax.ShapeDtypeStruct(mixed_grad.shape, BF16),
        jax.ShapeDtypeStruct(resid_grad.shape, F32),
    ]
    return pl.pallas_call(
        thoughts_back_kernel,
        grid=(1,),
        in_specs=[
            pl.BlockSpec(memory_space=pltpu.SMEM),
            pl.BlockSpec((middle, width), lambda i: (QUESTION // middle, 0)),
            pl.BlockSpec((3, PREFIX, width), lambda i: (0, 0, 0)),
            whole(lse),
            *(whole(x) for x in saved),
            whole(vec),
            *[anywhere] * 6,
        ],
        out_specs=[whole(out_shape[0]), whole(out_shape[1]), anywhere, anywhere],
        out_shape=out_shape,
        input_output_aliases={12: 2, 13: 3},
        scratch_shapes=[
            pltpu.VMEM(mixed_grad.shape, BF16),
            pltpu.VMEM((WINDOW, width), F32),
            pltpu.VMEM(mixed_grad.shape, BF16),
            pltpu.VMEM(mixed_grad.shape, BF16),
            pltpu.VMEM(near.shape, BF16),
            pltpu.VMEM(far.shape, BF16),
            pltpu.SemaphoreType.DMA((8,)),
        ],
        compiler_params=pltpu.CompilerParams(vmem_limit_bytes=VMEM_LIMIT),
        cost_estimate=cost(2.0),
        name="thought_rows_backward",
    )(
        info,
        hidden,
        qkv,
        lse,
        *saved,
        vec,
        near,
        far,
        qkv,
        mixed_low,
        mixed_grad,
        resid_grad,
    )


def forward_kernel(
    hid_ref, mixed_ref, wvo_ref, wfc_ref, wproj_ref, vec_ref, fcb_ref, out_ref, second_ref,
    act_ref, slope_ref, normed_ref, inverse_ref, first_ref,
):
    width = hid_ref.shape[1]
    out_bias, ln2_gain, ln2_bias, proj_bias = (vec_ref[i : i + 1, :] for i in range(2, 6))
    first, _, _ = row_norm(hid_ref[...], vec_ref[0:1, :], vec_ref[1:2, :])
    first_ref[...] = first.astype(BF16)
    resid = hid_ref[...] + dot(mixed_ref[...], wvo_ref[0]) + out_bias
    second, normed, inverse = row_norm(resid, ln2_gain, ln2_bias)
    low = second.astype(BF16)
    second_ref[...] = low
    normed_ref[...] = normed
    inverse_ref[...] = jnp.broadcast_to(inverse, inverse_ref.shape)
    total = resid + proj_bias
    for j in range(wfc_ref.shape[0]):
        span = slice(j * width, (j + 1) * width)
        pre = dot(low, wfc_ref[j]) + fcb_ref[:, span]
        square = pre * pre
        curve = jnp.tanh(GELU_A * pre * (1.0 + GELU_B * square))
        half = 0.5 + 0.5 * curve
        act = (pre * half).astype(BF16)
        rise = 0.5 * GELU_A + (1.5 * GELU_A * GELU_B) * square
        slope_ref[:, span] = (half + pre * rise * (1.0 - curve * curve)).astype(BF16)
        act_ref[:, span] = act
        total = total + dot(act, wproj_ref[j])
    out_ref[...] = total.astype(BF16)


def feed_forward(hidden, mixed_low, weights, vec, fc_bias):
    far = weights[1]
    seq_len, width = hidden.shape
    units = fc_bias.shape[1]

    def rows(columns):
        return pl.BlockSpec((BLOCK, columns), lambda i: (i, 0))

    return pl.pallas_call(
        forward_kernel,
        grid=(seq_len // BLOCK,),
        in_specs=[
            rows(width),
            rows(width),
            out_spec(far),
            fc_spec(far),
            proj_spec(far),
            whole(vec),
            whole(fc_bias),
        ],
        out_specs=[rows(n) for n in (width, width, units, units, width, LANES, width)],
        out_shape=[
            jax.ShapeDtypeStruct((seq_len, width), BF16),
            jax.ShapeDtypeStruct((seq_len, width), BF16),
            jax.ShapeDtypeStruct((seq_len, units), BF16),
            jax.ShapeDtypeStruct((seq_len, units), BF16),
            jax.ShapeDtypeStruct((seq_len, width), F32),
            jax.ShapeDtypeStruct((seq_len, LANES), F32),
            jax.ShapeDtypeStruct((seq_len, width), BF16),
        ],
        compiler_params=pltpu.CompilerParams(vmem_limit_bytes=VMEM_LIMIT),
        cost_estimate=cost(2.0),
        name="feed_forward",
    )(hidden, mixed_low, far, far, far, vec, fc_bias)


def back_kernel(
    up_ref, slope_ref, normed_ref, inverse_ref, wvo_ref, wfc_ref, wproj_ref, vec_ref, pg_ref,
    rg_ref, mg_ref, sum_ref,
):
    width = up_ref.shape[1]
    blocks = wfc_ref.shape[0]
    units = blocks * width
    ln2_gain = vec_ref[3:4, :]

    @pl.when(pl.program_id(0) == 0)
    def _():
        sum_ref[...] = jnp.zeros_like(sum_ref)

    up = up_ref[...]
    second_grad = jnp.zeros(up.shape, F32)
    for j in range(blocks):
        span = slice(j * width, (j + 1) * width)
        pre_grad = (dot_nt(up, wproj_ref[j]) * slope_ref[:, span].astype(F32)).astype(BF16)
        pg_ref[:, span] = pre_grad
        sum_ref[0:1, span] += jnp.sum(pre_grad.astype(F32), axis=0, keepdims=True)
        second_grad = second_grad + dot_nt(pre_grad, wfc_ref[j])
    normed = normed_ref[...]
    up32 = up.astype(F32)
    resid_grad = up32 + row_norm_back(second_grad, normed, inverse_ref[:, :1], ln2_gain)
    attn_grad = resid_grad.astype(BF16)
    rg_ref[...] = resid_grad
    mg_ref[...] = dot_nt(attn_grad, wvo_ref[0]).astype(BF16)
    sum_ref[1:2, :width] += jnp.sum(second_grad * normed, axis=0, keepdims=True)
    sum_ref[2:3, :width] += jnp.sum(second_grad, axis=0, keepdims=True)
    sum_ref[3:4, :width] += jnp.sum(up32, axis=0, keepdims=True)
    sum_ref[4:5, :width] += jnp.sum(attn_grad.astype(F32), axis=0, keepdims=True)


def feed_back(upstream_low, slope, normed, inverse, weights, vec):
    far = weights[1]
    count, width = upstream_low.shape
    units = slope.shape[1]
    skip = QUESTION // BLOCK

    def rows(columns, begin=0):
        return pl.BlockSpec((BLOCK, columns), lambda i, begin=begin: (i + begin, 0))

    sums = jax.ShapeDtypeStruct((8, units), F32)
    return pl.pallas_call(
        back_kernel,
        grid=(count // BLOCK,),
        in_specs=[
            rows(width),
            rows(units, skip),
            rows(width, skip),
            rows(LANES, skip),
            out_spec(far),
            fc_spec(far),
            proj_spec(far),
            whole(vec),
        ],
        out_specs=[rows(units), rows(width), rows(width), whole(sums)],
        out_shape=[
            jax.ShapeDtypeStruct((count, units), BF16),
            jax.ShapeDtypeStruct((count, width), F32),
            jax.ShapeDtypeStruct((count, width), BF16),
            sums,
        ],
        compiler_params=pltpu.CompilerParams(vmem_limit_bytes=VMEM_LIMIT),
        cost_estimate=cost(1.5),
        name="feed_backward",
    )(upstream_low, slope, normed, inverse, far, far, far, vec)


def first_back_kernel(
    info_ref, hid_ref, grad_ref, rg_ref, near_ref, vec_ref, in_ref, sum_ref
):
    rows, width = hid_ref.shape
    step = pl.program_id(0)
    slot = info_ref[0]
    count = info_ref[1]

    @pl.when(step == 0)
    def _():
        sum_ref[...] = jnp.zeros_like(sum_ref)

    gain = vec_ref[0:1, :]
    _, normed, inverse = row_norm(hid_ref[...], gain, vec_ref[1:2, :])
    first_grad = jnp.zeros((rows, width), F32)
    for i in range(3):
        first_grad = first_grad + dot_nt(grad_ref[i], near_ref[i])
        if i != 1:
            at = 2 + i // 2
            columns = jnp.sum(grad_ref[i].astype(F32), axis=0, keepdims=True)
            sum_ref[at : at + 1, :] += columns
    sum_ref[0:1, :] += jnp.sum(first_grad * normed, axis=0, keepdims=True)
    sum_ref[1:2, :] += jnp.sum(first_grad, axis=0, keepdims=True)
    late = (step >= QUESTION // BLOCK).astype(F32)
    grad = row_norm_back(first_grad, normed, inverse, gain) + late * rg_ref[...]
    position = step * rows + lax.broadcasted_iota(jnp.int32, (rows, 1), 0)
    replaced = (position >= slot) & (position < slot + jnp.minimum(count, THOUGHTS))
    in_ref[...] = jnp.where(replaced, 0.0, grad)


def first_back(info, hidden, qkv_grad, resid_grad, weights, vec):
    seq_len, width = hidden.shape
    skip = QUESTION // BLOCK
    sums = jax.ShapeDtypeStruct((8, width), F32)
    rows = pl.BlockSpec((BLOCK, width), lambda i: (i, 0))
    return pl.pallas_call(
        first_back_kernel,
        grid=(seq_len // BLOCK,),
        in_specs=[
            pl.BlockSpec(memory_space=pltpu.SMEM),
            rows,
            pl.BlockSpec((3, BLOCK, width), lambda i: (0, i, 0)),
            pl.BlockSpec((BLOCK, width), lambda i: (jnp.maximum(i - skip, 0), 0)),
            whole(weights[0]),
            whole(vec),
        ],
        out_specs=[rows, whole(sums)],
        out_shape=[
            jax.ShapeDtypeStruct((seq_len, width), F32),
            sums,
        ],
        compiler_params=pltpu.CompilerParams(vmem_limit_bytes=VMEM_LIMIT),
        cost_estimate=cost(0.83),
        name="first_norm_backward",
    )(info, hidden, qkv_grad, resid_grad, weights[0], vec)


def keep_and_send(value, core, chips, keep_ref, send_ref, at):
    own = value.shape[0] // (2 * len(chips))
    for spot, chip in enumerate(chips):
        even = value[2 * chip * own : (2 * chip + 1) * own]
        odd = value[(2 * chip + 1) * own : (2 * chip + 2) * own]
        keep_ref[spot, at] = jnp.where(core == 0, even, odd).astype(BF16)
        send_ref[spot, at] = jnp.where(core == 0, odd, even).astype(BF16)


def near_terms_kernel(
    chips_a, chips_b, core_ref, first_ref, grad_ref, mixed_ref, rg_ref, keep_a, send_a, keep_b, send_b
):
    core = core_ref[0]
    first = first_ref[...]
    for i in range(3):
        value = dot_tn(first, grad_ref[i])
        if i < 2:
            keep_and_send(value, core, chips_a, keep_a, send_a, i)
        else:
            keep_and_send(value, core, chips_b, keep_b, send_b, 0)
    value = dot_tn(mixed_ref[QUESTION:, :], rg_ref[...].astype(BF16))
    keep_and_send(value, core, chips_b, keep_b, send_b, 1)


def near_terms(core, first_low, qkv_grad, mixed_low, resid_grad, chips_a, chips_b):
    seq_len, width = first_low.shape
    half = jax.ShapeDtypeStruct((len(chips_a), 2, width // (2 * len(chips_a)), width), BF16)
    return pl.pallas_call(
        functools.partial(near_terms_kernel, chips_a, chips_b),
        grid=(1,),
        in_specs=[
            pl.BlockSpec(memory_space=pltpu.SMEM),
            whole(first_low),
            whole(qkv_grad),
            whole(mixed_low),
            whole(resid_grad),
        ],
        out_specs=[whole(half)] * 4,
        out_shape=[half] * 4,
        compiler_params=pltpu.CompilerParams(vmem_limit_bytes=VMEM_LIMIT),
        cost_estimate=cost(0.5),
        name="near_weight_terms",
    )(core, first_low, qkv_grad, mixed_low, resid_grad)


def fc_terms_kernel(chips, core_ref, second_ref, pg_ref, keep_ref, send_ref):
    value = dot_tn(second_ref[QUESTION:, :], pg_ref[...])
    keep_and_send(value, core_ref[0], chips, keep_ref, send_ref, 0)


def fc_terms(core, second_low, pre_grad, chips):
    seq_len, width = second_low.shape
    rows, units = pre_grad.shape
    blocks = units // width
    own = width // (2 * len(chips))
    half = jax.ShapeDtypeStruct((len(chips), blocks, own, width), BF16)
    out = pl.BlockSpec((len(chips), 1, own, width), lambda j: (0, j, 0, 0))
    return pl.pallas_call(
        functools.partial(fc_terms_kernel, chips),
        grid=(blocks,),
        in_specs=[
            pl.BlockSpec(memory_space=pltpu.SMEM),
            pl.BlockSpec((seq_len, width), lambda j: (0, 0)),
            pl.BlockSpec((rows, width), lambda j: (0, j)),
        ],
        out_specs=[out, out],
        out_shape=[half, half],
        compiler_params=pltpu.CompilerParams(vmem_limit_bytes=VMEM_LIMIT),
        cost_estimate=cost(0.5),
        name="fc_weight_terms",
    )(core, second_low, pre_grad)


def proj_terms_kernel(outer, inner, act_ref, up_ref, out_ref):
    value = dot_tn(act_ref[QUESTION:, :], up_ref[...])
    rows, width = value.shape
    value = value.reshape(outer, inner, rows // (outer * inner), width)
    for i in range(inner):
        out_ref[i, :, 0] = value[:, i].astype(BF16)


def proj_terms(act_low, upstream_low, outer, inner):
    seq_len, units = act_low.shape
    rows, width = upstream_low.shape
    blocks = units // width
    shape = (inner, outer, blocks, width // (outer * inner), width)
    return pl.pallas_call(
        functools.partial(proj_terms_kernel, outer, inner),
        grid=(blocks,),
        in_specs=[
            pl.BlockSpec((seq_len, width), lambda j: (0, j)),
            pl.BlockSpec((rows, width), lambda j: (0, 0)),
        ],
        out_specs=pl.BlockSpec((inner, outer, 1) + shape[3:], lambda j: (0, 0, j, 0, 0)),
        out_shape=jax.ShapeDtypeStruct(shape, BF16),
        compiler_params=pltpu.CompilerParams(vmem_limit_bytes=VMEM_LIMIT),
        cost_estimate=cost(0.5),
        name="proj_weight_terms",
    )(act_low, upstream_low)


def first_kernel(
    core_ref, tok_ref, left_mine, left_got, right_mine, right_got, vec_ref, qkvb_ref, qkv_ref,
    near_ref, rows_ref,
):
    width = tok_ref.shape[1]

    @pl.when(pl.program_id(0) == 0)
    def _():
        even_is_mine = core_ref[0] == 0
        chips, own, half = left_mine.shape[1:]
        for i in range(3):
            for side, (mine, got) in enumerate([(left_mine, left_got), (right_mine, right_got)]):
                for chip in range(chips):
                    a = mine[i, chip].astype(F32)
                    b = got[i, chip].astype(F32)
                    begin = 2 * chip * own
                    rows_ref[begin : begin + own, :] = jnp.where(even_is_mine, a, b)
                    rows_ref[begin + own : begin + 2 * own, :] = jnp.where(even_is_mine, b, a)
                near_ref[i, :, side * half : (side + 1) * half] = rows_ref[...].astype(BF16)

    first, _, _ = row_norm(tok_ref[...].astype(F32), vec_ref[0:1, :], vec_ref[1:2, :])
    first = first.astype(BF16)
    for i in range(3):
        span = slice(i * width, (i + 1) * width)
        qkv_ref[i] = (dot(first, near_ref[i]) + qkvb_ref[:, span]).astype(BF16)


def first_forward(core, tokens, pieces, vec, qkv_bias):
    seq_len, width = tokens.shape
    near = jax.ShapeDtypeStruct((3, width, width), BF16)
    return pl.pallas_call(
        first_kernel,
        grid=(seq_len // BLOCK,),
        in_specs=[
            pl.BlockSpec(memory_space=pltpu.SMEM),
            pl.BlockSpec((BLOCK, width), lambda i: (i, 0)),
            *(whole(piece) for piece in pieces),
            whole(vec),
            whole(qkv_bias),
        ],
        out_specs=[pl.BlockSpec((3, BLOCK, width), lambda i: (0, i, 0)), whole(near)],
        out_shape=[jax.ShapeDtypeStruct((3, seq_len, width), BF16), near],
        scratch_shapes=[pltpu.VMEM((width, width // 2), F32)],
        compiler_params=pltpu.CompilerParams(vmem_limit_bytes=VMEM_LIMIT),
        cost_estimate=cost(0.67),
        name="first_norm_forward",
    )(core, tokens, *pieces, vec, qkv_bias)


def group_of(blocks, own):
    each = blocks * own
    group = LANES // math.gcd(LANES, each)
    device, block, i = np.indices((group, blocks, own)).reshape(3, -1)
    swap = np.zeros((group * each, group * each), np.float32)
    swap[np.arange(group * each), block * (group * own) + device * own + i] = 1.0
    return group, jnp.asarray(swap, BF16)


def split_units_kernel(blocks, span, fc_ref, swap_ref, out_ref):
    own = fc_ref.shape[0]
    size = swap_ref.shape[0]
    groups = out_ref.shape[2] // span
    rows = [fc_ref[:, g * size : (g + 1) * size].astype(F32) for g in range(groups)]
    swapped = dot(jnp.concatenate(rows, axis=0).astype(BF16), swap_ref[...])
    for g in range(groups):
        part = swapped[g * own : (g + 1) * own]
        for j in range(blocks):
            piece = part[:, j * span : (j + 1) * span]
            out_ref[j, :, g * span : (g + 1) * span] = piece.astype(BF16)


def split_units(fc_shard, blocks):
    own, units = fc_shard.shape
    group, swap = group_of(blocks, own)
    return pl.pallas_call(
        functools.partial(split_units_kernel, blocks, group * own),
        out_shape=jax.ShapeDtypeStruct((blocks, own, units // blocks), BF16),
        compiler_params=pltpu.CompilerParams(vmem_limit_bytes=VMEM_LIMIT),
        name="units_split",
    )(fc_shard, swap)


def row_terms_kernel(span, index_ref, fac_ref, proj_ref, fc_ref, swap_ref, proj_out, fc_out):
    blocks, own, width = proj_ref.shape
    units = blocks * width
    shape = (width, own)
    mine = lax.broadcasted_iota(jnp.int32, shape, 0) - index_ref[0] * own
    select = (mine == lax.broadcasted_iota(jnp.int32, shape, 1)).astype(BF16)
    upstream = fac_ref[:, units : units + width]
    terms = []
    second = dot(fac_ref[:, units + width : units + 2 * width], select).astype(BF16)
    for j in range(blocks):
        act = dot(fac_ref[:, j * width : (j + 1) * width], select).astype(BF16)
        proj_out[j] = proj_ref[j] + dot_tn(act, upstream)
        begin = units + 2 * width + j * width
        terms.append(fc_ref[j] + dot_tn(second, fac_ref[:, begin : begin + width]))
    size = swap_ref.shape[0]
    groups = width // span
    rows = [
        jnp.concatenate([t[:, g * span : (g + 1) * span] for t in terms], axis=1)
        for g in range(groups)
    ]
    left = jnp.concatenate(rows, axis=0)
    pieces = []
    for _ in range(3):
        pieces.append(left.astype(BF16))
        left = left - pieces[-1].astype(F32)
    total = sum(dot_nt(piece, swap_ref[...]) for piece in pieces)
    for g in range(groups):
        fc_out[:, g * size : (g + 1) * size] = total[g * own : (g + 1) * own]


def row_terms(index, factors, proj_sum, fc_sum):
    blocks, own, width = fc_sum.shape
    out_shape = [
        jax.ShapeDtypeStruct(proj_sum.shape, F32),
        jax.ShapeDtypeStruct((own, blocks * width), F32),
    ]
    group, swap = group_of(blocks, own)
    return pl.pallas_call(
        functools.partial(row_terms_kernel, group * own),
        grid=(1,),
        in_specs=[
            pl.BlockSpec(memory_space=pltpu.SMEM),
            whole(factors),
            whole(proj_sum),
            whole(fc_sum),
            whole(swap),
        ],
        out_specs=[whole(x) for x in out_shape],
        out_shape=out_shape,
        compiler_params=pltpu.CompilerParams(vmem_limit_bytes=VMEM_LIMIT),
        cost_estimate=cost(0.33),
        name="thought_rows_terms",
    )(index, factors, proj_sum, fc_sum, swap)


def spread_matrix(shard, count):
    shape = (shard, shard * count)
    column = lax.broadcasted_iota(jnp.int32, shape, 1) % shard
    return (column == lax.broadcasted_iota(jnp.int32, shape, 0)).astype(BF16)


def owner_mask(shard, count):
    shape = (count, shard * count)
    owner = lax.broadcasted_iota(jnp.int32, shape, 1) // shard
    return owner == lax.broadcasted_iota(jnp.int32, shape, 0)


VECTOR_ROWS = ("ln1_gain", "ln1_bias", "out_bias", "ln2_gain", "ln2_bias", "proj_bias")


def unpack_kernel(sizes, devices, packed_ref, vec_ref, fcb_ref, qkvb_ref):
    vec_ref[...] = jnp.zeros_like(vec_ref)
    width = vec_ref.shape[1]
    for at, (name, size) in enumerate(sizes):
        if name == "fc_bias":
            own = width // devices
            for j in range(size // own):
                spread = dot(packed_ref[at][:, j * own : (j + 1) * own], spread_matrix(own, devices))
                spread = jnp.where(owner_mask(own, devices), spread, 0.0)
                span = slice(j * width, (j + 1) * width)
                fcb_ref[:, span] = jnp.sum(spread, axis=0, keepdims=True)
            continue
        block = packed_ref[at][:, :size]
        spread = dot(block, spread_matrix(size, devices))
        full = jnp.sum(jnp.where(owner_mask(size, devices), spread, 0.0), axis=0, keepdims=True)
        if name == "qv_bias":
            qkvb_ref[:, :width] = full[:, :width]
            qkvb_ref[:, width : 2 * width] = jnp.zeros((1, width), F32)
            qkvb_ref[:, 2 * width :] = full[:, width:]
        else:
            at = VECTOR_ROWS.index(name)
            vec_ref[at : at + 1, :] = full


def unpack(packed, sizes):
    devices = packed.shape[1]
    size = dict(sizes)
    width = size["ln1_gain"] * devices
    return pl.pallas_call(
        functools.partial(unpack_kernel, sizes, devices),
        out_shape=[
            jax.ShapeDtypeStruct((8, width), F32),
            jax.ShapeDtypeStruct((1, size["fc_bias"] * devices), F32),
            jax.ShapeDtypeStruct((1, 3 * width), F32),
        ],
        compiler_params=pltpu.CompilerParams(vmem_limit_bytes=VMEM_LIMIT),
        name="vectors_unpack",
    )(packed)


def pack_kernel(sizes, devices, *refs):
    out_ref = refs[-1]
    out_ref[...] = jnp.zeros_like(out_ref)
    width = refs[0].shape[1]
    for at, ((name, size), ref) in enumerate(zip(sizes, refs)):
        if name == "fc_bias":
            own = width // devices
            for j in range(size // own):
                row = jnp.broadcast_to(ref[:, j * width : (j + 1) * width], (devices, width))
                row = jnp.where(owner_mask(own, devices), row, 0.0).astype(BF16)
                piece = dot_nt(row, spread_matrix(own, devices))
                out_ref[at, :, j * own : (j + 1) * own] = piece.astype(BF16)
            continue
        row = jnp.broadcast_to(ref[...], (devices, ref.shape[1]))
        own = jnp.where(owner_mask(size, devices), row, 0.0).astype(BF16)
        out_ref[at, :, :size] = dot_nt(own, spread_matrix(size, devices)).astype(BF16)


def pack(rows, sizes, devices):
    return pl.pallas_call(
        functools.partial(pack_kernel, sizes, devices),
        out_shape=jax.ShapeDtypeStruct((len(sizes), devices, LANES), BF16),
        compiler_params=pltpu.CompilerParams(vmem_limit_bytes=VMEM_LIMIT),
        name="vectors_pack",
    )(*[rows[name] for name, _ in sizes])


def join_kernel(*refs):
    out_ref = refs[-1]
    out_ref[...] = jnp.zeros_like(out_ref)
    for at, ref in enumerate(refs[:-1]):
        out_ref[at : at + 1, : ref.shape[0]] = ref[...].astype(F32).reshape(1, ref.shape[0])


def join(vectors):
    return pl.pallas_call(
        join_kernel,
        out_shape=jax.ShapeDtypeStruct((len(vectors), LANES), F32),
        name="vectors_join",
    )(*vectors)


def part_kernel(joined_ref, *refs):
    for at, ref in enumerate(refs):
        ref[...] = joined_ref[at, : ref.shape[0]]


def part(joined, sizes):
    return pl.pallas_call(
        part_kernel,
        out_shape=[jax.ShapeDtypeStruct((size,), F32) for _, size in sizes],
        name="vectors_part",
    )(joined)


def norm_parts(hidden):
    mean = jnp.mean(hidden, axis=-1, keepdims=True)
    centred = hidden - mean
    inverse = lax.rsqrt(jnp.mean(centred * centred, axis=-1, keepdims=True) + EPSILON)
    return centred * inverse, inverse


def step_on_sequence(
    near_pieces, far, vectors, tokens, cotangent, slots, count, answer_start, devices, sizes, comm
):
    vec, fc_bias, qkv_bias = vectors
    seq_len, width = tokens.shape
    info = jnp.stack([slots[0], count])

    qkv_first, near = first_forward(comm.core, tokens, near_pieces, vec, qkv_bias)
    mixed_hidden, lse_hidden = attend(info, qkv_first)
    late = QUESTION + lax.iota(jnp.int32, seq_len - QUESTION)
    upstream_low = jnp.where(
        (late >= answer_start)[:, None], cotangent[QUESTION:], jnp.zeros((), BF16)
    )
    tokens32 = tokens.astype(F32)
    weights = (near, after(far, mixed_hidden, upstream_low, tokens32))
    lse, *saved, qkv, mixed_low, hidden = thoughts_forward(
        info, tokens, tokens32, qkv_first, mixed_hidden, lse_hidden, weights, vec, fc_bias, qkv_bias
    )
    output, second_low, act_low, slope, normed_two, inverse_two, first_low = feed_forward(
        hidden, mixed_low, weights, vec, fc_bias
    )

    proj_grad = comm.proj_terms(act_low, upstream_low)
    proj_half = comm.early(proj_grad)
    pre_grad, resid_grad, mixed_grad, sums = feed_back(
        after(upstream_low, proj_grad), slope, normed_two, inverse_two, weights, vec
    )
    fc_going = comm.scatter(fc_terms(comm.core, second_low, pre_grad, comm.chips("zyxc")), "zyxc")
    sent = fc_going.go()
    row_sums, factors, mixed_grad, resid_grad = thoughts_back(
        info,
        hidden,
        qkv,
        mixed_low,
        after(lse, sent),
        saved,
        weights,
        vec,
        mixed_grad,
        resid_grad,
    )
    join_after([fc_going], row_sums)
    spread = comm.factors(factors[:THOUGHTS].astype(BF16))
    sent = go_after([fc_going, spread])
    proj_half = after(proj_half, *sent)
    proj_going = comm.early_end(proj_half)
    lse, back_grad = after((lse, mixed_grad), sent, proj_half)
    qkv_grad = attend_back(qkv, mixed_low, lse, back_grad)
    join_after([fc_going, spread], qkv_grad)
    sent = go_after([fc_going, spread], qkv_grad)
    first_low = after(first_low, *sent)
    terms = near_terms(
        comm.core,
        first_low,
        qkv_grad,
        mixed_low,
        resid_grad,
        comm.chips("zxyc"),
        comm.chips("zyxc"),
    )
    first = comm.scatter(terms[:2], "zxyc")
    rest = comm.scatter(terms[2:], "zyxc")

    sent = go_after([first, rest])
    join_after([spread], *sent)
    go_after([spread])
    join_after([first, rest, fc_going])
    sent = go_after([first, rest, fc_going], spread.buf)
    input_grad, first_sums = first_back(info, hidden, after(qkv_grad, *sent), resid_grad, weights, vec)
    join_after([first, rest, fc_going], input_grad)
    sent = go_after([first, rest, fc_going])
    sums = after(sums, *sent) + row_sums
    small = {name: sums[i : i + 1, :width] for i, name in enumerate(SUM_ROWS)}
    small["fc_bias"] = sums[0:1]
    small["ln1_gain"] = first_sums[0:1]
    small["ln1_bias"] = first_sums[1:2]
    small["qv_bias"] = jnp.concatenate([first_sums[2:3], first_sums[3:4]], axis=1)
    vectors_going = comm.scatter_vectors(pack(small, sizes, devices))
    go_after([vectors_going])
    join_after([vectors_going])
    join_after([spread], vectors_going.buf)
    going = [first, rest, fc_going, spread, vectors_going]
    sent = go_after([spread, vectors_going])
    join_after(going, *sent)
    proj_g = fc_g = None
    while any(swap.todo for swap in going) or proj_g is None:
        group = [swap for swap in going if swap.todo]
        sent = go_after(group)
        done = ()
        behind = len(vectors_going.todo)
        if behind and behind >= max(len(swap.todo) for swap in going) and len(group) > 1:
            join_after([vectors_going], *sent)
            sent = go_after([vectors_going])
        if proj_g is None and fc_going not in group and spread not in group:
            factors = after(spread.finish(), *sent)
            proj_g, fc_g = comm.terms(factors, proj_going, fc_going.buf)
            done = (proj_g, fc_g)
        join_after(group, *done)
    return output, input_grad, first.buf, rest.buf, proj_g, fc_g, vectors_going.buf


SMALL = ("ln1_gain", "ln1_bias", "qv_bias", "out_bias", "ln2_gain", "ln2_bias", "fc_bias", "proj_bias")


def on_device(
    links,
    tokens,
    ln1_gain,
    ln1_bias,
    qkv_weight,
    qv_bias,
    out_weight,
    out_bias,
    ln2_gain,
    ln2_bias,
    fc_weight,
    fc_bias,
    proj_weight,
    proj_bias,
    cotangent,
    thought_slots,
    thought_count,
    answer_start,
):
    devices = links.sizes["dp"] * links.sizes["fsdp"]
    small_shards = dict(
        ln1_gain=ln1_gain,
        ln1_bias=ln1_bias,
        qv_bias=qv_bias,
        out_bias=out_bias,
        ln2_gain=ln2_gain,
        ln2_bias=ln2_bias,
        fc_bias=fc_bias,
        proj_bias=proj_bias,
    )
    sizes = tuple((n, small_shards[n].shape[0]) for n in SMALL)
    own, width = out_weight.shape
    blocks = proj_weight.shape[0] // own
    both = ("dp", "fsdp")

    far_shard = jnp.concatenate(
        [
            split_units(fc_weight, blocks),
            proj_weight.reshape(blocks, own, width),
            out_weight[None],
        ],
        axis=0,
    )
    far = lax.all_gather(far_shard, both, axis=1, tiled=True)

    packed = join([small_shards[n] for n in SMALL]).astype(BF16)
    small = links.gather(packed, "zxyc", axis=0).reshape(devices, len(sizes), LANES)
    half = width // 2
    near_pieces = []
    for side, text in enumerate(("zxyc", "zyxc")):
        part_columns = [
            qkv_weight[:, i * width + side * half : i * width + (side + 1) * half] for i in range(3)
        ]
        ring = Gather(links, jnp.stack(part_columns), text, axis=1)
        near_pieces += ring.last()

    class Comm:
        chips = links.chips
        core = (lax.axis_index("fsdp") % 2)[None].astype(jnp.int32)

        @staticmethod
        def proj_terms(act_low, upstream_low):
            return proj_terms(act_low, upstream_low, links.sizes["dp"], links.sizes["fsdp"])

        @staticmethod
        def early(value):
            return lax.psum_scatter(
                value.reshape(-1, width), "fsdp", scatter_dimension=0, tiled=True
            )

        @staticmethod
        def early_end(value):
            value = lax.psum_scatter(value, "dp", scatter_dimension=0, tiled=True)
            return value.reshape(blocks, own, width)

        @staticmethod
        def scatter(halves, text):
            return links.scatter(tuple(halves), text)

        @staticmethod
        def factors(rows):
            return Gather(links, rows, "zxyc")

        @staticmethod
        def scatter_vectors(value):
            return links.scatter(value.transpose(1, 0, 2), "zxyc")

        @staticmethod
        def terms(factors, proj_sum, fc_sum):
            index = lax.axis_index(both)[None].astype(jnp.int32)
            factors = factors.reshape(devices * THOUGHTS, -1)
            return row_terms(index, factors, proj_sum.astype(F32), fc_sum)

    output, input_grad, first, rest, proj_g, fc_g, vector_sums = step_on_sequence(
        near_pieces,
        far,
        unpack(small.transpose(1, 0, 2), sizes),
        tokens[0],
        cotangent[0],
        thought_slots[0],
        thought_count[0],
        answer_start[0],
        devices,
        sizes,
        Comm,
    )
    proj_g = proj_g.reshape(blocks * own, width)
    qkv_g = jnp.concatenate([first[0], first[1], rest[0]], axis=1)
    out_g = rest[1]
    owned = dict(zip(SMALL, part(vector_sums, sizes)))
    return (
        output[None],
        input_grad[None],
        owned["ln1_gain"],
        owned["ln1_bias"],
        qkv_g,
        owned["qv_bias"],
        out_g,
        owned["out_bias"],
        owned["ln2_gain"],
        owned["ln2_bias"],
        fc_g,
        owned["fc_bias"],
        proj_g,
        owned["proj_bias"],
    )


def solution(mesh):
    links = Links({name: mesh.shape[name] for name in ("dp", "fsdp")})
    both = ("dp", "fsdp")
    cube, matrix, vector = P(both, None, None), P(both, None), P(both)
    weight_specs = (
        vector,
        vector,
        matrix,
        vector,
        matrix,
        vector,
        vector,
        vector,
        matrix,
        vector,
        matrix,
        vector,
    )

    def per_device(*args):
        return on_device(links, *args)

    return jax.shard_map(
        per_device,
        mesh=mesh,
        in_specs=(cube,) + weight_specs + (cube, matrix, vector, vector),
        out_specs=(cube, cube) + weight_specs,
        check_vma=False,
    )
```

```python
import functools
import math

import jax
import jax.numpy as jnp
import numpy as np
from jax import lax
from jax.experimental import pallas as pl
from jax.experimental.pallas import tpu as pltpu
from jax.sharding import PartitionSpec as P

HD = 64
THOUGHTS = 2
PREFIX = 384
QUESTION = 256
SCALE = 0.125
EPSILON = 1e-05
BLOCK = 256
HEAD_ROWS = 16
WINDOW = 32
LANES = 128
FACTOR_ROWS = 32
PAIR = 2 * HD
NEG = -1e30

F32 = jnp.float32
BF16 = jnp.bfloat16
VMEM_LIMIT = 56 * 1024 * 1024


def cost(microseconds):
    return pl.CostEstimate(
        flops=int(microseconds * 1.15e9),
        bytes_accessed=int(microseconds * 3.6e6),
        transcendentals=0,
    )


def dot(a, b):
    return lax.dot_general(a, b, (((1,), (0,)), ((), ())), preferred_element_type=F32)


def dot_nt(a, b):
    return lax.dot_general(a, b, (((1,), (1,)), ((), ())), preferred_element_type=F32)


def dot_tn(a, b):
    return lax.dot_general(a, b, (((0,), (0,)), ((), ())), preferred_element_type=F32)


def bits_of(size):
    return [1 << i for i in reversed(range(int(math.log2(size))))]


class Links:
    def __init__(self, sizes):
        self.sizes = sizes
        self.canon = [("dp", b) for b in bits_of(sizes["dp"])] + [
            ("fsdp", b) for b in bits_of(sizes["fsdp"])
        ]
        dp_bits = [("dp", b) for b in bits_of(sizes["dp"])]
        f_bits = [("fsdp", b) for b in bits_of(sizes["fsdp"])]
        self.groups = {"x": dp_bits[-1:], "y": dp_bits[:-1], "z": f_bits[:-1], "c": f_bits[-1:]}

    def order(self, text):
        out = []
        for letter in text:
            out += self.groups[letter]
        return out

    def swap(self, value, stage):
        axis, bit = stage
        return lax.ppermute(value, axis, [(i, i ^ bit) for i in range(self.sizes[axis])])

    def mine(self, stage):
        axis, bit = stage
        return (lax.axis_index(axis) & bit) != 0

    def gather(self, shard, text, axis=0):
        return Gather(self, shard, text, axis).finish()

    def chips(self, text):
        stages = list(reversed(self.order(text)))[1:]
        rest = [c for c in self.canon if c in stages]
        order = []
        for spot in range(1 << len(stages)):
            chip = 0
            for at, stage in enumerate(stages):
                if spot & (1 << (len(stages) - 1 - at)):
                    chip |= 1 << (len(rest) - 1 - rest.index(stage))
            order.append(chip)
        return order

    def scatter(self, value, text):
        return Scatter(self, value, text)


class Gather:
    def __init__(self, links, shard, text, axis=0):
        self.links = links
        self.shape = shard.shape
        self.axis = axis
        self.todo = links.order(text)
        self.done = []
        self.buf = shard
        self.got = None

    def go(self):
        self.add()
        self.stage = self.todo.pop(0)
        self.got = self.links.swap(self.buf, self.stage)
        return self.buf

    def add(self):
        if self.got is not None:
            canon = self.links.canon
            place = sum(1 for d in self.done if canon.index(d) < canon.index(self.stage))
            high = self.links.mine(self.stage)
            pair = [jnp.where(high, self.got, self.buf), jnp.where(high, self.buf, self.got)]
            self.buf = jnp.stack(pair, axis=self.axis + place)
            self.done.append(self.stage)
            self.got = None
        return self.buf

    def hold(self, *deps):
        self.buf = after(self.buf, *deps)

    def join(self, *deps):
        self.got = after(self.got, *deps)
        self.add()

    def last(self):
        while self.todo:
            self.go()
        shape = self.shape
        shape = shape[: self.axis] + (-1,) + shape[self.axis :]
        return [self.buf.reshape(shape), self.got.reshape(shape)]

    def finish(self):
        while self.todo:
            self.go()
        self.add()
        shape = self.shape
        return self.buf.reshape(shape[: self.axis] + (-1,) + shape[self.axis + 1 :])


class Scatter:
    def __init__(self, links, value, text):
        self.links = links
        self.left = list(links.canon)
        self.todo = list(reversed(links.order(text)))
        self.got = None
        self.split = False
        if isinstance(value, tuple):
            self.split = True
            self.left = self.todo[1:]
            shape = (2,) * len(self.left) + value[0].shape[1:]
            self.keep, self.buf = (v.reshape(shape) for v in value)
        else:
            self.buf = value.reshape((2,) * len(self.left) + value.shape[1:])

    def go(self):
        stage = self.todo.pop(0)
        if self.split:
            self.split = False
            sent = self.buf
        else:
            place = self.left.index(stage)
            self.left.remove(stage)
            high = self.links.mine(stage).astype(jnp.int32)
            parts = [self.buf] if self.got is None else [self.keep, self.got]

            def half(side):
                cut = [lax.dynamic_index_in_dim(p, side, place, keepdims=False) for p in parts]
                return cut[0] if len(cut) == 1 else cut[0].astype(F32) + cut[1].astype(F32)

            sent = half(1 - high).astype(BF16)
            self.keep = half(high)
        self.got = self.links.swap(sent, stage)
        return sent

    def hold(self, *deps):
        if self.got is None:
            self.buf = after(self.buf, *deps)
        else:
            self.got = after(self.got, *deps)

    def join(self, *deps):
        self.got = after(self.got, *deps)

    def finish(self):
        return self.keep.astype(F32) + self.got.astype(F32)


def join_after(swaps, *deps):
    for swap in swaps:
        swap.join(*deps)


def go_after(swaps, *deps):
    for swap in swaps:
        swap.hold(*deps)
    return tuple(swap.go() for swap in swaps)


def after(value, *deps):
    return lax.optimization_barrier((value, deps))[0]


def attend_kernel(info_ref, q_ref, k_ref, v_ref, o_ref, lse_ref):
    seq_len = q_ref.shape[0]
    slot = info_ref[0]
    keys = k_ref[...]
    values_t = v_ref[...].T
    lane = lax.broadcasted_iota(jnp.int32, (BLOCK, PAIR), 1)
    sub = lax.broadcasted_iota(jnp.int32, (PAIR, BLOCK), 0)
    key_pos = lax.broadcasted_iota(jnp.int32, (BLOCK, BLOCK), 0)
    row_pos = lax.broadcasted_iota(jnp.int32, (BLOCK, BLOCK), 1)
    causal = key_pos <= row_pos
    middle_pos = QUESTION + lax.broadcasted_iota(jnp.int32, (PREFIX - QUESTION, BLOCK), 0)
    is_slot = (middle_pos >= slot) & (middle_pos < slot + THOUGHTS)

    def hide(scores):
        if scores.shape[0] <= QUESTION:
            return scores
        middle = jnp.where(is_slot, NEG, scores[QUESTION:PREFIX])
        return jnp.concatenate([scores[:QUESTION], middle, scores[PREFIX:]], axis=0)

    for begin in range(0, seq_len, BLOCK):
        end = begin + BLOCK
        queries = q_ref[begin:end, :] * jnp.asarray(SCALE, BF16)
        parts = []
        for head in range(2):
            own = jnp.where((lane >= HD) == bool(head), queries, jnp.zeros_like(queries))
            scores = dot_nt(keys[:end], own)
            last = jnp.where(causal, scores[begin:], NEG)
            if begin:
                last = jnp.concatenate([scores[:begin], last], axis=0)
            scores = hide(last)
            peak = jnp.max(scores, axis=0, keepdims=True)
            expo = jnp.exp(scores - peak)
            total = jnp.sum(expo, axis=0, keepdims=True)
            mixed = dot(values_t[:, :end], expo.astype(BF16))
            parts.append(mixed / total)
            lse_ref[pl.ds(2 * pl.program_id(0) + head, 1), begin:end] = peak + jnp.log(total)
        o_ref[begin:end, :] = jnp.where(sub < HD, parts[0], parts[1]).T.astype(BF16)


def attend(info, qkv):
    _, seq_len, width = qkv.shape
    pairs = width // PAIR

    def columns(i):
        return pl.BlockSpec((None, seq_len, PAIR), lambda g, i=i: (i, 0, g))

    return pl.pallas_call(
        attend_kernel,
        grid=(pairs,),
        in_specs=[
            pl.BlockSpec(memory_space=pltpu.SMEM),
            *(columns(i) for i in range(3)),
        ],
        out_specs=[
            pl.BlockSpec((seq_len, PAIR), lambda g: (0, g)),
            pl.BlockSpec((HEAD_ROWS, seq_len), lambda g: (0, 0)),
        ],
        out_shape=[
            jax.ShapeDtypeStruct((seq_len, width), BF16),
            jax.ShapeDtypeStruct((HEAD_ROWS, seq_len), F32),
        ],
        compiler_params=pltpu.CompilerParams(vmem_limit_bytes=VMEM_LIMIT),
        cost_estimate=cost(2.0),
        name="attention_forward",
    )(info, qkv, qkv, qkv)


def attend_back_kernel(
    q_ref, k_ref, v_ref, o_ref, lse_ref, g_ref, out_ref, dk_acc, dv_acc
):
    seq_len = q_ref.shape[0]
    pair = pl.program_id(0)
    first_row = seq_len - g_ref.shape[0]
    keys = k_ref[...]
    values = v_ref[...]
    keys_t = keys.T
    lane = lax.broadcasted_iota(jnp.int32, (BLOCK, PAIR), 1)
    sub = lax.broadcasted_iota(jnp.int32, (PAIR, BLOCK), 0)
    key_pos = lax.broadcasted_iota(jnp.int32, (BLOCK, BLOCK), 0)
    row_pos = lax.broadcasted_iota(jnp.int32, (BLOCK, BLOCK), 1)
    causal = key_pos <= row_pos
    dk_acc[...] = jnp.zeros_like(dk_acc)
    dv_acc[...] = jnp.zeros_like(dv_acc)
    for begin in range(first_row, seq_len, BLOCK):
        end = begin + BLOCK
        local = begin - first_row
        queries = q_ref[begin:end, :] * jnp.asarray(SCALE, BF16)
        grads = g_ref[local : local + BLOCK, :]
        product_t = (grads.astype(F32) * o_ref[begin:end, :].astype(F32)).T
        parts = []
        for head in range(2):
            chosen = (lane >= HD) == bool(head)
            own = jnp.where(chosen, queries, jnp.zeros_like(queries))
            own_grad = jnp.where(chosen, grads, jnp.zeros_like(grads))
            delta = jnp.sum(product_t[head * HD : (head + 1) * HD], axis=0, keepdims=True)
            lse = lse_ref[pl.ds(2 * pair + head, 1), begin:end]
            total = None
            for low, high in ((0, begin), (begin, end)):
                scores = dot_nt(keys[low:high], own)
                if high == end:
                    scores = jnp.where(causal, scores, NEG)
                probs = jnp.exp(scores - lse)
                prob_grad = dot_nt(values[low:high], own_grad)
                score_grad = (probs * (prob_grad - delta)).astype(BF16)
                dv_acc[low:high, :] += dot(probs.astype(BF16), own_grad)
                dk_acc[low:high, :] += dot(score_grad, own)
                part = dot(keys_t[:, low:high], score_grad)
                total = part if total is None else total + part
            parts.append(total)
        mine = jnp.where(sub < HD, parts[0], parts[1]).T * SCALE
        out_ref[0, begin:end, :] = mine.astype(BF16)
    out_ref[0, :first_row, :] = jnp.zeros((first_row, PAIR), BF16)
    out_ref[1] = dk_acc[...].astype(BF16)
    out_ref[2] = dv_acc[...].astype(BF16)


def attend_back(qkv, mixed_low, lse, mixed_grad):
    _, seq_len, width = qkv.shape
    rows = mixed_grad.shape[0]

    def columns(i):
        return pl.BlockSpec((None, seq_len, PAIR), lambda g, i=i: (i, 0, g))

    late = pl.BlockSpec((rows, PAIR), lambda g: (0, g))
    return pl.pallas_call(
        attend_back_kernel,
        grid=(width // PAIR,),
        in_specs=[
            *(columns(i) for i in range(3)),
            pl.BlockSpec((seq_len, PAIR), lambda g: (0, g)),
            pl.BlockSpec((HEAD_ROWS, seq_len), lambda g: (0, 0)),
            late,
        ],
        out_specs=pl.BlockSpec((3, seq_len, PAIR), lambda g: (0, 0, g)),
        out_shape=jax.ShapeDtypeStruct((3, seq_len, width), BF16),
        scratch_shapes=[pltpu.VMEM((seq_len, PAIR), F32), pltpu.VMEM((seq_len, PAIR), F32)],
        compiler_params=pltpu.CompilerParams(vmem_limit_bytes=VMEM_LIMIT),
        cost_estimate=cost(2.17),
        name="attention_backward",
    )(qkv, qkv, qkv, mixed_low, lse, mixed_grad)


def row_norm(row, gain, bias):
    mean = jnp.mean(row, axis=-1, keepdims=True)
    centred = row - mean
    inverse = lax.rsqrt(jnp.mean(centred * centred, axis=-1, keepdims=True) + EPSILON)
    normed = centred * inverse
    return normed * gain + bias, normed, inverse


def row_norm_back(incoming, normed, inverse, gain):
    scaled = incoming * gain
    inner = (
        scaled
        - jnp.mean(scaled, axis=-1, keepdims=True)
        - normed * jnp.mean(scaled * normed, axis=-1, keepdims=True)
    )
    return inner * inverse


GELU_A = 0.7978845608028654
GELU_B = 0.044715


def gelu(pre):
    return 0.5 * pre * (1.0 + jnp.tanh(GELU_A * (pre + GELU_B * pre * pre * pre)))


def gelu_slope(pre):
    square = pre * pre
    curve = jnp.tanh(GELU_A * pre * (1.0 + GELU_B * square))
    return 0.5 * (1.0 + curve) + 0.5 * pre * (1.0 - curve * curve) * GELU_A * (
        1.0 + 3.0 * GELU_B * square
    )


def widen(row):
    return jnp.broadcast_to(row, (8, row.shape[1])).astype(BF16)


def pick(block, index):
    rows = lax.broadcasted_iota(jnp.int32, block.shape, 0)
    return jnp.sum(jnp.where(rows == index, block.astype(F32), 0.0), axis=0, keepdims=True)


def put(block, index, row):
    rows = lax.broadcasted_iota(jnp.int32, block.shape, 0)
    return jnp.where(rows == index, row.astype(block.dtype), block)


def by_head(row, heads):
    shape = (heads, row.shape[1])
    lane_head = lax.broadcasted_iota(jnp.int32, shape, 1) // HD
    return jnp.where(lane_head == lax.broadcasted_iota(jnp.int32, shape, 0), row, 0.0)


def heads_only(block):
    lane_head = lax.broadcasted_iota(jnp.int32, block.shape, 1) // HD
    own = lane_head == lax.broadcasted_iota(jnp.int32, block.shape, 0)
    return jnp.sum(jnp.where(own, block, 0.0), axis=0, keepdims=True)


def thoughts_kernel(
    info_ref,
    tok_ref,
    lse_in_ref,
    vec_ref,
    fcb_ref,
    qkvb_ref,
    near_in,
    far_in,
    qkv_in,
    mixed_in,
    hid_in,
    lse_ref,
    pre_ref,
    prob_ref,
    res_ref,
    qkv_out,
    mixed_out,
    hid_out,
    kv_ref,
    late_q_ref,
    mixed_ref,
    hid_ref,
    near_ref,
    far_ref,
    sems,
):
    width = tok_ref.shape[1]
    blocks = (far_ref.shape[0] - 1) // 2
    rows = late_q_ref.shape[0]
    ln1_gain, ln1_bias, out_bias, ln2_gain, ln2_bias, proj_bias = (
        vec_ref[i : i + 1, :] for i in range(6)
    )
    slot = info_ref[0]
    count = info_ref[1]

    loads = [
        (qkv_in.at[:, pl.ds(0, PREFIX)], kv_ref),
        (far_in.at[pl.ds(2 * blocks, 1)], far_ref.at[pl.ds(2 * blocks, 1)]),
        (far_in.at[pl.ds(0, blocks)], far_ref.at[pl.ds(0, blocks)]),
        (far_in.at[pl.ds(blocks, blocks)], far_ref.at[pl.ds(blocks, blocks)]),
        (near_in, near_ref),
        (qkv_in.at[0, pl.ds(QUESTION, rows)], late_q_ref),
        (mixed_in.at[pl.ds(QUESTION, rows)], mixed_ref),
    ]
    loads = [pltpu.make_async_copy(a, b, sems.at[i]) for i, (a, b) in enumerate(loads)]
    for copy in loads:
        copy.start()
    hid_ref[...] = tok_ref[...].astype(F32)
    hidden_row = pick(hid_ref[...], slot - 1 - QUESTION)
    loads[0].wait()
    slot_rows = []
    slot_lse = []
    for step in range(THOUGHTS + 1):
        at = slot - 1 + step
        qkv_row = pick(kv_ref[0, QUESTION:, :], at - QUESTION)
        query = by_head(qkv_row * SCALE, HEAD_ROWS).astype(BF16)
        scores = dot_nt(query, kv_ref[1])
        key_pos = lax.broadcasted_iota(jnp.int32, scores.shape, 1)
        scores = jnp.where(key_pos <= at, scores, NEG)
        peak = jnp.max(scores, axis=1, keepdims=True)
        expo = jnp.exp(scores - peak)
        total = jnp.sum(expo, axis=1, keepdims=True)
        probs = expo / total
        mixed = heads_only(dot(probs.astype(BF16), kv_ref[2]))
        if step:
            slot_rows.append(mixed)
            slot_lse.append(peak + jnp.log(total))
        if step == THOUGHTS:
            break
        prob_ref[step * HEAD_ROWS : (step + 1) * HEAD_ROWS, :] = probs
        if not step:
            loads[1].wait()
        resid = hidden_row + dot(widen(mixed), far_ref[2 * blocks])[0:1] + out_bias
        res_ref[step : step + 1, :] = resid
        second, _, _ = row_norm(resid, ln2_gain, ln2_bias)
        second = widen(second)
        if not step:
            loads[2].wait()
        acts = []
        for j in range(blocks):
            span = slice(j * width, (j + 1) * width)
            pre = dot(second, far_ref[j])[0:1] + fcb_ref[0:1, span]
            pre_ref[step : step + 1, span] = pre
            acts.append(widen(gelu(pre)))
        if not step:
            loads[3].wait()
        fed = resid + proj_bias
        for j in range(blocks):
            fed = fed + dot(acts[j], far_ref[blocks + j])[0:1]
        first, _, _ = row_norm(fed, ln1_gain, ln1_bias)
        first = widen(first)
        hidden_row = fed
        spot = jnp.where(step < count, slot + step - QUESTION, -1)
        hid_ref[...] = put(hid_ref[...], spot, fed)
        if not step:
            loads[4].wait()
        for i in range(3):
            span = slice(i * width, (i + 1) * width)
            new_row = dot(first, near_ref[i])[0:1] + qkvb_ref[0:1, span]
            kv_ref[i, QUESTION:, :] = put(kv_ref[i, QUESTION:, :], spot, new_row)
    loads[5].wait()
    loads[6].wait()
    stores = [
        pltpu.make_async_copy(
            kv_ref.at[:, pl.ds(QUESTION, PREFIX - QUESTION)],
            qkv_out.at[:, pl.ds(QUESTION, PREFIX - QUESTION)],
            sems.at[0],
        ),
        pltpu.make_async_copy(
            hid_ref, hid_out.at[pl.ds(QUESTION, PREFIX - QUESTION)], sems.at[1]
        ),
    ]
    for copy in stores:
        copy.start()

    row_pos = QUESTION + lax.broadcasted_iota(jnp.int32, (HEAD_ROWS, rows), 1)
    late_q = late_q_ref[...]
    lse = lse_in_ref[:, QUESTION:]
    scores = []
    values = []
    top = lse
    for j in range(THOUGHTS):
        local = slot + j - QUESTION
        key = by_head(pick(kv_ref[1, QUESTION:, :], local) * SCALE, HEAD_ROWS)
        values.append(pick(kv_ref[2, QUESTION:, :], local))
        score = jnp.where(row_pos >= slot + j, dot_nt(key.astype(BF16), late_q), NEG)
        scores.append(score)
        top = jnp.maximum(top, score)
    whole_sum = jnp.exp(lse - top)
    for score in scores:
        whole_sum = whole_sum + jnp.exp(score - top)
    new_lse = top + jnp.log(whole_sum)
    ones = by_head(jnp.ones((1, width), F32), HEAD_ROWS).astype(BF16)
    share = jnp.exp(lse - new_lse)
    high = share.astype(BF16)
    low = (share - high.astype(F32)).astype(BF16)
    weights = [jnp.exp(score - new_lse).astype(BF16) for score in scores]
    step_rows = PREFIX - QUESTION
    for begin in range(0, rows, step_rows):
        span = slice(begin, begin + step_rows)
        part = mixed_ref[span, :].astype(F32) * (
            dot_tn(high[:, span], ones) + dot_tn(low[:, span], ones)
        )
        for weight, value in zip(weights, values):
            part = part + dot_tn(weight[:, span], ones) * value
        if not begin:
            for j in range(THOUGHTS):
                part = put(part, slot + j - QUESTION, slot_rows[j])
        mixed_ref[span, :] = part.astype(BF16)
    stores.append(
        pltpu.make_async_copy(mixed_ref, mixed_out.at[pl.ds(QUESTION, rows)], sems.at[2])
    )
    stores[-1].start()
    lse_ref[:, :QUESTION] = lse_in_ref[:, :QUESTION]
    column = lax.broadcasted_iota(jnp.int32, (HEAD_ROWS, step_rows), 1)
    middle = new_lse[:, :step_rows]
    for j in range(THOUGHTS):
        middle = jnp.where(column == slot + j - QUESTION, slot_lse[j], middle)
    lse_ref[:, QUESTION:PREFIX] = middle
    lse_ref[:, PREFIX:] = new_lse[:, step_rows:]
    for copy in stores:
        copy.wait()


def whole(array):
    zeros = (0,) * array.ndim
    return pl.BlockSpec(array.shape, lambda i, zeros=zeros: zeros)


def fc_spec(far):
    return pl.BlockSpec((far.shape[0] // 2,) + far.shape[1:], lambda i: (0, 0, 0))


def proj_spec(far):
    return pl.BlockSpec((far.shape[0] // 2,) + far.shape[1:], lambda i: (1, 0, 0))


def out_spec(far):
    last = far.shape[0] - 1
    return pl.BlockSpec((1,) + far.shape[1:], lambda i: (last, 0, 0))


def thoughts_forward(info, tokens, tokens32, qkv, mixed_low, lse, weights, vec, fc_bias, qkv_bias):
    near, far = weights
    seq_len, width = tokens.shape
    rows = seq_len - QUESTION
    middle = PREFIX - QUESTION
    anywhere = pl.BlockSpec(memory_space=pl.ANY)
    out_shape = [
        jax.ShapeDtypeStruct(lse.shape, F32),
        jax.ShapeDtypeStruct((8, fc_bias.shape[1]), F32),
        jax.ShapeDtypeStruct((THOUGHTS * HEAD_ROWS, PREFIX), F32),
        jax.ShapeDtypeStruct((8, width), F32),
        jax.ShapeDtypeStruct(qkv.shape, BF16),
        jax.ShapeDtypeStruct(mixed_low.shape, BF16),
        jax.ShapeDtypeStruct(tokens32.shape, F32),
    ]
    return pl.pallas_call(
        thoughts_kernel,
        grid=(1,),
        in_specs=[
            pl.BlockSpec(memory_space=pltpu.SMEM),
            pl.BlockSpec((middle, width), lambda i: (QUESTION // middle, 0)),
            whole(lse),
            whole(vec),
            whole(fc_bias),
            whole(qkv_bias),
            *[anywhere] * 5,
        ],
        out_specs=[*(whole(x) for x in out_shape[:4]), *[anywhere] * 3],
        out_shape=out_shape,
        input_output_aliases={8: 4, 9: 5, 10: 6},
        scratch_shapes=[
            pltpu.VMEM((3, PREFIX, width), BF16),
            pltpu.VMEM((rows, width), BF16),
            pltpu.VMEM((rows, width), BF16),
            pltpu.VMEM((middle, width), F32),
            pltpu.VMEM(near.shape, BF16),
            pltpu.VMEM(far.shape, BF16),
            pltpu.SemaphoreType.DMA((7,)),
        ],
        compiler_params=pltpu.CompilerParams(vmem_limit_bytes=VMEM_LIMIT),
        cost_estimate=cost(2),
        name="thought_rows_forward",
    )(info, tokens, lse, vec, fc_bias, qkv_bias, near, far, qkv, mixed_low, tokens32)


def thoughts_back_kernel(
    info_ref,
    hid_ref,
    qkv_ref,
    lse_ref,
    pre_ref,
    prob_ref,
    res_ref,
    vec_ref,
    near_in,
    far_in,
    qkv_in,
    mixed_in,
    mg_in,
    rg_in,
    sum_ref,
    fac_ref,
    mg_out,
    rg_out,
    mg_ref,
    rg_win,
    late_q_ref,
    mixed_ref,
    near_ref,
    far_ref,
    sems,
):
    width = hid_ref.shape[1]
    blocks = (far_ref.shape[0] - 1) // 2
    units = blocks * width
    rows = mg_ref.shape[0]
    ln1_gain, ln1_bias, _, ln2_gain, ln2_bias, _ = (vec_ref[i : i + 1, :] for i in range(6))
    slot = info_ref[0]
    count = info_ref[1]
    base = pl.multiple_of(((slot - 1 - QUESTION) // 16) * 16, 16)

    def window(ref):
        return ref.at[pl.ds(base, WINDOW)]

    loads = [
        (mg_in, mg_ref),
        (mixed_in.at[pl.ds(QUESTION, rows)], mixed_ref),
        (qkv_in.at[0, pl.ds(QUESTION, rows)], late_q_ref),
        (window(rg_in), rg_win),
        (near_in, near_ref),
        (far_in.at[pl.ds(blocks, blocks)], far_ref.at[pl.ds(blocks, blocks)]),
        (far_in.at[pl.ds(0, blocks)], far_ref.at[pl.ds(0, blocks)]),
        (far_in.at[pl.ds(2 * blocks, 1)], far_ref.at[pl.ds(2 * blocks, 1)]),
    ]
    loads = [pltpu.make_async_copy(a, b, sems.at[i]) for i, (a, b) in enumerate(loads)]
    for copy in loads:
        copy.start()
    for copy in loads[:4]:
        copy.wait()

    late_q = late_q_ref[...]
    mixed_grad = mg_ref[...]
    product = mixed_grad.astype(F32) * mixed_ref[...].astype(F32)
    high = product.astype(BF16)
    ones = by_head(jnp.ones((1, width), F32), HEAD_ROWS).astype(BF16)
    delta = dot_nt(ones, high) + dot_nt(ones, (product - high.astype(F32)).astype(BF16))
    row_pos = QUESTION + lax.broadcasted_iota(jnp.int32, (HEAD_ROWS, rows), 1)
    lse = lse_ref[:, QUESTION:]

    def at_slot(at):
        local = at - QUESTION
        key = by_head(pick(qkv_ref[1, QUESTION:PREFIX, :], local) * SCALE, HEAD_ROWS)
        value = by_head(pick(qkv_ref[2, QUESTION:PREFIX, :], local), HEAD_ROWS)
        scores = dot_nt(key.astype(BF16), late_q)
        probs = jnp.where(row_pos >= at, jnp.exp(jnp.minimum(scores - lse, 0.0)), 0.0)
        prob_grad = dot_nt(value.astype(BF16), mixed_grad)
        score_grad = (probs * (prob_grad - delta)).astype(BF16)
        return (
            heads_only(dot(score_grad, late_q)) * SCALE,
            heads_only(dot(probs.astype(BF16), mixed_grad)),
        )

    def through_first(at, query_grad, key_grad, value_grad):
        first_grad = (
            dot_nt(widen(query_grad), near_ref[0])
            + dot_nt(widen(key_grad), near_ref[1])
            + dot_nt(widen(value_grad), near_ref[2])
        )[0:1]
        _, normed, inverse = row_norm(hid_ref[pl.ds(at - QUESTION, 1), :], ln1_gain, ln1_bias)
        return row_norm_back(first_grad, normed, inverse, ln1_gain)

    sum_ref[...] = jnp.zeros_like(sum_ref)
    fac = {}
    slot_grads = at_slot(slot + 1)
    loads[4].wait()
    carried = through_first(slot + 1, jnp.zeros((1, width), F32), *slot_grads)
    for copy in loads[5:]:
        copy.wait()
    for step in reversed(range(THOUGHTS)):
        at = slot - 1 + step
        upstream = jnp.where(step < count, carried, 0.0)
        low = widen(upstream)
        act_grad = jnp.concatenate([dot_nt(low, far_ref[blocks + j])[0:1] for j in range(blocks)], axis=1)
        pre = pre_ref[step : step + 1, :]
        pre_grad = (act_grad * gelu_slope(pre)).astype(BF16).astype(F32)
        second_grad = jnp.zeros((1, width), F32)
        for j in range(blocks):
            piece = pre_grad[:, j * width : (j + 1) * width]
            second_grad = second_grad + dot_nt(widen(piece), far_ref[j])[0:1]
        second, normed, inverse = row_norm(res_ref[step : step + 1, :], ln2_gain, ln2_bias)
        resid_grad = upstream + row_norm_back(second_grad, normed, inverse, ln2_gain)
        mixed_row = dot_nt(widen(resid_grad), far_ref[2 * blocks])[0:1]
        local = at - QUESTION
        rg_win[...] = put(rg_win[...], local - base, resid_grad)
        mg_ref[: PREFIX - QUESTION, :] = put(mg_ref[: PREFIX - QUESTION, :], local, mixed_row)
        up_low = upstream.astype(BF16).astype(F32)
        sum_ref[0:1, :units] += pre_grad
        sum_ref[1:2, :width] += second_grad * normed
        sum_ref[2:3, :width] += second_grad
        sum_ref[3:4, :width] += up_low
        sum_ref[4:5, :width] += resid_grad.astype(BF16).astype(F32)
        act = gelu(pre)
        rows_here = [act[:, j * width : (j + 1) * width] for j in range(blocks)]
        rows_here += [up_low, second]
        rows_here += [pre_grad[:, j * width : (j + 1) * width] for j in range(blocks)]
        for j, row in enumerate(rows_here):
            fac[THOUGHTS * j + step] = row
        if step:
            own_grad = by_head(mixed_row, HEAD_ROWS).astype(BF16)
            query = by_head(pick(qkv_ref[0, QUESTION:PREFIX, :], local) * SCALE, HEAD_ROWS)
            query = query.astype(BF16)
            probs = prob_ref[step * HEAD_ROWS : (step + 1) * HEAD_ROWS, :]
            prob_grad = dot_nt(own_grad, qkv_ref[2])
            own_delta = jnp.sum(prob_grad * probs, axis=1, keepdims=True)
            score_grad = (probs * (prob_grad - own_delta)).astype(BF16)
            query_grad = heads_only(dot(score_grad, qkv_ref[1])) * SCALE
            key_grad, value_grad = at_slot(at)
            own = lax.broadcasted_iota(jnp.int32, probs.shape, 1) == at
            score_own = jnp.sum(jnp.where(own, score_grad.astype(F32), 0.0), axis=1, keepdims=True)
            prob_own = jnp.sum(jnp.where(own, probs, 0.0), axis=1, keepdims=True)
            key_grad += jnp.sum(score_own * query.astype(F32), axis=0, keepdims=True)
            value_grad += jnp.sum(prob_own * own_grad.astype(F32), axis=0, keepdims=True)
            carried = resid_grad + through_first(at, query_grad, key_grad, value_grad)
    padding = [jnp.zeros((1, width), F32)] * (fac_ref.shape[0] - len(fac))
    fac_ref[...] = jnp.concatenate([fac[i] for i in range(len(fac))] + padding, axis=0).astype(BF16)
    stores = [
        pltpu.make_async_copy(mg_ref, mg_out, sems.at[0]),
        pltpu.make_async_copy(rg_win, window(rg_out), sems.at[1]),
    ]
    for copy in stores:
        copy.start()
    for copy in stores:
        copy.wait()


SUM_ROWS = ("fc_bias", "ln2_gain", "ln2_bias", "proj_bias", "out_bias")


def thoughts_back(info, hidden, qkv, mixed_low, lse, saved, weights, vec, mixed_grad, resid_grad):
    near, far = weights
    width = hidden.shape[1]
    units = far.shape[0] // 2 * width
    middle = PREFIX - QUESTION
    anywhere = pl.BlockSpec(memory_space=pl.ANY)
    out_shape = [
        jax.ShapeDtypeStruct((8, units), F32),
        jax.ShapeDtypeStruct((FACTOR_ROWS, width), BF16),
        jax.ShapeDtypeStruct(mixed_grad.shape, BF16),
        jax.ShapeDtypeStruct(resid_grad.shape, F32),
    ]
    return pl.pallas_call(
        thoughts_back_kernel,
        grid=(1,),
        in_specs=[
            pl.BlockSpec(memory_space=pltpu.SMEM),
            pl.BlockSpec((middle, width), lambda i: (QUESTION // middle, 0)),
            pl.BlockSpec((3, PREFIX, width), lambda i: (0, 0, 0)),
            whole(lse),
            *(whole(x) for x in saved),
            whole(vec),
            *[anywhere] * 6,
        ],
        out_specs=[whole(out_shape[0]), whole(out_shape[1]), anywhere, anywhere],
        out_shape=out_shape,
        input_output_aliases={12: 2, 13: 3},
        scratch_shapes=[
            pltpu.VMEM(mixed_grad.shape, BF16),
            pltpu.VMEM((WINDOW, width), F32),
            pltpu.VMEM(mixed_grad.shape, BF16),
            pltpu.VMEM(mixed_grad.shape, BF16),
            pltpu.VMEM(near.shape, BF16),
            pltpu.VMEM(far.shape, BF16),
            pltpu.SemaphoreType.DMA((8,)),
        ],
        compiler_params=pltpu.CompilerParams(vmem_limit_bytes=VMEM_LIMIT),
        cost_estimate=cost(2.0),
        name="thought_rows_backward",
    )(
        info,
        hidden,
        qkv,
        lse,
        *saved,
        vec,
        near,
        far,
        qkv,
        mixed_low,
        mixed_grad,
        resid_grad,
    )


def feed_kernel(
    hid_ref, mixed_ref, up_ref, wout_ref, wfc_ref, wproj_ref, vec_ref, fcb_ref, out_ref, first_ref,
    second_ref, act_ref, pg_ref, rg_ref, mg_ref, sum_ref, slope_ref,
):
    width = hid_ref.shape[1]
    blocks = wfc_ref.shape[0]
    step = pl.program_id(0)
    skip = QUESTION // BLOCK
    out_bias, ln2_gain, ln2_bias, proj_bias = (vec_ref[i : i + 1, :] for i in range(2, 6))

    @pl.when(step == 0)
    def _():
        sum_ref[...] = jnp.zeros_like(sum_ref)

    hidden = hid_ref[...]
    _, first_normed, _ = row_norm(hidden, vec_ref[0:1, :], vec_ref[1:2, :])
    first_ref[...] = first_normed.astype(BF16)
    resid = hidden + dot(mixed_ref[...], wout_ref[0]) + out_bias
    second, normed, inverse = row_norm(resid, ln2_gain, ln2_bias)
    low = second.astype(BF16)
    second_ref[...] = low
    total = resid + proj_bias
    for j in range(blocks):
        span = slice(j * width, (j + 1) * width)
        pre = dot(low, wfc_ref[j]) + fcb_ref[:, span]
        square = pre * pre
        curve = jnp.tanh(GELU_A * pre * (1.0 + GELU_B * square))
        half = 0.5 + 0.5 * curve
        act = (pre * half).astype(BF16)
        rise = 0.5 * GELU_A + (1.5 * GELU_A * GELU_B) * square
        slope_ref[:, span] = (half + pre * rise * (1.0 - curve * curve)).astype(BF16)
        act_ref[:, span] = act
        total = total + dot(act, wproj_ref[j])
    out_ref[...] = total.astype(BF16)

    @pl.when(step >= skip)
    def _():
        up = up_ref[...]
        second_grad = jnp.zeros(up.shape, F32)
        for j in range(blocks):
            span = slice(j * width, (j + 1) * width)
            slope = slope_ref[:, span].astype(F32)
            pre_grad = (dot_nt(up, wproj_ref[j]) * slope).astype(BF16)
            pg_ref[:, span] = pre_grad
            sum_ref[0:1, span] += jnp.sum(pre_grad.astype(F32), axis=0, keepdims=True)
            second_grad = second_grad + dot_nt(pre_grad, wfc_ref[j])
        up32 = up.astype(F32)
        resid_grad = up32 + row_norm_back(second_grad, normed, inverse, ln2_gain)
        attn_grad = resid_grad.astype(BF16)
        rg_ref[...] = resid_grad
        mg_ref[...] = dot_nt(attn_grad, wout_ref[0]).astype(BF16)
        sum_ref[1:2, :width] += jnp.sum(second_grad * normed, axis=0, keepdims=True)
        sum_ref[2:3, :width] += jnp.sum(second_grad, axis=0, keepdims=True)
        sum_ref[3:4, :width] += jnp.sum(up32, axis=0, keepdims=True)
        sum_ref[4:5, :width] += jnp.sum(attn_grad.astype(F32), axis=0, keepdims=True)


def feed(hidden, mixed_low, upstream_low, weights, vec, fc_bias):
    far = weights[1]
    seq_len, width = hidden.shape
    late = seq_len - QUESTION
    units = fc_bias.shape[1]
    skip = QUESTION // BLOCK

    def rows(columns):
        return pl.BlockSpec((BLOCK, columns), lambda i: (i, 0))

    def late_rows(columns):
        return pl.BlockSpec((BLOCK, columns), lambda i: (jnp.maximum(i - skip, 0), 0))

    sums = jax.ShapeDtypeStruct((8, units), F32)
    return pl.pallas_call(
        feed_kernel,
        grid=(seq_len // BLOCK,),
        in_specs=[
            rows(width),
            rows(width),
            late_rows(width),
            out_spec(far),
            fc_spec(far),
            proj_spec(far),
            whole(vec),
            whole(fc_bias),
        ],
        out_specs=[
            rows(width),
            rows(width),
            late_rows(width),
            late_rows(units),
            late_rows(units),
            late_rows(width),
            late_rows(width),
            whole(sums),
        ],
        out_shape=[
            jax.ShapeDtypeStruct((seq_len, width), BF16),
            jax.ShapeDtypeStruct((seq_len, width), BF16),
            jax.ShapeDtypeStruct((late, width), BF16),
            jax.ShapeDtypeStruct((late, units), BF16),
            jax.ShapeDtypeStruct((late, units), BF16),
            jax.ShapeDtypeStruct((late, width), F32),
            jax.ShapeDtypeStruct((late, width), BF16),
            sums,
        ],
        scratch_shapes=[pltpu.VMEM((BLOCK, units), BF16)],
        compiler_params=pltpu.CompilerParams(vmem_limit_bytes=VMEM_LIMIT),
        cost_estimate=cost(3),
        name="feed_forward_and_back",
    )(hidden, mixed_low, upstream_low, far, far, far, vec, fc_bias)


def first_back_kernel(info_ref, hid_ref, grad_ref, rg_ref, near_ref, vec_ref, in_ref):
    rows, width = hid_ref.shape
    step = pl.program_id(0)
    slot = info_ref[0]
    count = info_ref[1]
    gain = vec_ref[0:1, :]
    _, normed, inverse = row_norm(hid_ref[...], gain, vec_ref[1:2, :])
    first_grad = jnp.zeros((rows, width), F32)
    for i in range(3):
        first_grad = first_grad + dot_nt(grad_ref[i], near_ref[i])
    late = (step >= QUESTION // BLOCK).astype(F32)
    grad = row_norm_back(first_grad, normed, inverse, gain) + late * rg_ref[...]
    position = step * rows + lax.broadcasted_iota(jnp.int32, (rows, 1), 0)
    replaced = (position >= slot) & (position < slot + jnp.minimum(count, THOUGHTS))
    in_ref[...] = jnp.where(replaced, 0.0, grad)


def first_back(info, hidden, qkv_grad, resid_grad, weights, vec):
    seq_len, width = hidden.shape
    skip = QUESTION // BLOCK
    rows = pl.BlockSpec((BLOCK, width), lambda i: (i, 0))
    return pl.pallas_call(
        first_back_kernel,
        grid=(seq_len // BLOCK,),
        in_specs=[
            pl.BlockSpec(memory_space=pltpu.SMEM),
            rows,
            pl.BlockSpec((3, BLOCK, width), lambda i: (0, i, 0)),
            pl.BlockSpec((BLOCK, width), lambda i: (jnp.maximum(i - skip, 0), 0)),
            whole(weights[0]),
            whole(vec),
        ],
        out_specs=rows,
        out_shape=jax.ShapeDtypeStruct((seq_len, width), F32),
        compiler_params=pltpu.CompilerParams(vmem_limit_bytes=VMEM_LIMIT),
        cost_estimate=cost(0.83),
        name="first_norm_backward",
    )(info, hidden, qkv_grad, resid_grad, weights[0], vec)


def in_pieces(value, count=3):
    pieces = []
    for _ in range(count):
        pieces.append(value.astype(BF16))
        value = value - pieces[-1].astype(F32)
    return pieces


def keep_and_send(value, core, chips, keep_ref, send_ref, at):
    own = value.shape[0] // (2 * len(chips))
    for spot, chip in enumerate(chips):
        even = value[2 * chip * own : (2 * chip + 1) * own]
        odd = value[(2 * chip + 1) * own : (2 * chip + 2) * own]
        keep_ref[spot, at] = jnp.where(core == 0, even, odd).astype(BF16)
        send_ref[spot, at] = jnp.where(core == 0, odd, even).astype(BF16)


def near_terms_kernel(
    sizes, chips_a, chips_b, core_ref, normed_ref, grad_ref, mixed_ref, rg_ref, near_ref, vec_ref,
    feed_sum_ref, row_sum_ref, keep_a, send_a, keep_b, send_b, packed_ref,
):
    core = core_ref[0]
    width = normed_ref.shape[1]
    columns = vec_ref[...].T
    gain, bias = columns[:, 0:1], columns[:, 1:2]
    normed_t = normed_ref[...].T
    gain_terms = jnp.zeros((width, width), F32)
    bias_rows = jnp.zeros((16, width), F32)
    column_sums = []
    for i in range(3):
        inner = dot(normed_t, grad_ref[i])
        sums = jnp.sum(grad_ref[i].astype(F32), axis=0, keepdims=True)
        value = inner * gain + bias * sums
        if i < 2:
            keep_and_send(value, core, chips_a, keep_a, send_a, i)
        else:
            keep_and_send(value, core, chips_b, keep_b, send_b, 0)
        gain_terms = gain_terms + inner * near_ref[i].astype(F32)
        pieces = in_pieces(jnp.broadcast_to(sums, (8, width)), 2)
        bias_rows = bias_rows + dot_nt(jnp.concatenate(pieces, axis=0), near_ref[i])
        column_sums.append(sums)
    ones = jnp.ones((16, width), BF16)
    totals = feed_sum_ref[...] + row_sum_ref[...]
    small = {name: totals[i : i + 1, :width] for i, name in enumerate(SUM_ROWS)}
    small["fc_bias"] = totals[0:1]
    small["ln1_gain"] = sum(dot_nt(ones, piece) for piece in in_pieces(gain_terms, 2))[0:1]
    small["ln1_bias"] = bias_rows[0:1] + bias_rows[8:9]
    small["qv_bias"] = jnp.concatenate([column_sums[0], column_sums[2]], axis=1)
    pack(small, sizes, 2 * len(chips_a), packed_ref)
    value = dot_tn(mixed_ref[QUESTION:, :], rg_ref[...].astype(BF16))
    keep_and_send(value, core, chips_b, keep_b, send_b, 1)


def near_terms(
    core, normed_low, qkv_grad, mixed_low, resid_grad, near, vec, feed_sums, row_sums, sizes, chips_a, chips_b
):
    seq_len, width = normed_low.shape
    half = jax.ShapeDtypeStruct((len(chips_a), 2, width // (2 * len(chips_a)), width), BF16)
    packed = jax.ShapeDtypeStruct((len(sizes), 2 * len(chips_a), LANES), BF16)
    out_shape = [half] * 4 + [packed]
    return pl.pallas_call(
        functools.partial(near_terms_kernel, sizes, chips_a, chips_b),
        grid=(1,),
        in_specs=[
            pl.BlockSpec(memory_space=pltpu.SMEM),
            whole(normed_low),
            whole(qkv_grad),
            whole(mixed_low),
            whole(resid_grad),
            whole(near),
            whole(vec),
            whole(feed_sums),
            whole(row_sums),
        ],
        out_specs=[whole(x) for x in out_shape],
        out_shape=out_shape,
        compiler_params=pltpu.CompilerParams(vmem_limit_bytes=VMEM_LIMIT),
        cost_estimate=cost(0.5),
        name="near_weight_terms",
    )(core, normed_low, qkv_grad, mixed_low, resid_grad, near, vec, feed_sums, row_sums)


def fc_terms_kernel(chips, core_ref, second_ref, pg_ref, keep_ref, send_ref, second_t):
    @pl.when(pl.program_id(0) == 0)
    def _():
        second_t[...] = second_ref[...].T

    value = dot(second_t[...], pg_ref[...])
    keep_and_send(value, core_ref[0], chips, keep_ref, send_ref, 0)


def fc_terms(core, second_low, pre_grad, chips):
    width = second_low.shape[1]
    rows, units = pre_grad.shape
    blocks = units // width
    own = width // (2 * len(chips))
    half = jax.ShapeDtypeStruct((len(chips), blocks, own, width), BF16)
    out = pl.BlockSpec((len(chips), 1, own, width), lambda j: (0, j, 0, 0))
    return pl.pallas_call(
        functools.partial(fc_terms_kernel, chips),
        grid=(blocks,),
        in_specs=[
            pl.BlockSpec(memory_space=pltpu.SMEM),
            pl.BlockSpec((rows, width), lambda j: (0, 0)),
            pl.BlockSpec((rows, width), lambda j: (0, j)),
        ],
        out_specs=[out, out],
        out_shape=[half, half],
        scratch_shapes=[pltpu.VMEM((width, rows), BF16)],
        compiler_params=pltpu.CompilerParams(vmem_limit_bytes=VMEM_LIMIT),
        cost_estimate=cost(0.5),
        name="fc_weight_terms",
    )(core, second_low, pre_grad)


def proj_terms_kernel(outer, inner, act_ref, up_ref, out_ref):
    value = dot_tn(act_ref[...], up_ref[...])
    rows, width = value.shape
    value = value.reshape(outer, inner, rows // (outer * inner), width)
    for i in range(inner):
        out_ref[i, :, 0] = value[:, i].astype(BF16)


def proj_terms(act_low, upstream_low, outer, inner):
    units = act_low.shape[1]
    rows, width = upstream_low.shape
    blocks = units // width
    shape = (inner, outer, blocks, width // (outer * inner), width)
    return pl.pallas_call(
        functools.partial(proj_terms_kernel, outer, inner),
        grid=(blocks,),
        in_specs=[
            pl.BlockSpec((rows, width), lambda j: (0, j)),
            pl.BlockSpec((rows, width), lambda j: (0, 0)),
        ],
        out_specs=pl.BlockSpec((inner, outer, 1) + shape[3:], lambda j: (0, 0, j, 0, 0)),
        out_shape=jax.ShapeDtypeStruct(shape, BF16),
        compiler_params=pltpu.CompilerParams(vmem_limit_bytes=VMEM_LIMIT),
        cost_estimate=cost(0.5),
        name="proj_weight_terms",
    )(act_low, upstream_low)


def first_kernel(
    core_ref, tok_ref, left_mine, left_got, right_mine, right_got, vec_ref, qkvb_ref, qkv_ref,
    near_ref, rows_ref,
):
    width = tok_ref.shape[1]

    @pl.when(pl.program_id(0) == 0)
    def _():
        even_is_mine = core_ref[0] == 0
        chips, own, half = left_mine.shape[1:]
        for i in range(3):
            for side, (mine, got) in enumerate([(left_mine, left_got), (right_mine, right_got)]):
                for chip in range(chips):
                    a = mine[i, chip].astype(F32)
                    b = got[i, chip].astype(F32)
                    begin = 2 * chip * own
                    rows_ref[begin : begin + own, :] = jnp.where(even_is_mine, a, b)
                    rows_ref[begin + own : begin + 2 * own, :] = jnp.where(even_is_mine, b, a)
                near_ref[i, :, side * half : (side + 1) * half] = rows_ref[...].astype(BF16)

    first, _, _ = row_norm(tok_ref[...].astype(F32), vec_ref[0:1, :], vec_ref[1:2, :])
    first = first.astype(BF16)
    for i in range(3):
        span = slice(i * width, (i + 1) * width)
        qkv_ref[i] = (dot(first, near_ref[i]) + qkvb_ref[:, span]).astype(BF16)


def first_forward(core, tokens, pieces, vec, qkv_bias):
    seq_len, width = tokens.shape
    near = jax.ShapeDtypeStruct((3, width, width), BF16)
    return pl.pallas_call(
        first_kernel,
        grid=(seq_len // BLOCK,),
        in_specs=[
            pl.BlockSpec(memory_space=pltpu.SMEM),
            pl.BlockSpec((BLOCK, width), lambda i: (i, 0)),
            *(whole(piece) for piece in pieces),
            whole(vec),
            whole(qkv_bias),
        ],
        out_specs=[pl.BlockSpec((3, BLOCK, width), lambda i: (0, i, 0)), whole(near)],
        out_shape=[jax.ShapeDtypeStruct((3, seq_len, width), BF16), near],
        scratch_shapes=[pltpu.VMEM((width, width // 2), F32)],
        compiler_params=pltpu.CompilerParams(vmem_limit_bytes=VMEM_LIMIT),
        cost_estimate=cost(0.67),
        name="first_norm_forward",
    )(core, tokens, *pieces, vec, qkv_bias)


def group_of(blocks, own):
    each = blocks * own
    group = LANES // math.gcd(LANES, each)
    device, block, i = np.indices((group, blocks, own)).reshape(3, -1)
    swap = np.zeros((group * each, group * each), np.float32)
    swap[np.arange(group * each), block * (group * own) + device * own + i] = 1.0
    return group, jnp.asarray(swap, BF16)


def split_units_kernel(blocks, span, fc_ref, swap_ref, out_ref):
    own = fc_ref.shape[0]
    size = swap_ref.shape[0]
    groups = out_ref.shape[2] // span
    rows = [fc_ref[:, g * size : (g + 1) * size].astype(F32) for g in range(groups)]
    swapped = dot(jnp.concatenate(rows, axis=0).astype(BF16), swap_ref[...])
    for g in range(groups):
        part = swapped[g * own : (g + 1) * own]
        for j in range(blocks):
            piece = part[:, j * span : (j + 1) * span]
            out_ref[j, :, g * span : (g + 1) * span] = piece.astype(BF16)


def split_units(fc_shard, blocks):
    own, units = fc_shard.shape
    group, swap = group_of(blocks, own)
    return pl.pallas_call(
        functools.partial(split_units_kernel, blocks, group * own),
        out_shape=jax.ShapeDtypeStruct((blocks, own, units // blocks), BF16),
        compiler_params=pltpu.CompilerParams(vmem_limit_bytes=VMEM_LIMIT),
        name="units_split",
    )(fc_shard, swap)


def row_terms_kernel(span, index_ref, fac_ref, proj_ref, fc_ref, swap_ref, proj_out, fc_out):
    blocks, own, width = proj_ref.shape
    shape = (width, own)
    mine = lax.broadcasted_iota(jnp.int32, shape, 0) - index_ref[0] * own
    select = (mine == lax.broadcasted_iota(jnp.int32, shape, 1)).astype(BF16)

    def factor(j):
        return jnp.concatenate([fac_ref[THOUGHTS * j + i] for i in range(THOUGHTS)], axis=0)

    upstream = factor(blocks)
    terms = []
    second = dot(factor(blocks + 1), select).astype(BF16)
    for j in range(blocks):
        act = dot(factor(j), select).astype(BF16)
        proj_out[j] = proj_ref[j].astype(F32) + dot_tn(act, upstream)
        terms.append(fc_ref[j] + dot_tn(second, factor(blocks + 2 + j)))
    size = swap_ref.shape[0]
    groups = width // span
    rows = [
        jnp.concatenate([t[:, g * span : (g + 1) * span] for t in terms], axis=1)
        for g in range(groups)
    ]
    left = jnp.concatenate(rows, axis=0)
    total = sum(dot_nt(piece, swap_ref[...]) for piece in in_pieces(left))
    for g in range(groups):
        fc_out[:, g * size : (g + 1) * size] = total[g * own : (g + 1) * own]


def row_terms(index, factors, proj_sum, fc_sum):
    blocks, own, width = fc_sum.shape
    out_shape = [
        jax.ShapeDtypeStruct(proj_sum.shape, F32),
        jax.ShapeDtypeStruct((own, blocks * width), F32),
    ]
    group, swap = group_of(blocks, own)
    return pl.pallas_call(
        functools.partial(row_terms_kernel, group * own),
        grid=(1,),
        in_specs=[
            pl.BlockSpec(memory_space=pltpu.SMEM),
            whole(factors),
            whole(proj_sum),
            whole(fc_sum),
            whole(swap),
        ],
        out_specs=[whole(x) for x in out_shape],
        out_shape=out_shape,
        compiler_params=pltpu.CompilerParams(vmem_limit_bytes=VMEM_LIMIT),
        cost_estimate=cost(0.33),
        name="thought_rows_terms",
    )(index, factors, proj_sum, fc_sum, swap)


def spread_matrix(shard, count):
    shape = (shard, shard * count)
    column = lax.broadcasted_iota(jnp.int32, shape, 1) % shard
    return (column == lax.broadcasted_iota(jnp.int32, shape, 0)).astype(BF16)


def owner_mask(shard, count):
    shape = (count, shard * count)
    owner = lax.broadcasted_iota(jnp.int32, shape, 1) // shard
    return owner == lax.broadcasted_iota(jnp.int32, shape, 0)


VECTOR_ROWS = ("ln1_gain", "ln1_bias", "out_bias", "ln2_gain", "ln2_bias", "proj_bias")


def unpack_kernel(sizes, devices, packed_ref, vec_ref, fcb_ref, qkvb_ref):
    vec_ref[...] = jnp.zeros_like(vec_ref)
    width = vec_ref.shape[1]
    for at, (name, size) in enumerate(sizes):
        if name == "fc_bias":
            own = width // devices
            for j in range(size // own):
                spread = dot(packed_ref[at][:, j * own : (j + 1) * own], spread_matrix(own, devices))
                spread = jnp.where(owner_mask(own, devices), spread, 0.0)
                span = slice(j * width, (j + 1) * width)
                fcb_ref[:, span] = jnp.sum(spread, axis=0, keepdims=True)
            continue
        block = packed_ref[at][:, :size]
        spread = dot(block, spread_matrix(size, devices))
        full = jnp.sum(jnp.where(owner_mask(size, devices), spread, 0.0), axis=0, keepdims=True)
        if name == "qv_bias":
            qkvb_ref[:, :width] = full[:, :width]
            qkvb_ref[:, width : 2 * width] = jnp.zeros((1, width), F32)
            qkvb_ref[:, 2 * width :] = full[:, width:]
        else:
            at = VECTOR_ROWS.index(name)
            vec_ref[at : at + 1, :] = full


def unpack(packed, sizes):
    devices = packed.shape[1]
    size = dict(sizes)
    width = size["ln1_gain"] * devices
    return pl.pallas_call(
        functools.partial(unpack_kernel, sizes, devices),
        out_shape=[
            jax.ShapeDtypeStruct((8, width), F32),
            jax.ShapeDtypeStruct((1, size["fc_bias"] * devices), F32),
            jax.ShapeDtypeStruct((1, 3 * width), F32),
        ],
        compiler_params=pltpu.CompilerParams(vmem_limit_bytes=VMEM_LIMIT),
        name="vectors_unpack",
    )(packed)


def pack(rows, sizes, devices, out_ref):
    out_ref[...] = jnp.zeros_like(out_ref)
    width = rows["ln1_gain"].shape[1]
    for at, (name, size) in enumerate(sizes):
        own = width // devices if name == "fc_bias" else size
        span = own * devices
        for j in range(size // own):
            row = jnp.broadcast_to(rows[name][:, j * span : (j + 1) * span], (devices, span))
            row = jnp.where(owner_mask(own, devices), row, 0.0).astype(BF16)
            piece = dot_nt(row, spread_matrix(own, devices)).astype(BF16)
            out_ref[at, :, j * own : (j + 1) * own] = piece


def join_kernel(*refs):
    out_ref = refs[-1]
    out_ref[...] = jnp.zeros_like(out_ref)
    for at, ref in enumerate(refs[:-1]):
        out_ref[at : at + 1, : ref.shape[0]] = ref[...].astype(F32).reshape(1, ref.shape[0])


def join(vectors):
    return pl.pallas_call(
        join_kernel,
        out_shape=jax.ShapeDtypeStruct((len(vectors), LANES), F32),
        name="vectors_join",
    )(*vectors)


def part_kernel(joined_ref, *refs):
    for at, ref in enumerate(refs):
        ref[...] = joined_ref[at, : ref.shape[0]]


def part(joined, sizes):
    return pl.pallas_call(
        part_kernel,
        out_shape=[jax.ShapeDtypeStruct((size,), F32) for _, size in sizes],
        name="vectors_part",
    )(joined)


def step_on_sequence(
    near_pieces, far, vectors, tokens, cotangent, slots, count, answer_start, devices, sizes, comm
):
    vec, fc_bias, qkv_bias = vectors
    seq_len, width = tokens.shape
    info = jnp.stack([slots[0], count])

    qkv_first, near = first_forward(comm.core, tokens, near_pieces, vec, qkv_bias)
    mixed_hidden, lse_hidden = attend(info, qkv_first)
    late = QUESTION + lax.iota(jnp.int32, seq_len - QUESTION)
    upstream_low = jnp.where(
        (late >= answer_start)[:, None], cotangent[QUESTION:], jnp.zeros((), BF16)
    )
    tokens32 = tokens.astype(F32)
    weights = (near, after(far, mixed_hidden, upstream_low, tokens32))
    lse, *saved, qkv, mixed_low, hidden = thoughts_forward(
        info, tokens, tokens32, qkv_first, mixed_hidden, lse_hidden, weights, vec, fc_bias, qkv_bias
    )
    output, normed_low, second_low, act_low, pre_grad, resid_grad, mixed_grad, sums = feed(
        hidden, mixed_low, upstream_low, weights, vec, fc_bias
    )

    proj_grad = comm.proj_terms(act_low, upstream_low)
    proj_half = comm.early(proj_grad)
    halves = fc_terms(comm.core, after(second_low, proj_grad), pre_grad, comm.chips("zyxc"))
    fc_going = comm.scatter(halves, "zyxc")
    sent = go_after([fc_going])
    row_sums, factors, mixed_grad, resid_grad = thoughts_back(
        info,
        hidden,
        qkv,
        mixed_low,
        after(lse, *sent),
        saved,
        weights,
        vec,
        mixed_grad,
        resid_grad,
    )
    join_after([fc_going], row_sums)
    spread = comm.factors(factors)
    sent = go_after([fc_going, spread])
    lse, back_grad = after((lse, mixed_grad), *sent)
    qkv_grad = attend_back(qkv, mixed_low, lse, back_grad)
    join_after([fc_going, spread], qkv_grad)
    proj_half = after(proj_half, qkv_grad)
    proj_going = comm.early_end(proj_half)
    sent = (*go_after([fc_going, spread]), proj_half)
    *terms, packed = near_terms(
        comm.core,
        after(normed_low, *sent),
        qkv_grad,
        mixed_low,
        resid_grad,
        near,
        vec,
        sums,
        row_sums,
        sizes,
        comm.chips("zxyc"),
        comm.chips("zyxc"),
    )
    first = comm.scatter(terms[:2], "zxyc")
    rest = comm.scatter(terms[2:], "zyxc")
    vectors_going = comm.scatter_vectors(packed)

    sent = go_after([first, rest, vectors_going])
    join_after([spread], *sent)
    sent = go_after([spread])
    going = [first, rest, vectors_going, fc_going, spread]
    join_after(going, *sent)
    sent = go_after(going)
    input_grad = first_back(info, hidden, after(qkv_grad, *sent), resid_grad, weights, vec)
    join_after(going, input_grad)
    proj_g = fc_g = None
    while any(swap.todo for swap in going) or proj_g is None:
        group = [swap for swap in going if swap.todo]
        sent = go_after(group)
        done = sent
        if proj_g is None and fc_going not in group and spread not in group:
            factors, fc_sum = after((spread.finish(), fc_going.finish()), *sent)
            proj_g, fc_g = comm.terms(factors, proj_going, fc_sum)
            done = (proj_g, fc_g)
        join_after(group, *done)
    return (
        output,
        input_grad,
        first.finish(),
        rest.finish(),
        proj_g,
        fc_g,
        vectors_going.finish(),
    )


SMALL = ("ln1_gain", "ln1_bias", "qv_bias", "out_bias", "ln2_gain", "ln2_bias", "fc_bias", "proj_bias")


def on_device(
    links,
    tokens,
    ln1_gain,
    ln1_bias,
    qkv_weight,
    qv_bias,
    out_weight,
    out_bias,
    ln2_gain,
    ln2_bias,
    fc_weight,
    fc_bias,
    proj_weight,
    proj_bias,
    cotangent,
    thought_slots,
    thought_count,
    answer_start,
):
    devices = links.sizes["dp"] * links.sizes["fsdp"]
    small_shards = dict(
        ln1_gain=ln1_gain,
        ln1_bias=ln1_bias,
        qv_bias=qv_bias,
        out_bias=out_bias,
        ln2_gain=ln2_gain,
        ln2_bias=ln2_bias,
        fc_bias=fc_bias,
        proj_bias=proj_bias,
    )
    sizes = tuple((n, small_shards[n].shape[0]) for n in SMALL)
    own, width = out_weight.shape
    blocks = proj_weight.shape[0] // own
    both = ("dp", "fsdp")

    far_shard = jnp.concatenate(
        [
            split_units(fc_weight, blocks),
            proj_weight.reshape(blocks, own, width),
            out_weight[None],
        ],
        axis=0,
    )
    far = lax.all_gather(far_shard, both, axis=1, tiled=True)

    packed = join([small_shards[n] for n in SMALL]).astype(BF16)
    small = links.gather(packed, "zxyc", axis=0).reshape(devices, len(sizes), LANES)
    half = width // 2
    near_pieces = []
    for side, text in enumerate(("zxyc", "zyxc")):
        part_columns = [
            qkv_weight[:, i * width + side * half : i * width + (side + 1) * half] for i in range(3)
        ]
        ring = Gather(links, jnp.stack(part_columns), text, axis=1)
        near_pieces += ring.last()

    class Comm:
        chips = links.chips
        core = (lax.axis_index("fsdp") % 2)[None].astype(jnp.int32)

        @staticmethod
        def proj_terms(act_low, upstream_low):
            return proj_terms(act_low, upstream_low, links.sizes["dp"], links.sizes["fsdp"])

        @staticmethod
        def early(value):
            return lax.psum_scatter(
                value.reshape(-1, width), "fsdp", scatter_dimension=0, tiled=True
            )

        @staticmethod
        def early_end(value):
            value = lax.psum_scatter(value, "dp", scatter_dimension=0, tiled=True)
            return value.reshape(blocks, own, width)

        @staticmethod
        def scatter(halves, text):
            return links.scatter(tuple(halves), text)

        @staticmethod
        def factors(rows):
            return Gather(links, rows, "zxyc")

        @staticmethod
        def scatter_vectors(value):
            return links.scatter(value.transpose(1, 0, 2), "zxyc")

        @staticmethod
        def terms(factors, proj_sum, fc_sum):
            index = lax.axis_index(both)[None].astype(jnp.int32)
            factors = factors.reshape(devices, FACTOR_ROWS, width).transpose(1, 0, 2)
            return row_terms(index, factors, proj_sum, fc_sum)

    output, input_grad, first, rest, proj_g, fc_g, vector_sums = step_on_sequence(
        near_pieces,
        far,
        unpack(small.transpose(1, 0, 2), sizes),
        tokens[0],
        cotangent[0],
        thought_slots[0],
        thought_count[0],
        answer_start[0],
        devices,
        sizes,
        Comm,
    )
    proj_g = proj_g.reshape(blocks * own, width)
    qkv_g = jnp.concatenate([first[0], first[1], rest[0]], axis=1)
    out_g = rest[1]
    owned = dict(zip(SMALL, part(vector_sums, sizes)))
    return (
        output[None],
        input_grad[None],
        owned["ln1_gain"],
        owned["ln1_bias"],
        qkv_g,
        owned["qv_bias"],
        out_g,
        owned["out_bias"],
        owned["ln2_gain"],
        owned["ln2_bias"],
        fc_g,
        owned["fc_bias"],
        proj_g,
        owned["proj_bias"],
    )


def solution(mesh):
    links = Links({name: mesh.shape[name] for name in ("dp", "fsdp")})
    both = ("dp", "fsdp")
    cube, matrix, vector = P(both, None, None), P(both, None), P(both)
    weight_specs = (
        vector,
        vector,
        matrix,
        vector,
        matrix,
        vector,
        vector,
        vector,
        matrix,
        vector,
        matrix,
        vector,
    )

    def per_device(*args):
        return on_device(links, *args)

    return jax.shard_map(
        per_device,
        mesh=mesh,
        in_specs=(cube,) + weight_specs + (cube, matrix, vector, vector),
        out_specs=(cube, cube) + weight_specs,
        check_vma=False,
    )
```

```python
import functools
import math

import jax
import jax.numpy as jnp
import numpy as np
from jax import lax
from jax.experimental import pallas as pl
from jax.experimental.pallas import tpu as pltpu
from jax.sharding import PartitionSpec as P

HD = 64
THOUGHTS = 2
PREFIX = 384
QUESTION = 256
SCALE = 0.125
EPSILON = 1e-05
BLOCK = 256
HEAD_ROWS = 16
WINDOW = 32
LANES = 128
FACTOR_ROWS = 24
PAIR = 2 * HD
NEG = -1e30

F32 = jnp.float32
BF16 = jnp.bfloat16
VMEM_LIMIT = 56 * 1024 * 1024


def cost(microseconds):
    return pl.CostEstimate(
        flops=int(microseconds * 1.15e9),
        bytes_accessed=int(microseconds * 3.6e6),
        transcendentals=0,
    )


def dot(a, b):
    return lax.dot_general(a, b, (((1,), (0,)), ((), ())), preferred_element_type=F32)


def dot_nt(a, b):
    return lax.dot_general(a, b, (((1,), (1,)), ((), ())), preferred_element_type=F32)


def dot_tn(a, b):
    return lax.dot_general(a, b, (((0,), (0,)), ((), ())), preferred_element_type=F32)


def bits_of(size):
    return [1 << i for i in reversed(range(int(math.log2(size))))]


class Links:
    def __init__(self, sizes):
        self.sizes = sizes
        self.canon = [("dp", b) for b in bits_of(sizes["dp"])] + [
            ("fsdp", b) for b in bits_of(sizes["fsdp"])
        ]
        dp_bits = [("dp", b) for b in bits_of(sizes["dp"])]
        f_bits = [("fsdp", b) for b in bits_of(sizes["fsdp"])]
        self.groups = {"x": dp_bits[-1:], "y": dp_bits[:-1], "z": f_bits[:-1], "c": f_bits[-1:]}

    def order(self, text):
        out = []
        for letter in text:
            out += self.groups[letter]
        return out

    def swap(self, value, stage):
        axis, bit = stage
        return lax.ppermute(value, axis, [(i, i ^ bit) for i in range(self.sizes[axis])])

    def mine(self, stage):
        axis, bit = stage
        return (lax.axis_index(axis) & bit) != 0

    def gather(self, shard, text, axis=0):
        return Gather(self, shard, text, axis).finish()

    def chips(self, text):
        stages = list(reversed(self.order(text)))[1:]
        rest = [c for c in self.canon if c in stages]
        order = []
        for spot in range(1 << len(stages)):
            chip = 0
            for at, stage in enumerate(stages):
                if spot & (1 << (len(stages) - 1 - at)):
                    chip |= 1 << (len(rest) - 1 - rest.index(stage))
            order.append(chip)
        return order

    def spots(self, text):
        stages = [c for c in reversed(self.order(text)) if c not in self.groups["c"]]
        rest = [c for c in self.canon if c in stages]
        order = []
        for spot in range(1 << len(stages)):
            chip = 0
            for at, stage in enumerate(stages):
                if spot & (1 << (len(stages) - 1 - at)):
                    chip |= 1 << (len(rest) - 1 - rest.index(stage))
            order.append(chip)
        return order

    def scatter(self, value, text):
        return Scatter(self, value, text)


class Gather:
    def __init__(self, links, shard, text, axis=0):
        self.links = links
        self.shape = shard.shape
        self.axis = axis
        self.todo = links.order(text)
        self.done = []
        self.buf = shard
        self.got = None

    def go(self):
        self.add()
        self.stage = self.todo.pop(0)
        self.got = self.links.swap(self.buf, self.stage)
        return self.buf

    def add(self):
        if self.got is not None:
            canon = self.links.canon
            place = sum(1 for d in self.done if canon.index(d) < canon.index(self.stage))
            high = self.links.mine(self.stage)
            pair = [jnp.where(high, self.got, self.buf), jnp.where(high, self.buf, self.got)]
            self.buf = jnp.stack(pair, axis=self.axis + place)
            self.done.append(self.stage)
            self.got = None
        return self.buf

    def hold(self, *deps):
        self.buf = after(self.buf, *deps)

    def join(self, *deps):
        self.got = after(self.got, *deps)
        self.add()

    def last(self):
        for stage in self.todo:
            if self.got is not None:
                high = self.links.mine(self.stage)
                pair = [jnp.where(high, self.got, self.buf), jnp.where(high, self.buf, self.got)]
                self.buf = jnp.concatenate(pair, axis=0)
            self.stage = stage
            self.got = self.links.swap(self.buf, stage)
        return [self.buf, self.got]

    def finish(self):
        while self.todo:
            self.go()
        self.add()
        shape = self.shape
        return self.buf.reshape(shape[: self.axis] + (-1,) + shape[self.axis + 1 :])


class Scatter:
    def __init__(self, links, value, text):
        self.links = links
        self.left = list(links.canon)
        self.todo = list(reversed(links.order(text)))
        self.got = None
        self.split = False
        if isinstance(value, tuple):
            self.split = True
            self.left = self.todo[1:]
            shape = (2,) * len(self.left) + value[0].shape[1:]
            self.keep, self.buf = (v.reshape(shape) for v in value)
        else:
            self.buf = value.reshape((2,) * len(self.left) + value.shape[1:])

    def go(self):
        stage = self.todo.pop(0)
        if self.split:
            self.split = False
            sent = self.buf
        else:
            place = self.left.index(stage)
            self.left.remove(stage)
            high = self.links.mine(stage).astype(jnp.int32)
            parts = [self.buf] if self.got is None else [self.keep, self.got]

            def half(side):
                cut = [lax.dynamic_index_in_dim(p, side, place, keepdims=False) for p in parts]
                return cut[0] if len(cut) == 1 else cut[0].astype(F32) + cut[1].astype(F32)

            sent = half(1 - high).astype(BF16)
            self.keep = half(high)
        self.got = self.links.swap(sent, stage)
        return sent

    def hold(self, *deps):
        if self.got is None:
            self.buf = after(self.buf, *deps)
        else:
            self.got = after(self.got, *deps)

    def join(self, *deps):
        self.got = after(self.got, *deps)

    def finish(self):
        return self.keep.astype(F32) + self.got.astype(F32)


def join_after(swaps, *deps):
    for swap in swaps:
        swap.join(*deps)


def go_after(swaps, *deps):
    for swap in swaps:
        swap.hold(*deps)
    return tuple(swap.go() for swap in swaps)


def after(value, *deps):
    return lax.optimization_barrier((value, deps))[0]


def attend_kernel(info_ref, q_ref, k_ref, v_ref, o_ref, lse_ref):
    seq_len = q_ref.shape[0]
    slot = info_ref[0]
    keys = k_ref[...]
    values_t = v_ref[...].T
    lane = lax.broadcasted_iota(jnp.int32, (BLOCK, PAIR), 1)
    sub = lax.broadcasted_iota(jnp.int32, (PAIR, BLOCK), 0)
    key_pos = lax.broadcasted_iota(jnp.int32, (BLOCK, BLOCK), 0)
    row_pos = lax.broadcasted_iota(jnp.int32, (BLOCK, BLOCK), 1)
    causal = key_pos <= row_pos
    middle_pos = QUESTION + lax.broadcasted_iota(jnp.int32, (PREFIX - QUESTION, BLOCK), 0)
    is_slot = (middle_pos >= slot) & (middle_pos < slot + THOUGHTS)

    def hide(scores):
        if scores.shape[0] <= QUESTION:
            return scores
        middle = jnp.where(is_slot, NEG, scores[QUESTION:PREFIX])
        return jnp.concatenate([scores[:QUESTION], middle, scores[PREFIX:]], axis=0)

    for begin in range(0, seq_len, BLOCK):
        end = begin + BLOCK
        queries = q_ref[begin:end, :] * jnp.asarray(SCALE, BF16)
        parts = []
        for head in range(2):
            own = jnp.where((lane >= HD) == bool(head), queries, jnp.zeros_like(queries))
            scores = dot_nt(keys[:end], own)
            last = jnp.where(causal, scores[begin:], NEG)
            if begin:
                last = jnp.concatenate([scores[:begin], last], axis=0)
            scores = hide(last)
            peak = jnp.max(scores, axis=0, keepdims=True)
            expo = jnp.exp(scores - peak)
            total = jnp.sum(expo, axis=0, keepdims=True)
            mixed = dot(values_t[:, :end], expo.astype(BF16))
            parts.append(mixed / total)
            lse_ref[pl.ds(2 * pl.program_id(0) + head, 1), begin:end] = peak + jnp.log(total)
        o_ref[begin:end, :] = jnp.where(sub < HD, parts[0], parts[1]).T.astype(BF16)


def attend(info, qkv):
    _, seq_len, width = qkv.shape
    pairs = width // PAIR

    def columns(i):
        return pl.BlockSpec((None, seq_len, PAIR), lambda g, i=i: (i, 0, g))

    return pl.pallas_call(
        attend_kernel,
        grid=(pairs,),
        in_specs=[
            pl.BlockSpec(memory_space=pltpu.SMEM),
            *(columns(i) for i in range(3)),
        ],
        out_specs=[
            pl.BlockSpec((seq_len, PAIR), lambda g: (0, g)),
            pl.BlockSpec((HEAD_ROWS, seq_len), lambda g: (0, 0)),
        ],
        out_shape=[
            jax.ShapeDtypeStruct((seq_len, width), BF16),
            jax.ShapeDtypeStruct((HEAD_ROWS, seq_len), F32),
        ],
        compiler_params=pltpu.CompilerParams(vmem_limit_bytes=VMEM_LIMIT),
        cost_estimate=cost(2.0),
        name="attention_forward",
    )(info, qkv, qkv, qkv)


def attend_back_kernel(
    q_ref, k_ref, v_ref, o_ref, lse_ref, g_ref, out_ref, dk_acc, dv_acc
):
    seq_len = q_ref.shape[0]
    pair = pl.program_id(0)
    first_row = seq_len - g_ref.shape[0]
    keys = k_ref[...]
    values = v_ref[...]
    keys_t = keys.T
    lane = lax.broadcasted_iota(jnp.int32, (BLOCK, PAIR), 1)
    sub = lax.broadcasted_iota(jnp.int32, (PAIR, BLOCK), 0)
    key_pos = lax.broadcasted_iota(jnp.int32, (BLOCK, BLOCK), 0)
    row_pos = lax.broadcasted_iota(jnp.int32, (BLOCK, BLOCK), 1)
    causal = key_pos <= row_pos
    dk_acc[...] = jnp.zeros_like(dk_acc)
    dv_acc[...] = jnp.zeros_like(dv_acc)
    for begin in range(first_row, seq_len, BLOCK):
        end = begin + BLOCK
        local = begin - first_row
        queries = q_ref[begin:end, :] * jnp.asarray(SCALE, BF16)
        grads = g_ref[local : local + BLOCK, :]
        product_t = (grads.astype(F32) * o_ref[begin:end, :].astype(F32)).T
        parts = []
        for head in range(2):
            chosen = (lane >= HD) == bool(head)
            own = jnp.where(chosen, queries, jnp.zeros_like(queries))
            own_grad = jnp.where(chosen, grads, jnp.zeros_like(grads))
            delta = jnp.sum(product_t[head * HD : (head + 1) * HD], axis=0, keepdims=True)
            lse = lse_ref[pl.ds(2 * pair + head, 1), begin:end]
            total = None
            for low, high in ((0, begin), (begin, end)):
                scores = dot_nt(keys[low:high], own)
                if high == end:
                    scores = jnp.where(causal, scores, NEG)
                probs = jnp.exp(scores - lse)
                prob_grad = dot_nt(values[low:high], own_grad)
                score_grad = (probs * (prob_grad - delta)).astype(BF16)
                dv_acc[low:high, :] += dot(probs.astype(BF16), own_grad)
                dk_acc[low:high, :] += dot(score_grad, own)
                part = dot(keys_t[:, low:high], score_grad)
                total = part if total is None else total + part
            parts.append(total)
        mine = jnp.where(sub < HD, parts[0], parts[1]).T * SCALE
        out_ref[0, begin:end, :] = mine.astype(BF16)
    out_ref[0, :first_row, :] = jnp.zeros((first_row, PAIR), BF16)
    out_ref[1] = dk_acc[...].astype(BF16)
    out_ref[2] = dv_acc[...].astype(BF16)


def attend_back(qkv, mixed_low, lse, mixed_grad):
    _, seq_len, width = qkv.shape
    rows = mixed_grad.shape[0]

    def columns(i):
        return pl.BlockSpec((None, seq_len, PAIR), lambda g, i=i: (i, 0, g))

    late = pl.BlockSpec((rows, PAIR), lambda g: (0, g))
    return pl.pallas_call(
        attend_back_kernel,
        grid=(width // PAIR,),
        in_specs=[
            *(columns(i) for i in range(3)),
            pl.BlockSpec((seq_len, PAIR), lambda g: (0, g)),
            pl.BlockSpec((HEAD_ROWS, seq_len), lambda g: (0, 0)),
            late,
        ],
        out_specs=pl.BlockSpec((3, seq_len, PAIR), lambda g: (0, 0, g)),
        out_shape=jax.ShapeDtypeStruct((3, seq_len, width), BF16),
        scratch_shapes=[pltpu.VMEM((seq_len, PAIR), F32), pltpu.VMEM((seq_len, PAIR), F32)],
        compiler_params=pltpu.CompilerParams(vmem_limit_bytes=VMEM_LIMIT),
        cost_estimate=cost(2.17),
        name="attention_backward",
    )(qkv, qkv, qkv, mixed_low, lse, mixed_grad)


def row_norm(row, gain, bias):
    mean = jnp.mean(row, axis=-1, keepdims=True)
    centred = row - mean
    inverse = lax.rsqrt(jnp.mean(centred * centred, axis=-1, keepdims=True) + EPSILON)
    normed = centred * inverse
    return normed * gain + bias, normed, inverse


def row_norm_back(incoming, normed, inverse, gain):
    scaled = incoming * gain
    inner = (
        scaled
        - jnp.mean(scaled, axis=-1, keepdims=True)
        - normed * jnp.mean(scaled * normed, axis=-1, keepdims=True)
    )
    return inner * inverse


GELU_A = 0.7978845608028654
GELU_B = 0.044715


def gelu(pre):
    return 0.5 * pre * (1.0 + jnp.tanh(GELU_A * (pre + GELU_B * pre * pre * pre)))


def gelu_slope(pre):
    square = pre * pre
    curve = jnp.tanh(GELU_A * pre * (1.0 + GELU_B * square))
    return 0.5 * (1.0 + curve) + 0.5 * pre * (1.0 - curve * curve) * GELU_A * (
        1.0 + 3.0 * GELU_B * square
    )


def widen(row):
    return jnp.broadcast_to(row, (8, row.shape[1])).astype(BF16)


def pick(block, index):
    rows = lax.broadcasted_iota(jnp.int32, block.shape, 0)
    return jnp.sum(jnp.where(rows == index, block.astype(F32), 0.0), axis=0, keepdims=True)


def put(block, index, row):
    rows = lax.broadcasted_iota(jnp.int32, block.shape, 0)
    return jnp.where(rows == index, row.astype(block.dtype), block)


def by_head(row, heads):
    shape = (heads, row.shape[1])
    lane_head = lax.broadcasted_iota(jnp.int32, shape, 1) // HD
    return jnp.where(lane_head == lax.broadcasted_iota(jnp.int32, shape, 0), row, 0.0)


def heads_only(block):
    lane_head = lax.broadcasted_iota(jnp.int32, block.shape, 1) // HD
    own = lane_head == lax.broadcasted_iota(jnp.int32, block.shape, 0)
    return jnp.sum(jnp.where(own, block, 0.0), axis=0, keepdims=True)


def thoughts_kernel(
    info_ref,
    tok_ref,
    lse_in_ref,
    vec_ref,
    fcb_ref,
    qkvb_ref,
    near_in,
    far_in,
    qkv_in,
    mixed_in,
    hid_in,
    lse_ref,
    pre_ref,
    prob_ref,
    res_ref,
    qkv_out,
    mixed_out,
    hid_out,
    kv_ref,
    late_q_ref,
    mixed_ref,
    hid_ref,
    near_ref,
    far_ref,
    sems,
):
    width = tok_ref.shape[1]
    blocks = (far_ref.shape[0] - 1) // 2
    rows = late_q_ref.shape[0]
    ln1_gain, ln1_bias, out_bias, ln2_gain, ln2_bias, proj_bias = (
        vec_ref[i : i + 1, :] for i in range(6)
    )
    slot = info_ref[0]
    count = info_ref[1]

    loads = [
        (qkv_in.at[:, pl.ds(0, PREFIX)], kv_ref),
        (far_in.at[pl.ds(2 * blocks, 1)], far_ref.at[pl.ds(2 * blocks, 1)]),
        (far_in.at[pl.ds(0, blocks)], far_ref.at[pl.ds(0, blocks)]),
        (far_in.at[pl.ds(blocks, blocks)], far_ref.at[pl.ds(blocks, blocks)]),
        (near_in, near_ref),
        (qkv_in.at[0, pl.ds(QUESTION, rows)], late_q_ref),
        (mixed_in.at[pl.ds(QUESTION, rows)], mixed_ref),
    ]
    loads = [pltpu.make_async_copy(a, b, sems.at[i]) for i, (a, b) in enumerate(loads)]
    for copy in loads:
        copy.start()
    hid_ref[...] = tok_ref[...].astype(F32)
    hidden_row = pick(hid_ref[...], slot - 1 - QUESTION)
    loads[0].wait()
    slot_rows = []
    slot_lse = []
    for step in range(THOUGHTS + 1):
        at = slot - 1 + step
        qkv_row = pick(kv_ref[0, QUESTION:, :], at - QUESTION)
        query = by_head(qkv_row * SCALE, HEAD_ROWS).astype(BF16)
        scores = dot_nt(query, kv_ref[1])
        key_pos = lax.broadcasted_iota(jnp.int32, scores.shape, 1)
        scores = jnp.where(key_pos <= at, scores, NEG)
        peak = jnp.max(scores, axis=1, keepdims=True)
        expo = jnp.exp(scores - peak)
        total = jnp.sum(expo, axis=1, keepdims=True)
        probs = expo / total
        mixed = heads_only(dot(probs.astype(BF16), kv_ref[2]))
        if step:
            slot_rows.append(mixed)
            slot_lse.append(peak + jnp.log(total))
        if step == THOUGHTS:
            break
        prob_ref[step * HEAD_ROWS : (step + 1) * HEAD_ROWS, :] = probs
        if not step:
            loads[1].wait()
        resid = hidden_row + dot(widen(mixed), far_ref[2 * blocks])[0:1] + out_bias
        res_ref[step : step + 1, :] = resid
        second, _, _ = row_norm(resid, ln2_gain, ln2_bias)
        second = widen(second)
        if not step:
            loads[2].wait()
        acts = []
        for j in range(blocks):
            span = slice(j * width, (j + 1) * width)
            pre = dot(second, far_ref[j])[0:1] + fcb_ref[0:1, span]
            pre_ref[step : step + 1, span] = pre
            acts.append(widen(gelu(pre)))
        if not step:
            loads[3].wait()
        fed = resid + proj_bias
        for j in range(blocks):
            fed = fed + dot(acts[j], far_ref[blocks + j])[0:1]
        first, _, _ = row_norm(fed, ln1_gain, ln1_bias)
        first = widen(first)
        hidden_row = fed
        spot = jnp.where(step < count, slot + step - QUESTION, -1)
        hid_ref[...] = put(hid_ref[...], spot, fed)
        if not step:
            loads[4].wait()
        for i in range(3):
            span = slice(i * width, (i + 1) * width)
            new_row = dot(first, near_ref[i])[0:1] + qkvb_ref[0:1, span]
            kv_ref[i, QUESTION:, :] = put(kv_ref[i, QUESTION:, :], spot, new_row)
    loads[5].wait()
    loads[6].wait()
    stores = [
        pltpu.make_async_copy(
            kv_ref.at[:, pl.ds(QUESTION, PREFIX - QUESTION)],
            qkv_out.at[:, pl.ds(QUESTION, PREFIX - QUESTION)],
            sems.at[0],
        ),
        pltpu.make_async_copy(
            hid_ref, hid_out.at[pl.ds(QUESTION, PREFIX - QUESTION)], sems.at[1]
        ),
    ]
    for copy in stores:
        copy.start()

    row_pos = QUESTION + lax.broadcasted_iota(jnp.int32, (HEAD_ROWS, rows), 1)
    late_q = late_q_ref[...]
    lse = lse_in_ref[:, QUESTION:]
    scores = []
    values = []
    top = lse
    for j in range(THOUGHTS):
        local = slot + j - QUESTION
        key = by_head(pick(kv_ref[1, QUESTION:, :], local) * SCALE, HEAD_ROWS)
        values.append(pick(kv_ref[2, QUESTION:, :], local))
        score = jnp.where(row_pos >= slot + j, dot_nt(key.astype(BF16), late_q), NEG)
        scores.append(score)
        top = jnp.maximum(top, score)
    whole_sum = jnp.exp(lse - top)
    for score in scores:
        whole_sum = whole_sum + jnp.exp(score - top)
    new_lse = top + jnp.log(whole_sum)
    ones = by_head(jnp.ones((1, width), F32), HEAD_ROWS).astype(BF16)
    share = jnp.exp(lse - new_lse)
    high = share.astype(BF16)
    low = (share - high.astype(F32)).astype(BF16)
    weights = [jnp.exp(score - new_lse).astype(BF16) for score in scores]
    step_rows = PREFIX - QUESTION
    for begin in range(0, rows, step_rows):
        span = slice(begin, begin + step_rows)
        part = mixed_ref[span, :].astype(F32) * (
            dot_tn(high[:, span], ones) + dot_tn(low[:, span], ones)
        )
        for weight, value in zip(weights, values):
            part = part + dot_tn(weight[:, span], ones) * value
        if not begin:
            for j in range(THOUGHTS):
                part = put(part, slot + j - QUESTION, slot_rows[j])
        mixed_ref[span, :] = part.astype(BF16)
    stores.append(
        pltpu.make_async_copy(mixed_ref, mixed_out.at[pl.ds(QUESTION, rows)], sems.at[2])
    )
    stores[-1].start()
    lse_ref[:, :QUESTION] = lse_in_ref[:, :QUESTION]
    column = lax.broadcasted_iota(jnp.int32, (HEAD_ROWS, step_rows), 1)
    middle = new_lse[:, :step_rows]
    for j in range(THOUGHTS):
        middle = jnp.where(column == slot + j - QUESTION, slot_lse[j], middle)
    lse_ref[:, QUESTION:PREFIX] = middle
    lse_ref[:, PREFIX:] = new_lse[:, step_rows:]
    for copy in stores:
        copy.wait()


def whole(array):
    zeros = (0,) * array.ndim
    return pl.BlockSpec(array.shape, lambda i, zeros=zeros: zeros)


def fc_spec(far):
    return pl.BlockSpec((far.shape[0] // 2,) + far.shape[1:], lambda i: (0, 0, 0))


def proj_spec(far):
    return pl.BlockSpec((far.shape[0] // 2,) + far.shape[1:], lambda i: (1, 0, 0))


def out_spec(far):
    last = far.shape[0] - 1
    return pl.BlockSpec((1,) + far.shape[1:], lambda i: (last, 0, 0))


def thoughts_forward(info, tokens, tokens32, qkv, mixed_low, lse, weights, vec, fc_bias, qkv_bias):
    near, far = weights
    seq_len, width = tokens.shape
    rows = seq_len - QUESTION
    middle = PREFIX - QUESTION
    anywhere = pl.BlockSpec(memory_space=pl.ANY)
    out_shape = [
        jax.ShapeDtypeStruct(lse.shape, F32),
        jax.ShapeDtypeStruct((8, fc_bias.shape[1]), F32),
        jax.ShapeDtypeStruct((THOUGHTS * HEAD_ROWS, PREFIX), F32),
        jax.ShapeDtypeStruct((8, width), F32),
        jax.ShapeDtypeStruct(qkv.shape, BF16),
        jax.ShapeDtypeStruct(mixed_low.shape, BF16),
        jax.ShapeDtypeStruct(tokens32.shape, F32),
    ]
    return pl.pallas_call(
        thoughts_kernel,
        grid=(1,),
        in_specs=[
            pl.BlockSpec(memory_space=pltpu.SMEM),
            pl.BlockSpec((middle, width), lambda i: (QUESTION // middle, 0)),
            whole(lse),
            whole(vec),
            whole(fc_bias),
            whole(qkv_bias),
            *[anywhere] * 5,
        ],
        out_specs=[*(whole(x) for x in out_shape[:4]), *[anywhere] * 3],
        out_shape=out_shape,
        input_output_aliases={8: 4, 9: 5, 10: 6},
        scratch_shapes=[
            pltpu.VMEM((3, PREFIX, width), BF16),
            pltpu.VMEM((rows, width), BF16),
            pltpu.VMEM((rows, width), BF16),
            pltpu.VMEM((middle, width), F32),
            pltpu.VMEM(near.shape, BF16),
            pltpu.VMEM(far.shape, BF16),
            pltpu.SemaphoreType.DMA((7,)),
        ],
        compiler_params=pltpu.CompilerParams(vmem_limit_bytes=VMEM_LIMIT),
        cost_estimate=cost(2),
        name="thought_rows_forward",
    )(info, tokens, lse, vec, fc_bias, qkv_bias, near, far, qkv, mixed_low, tokens32)


def thoughts_back_kernel(
    info_ref,
    hid_ref,
    qkv_ref,
    lse_ref,
    pre_ref,
    prob_ref,
    res_ref,
    vec_ref,
    near_in,
    far_in,
    qkv_in,
    mixed_in,
    mg_in,
    rg_in,
    sum_ref,
    fac_ref,
    mg_out,
    rg_out,
    mg_ref,
    rg_win,
    late_q_ref,
    mixed_ref,
    near_ref,
    far_ref,
    sems,
):
    width = hid_ref.shape[1]
    blocks = (far_ref.shape[0] - 1) // 2
    units = blocks * width
    rows = mg_ref.shape[0]
    ln1_gain, ln1_bias, _, ln2_gain, ln2_bias, _ = (vec_ref[i : i + 1, :] for i in range(6))
    slot = info_ref[0]
    count = info_ref[1]
    base = pl.multiple_of(((slot - 1 - QUESTION) // 16) * 16, 16)

    def window(ref):
        return ref.at[pl.ds(base, WINDOW)]

    loads = [
        (mg_in, mg_ref),
        (mixed_in.at[pl.ds(QUESTION, rows)], mixed_ref),
        (qkv_in.at[0, pl.ds(QUESTION, rows)], late_q_ref),
        (window(rg_in), rg_win),
        (near_in, near_ref),
        (far_in.at[pl.ds(blocks, blocks)], far_ref.at[pl.ds(blocks, blocks)]),
        (far_in.at[pl.ds(0, blocks)], far_ref.at[pl.ds(0, blocks)]),
        (far_in.at[pl.ds(2 * blocks, 1)], far_ref.at[pl.ds(2 * blocks, 1)]),
    ]
    loads = [pltpu.make_async_copy(a, b, sems.at[i]) for i, (a, b) in enumerate(loads)]
    for copy in loads:
        copy.start()
    for copy in loads[:4]:
        copy.wait()

    late_q = late_q_ref[...]
    mixed_grad = mg_ref[...]
    product = mixed_grad.astype(F32) * mixed_ref[...].astype(F32)
    high = product.astype(BF16)
    ones = by_head(jnp.ones((1, width), F32), HEAD_ROWS).astype(BF16)
    delta = dot_nt(ones, high) + dot_nt(ones, (product - high.astype(F32)).astype(BF16))
    lse = lse_ref[:, QUESTION:]

    def columns(block, scale):
        rows_here = [
            by_head(pick(block, slot + j - QUESTION) * scale, HEAD_ROWS) for j in range(THOUGHTS)
        ]
        return jnp.concatenate(rows_here, axis=0).astype(BF16)

    def twice(block):
        return jnp.concatenate([block] * THOUGHTS, axis=0)

    slot_pos = jnp.concatenate(
        [jnp.full((HEAD_ROWS, rows), QUESTION - j, jnp.int32) for j in range(THOUGHTS)], axis=0
    )
    seen = slot_pos + lax.broadcasted_iota(jnp.int32, slot_pos.shape, 1) >= slot
    scores = dot_nt(columns(qkv_ref[1, QUESTION:PREFIX, :], SCALE), late_q)
    probs = jnp.where(seen, jnp.exp(jnp.minimum(scores - twice(lse), 0.0)), 0.0)
    prob_grad = dot_nt(columns(qkv_ref[2, QUESTION:PREFIX, :], 1.0), mixed_grad)
    score_grad = (probs * (prob_grad - twice(delta))).astype(BF16)
    slot_keys = dot(score_grad, late_q)
    slot_values = dot(probs.astype(BF16), mixed_grad)
    slot_grads = []
    for j in range(THOUGHTS):
        span = slice(j * HEAD_ROWS, (j + 1) * HEAD_ROWS)
        slot_grads.append((heads_only(slot_keys[span]) * SCALE, heads_only(slot_values[span])))

    def through_first(at, query_grad, key_grad, value_grad):
        first_grad = (
            dot_nt(widen(query_grad), near_ref[0])
            + dot_nt(widen(key_grad), near_ref[1])
            + dot_nt(widen(value_grad), near_ref[2])
        )[0:1]
        _, normed, inverse = row_norm(hid_ref[pl.ds(at - QUESTION, 1), :], ln1_gain, ln1_bias)
        return row_norm_back(first_grad, normed, inverse, ln1_gain)

    sum_ref[...] = jnp.zeros_like(sum_ref)
    fac = {}
    loads[4].wait()
    carried = through_first(slot + 1, jnp.zeros((1, width), F32), *slot_grads[1])
    for copy in loads[5:]:
        copy.wait()
    for step in reversed(range(THOUGHTS)):
        at = slot - 1 + step
        upstream = jnp.where(step < count, carried, 0.0)
        low = widen(upstream)
        act_grad = jnp.concatenate([dot_nt(low, far_ref[blocks + j])[0:1] for j in range(blocks)], axis=1)
        pre = pre_ref[step : step + 1, :]
        pre_grad = (act_grad * gelu_slope(pre)).astype(BF16).astype(F32)
        second_grad = jnp.zeros((1, width), F32)
        for j in range(blocks):
            piece = pre_grad[:, j * width : (j + 1) * width]
            second_grad = second_grad + dot_nt(widen(piece), far_ref[j])[0:1]
        second, normed, inverse = row_norm(res_ref[step : step + 1, :], ln2_gain, ln2_bias)
        resid_grad = upstream + row_norm_back(second_grad, normed, inverse, ln2_gain)
        mixed_row = dot_nt(widen(resid_grad), far_ref[2 * blocks])[0:1]
        local = at - QUESTION
        rg_win[...] = put(rg_win[...], local - base, resid_grad)
        mg_ref[: PREFIX - QUESTION, :] = put(mg_ref[: PREFIX - QUESTION, :], local, mixed_row)
        up_low = upstream.astype(BF16).astype(F32)
        sum_ref[0:1, :units] += pre_grad
        sum_ref[1:2, :width] += second_grad * normed
        sum_ref[2:3, :width] += second_grad
        sum_ref[3:4, :width] += up_low
        sum_ref[4:5, :width] += resid_grad.astype(BF16).astype(F32)
        act = gelu(pre)
        rows_here = [act[:, j * width : (j + 1) * width] for j in range(blocks)]
        rows_here += [up_low, second]
        rows_here += [pre_grad[:, j * width : (j + 1) * width] for j in range(blocks)]
        for j, row in enumerate(rows_here):
            fac[THOUGHTS * j + step] = row
        if step:
            own_grad = by_head(mixed_row, HEAD_ROWS).astype(BF16)
            query = by_head(pick(qkv_ref[0, QUESTION:PREFIX, :], local) * SCALE, HEAD_ROWS)
            query = query.astype(BF16)
            probs = prob_ref[step * HEAD_ROWS : (step + 1) * HEAD_ROWS, :]
            prob_grad = dot_nt(own_grad, qkv_ref[2])
            own_delta = jnp.sum(prob_grad * probs, axis=1, keepdims=True)
            score_grad = (probs * (prob_grad - own_delta)).astype(BF16)
            query_grad = heads_only(dot(score_grad, qkv_ref[1])) * SCALE
            key_grad, value_grad = slot_grads[0]
            own = lax.broadcasted_iota(jnp.int32, probs.shape, 1) == at
            score_own = jnp.sum(jnp.where(own, score_grad.astype(F32), 0.0), axis=1, keepdims=True)
            prob_own = jnp.sum(jnp.where(own, probs, 0.0), axis=1, keepdims=True)
            key_grad += jnp.sum(score_own * query.astype(F32), axis=0, keepdims=True)
            value_grad += jnp.sum(prob_own * own_grad.astype(F32), axis=0, keepdims=True)
            carried = resid_grad + through_first(at, query_grad, key_grad, value_grad)
    padding = [jnp.zeros((1, width), F32)] * (fac_ref.shape[0] - len(fac))
    fac_ref[...] = jnp.concatenate([fac[i] for i in range(len(fac))] + padding, axis=0).astype(BF16)
    stores = [
        pltpu.make_async_copy(mg_ref, mg_out, sems.at[0]),
        pltpu.make_async_copy(rg_win, window(rg_out), sems.at[1]),
    ]
    for copy in stores:
        copy.start()
    for copy in stores:
        copy.wait()


SUM_ROWS = ("fc_bias", "ln2_gain", "ln2_bias", "proj_bias", "out_bias")


def thoughts_back(info, hidden, qkv, mixed_low, lse, saved, weights, vec, mixed_grad, resid_grad):
    near, far = weights
    width = hidden.shape[1]
    units = far.shape[0] // 2 * width
    middle = PREFIX - QUESTION
    anywhere = pl.BlockSpec(memory_space=pl.ANY)
    out_shape = [
        jax.ShapeDtypeStruct((8, units), F32),
        jax.ShapeDtypeStruct((FACTOR_ROWS, width), BF16),
        jax.ShapeDtypeStruct(mixed_grad.shape, BF16),
        jax.ShapeDtypeStruct(resid_grad.shape, F32),
    ]
    return pl.pallas_call(
        thoughts_back_kernel,
        grid=(1,),
        in_specs=[
            pl.BlockSpec(memory_space=pltpu.SMEM),
            pl.BlockSpec((middle, width), lambda i: (QUESTION // middle, 0)),
            pl.BlockSpec((3, PREFIX, width), lambda i: (0, 0, 0)),
            whole(lse),
            *(whole(x) for x in saved),
            whole(vec),
            *[anywhere] * 6,
        ],
        out_specs=[whole(out_shape[0]), whole(out_shape[1]), anywhere, anywhere],
        out_shape=out_shape,
        input_output_aliases={12: 2, 13: 3},
        scratch_shapes=[
            pltpu.VMEM(mixed_grad.shape, BF16),
            pltpu.VMEM((WINDOW, width), F32),
            pltpu.VMEM(mixed_grad.shape, BF16),
            pltpu.VMEM(mixed_grad.shape, BF16),
            pltpu.VMEM(near.shape, BF16),
            pltpu.VMEM(far.shape, BF16),
            pltpu.SemaphoreType.DMA((8,)),
        ],
        compiler_params=pltpu.CompilerParams(vmem_limit_bytes=VMEM_LIMIT),
        cost_estimate=cost(2.0),
        name="thought_rows_backward",
    )(
        info,
        hidden,
        qkv,
        lse,
        *saved,
        vec,
        near,
        far,
        qkv,
        mixed_low,
        mixed_grad,
        resid_grad,
    )


def feed_kernel(
    hid_ref, mixed_ref, up_ref, wout_ref, wfc_ref, wproj_ref, vec_ref, fcb_ref, out_ref, first_ref,
    second_ref, act_ref, pg_ref, rg_ref, mg_ref, sum_ref, slope_ref,
):
    width = hid_ref.shape[1]
    blocks = wfc_ref.shape[0]
    step = pl.program_id(0)
    skip = QUESTION // BLOCK
    out_bias, ln2_gain, ln2_bias, proj_bias = (vec_ref[i : i + 1, :] for i in range(2, 6))

    @pl.when(step == 0)
    def _():
        sum_ref[...] = jnp.zeros_like(sum_ref)

    hidden = hid_ref[...]
    _, first_normed, _ = row_norm(hidden, vec_ref[0:1, :], vec_ref[1:2, :])
    first_ref[...] = first_normed.astype(BF16)
    resid = hidden + dot(mixed_ref[...], wout_ref[0]) + out_bias
    second, normed, inverse = row_norm(resid, ln2_gain, ln2_bias)
    low = second.astype(BF16)
    second_ref[...] = low
    total = resid + proj_bias
    for j in range(blocks):
        span = slice(j * width, (j + 1) * width)
        pre = dot(low, wfc_ref[j]) + fcb_ref[:, span]
        square = pre * pre
        curve = jnp.tanh(GELU_A * pre * (1.0 + GELU_B * square))
        half = 0.5 + 0.5 * curve
        act = (pre * half).astype(BF16)
        rise = 0.5 * GELU_A + (1.5 * GELU_A * GELU_B) * square
        slope_ref[:, span] = (half + pre * rise * (1.0 - curve * curve)).astype(BF16)
        act_ref[:, span] = act
        total = total + dot(act, wproj_ref[j])
    out_ref[...] = total.astype(BF16)

    @pl.when(step >= skip)
    def _():
        up = up_ref[...]
        second_grad = jnp.zeros(up.shape, F32)
        for j in range(blocks):
            span = slice(j * width, (j + 1) * width)
            slope = slope_ref[:, span].astype(F32)
            pre_grad = (dot_nt(up, wproj_ref[j]) * slope).astype(BF16)
            pg_ref[:, span] = pre_grad
            sum_ref[0:1, span] += jnp.sum(pre_grad.astype(F32), axis=0, keepdims=True)
            second_grad = second_grad + dot_nt(pre_grad, wfc_ref[j])
        up32 = up.astype(F32)
        resid_grad = up32 + row_norm_back(second_grad, normed, inverse, ln2_gain)
        attn_grad = resid_grad.astype(BF16)
        rg_ref[...] = resid_grad
        mg_ref[...] = dot_nt(attn_grad, wout_ref[0]).astype(BF16)
        sum_ref[1:2, :width] += jnp.sum(second_grad * normed, axis=0, keepdims=True)
        sum_ref[2:3, :width] += jnp.sum(second_grad, axis=0, keepdims=True)
        sum_ref[3:4, :width] += jnp.sum(up32, axis=0, keepdims=True)
        sum_ref[4:5, :width] += jnp.sum(attn_grad.astype(F32), axis=0, keepdims=True)


def feed(hidden, mixed_low, upstream_low, weights, vec, fc_bias):
    far = weights[1]
    seq_len, width = hidden.shape
    late = seq_len - QUESTION
    units = fc_bias.shape[1]
    skip = QUESTION // BLOCK

    def rows(columns):
        return pl.BlockSpec((BLOCK, columns), lambda i: (i, 0))

    def late_rows(columns):
        return pl.BlockSpec((BLOCK, columns), lambda i: (jnp.maximum(i - skip, 0), 0))

    sums = jax.ShapeDtypeStruct((8, units), F32)
    return pl.pallas_call(
        feed_kernel,
        grid=(seq_len // BLOCK,),
        in_specs=[
            rows(width),
            rows(width),
            late_rows(width),
            out_spec(far),
            fc_spec(far),
            proj_spec(far),
            whole(vec),
            whole(fc_bias),
        ],
        out_specs=[
            rows(width),
            rows(width),
            late_rows(width),
            late_rows(units),
            late_rows(units),
            late_rows(width),
            late_rows(width),
            whole(sums),
        ],
        out_shape=[
            jax.ShapeDtypeStruct((seq_len, width), BF16),
            jax.ShapeDtypeStruct((seq_len, width), BF16),
            jax.ShapeDtypeStruct((late, width), BF16),
            jax.ShapeDtypeStruct((late, units), BF16),
            jax.ShapeDtypeStruct((late, units), BF16),
            jax.ShapeDtypeStruct((late, width), F32),
            jax.ShapeDtypeStruct((late, width), BF16),
            sums,
        ],
        scratch_shapes=[pltpu.VMEM((BLOCK, units), BF16)],
        compiler_params=pltpu.CompilerParams(vmem_limit_bytes=VMEM_LIMIT),
        cost_estimate=cost(3),
        name="feed_forward_and_back",
    )(hidden, mixed_low, upstream_low, far, far, far, vec, fc_bias)


def first_back_kernel(info_ref, hid_ref, grad_ref, rg_ref, near_ref, vec_ref, in_ref):
    rows, width = hid_ref.shape
    step = pl.program_id(0)
    slot = info_ref[0]
    count = info_ref[1]
    gain = vec_ref[0:1, :]
    _, normed, inverse = row_norm(hid_ref[...], gain, vec_ref[1:2, :])
    first_grad = jnp.zeros((rows, width), F32)
    for i in range(3):
        first_grad = first_grad + dot_nt(grad_ref[i], near_ref[i])
    late = (step >= QUESTION // BLOCK).astype(F32)
    grad = row_norm_back(first_grad, normed, inverse, gain) + late * rg_ref[...]
    position = step * rows + lax.broadcasted_iota(jnp.int32, (rows, 1), 0)
    replaced = (position >= slot) & (position < slot + jnp.minimum(count, THOUGHTS))
    in_ref[...] = jnp.where(replaced, 0.0, grad)


def first_back(info, hidden, qkv_grad, resid_grad, weights, vec):
    seq_len, width = hidden.shape
    skip = QUESTION // BLOCK
    rows = pl.BlockSpec((BLOCK, width), lambda i: (i, 0))
    return pl.pallas_call(
        first_back_kernel,
        grid=(seq_len // BLOCK,),
        in_specs=[
            pl.BlockSpec(memory_space=pltpu.SMEM),
            rows,
            pl.BlockSpec((3, BLOCK, width), lambda i: (0, i, 0)),
            pl.BlockSpec((BLOCK, width), lambda i: (jnp.maximum(i - skip, 0), 0)),
            whole(weights[0]),
            whole(vec),
        ],
        out_specs=rows,
        out_shape=jax.ShapeDtypeStruct((seq_len, width), F32),
        compiler_params=pltpu.CompilerParams(vmem_limit_bytes=VMEM_LIMIT),
        cost_estimate=cost(0.83),
        name="first_norm_backward",
    )(info, hidden, qkv_grad, resid_grad, weights[0], vec)


def in_pieces(value, count=3):
    pieces = []
    for _ in range(count):
        pieces.append(value.astype(BF16))
        value = value - pieces[-1].astype(F32)
    return pieces


def keep_and_send(value, core, chips, keep_ref, send_ref, at):
    own = value.shape[0] // (2 * len(chips))
    for spot, chip in enumerate(chips):
        even = value[2 * chip * own : (2 * chip + 1) * own]
        odd = value[(2 * chip + 1) * own : (2 * chip + 2) * own]
        keep_ref[spot, at] = jnp.where(core == 0, even, odd).astype(BF16)
        send_ref[spot, at] = jnp.where(core == 0, odd, even).astype(BF16)


def near_terms_kernel(
    sizes, chips_a, chips_b, core_ref, normed_ref, grad_ref, mixed_ref, rg_ref, near_ref, vec_ref,
    feed_sum_ref, row_sum_ref, keep_a, send_a, keep_b, send_b, packed_ref,
):
    core = core_ref[0]
    width = normed_ref.shape[1]
    columns = vec_ref[...].T
    gain, bias = columns[:, 0:1], columns[:, 1:2]
    normed_t = normed_ref[...].T
    gain_terms = jnp.zeros((width, width), F32)
    bias_rows = jnp.zeros((16, width), F32)
    column_sums = []
    for i in range(3):
        inner = dot(normed_t, grad_ref[i])
        sums = jnp.sum(grad_ref[i].astype(F32), axis=0, keepdims=True)
        value = inner * gain + bias * sums
        if i < 2:
            keep_and_send(value, core, chips_a, keep_a, send_a, i)
        else:
            keep_and_send(value, core, chips_b, keep_b, send_b, 0)
        gain_terms = gain_terms + inner * near_ref[i].astype(F32)
        pieces = in_pieces(jnp.broadcast_to(sums, (8, width)), 2)
        bias_rows = bias_rows + dot_nt(jnp.concatenate(pieces, axis=0), near_ref[i])
        column_sums.append(sums)
    ones = jnp.ones((16, width), BF16)
    totals = feed_sum_ref[...] + row_sum_ref[...]
    small = {name: totals[i : i + 1, :width] for i, name in enumerate(SUM_ROWS)}
    small["fc_bias"] = totals[0:1]
    small["ln1_gain"] = sum(dot_nt(ones, piece) for piece in in_pieces(gain_terms, 2))[0:1]
    small["ln1_bias"] = bias_rows[0:1] + bias_rows[8:9]
    small["qv_bias"] = jnp.concatenate([column_sums[0], column_sums[2]], axis=1)
    pack(small, sizes, 2 * len(chips_a), packed_ref)
    value = dot_tn(mixed_ref[QUESTION:, :], rg_ref[...].astype(BF16))
    keep_and_send(value, core, chips_b, keep_b, send_b, 1)


def near_terms(
    core, normed_low, qkv_grad, mixed_low, resid_grad, near, vec, feed_sums, row_sums, sizes, chips_a, chips_b
):
    seq_len, width = normed_low.shape
    half = jax.ShapeDtypeStruct((len(chips_a), 2, width // (2 * len(chips_a)), width), BF16)
    packed = jax.ShapeDtypeStruct((len(sizes), 2 * len(chips_a), LANES), BF16)
    out_shape = [half] * 4 + [packed]
    return pl.pallas_call(
        functools.partial(near_terms_kernel, sizes, chips_a, chips_b),
        grid=(1,),
        in_specs=[
            pl.BlockSpec(memory_space=pltpu.SMEM),
            whole(normed_low),
            whole(qkv_grad),
            whole(mixed_low),
            whole(resid_grad),
            whole(near),
            whole(vec),
            whole(feed_sums),
            whole(row_sums),
        ],
        out_specs=[whole(x) for x in out_shape],
        out_shape=out_shape,
        compiler_params=pltpu.CompilerParams(vmem_limit_bytes=VMEM_LIMIT),
        cost_estimate=cost(0.5),
        name="near_weight_terms",
    )(core, normed_low, qkv_grad, mixed_low, resid_grad, near, vec, feed_sums, row_sums)


def fc_terms_kernel(chips, core_ref, second_ref, pg_ref, keep_ref, send_ref, second_t):
    @pl.when(pl.program_id(0) == 0)
    def _():
        second_t[...] = second_ref[...].T

    value = dot(second_t[...], pg_ref[...])
    keep_and_send(value, core_ref[0], chips, keep_ref, send_ref, 0)


def fc_terms(core, second_low, pre_grad, chips):
    width = second_low.shape[1]
    rows, units = pre_grad.shape
    blocks = units // width
    own = width // (2 * len(chips))
    half = jax.ShapeDtypeStruct((len(chips), blocks, own, width), BF16)
    out = pl.BlockSpec((len(chips), 1, own, width), lambda j: (0, j, 0, 0))
    return pl.pallas_call(
        functools.partial(fc_terms_kernel, chips),
        grid=(blocks,),
        in_specs=[
            pl.BlockSpec(memory_space=pltpu.SMEM),
            pl.BlockSpec((rows, width), lambda j: (0, 0)),
            pl.BlockSpec((rows, width), lambda j: (0, j)),
        ],
        out_specs=[out, out],
        out_shape=[half, half],
        scratch_shapes=[pltpu.VMEM((width, rows), BF16)],
        compiler_params=pltpu.CompilerParams(vmem_limit_bytes=VMEM_LIMIT),
        cost_estimate=cost(0.5),
        name="fc_weight_terms",
    )(core, second_low, pre_grad)


def proj_terms_kernel(outer, inner, act_ref, up_ref, out_ref):
    value = dot_tn(act_ref[...], up_ref[...])
    rows, width = value.shape
    value = value.reshape(outer, inner, rows // (outer * inner), width)
    for i in range(inner):
        out_ref[i, :, 0] = value[:, i].astype(BF16)


def proj_terms(act_low, upstream_low, outer, inner):
    units = act_low.shape[1]
    rows, width = upstream_low.shape
    blocks = units // width
    shape = (inner, outer, blocks, width // (outer * inner), width)
    return pl.pallas_call(
        functools.partial(proj_terms_kernel, outer, inner),
        grid=(blocks,),
        in_specs=[
            pl.BlockSpec((rows, width), lambda j: (0, j)),
            pl.BlockSpec((rows, width), lambda j: (0, 0)),
        ],
        out_specs=pl.BlockSpec((inner, outer, 1) + shape[3:], lambda j: (0, 0, j, 0, 0)),
        out_shape=jax.ShapeDtypeStruct(shape, BF16),
        compiler_params=pltpu.CompilerParams(vmem_limit_bytes=VMEM_LIMIT),
        cost_estimate=cost(0.5),
        name="proj_weight_terms",
    )(act_low, upstream_low)


def first_kernel(
    orders, core_ref, tok_ref, left_mine, left_got, right_mine, right_got, vec_ref, qkvb_ref, qkv_ref,
    near_ref, rows_ref,
):
    width = tok_ref.shape[1]

    @pl.when(pl.program_id(0) == 0)
    def _():
        even_is_mine = core_ref[0] == 0
        own, half = left_mine.shape[2:]
        for i in range(3):
            for side, (mine, got) in enumerate([(left_mine, left_got), (right_mine, right_got)]):
                for spot, chip in enumerate(orders[side]):
                    a = mine[spot, i].astype(F32)
                    b = got[spot, i].astype(F32)
                    begin = 2 * chip * own
                    rows_ref[begin : begin + own, :] = jnp.where(even_is_mine, a, b)
                    rows_ref[begin + own : begin + 2 * own, :] = jnp.where(even_is_mine, b, a)
                near_ref[i, :, side * half : (side + 1) * half] = rows_ref[...].astype(BF16)

    first, _, _ = row_norm(tok_ref[...].astype(F32), vec_ref[0:1, :], vec_ref[1:2, :])
    first = first.astype(BF16)
    for i in range(3):
        span = slice(i * width, (i + 1) * width)
        qkv_ref[i] = (dot(first, near_ref[i]) + qkvb_ref[:, span]).astype(BF16)


def first_forward(core, tokens, pieces, orders, vec, qkv_bias):
    seq_len, width = tokens.shape
    near = jax.ShapeDtypeStruct((3, width, width), BF16)
    return pl.pallas_call(
        functools.partial(first_kernel, orders),
        grid=(seq_len // BLOCK,),
        in_specs=[
            pl.BlockSpec(memory_space=pltpu.SMEM),
            pl.BlockSpec((BLOCK, width), lambda i: (i, 0)),
            *(whole(piece) for piece in pieces),
            whole(vec),
            whole(qkv_bias),
        ],
        out_specs=[pl.BlockSpec((3, BLOCK, width), lambda i: (0, i, 0)), whole(near)],
        out_shape=[jax.ShapeDtypeStruct((3, seq_len, width), BF16), near],
        scratch_shapes=[pltpu.VMEM((width, width // 2), F32)],
        compiler_params=pltpu.CompilerParams(vmem_limit_bytes=VMEM_LIMIT),
        cost_estimate=cost(0.67),
        name="first_norm_forward",
    )(core, tokens, *pieces, vec, qkv_bias)


def group_of(blocks, own):
    each = blocks * own
    group = LANES // math.gcd(LANES, each)
    device, block, i = np.indices((group, blocks, own)).reshape(3, -1)
    swap = np.zeros((group * each, group * each), np.float32)
    swap[np.arange(group * each), block * (group * own) + device * own + i] = 1.0
    return group, jnp.asarray(swap, BF16)


def far_shard_kernel(blocks, span, fc_ref, proj_ref, out_w_ref, swap_ref, out_ref):
    own, width = out_w_ref.shape
    size = swap_ref.shape[0]
    groups = width // span
    rows = [fc_ref[:, g * size : (g + 1) * size].astype(F32) for g in range(groups)]
    swapped = dot(jnp.concatenate(rows, axis=0).astype(BF16), swap_ref[...])
    for g in range(groups):
        part = swapped[g * own : (g + 1) * own]
        for j in range(blocks):
            piece = part[:, j * span : (j + 1) * span]
            out_ref[j, :, g * span : (g + 1) * span] = piece.astype(BF16)
    for j in range(blocks):
        out_ref[blocks + j] = proj_ref[j]
    out_ref[2 * blocks] = out_w_ref[...]


def join_far(fc_shard, proj_shard, out_shard):
    own, width = out_shard.shape
    blocks = fc_shard.shape[1] // width
    group, swap = group_of(blocks, own)
    return pl.pallas_call(
        functools.partial(far_shard_kernel, blocks, group * own),
        out_shape=jax.ShapeDtypeStruct((2 * blocks + 1, own, width), BF16),
        compiler_params=pltpu.CompilerParams(vmem_limit_bytes=VMEM_LIMIT),
        name="far_shard",
    )(fc_shard, proj_shard.reshape(blocks, own, width), out_shard, swap)


def row_terms_kernel(span, index_ref, fac_ref, proj_ref, fc_ref, swap_ref, proj_out, fc_out):
    blocks, own, width = proj_ref.shape
    shape = (width, own)
    mine = lax.broadcasted_iota(jnp.int32, shape, 0) - index_ref[0] * own
    select = (mine == lax.broadcasted_iota(jnp.int32, shape, 1)).astype(BF16)

    def factor(j):
        return jnp.concatenate([fac_ref[THOUGHTS * j + i] for i in range(THOUGHTS)], axis=0)

    upstream = factor(blocks)
    terms = []
    second = dot(factor(blocks + 1), select).astype(BF16)
    for j in range(blocks):
        act = dot(factor(j), select).astype(BF16)
        proj_out[j] = proj_ref[j].astype(F32) + dot_tn(act, upstream)
        terms.append(fc_ref[j] + dot_tn(second, factor(blocks + 2 + j)))
    size = swap_ref.shape[0]
    groups = width // span
    rows = [
        jnp.concatenate([t[:, g * span : (g + 1) * span] for t in terms], axis=1)
        for g in range(groups)
    ]
    left = jnp.concatenate(rows, axis=0)
    total = sum(dot_nt(piece, swap_ref[...]) for piece in in_pieces(left))
    for g in range(groups):
        fc_out[:, g * size : (g + 1) * size] = total[g * own : (g + 1) * own]


def row_terms(index, factors, proj_sum, fc_sum):
    blocks, own, width = fc_sum.shape
    out_shape = [
        jax.ShapeDtypeStruct(proj_sum.shape, F32),
        jax.ShapeDtypeStruct((own, blocks * width), F32),
    ]
    group, swap = group_of(blocks, own)
    return pl.pallas_call(
        functools.partial(row_terms_kernel, group * own),
        grid=(1,),
        in_specs=[
            pl.BlockSpec(memory_space=pltpu.SMEM),
            whole(factors),
            whole(proj_sum),
            whole(fc_sum),
            whole(swap),
        ],
        out_specs=[whole(x) for x in out_shape],
        out_shape=out_shape,
        compiler_params=pltpu.CompilerParams(vmem_limit_bytes=VMEM_LIMIT),
        cost_estimate=cost(0.33),
        name="thought_rows_terms",
    )(index, factors, proj_sum, fc_sum, swap)


def spread_matrix(shard, count):
    shape = (shard, shard * count)
    column = lax.broadcasted_iota(jnp.int32, shape, 1) % shard
    return (column == lax.broadcasted_iota(jnp.int32, shape, 0)).astype(BF16)


def owner_mask(shard, count):
    shape = (count, shard * count)
    owner = lax.broadcasted_iota(jnp.int32, shape, 1) // shard
    return owner == lax.broadcasted_iota(jnp.int32, shape, 0)


VECTOR_ROWS = ("ln1_gain", "ln1_bias", "out_bias", "ln2_gain", "ln2_bias", "proj_bias")


def unpack_kernel(sizes, devices, packed_ref, vec_ref, fcb_ref, qkvb_ref):
    vec_ref[...] = jnp.zeros_like(vec_ref)
    width = vec_ref.shape[1]
    for at, (name, size) in enumerate(sizes):
        if name == "fc_bias":
            own = width // devices
            for j in range(size // own):
                spread = dot(packed_ref[at][:, j * own : (j + 1) * own], spread_matrix(own, devices))
                spread = jnp.where(owner_mask(own, devices), spread, 0.0)
                span = slice(j * width, (j + 1) * width)
                fcb_ref[:, span] = jnp.sum(spread, axis=0, keepdims=True)
            continue
        block = packed_ref[at][:, :size]
        spread = dot(block, spread_matrix(size, devices))
        full = jnp.sum(jnp.where(owner_mask(size, devices), spread, 0.0), axis=0, keepdims=True)
        if name == "qv_bias":
            qkvb_ref[:, :width] = full[:, :width]
            qkvb_ref[:, width : 2 * width] = jnp.zeros((1, width), F32)
            qkvb_ref[:, 2 * width :] = full[:, width:]
        else:
            at = VECTOR_ROWS.index(name)
            vec_ref[at : at + 1, :] = full


def unpack(packed, sizes):
    devices = packed.shape[1]
    size = dict(sizes)
    width = size["ln1_gain"] * devices
    return pl.pallas_call(
        functools.partial(unpack_kernel, sizes, devices),
        out_shape=[
            jax.ShapeDtypeStruct((8, width), F32),
            jax.ShapeDtypeStruct((1, size["fc_bias"] * devices), F32),
            jax.ShapeDtypeStruct((1, 3 * width), F32),
        ],
        compiler_params=pltpu.CompilerParams(vmem_limit_bytes=VMEM_LIMIT),
        name="vectors_unpack",
    )(packed)


def pack(rows, sizes, devices, out_ref):
    out_ref[...] = jnp.zeros_like(out_ref)
    width = rows["ln1_gain"].shape[1]
    for at, (name, size) in enumerate(sizes):
        own = width // devices if name == "fc_bias" else size
        span = own * devices
        for j in range(size // own):
            row = jnp.broadcast_to(rows[name][:, j * span : (j + 1) * span], (devices, span))
            row = jnp.where(owner_mask(own, devices), row, 0.0).astype(BF16)
            piece = dot_nt(row, spread_matrix(own, devices)).astype(BF16)
            out_ref[at, :, j * own : (j + 1) * own] = piece


def join_kernel(*refs):
    out_ref = refs[-1]
    out_ref[...] = jnp.zeros_like(out_ref)
    for at, ref in enumerate(refs[:-1]):
        out_ref[at : at + 1, : ref.shape[0]] = ref[...].astype(F32).reshape(1, ref.shape[0])


def join(vectors):
    return pl.pallas_call(
        join_kernel,
        out_shape=jax.ShapeDtypeStruct((len(vectors), LANES), F32),
        name="vectors_join",
    )(*vectors)


def part_kernel(joined_ref, *refs):
    for at, ref in enumerate(refs):
        ref[...] = joined_ref[at, : ref.shape[0]]


def part(joined, sizes):
    return pl.pallas_call(
        part_kernel,
        out_shape=[jax.ShapeDtypeStruct((size,), F32) for _, size in sizes],
        name="vectors_part",
    )(joined)


def step_on_sequence(
    near_pieces, far, vectors, tokens, cotangent, slots, count, answer_start, devices, sizes, comm
):
    vec, fc_bias, qkv_bias = vectors
    seq_len, width = tokens.shape
    info = jnp.stack([slots[0], count])

    qkv_first, near = first_forward(
        comm.core, tokens, near_pieces, comm.near_orders, vec, qkv_bias
    )
    mixed_hidden, lse_hidden = attend(info, qkv_first)
    late = QUESTION + lax.iota(jnp.int32, seq_len - QUESTION)
    upstream_low = jnp.where(
        (late >= answer_start)[:, None], cotangent[QUESTION:], jnp.zeros((), BF16)
    )
    tokens32 = tokens.astype(F32)
    weights = (near, after(far, mixed_hidden, upstream_low, tokens32))
    lse, *saved, qkv, mixed_low, hidden = thoughts_forward(
        info, tokens, tokens32, qkv_first, mixed_hidden, lse_hidden, weights, vec, fc_bias, qkv_bias
    )
    output, normed_low, second_low, act_low, pre_grad, resid_grad, mixed_grad, sums = feed(
        hidden, mixed_low, upstream_low, weights, vec, fc_bias
    )

    proj_grad = comm.proj_terms(act_low, upstream_low)
    proj_half = comm.early(proj_grad)
    halves = fc_terms(comm.core, after(second_low, proj_grad), pre_grad, comm.chips("zyxc"))
    fc_going = comm.scatter(halves, "zyxc")
    sent = go_after([fc_going])
    row_sums, factors, mixed_grad, resid_grad = thoughts_back(
        info,
        hidden,
        qkv,
        mixed_low,
        after(lse, *sent),
        saved,
        weights,
        vec,
        mixed_grad,
        resid_grad,
    )
    join_after([fc_going], row_sums)
    spread = comm.factors(factors)
    sent = go_after([fc_going, spread])
    lse, back_grad = after((lse, mixed_grad), *sent)
    qkv_grad = attend_back(qkv, mixed_low, lse, back_grad)
    join_after([fc_going, spread], qkv_grad)
    proj_half = after(proj_half, qkv_grad)
    proj_going = comm.early_end(proj_half)
    sent = (*go_after([fc_going, spread]), proj_half)
    *terms, packed = near_terms(
        comm.core,
        after(normed_low, *sent),
        qkv_grad,
        mixed_low,
        resid_grad,
        near,
        vec,
        sums,
        row_sums,
        sizes,
        comm.chips("zxyc"),
        comm.chips("zyxc"),
    )
    first = comm.scatter(terms[:2], "zxyc")
    rest = comm.scatter(terms[2:], "zyxc")
    vectors_going = comm.scatter_vectors(packed)

    join_after([fc_going, spread], packed)

    going = [first, rest, vectors_going]
    sent = go_after(going, fc_going.got, spread.buf)
    sent += go_after([fc_going, spread], *sent)
    join_after(going, *sent)
    sent = go_after(going)
    input_grad = first_back(info, hidden, after(qkv_grad, *sent), resid_grad, weights, vec)
    going += [fc_going, spread]
    join_after(going, input_grad)
    proj_g = fc_g = None
    while any(swap.todo for swap in going) or proj_g is None:
        group = [swap for swap in going if swap.todo]
        sent = go_after(group)
        done = sent
        if proj_g is None and fc_going not in group and spread not in group:
            factors, fc_sum = after((spread.finish(), fc_going.finish()), *sent)
            proj_g, fc_g = comm.terms(factors, proj_going, fc_sum)
            done = (proj_g, fc_g)
        join_after(group, *done)
    return (
        output,
        input_grad,
        first.finish(),
        rest.finish(),
        proj_g,
        fc_g,
        vectors_going.finish(),
    )


SMALL = ("ln1_gain", "ln1_bias", "qv_bias", "out_bias", "ln2_gain", "ln2_bias", "fc_bias", "proj_bias")


def on_device(
    links,
    tokens,
    ln1_gain,
    ln1_bias,
    qkv_weight,
    qv_bias,
    out_weight,
    out_bias,
    ln2_gain,
    ln2_bias,
    fc_weight,
    fc_bias,
    proj_weight,
    proj_bias,
    cotangent,
    thought_slots,
    thought_count,
    answer_start,
):
    devices = links.sizes["dp"] * links.sizes["fsdp"]
    small_shards = dict(
        ln1_gain=ln1_gain,
        ln1_bias=ln1_bias,
        qv_bias=qv_bias,
        out_bias=out_bias,
        ln2_gain=ln2_gain,
        ln2_bias=ln2_bias,
        fc_bias=fc_bias,
        proj_bias=proj_bias,
    )
    sizes = tuple((n, small_shards[n].shape[0]) for n in SMALL)
    own, width = out_weight.shape
    blocks = proj_weight.shape[0] // own
    both = ("dp", "fsdp")

    far_shard = join_far(fc_weight, proj_weight, out_weight)
    far = lax.all_gather(far_shard, both, axis=1, tiled=True)

    packed = join([small_shards[n] for n in SMALL]).astype(BF16)
    small = links.gather(packed, "zxyc", axis=0).reshape(devices, len(sizes), LANES)
    half = width // 2
    near_pieces = []
    near_texts = ("zxyc", "zyxc")
    for side, text in enumerate(near_texts):
        part_columns = [
            qkv_weight[:, i * width + side * half : i * width + (side + 1) * half] for i in range(3)
        ]
        ring = Gather(links, jnp.stack(part_columns)[None], text)
        near_pieces += ring.last()

    class Comm:
        chips = links.chips
        near_orders = [links.spots(text) for text in near_texts]
        core = (lax.axis_index("fsdp") % 2)[None].astype(jnp.int32)

        @staticmethod
        def proj_terms(act_low, upstream_low):
            return proj_terms(act_low, upstream_low, links.sizes["dp"], links.sizes["fsdp"])

        @staticmethod
        def early(value):
            return lax.psum_scatter(
                value.reshape(-1, width), "fsdp", scatter_dimension=0, tiled=True
            )

        @staticmethod
        def early_end(value):
            value = lax.psum_scatter(value, "dp", scatter_dimension=0, tiled=True)
            return value.reshape(blocks, own, width)

        @staticmethod
        def scatter(halves, text):
            return links.scatter(tuple(halves), text)

        @staticmethod
        def factors(rows):
            return Gather(links, rows, "zyxc")

        @staticmethod
        def scatter_vectors(value):
            return links.scatter(value.transpose(1, 0, 2), "zxyc")

        @staticmethod
        def terms(factors, proj_sum, fc_sum):
            index = lax.axis_index(both)[None].astype(jnp.int32)
            factors = factors.reshape(devices, FACTOR_ROWS, width).transpose(1, 0, 2)
            return row_terms(index, factors, proj_sum, fc_sum)

    output, input_grad, first, rest, proj_g, fc_g, vector_sums = step_on_sequence(
        near_pieces,
        far,
        unpack(small.transpose(1, 0, 2), sizes),
        tokens[0],
        cotangent[0],
        thought_slots[0],
        thought_count[0],
        answer_start[0],
        devices,
        sizes,
        Comm,
    )
    proj_g = proj_g.reshape(blocks * own, width)
    qkv_g = jnp.concatenate([first[0], first[1], rest[0]], axis=1)
    out_g = rest[1]
    owned = dict(zip(SMALL, part(vector_sums, sizes)))
    return (
        output[None],
        input_grad[None],
        owned["ln1_gain"],
        owned["ln1_bias"],
        qkv_g,
        owned["qv_bias"],
        out_g,
        owned["out_bias"],
        owned["ln2_gain"],
        owned["ln2_bias"],
        fc_g,
        owned["fc_bias"],
        proj_g,
        owned["proj_bias"],
    )


def solution(mesh):
    links = Links({name: mesh.shape[name] for name in ("dp", "fsdp")})
    both = ("dp", "fsdp")
    cube, matrix, vector = P(both, None, None), P(both, None), P(both)
    weight_specs = (
        vector,
        vector,
        matrix,
        vector,
        matrix,
        vector,
        vector,
        vector,
        matrix,
        vector,
        matrix,
        vector,
    )

    def per_device(*args):
        return on_device(links, *args)

    return jax.shard_map(
        per_device,
        mesh=mesh,
        in_specs=(cube,) + weight_specs + (cube, matrix, vector, vector),
        out_specs=(cube, cube) + weight_specs,
        check_vma=False,
    )
```

```python
import functools
import math

import jax
import jax.numpy as jnp
import numpy as np
from jax import lax
from jax.experimental import pallas as pl
from jax.experimental.pallas import tpu as pltpu
from jax.sharding import PartitionSpec as P

HD = 64
THOUGHTS = 2
PREFIX = 384
QUESTION = 256
SCALE = 0.125
EPSILON = 1e-05
BLOCK = 256
HEAD_ROWS = 16
WINDOW = 32
LANES = 128
FACTOR_ROWS = 24
PAIR = 2 * HD
NEG = -1e30

F32 = jnp.float32
BF16 = jnp.bfloat16
VMEM_LIMIT = 56 * 1024 * 1024


def cost(microseconds):
    return pl.CostEstimate(
        flops=int(microseconds * 1.15e9),
        bytes_accessed=int(microseconds * 3.6e6),
        transcendentals=0,
    )


def dot(a, b):
    return lax.dot_general(a, b, (((1,), (0,)), ((), ())), preferred_element_type=F32)


def dot_nt(a, b):
    return lax.dot_general(a, b, (((1,), (1,)), ((), ())), preferred_element_type=F32)


def dot_tn(a, b):
    return lax.dot_general(a, b, (((0,), (0,)), ((), ())), preferred_element_type=F32)


def bits_of(size):
    return [1 << i for i in reversed(range(int(math.log2(size))))]


class Links:
    def __init__(self, sizes):
        self.sizes = sizes
        self.canon = [("dp", b) for b in bits_of(sizes["dp"])] + [
            ("fsdp", b) for b in bits_of(sizes["fsdp"])
        ]
        dp_bits = [("dp", b) for b in bits_of(sizes["dp"])]
        f_bits = [("fsdp", b) for b in bits_of(sizes["fsdp"])]
        self.groups = {"x": dp_bits[-1:], "y": dp_bits[:-1], "z": f_bits[:-1], "c": f_bits[-1:]}

    def order(self, text):
        out = []
        for letter in text:
            out += self.groups[letter]
        return out

    def swap(self, value, stage):
        axis, bit = stage
        return lax.ppermute(value, axis, [(i, i ^ bit) for i in range(self.sizes[axis])])

    def mine(self, stage):
        axis, bit = stage
        return (lax.axis_index(axis) & bit) != 0

    def gather(self, shard, text, axis=0):
        return Gather(self, shard, text, axis).finish()

    def chips(self, text):
        stages = list(reversed(self.order(text)))[1:]
        rest = [c for c in self.canon if c in stages]
        order = []
        for spot in range(1 << len(stages)):
            chip = 0
            for at, stage in enumerate(stages):
                if spot & (1 << (len(stages) - 1 - at)):
                    chip |= 1 << (len(rest) - 1 - rest.index(stage))
            order.append(chip)
        return order

    def spots(self, text):
        stages = [c for c in reversed(self.order(text)) if c not in self.groups["c"]]
        rest = [c for c in self.canon if c in stages]
        order = []
        for spot in range(1 << len(stages)):
            chip = 0
            for at, stage in enumerate(stages):
                if spot & (1 << (len(stages) - 1 - at)):
                    chip |= 1 << (len(rest) - 1 - rest.index(stage))
            order.append(chip)
        return order

    def scatter(self, value, text):
        return Scatter(self, value, text)


class Gather:
    def __init__(self, links, shard, text, axis=0):
        self.links = links
        self.shape = shard.shape
        self.axis = axis
        self.todo = links.order(text)
        self.done = []
        self.buf = shard
        self.got = None

    def go(self):
        self.add()
        self.stage = self.todo.pop(0)
        self.got = self.links.swap(self.buf, self.stage)
        return self.buf

    def add(self):
        if self.got is not None:
            canon = self.links.canon
            place = sum(1 for d in self.done if canon.index(d) < canon.index(self.stage))
            high = self.links.mine(self.stage)
            pair = [jnp.where(high, self.got, self.buf), jnp.where(high, self.buf, self.got)]
            self.buf = jnp.stack(pair, axis=self.axis + place)
            self.done.append(self.stage)
            self.got = None
        return self.buf

    def hold(self, *deps):
        self.buf = after(self.buf, *deps)

    def join(self, *deps):
        self.got = after(self.got, *deps)
        self.add()

    def last(self):
        for stage in self.todo:
            if self.got is not None:
                high = self.links.mine(self.stage)
                pair = [jnp.where(high, self.got, self.buf), jnp.where(high, self.buf, self.got)]
                self.buf = jnp.concatenate(pair, axis=0)
            self.stage = stage
            self.got = self.links.swap(self.buf, stage)
        return [self.buf, self.got]

    def finish(self):
        while self.todo:
            self.go()
        self.add()
        shape = self.shape
        return self.buf.reshape(shape[: self.axis] + (-1,) + shape[self.axis + 1 :])


class Scatter:
    def __init__(self, links, value, text):
        self.links = links
        self.left = list(links.canon)
        self.todo = list(reversed(links.order(text)))
        self.got = None
        self.split = False
        if isinstance(value, tuple):
            self.split = True
            self.left = self.todo[1:]
            shape = (2,) * len(self.left) + value[0].shape[1:]
            self.keep, self.buf = (v.reshape(shape) for v in value)
        else:
            self.buf = value.reshape((2,) * len(self.left) + value.shape[1:])

    def go(self):
        stage = self.todo.pop(0)
        if self.split:
            self.split = False
            sent = self.buf
        else:
            place = self.left.index(stage)
            self.left.remove(stage)
            high = self.links.mine(stage).astype(jnp.int32)
            parts = [self.buf] if self.got is None else [self.keep, self.got]

            def half(side):
                cut = [lax.dynamic_index_in_dim(p, side, place, keepdims=False) for p in parts]
                return cut[0] if len(cut) == 1 else cut[0].astype(F32) + cut[1].astype(F32)

            sent = half(1 - high).astype(BF16)
            self.keep = half(high)
        self.got = self.links.swap(sent, stage)
        return sent

    def hold(self, *deps):
        if self.got is None:
            self.buf = after(self.buf, *deps)
        else:
            self.got = after(self.got, *deps)

    def join(self, *deps):
        self.got = after(self.got, *deps)

    def finish(self):
        return self.keep.astype(F32) + self.got.astype(F32)


def join_after(swaps, *deps):
    for swap in swaps:
        swap.join(*deps)


def go_after(swaps, *deps):
    for swap in swaps:
        swap.hold(*deps)
    return tuple(swap.go() for swap in swaps)


def after(value, *deps):
    return lax.optimization_barrier((value, deps))[0]


def attend_kernel(info_ref, q_ref, k_ref, v_ref, o_ref, lse_ref):
    seq_len = q_ref.shape[0]
    slot = info_ref[0]
    keys = k_ref[...]
    values_t = v_ref[...].T
    lane = lax.broadcasted_iota(jnp.int32, (BLOCK, PAIR), 1)
    key_pos = lax.broadcasted_iota(jnp.int32, (BLOCK, BLOCK), 0)
    row_pos = lax.broadcasted_iota(jnp.int32, (BLOCK, BLOCK), 1)
    causal = key_pos <= row_pos
    middle_pos = QUESTION + lax.broadcasted_iota(jnp.int32, (PREFIX - QUESTION, BLOCK), 0)
    is_slot = (middle_pos >= slot) & (middle_pos < slot + THOUGHTS)

    def hide(scores):
        if scores.shape[0] <= QUESTION:
            return scores
        middle = jnp.where(is_slot, NEG, scores[QUESTION:PREFIX])
        return jnp.concatenate([scores[:QUESTION], middle, scores[PREFIX:]], axis=0)

    for begin in range(0, seq_len, BLOCK):
        end = begin + BLOCK
        queries = q_ref[begin:end, :] * jnp.asarray(SCALE, BF16)
        parts = []
        for head in range(2):
            own = jnp.where((lane >= HD) == bool(head), queries, jnp.zeros_like(queries))
            scores = dot_nt(keys[:end], own)
            last = jnp.where(causal, scores[begin:], NEG)
            if begin:
                last = jnp.concatenate([scores[:begin], last], axis=0)
            scores = hide(last)
            peak = jnp.max(scores, axis=0, keepdims=True)
            expo = jnp.exp(scores - peak)
            total = jnp.sum(expo, axis=0, keepdims=True)
            mixed = dot(values_t[head * HD : (head + 1) * HD, :end], expo.astype(BF16))
            parts.append(mixed / total)
            lse_ref[pl.ds(2 * pl.program_id(0) + head, 1), begin:end] = peak + jnp.log(total)
        o_ref[begin:end, :] = jnp.concatenate(parts, axis=0).T.astype(BF16)


def attend(info, qkv):
    _, seq_len, width = qkv.shape
    pairs = width // PAIR

    def columns(i):
        return pl.BlockSpec((None, seq_len, PAIR), lambda g, i=i: (i, 0, g))

    return pl.pallas_call(
        attend_kernel,
        grid=(pairs,),
        in_specs=[
            pl.BlockSpec(memory_space=pltpu.SMEM),
            *(columns(i) for i in range(3)),
        ],
        out_specs=[
            pl.BlockSpec((seq_len, PAIR), lambda g: (0, g)),
            pl.BlockSpec((HEAD_ROWS, seq_len), lambda g: (0, 0)),
        ],
        out_shape=[
            jax.ShapeDtypeStruct((seq_len, width), BF16),
            jax.ShapeDtypeStruct((HEAD_ROWS, seq_len), F32),
        ],
        compiler_params=pltpu.CompilerParams(vmem_limit_bytes=VMEM_LIMIT),
        cost_estimate=cost(2.0),
        name="attention_forward",
    )(info, qkv, qkv, qkv)


def attend_back_kernel(
    q_ref, k_ref, v_ref, o_ref, lse_ref, g_ref, out_ref, dk_acc, dv_acc
):
    seq_len = q_ref.shape[0]
    pair = pl.program_id(0)
    first_row = seq_len - g_ref.shape[0]
    keys = k_ref[...]
    values = v_ref[...]
    keys_t = keys.T
    lane = lax.broadcasted_iota(jnp.int32, (BLOCK, PAIR), 1)
    key_pos = lax.broadcasted_iota(jnp.int32, (BLOCK, BLOCK), 0)
    row_pos = lax.broadcasted_iota(jnp.int32, (BLOCK, BLOCK), 1)
    causal = key_pos <= row_pos
    dk_acc[...] = jnp.zeros_like(dk_acc)
    dv_acc[...] = jnp.zeros_like(dv_acc)
    for begin in range(first_row, seq_len, BLOCK):
        end = begin + BLOCK
        local = begin - first_row
        queries = q_ref[begin:end, :] * jnp.asarray(SCALE, BF16)
        grads = g_ref[local : local + BLOCK, :]
        product_t = (grads.astype(F32) * o_ref[begin:end, :].astype(F32)).T
        owns, own_grads, probs_low, score_grads, parts = [], [], [], [], []
        for head in range(2):
            chosen = (lane >= HD) == bool(head)
            own = jnp.where(chosen, queries, jnp.zeros_like(queries))
            own_grad = jnp.where(chosen, grads, jnp.zeros_like(grads))
            rows_here = slice(head * HD, (head + 1) * HD)
            delta = jnp.sum(product_t[rows_here], axis=0, keepdims=True)
            lse = lse_ref[pl.ds(2 * pair + head, 1), begin:end]
            scores = dot_nt(keys[:end], own)
            last = jnp.where(causal, scores[begin:], NEG)
            scores = jnp.concatenate([scores[:begin], last], axis=0) if begin else last
            probs = jnp.exp(scores - lse)
            prob_grad = dot_nt(values[:end], own_grad)
            score_grad = (probs * (prob_grad - delta)).astype(BF16)
            parts.append(dot(keys_t[rows_here, :end], score_grad))
            owns.append(own)
            own_grads.append(own_grad)
            probs_low.append(probs.astype(BF16))
            score_grads.append(score_grad)
        dv_acc[:end, :] += dot(
            jnp.concatenate(probs_low, axis=1), jnp.concatenate(own_grads, axis=0)
        )
        dk_acc[:end, :] += dot(jnp.concatenate(score_grads, axis=1), jnp.concatenate(owns, axis=0))
        mine = jnp.concatenate(parts, axis=0).T * SCALE
        out_ref[0, begin:end, :] = mine.astype(BF16)
    out_ref[0, :first_row, :] = jnp.zeros((first_row, PAIR), BF16)
    out_ref[1] = dk_acc[...].astype(BF16)
    out_ref[2] = dv_acc[...].astype(BF16)


def attend_back(qkv, mixed_low, lse, mixed_grad):
    _, seq_len, width = qkv.shape
    rows = mixed_grad.shape[0]

    def columns(i):
        return pl.BlockSpec((None, seq_len, PAIR), lambda g, i=i: (i, 0, g))

    late = pl.BlockSpec((rows, PAIR), lambda g: (0, g))
    return pl.pallas_call(
        attend_back_kernel,
        grid=(width // PAIR,),
        in_specs=[
            *(columns(i) for i in range(3)),
            pl.BlockSpec((seq_len, PAIR), lambda g: (0, g)),
            pl.BlockSpec((HEAD_ROWS, seq_len), lambda g: (0, 0)),
            late,
        ],
        out_specs=pl.BlockSpec((3, seq_len, PAIR), lambda g: (0, 0, g)),
        out_shape=jax.ShapeDtypeStruct((3, seq_len, width), BF16),
        scratch_shapes=[pltpu.VMEM((seq_len, PAIR), F32), pltpu.VMEM((seq_len, PAIR), F32)],
        compiler_params=pltpu.CompilerParams(vmem_limit_bytes=VMEM_LIMIT),
        cost_estimate=cost(2.17),
        name="attention_backward",
    )(qkv, qkv, qkv, mixed_low, lse, mixed_grad)


def row_norm(row, gain, bias):
    mean = jnp.mean(row, axis=-1, keepdims=True)
    centred = row - mean
    inverse = lax.rsqrt(jnp.mean(centred * centred, axis=-1, keepdims=True) + EPSILON)
    normed = centred * inverse
    return normed * gain + bias, normed, inverse


def row_norm_back(incoming, normed, inverse, gain):
    scaled = incoming * gain
    inner = (
        scaled
        - jnp.mean(scaled, axis=-1, keepdims=True)
        - normed * jnp.mean(scaled * normed, axis=-1, keepdims=True)
    )
    return inner * inverse


GELU_A = 0.7978845608028654
GELU_B = 0.044715


def gelu(pre):
    return 0.5 * pre * (1.0 + jnp.tanh(GELU_A * (pre + GELU_B * pre * pre * pre)))


def gelu_slope(pre):
    square = pre * pre
    curve = jnp.tanh(GELU_A * pre * (1.0 + GELU_B * square))
    return 0.5 * (1.0 + curve) + 0.5 * pre * (1.0 - curve * curve) * GELU_A * (
        1.0 + 3.0 * GELU_B * square
    )


def widen(row):
    return jnp.broadcast_to(row, (8, row.shape[1])).astype(BF16)


def pick(block, index):
    rows = lax.broadcasted_iota(jnp.int32, block.shape, 0)
    return jnp.sum(jnp.where(rows == index, block.astype(F32), 0.0), axis=0, keepdims=True)


def put(block, index, row):
    rows = lax.broadcasted_iota(jnp.int32, block.shape, 0)
    return jnp.where(rows == index, row.astype(block.dtype), block)


def by_head(row, heads):
    shape = (heads, row.shape[1])
    lane_head = lax.broadcasted_iota(jnp.int32, shape, 1) // HD
    return jnp.where(lane_head == lax.broadcasted_iota(jnp.int32, shape, 0), row, 0.0)


def heads_only(block):
    lane_head = lax.broadcasted_iota(jnp.int32, block.shape, 1) // HD
    own = lane_head == lax.broadcasted_iota(jnp.int32, block.shape, 0)
    return jnp.sum(jnp.where(own, block, 0.0), axis=0, keepdims=True)


def thoughts_kernel(
    info_ref,
    tok_ref,
    lse_in_ref,
    vec_ref,
    fcb_ref,
    qkvb_ref,
    near_in,
    far_in,
    qkv_in,
    mixed_in,
    hid_in,
    lse_ref,
    pre_ref,
    prob_ref,
    res_ref,
    qkv_out,
    mixed_out,
    hid_out,
    kv_ref,
    late_q_ref,
    mixed_ref,
    hid_ref,
    near_ref,
    far_ref,
    sems,
):
    width = tok_ref.shape[1]
    blocks = (far_ref.shape[0] - 1) // 2
    rows = late_q_ref.shape[0]
    ln1_gain, ln1_bias, out_bias, ln2_gain, ln2_bias, proj_bias = (
        vec_ref[i : i + 1, :] for i in range(6)
    )
    slot = info_ref[0]
    count = info_ref[1]

    loads = [
        (qkv_in.at[:, pl.ds(0, PREFIX)], kv_ref),
        (far_in.at[pl.ds(2 * blocks, 1)], far_ref.at[pl.ds(2 * blocks, 1)]),
        (far_in.at[pl.ds(0, blocks)], far_ref.at[pl.ds(0, blocks)]),
        (far_in.at[pl.ds(blocks, blocks)], far_ref.at[pl.ds(blocks, blocks)]),
        (near_in, near_ref),
        (qkv_in.at[0, pl.ds(QUESTION, rows)], late_q_ref),
        (mixed_in.at[pl.ds(QUESTION, rows)], mixed_ref),
    ]
    loads = [pltpu.make_async_copy(a, b, sems.at[i]) for i, (a, b) in enumerate(loads)]
    for copy in loads:
        copy.start()
    hid_ref[...] = tok_ref[...].astype(F32)
    hidden_row = pick(hid_ref[...], slot - 1 - QUESTION)
    loads[0].wait()
    slot_rows = []
    slot_lse = []
    for step in range(THOUGHTS + 1):
        at = slot - 1 + step
        qkv_row = pick(kv_ref[0, QUESTION:, :], at - QUESTION)
        query = by_head(qkv_row * SCALE, HEAD_ROWS).astype(BF16)
        scores = dot_nt(query, kv_ref[1])
        key_pos = lax.broadcasted_iota(jnp.int32, scores.shape, 1)
        scores = jnp.where(key_pos <= at, scores, NEG)
        peak = jnp.max(scores, axis=1, keepdims=True)
        expo = jnp.exp(scores - peak)
        total = jnp.sum(expo, axis=1, keepdims=True)
        probs = expo / total
        mixed = heads_only(dot(probs.astype(BF16), kv_ref[2]))
        if step:
            slot_rows.append(mixed)
            slot_lse.append(peak + jnp.log(total))
        if step == THOUGHTS:
            break
        prob_ref[step * HEAD_ROWS : (step + 1) * HEAD_ROWS, :] = probs
        if not step:
            loads[1].wait()
        resid = hidden_row + dot(widen(mixed), far_ref[2 * blocks])[0:1] + out_bias
        res_ref[step : step + 1, :] = resid
        second, _, _ = row_norm(resid, ln2_gain, ln2_bias)
        second = widen(second)
        if not step:
            loads[2].wait()
        acts = []
        for j in range(blocks):
            span = slice(j * width, (j + 1) * width)
            pre = dot(second, far_ref[j])[0:1] + fcb_ref[0:1, span]
            pre_ref[step : step + 1, span] = pre
            acts.append(widen(gelu(pre)))
        if not step:
            loads[3].wait()
        fed = resid + proj_bias
        for j in range(blocks):
            fed = fed + dot(acts[j], far_ref[blocks + j])[0:1]
        first, _, _ = row_norm(fed, ln1_gain, ln1_bias)
        first = widen(first)
        hidden_row = fed
        spot = jnp.where(step < count, slot + step - QUESTION, -1)
        hid_ref[...] = put(hid_ref[...], spot, fed)
        if not step:
            loads[4].wait()
        for i in range(3):
            span = slice(i * width, (i + 1) * width)
            new_row = dot(first, near_ref[i])[0:1] + qkvb_ref[0:1, span]
            kv_ref[i, QUESTION:, :] = put(kv_ref[i, QUESTION:, :], spot, new_row)
    loads[5].wait()
    loads[6].wait()
    stores = [
        pltpu.make_async_copy(
            kv_ref.at[:, pl.ds(QUESTION, PREFIX - QUESTION)],
            qkv_out.at[:, pl.ds(QUESTION, PREFIX - QUESTION)],
            sems.at[0],
        ),
        pltpu.make_async_copy(
            hid_ref, hid_out.at[pl.ds(QUESTION, PREFIX - QUESTION)], sems.at[1]
        ),
    ]
    for copy in stores:
        copy.start()

    row_pos = QUESTION + lax.broadcasted_iota(jnp.int32, (HEAD_ROWS, rows), 1)
    late_q = late_q_ref[...]
    lse = lse_in_ref[:, QUESTION:]
    scores = []
    values = []
    top = lse
    for j in range(THOUGHTS):
        local = slot + j - QUESTION
        key = by_head(pick(kv_ref[1, QUESTION:, :], local) * SCALE, HEAD_ROWS)
        values.append(pick(kv_ref[2, QUESTION:, :], local))
        score = jnp.where(row_pos >= slot + j, dot_nt(key.astype(BF16), late_q), NEG)
        scores.append(score)
        top = jnp.maximum(top, score)
    whole_sum = jnp.exp(lse - top)
    for score in scores:
        whole_sum = whole_sum + jnp.exp(score - top)
    new_lse = top + jnp.log(whole_sum)
    ones = by_head(jnp.ones((1, width), F32), HEAD_ROWS).astype(BF16)
    share = jnp.exp(lse - new_lse)
    high = share.astype(BF16)
    low = (share - high.astype(F32)).astype(BF16)
    weights = [jnp.exp(score - new_lse).astype(BF16) for score in scores]
    step_rows = PREFIX - QUESTION
    for begin in range(0, rows, step_rows):
        span = slice(begin, begin + step_rows)
        part = mixed_ref[span, :].astype(F32) * (
            dot_tn(high[:, span], ones) + dot_tn(low[:, span], ones)
        )
        for weight, value in zip(weights, values):
            part = part + dot_tn(weight[:, span], ones) * value
        if not begin:
            for j in range(THOUGHTS):
                part = put(part, slot + j - QUESTION, slot_rows[j])
        mixed_ref[span, :] = part.astype(BF16)
    stores.append(
        pltpu.make_async_copy(mixed_ref, mixed_out.at[pl.ds(QUESTION, rows)], sems.at[2])
    )
    stores[-1].start()
    lse_ref[:, :QUESTION] = lse_in_ref[:, :QUESTION]
    column = lax.broadcasted_iota(jnp.int32, (HEAD_ROWS, step_rows), 1)
    middle = new_lse[:, :step_rows]
    for j in range(THOUGHTS):
        middle = jnp.where(column == slot + j - QUESTION, slot_lse[j], middle)
    lse_ref[:, QUESTION:PREFIX] = middle
    lse_ref[:, PREFIX:] = new_lse[:, step_rows:]
    for copy in stores:
        copy.wait()


def whole(array):
    zeros = (0,) * array.ndim
    return pl.BlockSpec(array.shape, lambda i, zeros=zeros: zeros)


def fc_spec(far):
    return pl.BlockSpec((far.shape[0] // 2,) + far.shape[1:], lambda i: (0, 0, 0))


def proj_spec(far):
    return pl.BlockSpec((far.shape[0] // 2,) + far.shape[1:], lambda i: (1, 0, 0))


def out_spec(far):
    last = far.shape[0] - 1
    return pl.BlockSpec((1,) + far.shape[1:], lambda i: (last, 0, 0))


def thoughts_forward(info, tokens, tokens32, qkv, mixed_low, lse, weights, vec, fc_bias, qkv_bias):
    near, far = weights
    seq_len, width = tokens.shape
    rows = seq_len - QUESTION
    middle = PREFIX - QUESTION
    anywhere = pl.BlockSpec(memory_space=pl.ANY)
    out_shape = [
        jax.ShapeDtypeStruct(lse.shape, F32),
        jax.ShapeDtypeStruct((8, fc_bias.shape[1]), F32),
        jax.ShapeDtypeStruct((THOUGHTS * HEAD_ROWS, PREFIX), F32),
        jax.ShapeDtypeStruct((8, width), F32),
        jax.ShapeDtypeStruct(qkv.shape, BF16),
        jax.ShapeDtypeStruct(mixed_low.shape, BF16),
        jax.ShapeDtypeStruct(tokens32.shape, F32),
    ]
    return pl.pallas_call(
        thoughts_kernel,
        grid=(1,),
        in_specs=[
            pl.BlockSpec(memory_space=pltpu.SMEM),
            pl.BlockSpec((middle, width), lambda i: (QUESTION // middle, 0)),
            whole(lse),
            whole(vec),
            whole(fc_bias),
            whole(qkv_bias),
            *[anywhere] * 5,
        ],
        out_specs=[*(whole(x) for x in out_shape[:4]), *[anywhere] * 3],
        out_shape=out_shape,
        input_output_aliases={8: 4, 9: 5, 10: 6},
        scratch_shapes=[
            pltpu.VMEM((3, PREFIX, width), BF16),
            pltpu.VMEM((rows, width), BF16),
            pltpu.VMEM((rows, width), BF16),
            pltpu.VMEM((middle, width), F32),
            pltpu.VMEM(near.shape, BF16),
            pltpu.VMEM(far.shape, BF16),
            pltpu.SemaphoreType.DMA((7,)),
        ],
        compiler_params=pltpu.CompilerParams(vmem_limit_bytes=VMEM_LIMIT),
        cost_estimate=cost(2),
        name="thought_rows_forward",
    )(info, tokens, lse, vec, fc_bias, qkv_bias, near, far, qkv, mixed_low, tokens32)


def thoughts_back_kernel(
    info_ref,
    hid_ref,
    qkv_ref,
    lse_ref,
    pre_ref,
    prob_ref,
    res_ref,
    vec_ref,
    near_in,
    far_in,
    qkv_in,
    mixed_in,
    mg_in,
    rg_in,
    sum_ref,
    fac_ref,
    mg_out,
    rg_out,
    mg_ref,
    rg_win,
    late_q_ref,
    mixed_ref,
    near_ref,
    far_ref,
    sems,
):
    width = hid_ref.shape[1]
    blocks = (far_ref.shape[0] - 1) // 2
    units = blocks * width
    rows = mg_ref.shape[0]
    ln1_gain, ln1_bias, _, ln2_gain, ln2_bias, _ = (vec_ref[i : i + 1, :] for i in range(6))
    slot = info_ref[0]
    count = info_ref[1]
    base = pl.multiple_of(((slot - 1 - QUESTION) // 16) * 16, 16)

    def window(ref):
        return ref.at[pl.ds(base, WINDOW)]

    loads = [
        (mg_in, mg_ref),
        (mixed_in.at[pl.ds(QUESTION, rows)], mixed_ref),
        (qkv_in.at[0, pl.ds(QUESTION, rows)], late_q_ref),
        (window(rg_in), rg_win),
        (near_in, near_ref),
        (far_in.at[pl.ds(blocks, blocks)], far_ref.at[pl.ds(blocks, blocks)]),
        (far_in.at[pl.ds(0, blocks)], far_ref.at[pl.ds(0, blocks)]),
        (far_in.at[pl.ds(2 * blocks, 1)], far_ref.at[pl.ds(2 * blocks, 1)]),
    ]
    loads = [pltpu.make_async_copy(a, b, sems.at[i]) for i, (a, b) in enumerate(loads)]
    for copy in loads:
        copy.start()
    for copy in loads[:4]:
        copy.wait()

    late_q = late_q_ref[...]
    mixed_grad = mg_ref[...]
    product = mixed_grad.astype(F32) * mixed_ref[...].astype(F32)
    high = product.astype(BF16)
    ones = by_head(jnp.ones((1, width), F32), HEAD_ROWS).astype(BF16)
    delta = dot_nt(ones, high) + dot_nt(ones, (product - high.astype(F32)).astype(BF16))
    lse = lse_ref[:, QUESTION:]

    def columns(block, scale):
        rows_here = [
            by_head(pick(block, slot + j - QUESTION) * scale, HEAD_ROWS) for j in range(THOUGHTS)
        ]
        return jnp.concatenate(rows_here, axis=0).astype(BF16)

    def twice(block):
        return jnp.concatenate([block] * THOUGHTS, axis=0)

    slot_pos = jnp.concatenate(
        [jnp.full((HEAD_ROWS, rows), QUESTION - j, jnp.int32) for j in range(THOUGHTS)], axis=0
    )
    seen = slot_pos + lax.broadcasted_iota(jnp.int32, slot_pos.shape, 1) >= slot
    scores = dot_nt(columns(qkv_ref[1, QUESTION:PREFIX, :], SCALE), late_q)
    probs = jnp.where(seen, jnp.exp(jnp.minimum(scores - twice(lse), 0.0)), 0.0)
    prob_grad = dot_nt(columns(qkv_ref[2, QUESTION:PREFIX, :], 1.0), mixed_grad)
    score_grad = (probs * (prob_grad - twice(delta))).astype(BF16)
    slot_keys = dot(score_grad, late_q)
    slot_values = dot(probs.astype(BF16), mixed_grad)
    slot_grads = []
    for j in range(THOUGHTS):
        span = slice(j * HEAD_ROWS, (j + 1) * HEAD_ROWS)
        slot_grads.append((heads_only(slot_keys[span]) * SCALE, heads_only(slot_values[span])))

    def through_first(at, query_grad, key_grad, value_grad):
        first_grad = (
            dot_nt(widen(query_grad), near_ref[0])
            + dot_nt(widen(key_grad), near_ref[1])
            + dot_nt(widen(value_grad), near_ref[2])
        )[0:1]
        _, normed, inverse = row_norm(hid_ref[pl.ds(at - QUESTION, 1), :], ln1_gain, ln1_bias)
        return row_norm_back(first_grad, normed, inverse, ln1_gain)

    sum_ref[...] = jnp.zeros_like(sum_ref)
    fac = {}
    loads[4].wait()
    carried = through_first(slot + 1, jnp.zeros((1, width), F32), *slot_grads[1])
    for copy in loads[5:]:
        copy.wait()
    for step in reversed(range(THOUGHTS)):
        at = slot - 1 + step
        upstream = jnp.where(step < count, carried, 0.0)
        low = widen(upstream)
        act_grad = jnp.concatenate([dot_nt(low, far_ref[blocks + j])[0:1] for j in range(blocks)], axis=1)
        pre = pre_ref[step : step + 1, :]
        pre_grad = (act_grad * gelu_slope(pre)).astype(BF16).astype(F32)
        second_grad = jnp.zeros((1, width), F32)
        for j in range(blocks):
            piece = pre_grad[:, j * width : (j + 1) * width]
            second_grad = second_grad + dot_nt(widen(piece), far_ref[j])[0:1]
        second, normed, inverse = row_norm(res_ref[step : step + 1, :], ln2_gain, ln2_bias)
        resid_grad = upstream + row_norm_back(second_grad, normed, inverse, ln2_gain)
        mixed_row = dot_nt(widen(resid_grad), far_ref[2 * blocks])[0:1]
        local = at - QUESTION
        rg_win[...] = put(rg_win[...], local - base, resid_grad)
        mg_ref[: PREFIX - QUESTION, :] = put(mg_ref[: PREFIX - QUESTION, :], local, mixed_row)
        up_low = upstream.astype(BF16).astype(F32)
        sum_ref[0:1, :units] += pre_grad
        sum_ref[1:2, :width] += second_grad * normed
        sum_ref[2:3, :width] += second_grad
        sum_ref[3:4, :width] += up_low
        sum_ref[4:5, :width] += resid_grad.astype(BF16).astype(F32)
        act = gelu(pre)
        rows_here = [act[:, j * width : (j + 1) * width] for j in range(blocks)]
        rows_here += [up_low, second]
        rows_here += [pre_grad[:, j * width : (j + 1) * width] for j in range(blocks)]
        for j, row in enumerate(rows_here):
            fac[THOUGHTS * j + step] = row
        if step:
            own_grad = by_head(mixed_row, HEAD_ROWS).astype(BF16)
            query = by_head(pick(qkv_ref[0, QUESTION:PREFIX, :], local) * SCALE, HEAD_ROWS)
            query = query.astype(BF16)
            probs = prob_ref[step * HEAD_ROWS : (step + 1) * HEAD_ROWS, :]
            prob_grad = dot_nt(own_grad, qkv_ref[2])
            own_delta = jnp.sum(prob_grad * probs, axis=1, keepdims=True)
            score_grad = (probs * (prob_grad - own_delta)).astype(BF16)
            query_grad = heads_only(dot(score_grad, qkv_ref[1])) * SCALE
            key_grad, value_grad = slot_grads[0]
            own = lax.broadcasted_iota(jnp.int32, probs.shape, 1) == at
            score_own = jnp.sum(jnp.where(own, score_grad.astype(F32), 0.0), axis=1, keepdims=True)
            prob_own = jnp.sum(jnp.where(own, probs, 0.0), axis=1, keepdims=True)
            key_grad += jnp.sum(score_own * query.astype(F32), axis=0, keepdims=True)
            value_grad += jnp.sum(prob_own * own_grad.astype(F32), axis=0, keepdims=True)
            carried = resid_grad + through_first(at, query_grad, key_grad, value_grad)
    padding = [jnp.zeros((1, width), F32)] * (fac_ref.shape[0] - len(fac))
    fac_ref[...] = jnp.concatenate([fac[i] for i in range(len(fac))] + padding, axis=0).astype(BF16)
    stores = [
        pltpu.make_async_copy(mg_ref, mg_out, sems.at[0]),
        pltpu.make_async_copy(rg_win, window(rg_out), sems.at[1]),
    ]
    for copy in stores:
        copy.start()
    for copy in stores:
        copy.wait()


SUM_ROWS = ("fc_bias", "ln2_gain", "ln2_bias", "proj_bias", "out_bias")


def thoughts_back(info, hidden, qkv, mixed_low, lse, saved, weights, vec, mixed_grad, resid_grad):
    near, far = weights
    width = hidden.shape[1]
    units = far.shape[0] // 2 * width
    middle = PREFIX - QUESTION
    anywhere = pl.BlockSpec(memory_space=pl.ANY)
    out_shape = [
        jax.ShapeDtypeStruct((8, units), F32),
        jax.ShapeDtypeStruct((FACTOR_ROWS, width), BF16),
        jax.ShapeDtypeStruct(mixed_grad.shape, BF16),
        jax.ShapeDtypeStruct(resid_grad.shape, F32),
    ]
    return pl.pallas_call(
        thoughts_back_kernel,
        grid=(1,),
        in_specs=[
            pl.BlockSpec(memory_space=pltpu.SMEM),
            pl.BlockSpec((middle, width), lambda i: (QUESTION // middle, 0)),
            pl.BlockSpec((3, PREFIX, width), lambda i: (0, 0, 0)),
            whole(lse),
            *(whole(x) for x in saved),
            whole(vec),
            *[anywhere] * 6,
        ],
        out_specs=[whole(out_shape[0]), whole(out_shape[1]), anywhere, anywhere],
        out_shape=out_shape,
        input_output_aliases={12: 2, 13: 3},
        scratch_shapes=[
            pltpu.VMEM(mixed_grad.shape, BF16),
            pltpu.VMEM((WINDOW, width), F32),
            pltpu.VMEM(mixed_grad.shape, BF16),
            pltpu.VMEM(mixed_grad.shape, BF16),
            pltpu.VMEM(near.shape, BF16),
            pltpu.VMEM(far.shape, BF16),
            pltpu.SemaphoreType.DMA((8,)),
        ],
        compiler_params=pltpu.CompilerParams(vmem_limit_bytes=VMEM_LIMIT),
        cost_estimate=cost(2.0),
        name="thought_rows_backward",
    )(
        info,
        hidden,
        qkv,
        lse,
        *saved,
        vec,
        near,
        far,
        qkv,
        mixed_low,
        mixed_grad,
        resid_grad,
    )


def feed_kernel(
    hid_ref, mixed_ref, up_ref, wout_ref, wfc_ref, wproj_ref, vec_ref, fcb_ref, out_ref, first_ref,
    second_ref, act_ref, pg_ref, rg_ref, mg_ref, sum_ref, slope_ref,
):
    width = hid_ref.shape[1]
    blocks = wfc_ref.shape[0]
    step = pl.program_id(0)
    skip = QUESTION // BLOCK
    out_bias, ln2_gain, ln2_bias, proj_bias = (vec_ref[i : i + 1, :] for i in range(2, 6))

    @pl.when(step == 0)
    def _():
        sum_ref[...] = jnp.zeros_like(sum_ref)

    hidden = hid_ref[...]
    _, first_normed, _ = row_norm(hidden, vec_ref[0:1, :], vec_ref[1:2, :])
    first_ref[...] = first_normed.astype(BF16)
    resid = hidden + dot(mixed_ref[...], wout_ref[0]) + out_bias
    second, normed, inverse = row_norm(resid, ln2_gain, ln2_bias)
    low = second.astype(BF16)
    second_ref[...] = low
    total = resid + proj_bias
    for j in range(blocks):
        span = slice(j * width, (j + 1) * width)
        pre = dot(low, wfc_ref[j]) + fcb_ref[:, span]
        square = pre * pre
        curve = jnp.tanh(GELU_A * pre * (1.0 + GELU_B * square))
        half = 0.5 + 0.5 * curve
        act = (pre * half).astype(BF16)
        rise = 0.5 * GELU_A + (1.5 * GELU_A * GELU_B) * square
        slope_ref[:, span] = (half + pre * rise * (1.0 - curve * curve)).astype(BF16)
        act_ref[:, span] = act
        total = total + dot(act, wproj_ref[j])
    out_ref[...] = total.astype(BF16)

    @pl.when(step >= skip)
    def _():
        up = up_ref[...]
        second_grad = jnp.zeros(up.shape, F32)
        for j in range(blocks):
            span = slice(j * width, (j + 1) * width)
            slope = slope_ref[:, span].astype(F32)
            pre_grad = (dot_nt(up, wproj_ref[j]) * slope).astype(BF16)
            pg_ref[:, span] = pre_grad
            sum_ref[0:1, span] += jnp.sum(pre_grad.astype(F32), axis=0, keepdims=True)
            second_grad = second_grad + dot_nt(pre_grad, wfc_ref[j])
        up32 = up.astype(F32)
        resid_grad = up32 + row_norm_back(second_grad, normed, inverse, ln2_gain)
        attn_grad = resid_grad.astype(BF16)
        rg_ref[...] = resid_grad
        mg_ref[...] = dot_nt(attn_grad, wout_ref[0]).astype(BF16)
        sum_ref[1:2, :width] += jnp.sum(second_grad * normed, axis=0, keepdims=True)
        sum_ref[2:3, :width] += jnp.sum(second_grad, axis=0, keepdims=True)
        sum_ref[3:4, :width] += jnp.sum(up32, axis=0, keepdims=True)
        sum_ref[4:5, :width] += jnp.sum(attn_grad.astype(F32), axis=0, keepdims=True)


def feed(hidden, mixed_low, upstream_low, weights, vec, fc_bias):
    far = weights[1]
    seq_len, width = hidden.shape
    late = seq_len - QUESTION
    units = fc_bias.shape[1]
    skip = QUESTION // BLOCK

    def rows(columns):
        return pl.BlockSpec((BLOCK, columns), lambda i: (i, 0))

    def late_rows(columns):
        return pl.BlockSpec((BLOCK, columns), lambda i: (jnp.maximum(i - skip, 0), 0))

    sums = jax.ShapeDtypeStruct((8, units), F32)
    return pl.pallas_call(
        feed_kernel,
        grid=(seq_len // BLOCK,),
        in_specs=[
            rows(width),
            rows(width),
            late_rows(width),
            out_spec(far),
            fc_spec(far),
            proj_spec(far),
            whole(vec),
            whole(fc_bias),
        ],
        out_specs=[
            rows(width),
            rows(width),
            late_rows(width),
            late_rows(units),
            late_rows(units),
            late_rows(width),
            late_rows(width),
            whole(sums),
        ],
        out_shape=[
            jax.ShapeDtypeStruct((seq_len, width), BF16),
            jax.ShapeDtypeStruct((seq_len, width), BF16),
            jax.ShapeDtypeStruct((late, width), BF16),
            jax.ShapeDtypeStruct((late, units), BF16),
            jax.ShapeDtypeStruct((late, units), BF16),
            jax.ShapeDtypeStruct((late, width), F32),
            jax.ShapeDtypeStruct((late, width), BF16),
            sums,
        ],
        scratch_shapes=[pltpu.VMEM((BLOCK, units), BF16)],
        compiler_params=pltpu.CompilerParams(vmem_limit_bytes=VMEM_LIMIT),
        cost_estimate=cost(3),
        name="feed_forward_and_back",
    )(hidden, mixed_low, upstream_low, far, far, far, vec, fc_bias)


def first_back_kernel(info_ref, hid_ref, grad_ref, rg_ref, near_ref, vec_ref, in_ref):
    rows, width = hid_ref.shape
    step = pl.program_id(0)
    slot = info_ref[0]
    count = info_ref[1]
    gain = vec_ref[0:1, :]
    _, normed, inverse = row_norm(hid_ref[...], gain, vec_ref[1:2, :])
    first_grad = jnp.zeros((rows, width), F32)
    for i in range(3):
        first_grad = first_grad + dot_nt(grad_ref[i], near_ref[i])
    late = (step >= QUESTION // BLOCK).astype(F32)
    grad = row_norm_back(first_grad, normed, inverse, gain) + late * rg_ref[...]
    position = step * rows + lax.broadcasted_iota(jnp.int32, (rows, 1), 0)
    replaced = (position >= slot) & (position < slot + jnp.minimum(count, THOUGHTS))
    in_ref[...] = jnp.where(replaced, 0.0, grad)


def first_back(info, hidden, qkv_grad, resid_grad, weights, vec):
    seq_len, width = hidden.shape
    skip = QUESTION // BLOCK
    rows = pl.BlockSpec((BLOCK, width), lambda i: (i, 0))
    return pl.pallas_call(
        first_back_kernel,
        grid=(seq_len // BLOCK,),
        in_specs=[
            pl.BlockSpec(memory_space=pltpu.SMEM),
            rows,
            pl.BlockSpec((3, BLOCK, width), lambda i: (0, i, 0)),
            pl.BlockSpec((BLOCK, width), lambda i: (jnp.maximum(i - skip, 0), 0)),
            whole(weights[0]),
            whole(vec),
        ],
        out_specs=rows,
        out_shape=jax.ShapeDtypeStruct((seq_len, width), F32),
        compiler_params=pltpu.CompilerParams(vmem_limit_bytes=VMEM_LIMIT),
        cost_estimate=cost(0.83),
        name="first_norm_backward",
    )(info, hidden, qkv_grad, resid_grad, weights[0], vec)


def in_pieces(value, count=3):
    pieces = []
    for _ in range(count):
        pieces.append(value.astype(BF16))
        value = value - pieces[-1].astype(F32)
    return pieces


def keep_and_send(value, core, chips, keep_ref, send_ref, at):
    own = value.shape[0] // (2 * len(chips))
    for spot, chip in enumerate(chips):
        even = value[2 * chip * own : (2 * chip + 1) * own]
        odd = value[(2 * chip + 1) * own : (2 * chip + 2) * own]
        keep_ref[spot, at] = jnp.where(core == 0, even, odd).astype(BF16)
        send_ref[spot, at] = jnp.where(core == 0, odd, even).astype(BF16)


def near_terms_kernel(
    sizes, chips_a, chips_b, core_ref, normed_ref, grad_ref, mixed_ref, rg_ref, near_ref, vec_ref,
    feed_sum_ref, row_sum_ref, place_a, owner_a, place_b, owner_b, keep_a, send_a, keep_b, send_b,
    packed_ref, normed_t, gain_ref, bias_ref, column_ref,
):
    core = core_ref[0]
    step = pl.program_id(0)
    width = normed_ref.shape[1]

    @pl.when(step == 0)
    def _():
        normed_t[...] = normed_ref[...].T
        gain_ref[...] = jnp.zeros_like(gain_ref)
        bias_ref[...] = jnp.zeros_like(bias_ref)

    def term():
        columns = vec_ref[...].T
        inner = dot(normed_t[...], grad_ref[...])
        sums = jnp.sum(grad_ref[...].astype(F32), axis=0, keepdims=True)
        gain_ref[...] += inner * near_ref[...].astype(F32)
        pieces = in_pieces(jnp.broadcast_to(sums, (8, width)), 2)
        bias_ref[...] += dot_nt(jnp.concatenate(pieces, axis=0), near_ref[...])
        column_ref[pl.ds(step, 1), :] = sums
        return inner * columns[:, 0:1] + columns[:, 1:2] * sums

    @pl.when(step < 2)
    def _():
        keep_and_send(term(), core, chips_a, keep_a, send_a, 0)

    @pl.when(step == 2)
    def _():
        keep_and_send(term(), core, chips_b, keep_b, send_b, 0)

    @pl.when(step == 3)
    def _():
        value = dot_tn(mixed_ref[QUESTION:, :], rg_ref[...].astype(BF16))
        keep_and_send(value, core, chips_b, keep_b, send_b, 0)
        ones = jnp.ones((16, width), BF16)
        totals = feed_sum_ref[...] + row_sum_ref[...]
        small = {name: totals[i : i + 1, :width] for i, name in enumerate(SUM_ROWS)}
        small["fc_bias"] = totals[0:1]
        small["ln1_gain"] = sum(dot_nt(ones, p) for p in in_pieces(gain_ref[...], 2))[0:1]
        small["ln1_bias"] = bias_ref[0:1, :] + bias_ref[8:9, :]
        small["qv_bias"] = jnp.concatenate([column_ref[0:1, :], column_ref[2:3, :]], axis=1)
        pack(small, sizes, 2 * len(chips_a), (place_a, owner_a, place_b, owner_b), packed_ref)


def near_terms(
    core, normed_low, qkv_grad, mixed_low, resid_grad, near, vec, feed_sums, row_sums, sizes, chips_a, chips_b
):
    seq_len, width = normed_low.shape
    half = jax.ShapeDtypeStruct((len(chips_a), 2, width // (2 * len(chips_a)), width), BF16)
    piece = (len(chips_a), 1) + half.shape[2:]
    left = pl.BlockSpec(piece, lambda i: (0, jnp.minimum(i, 1), 0, 0))
    right = pl.BlockSpec(piece, lambda i: (0, jnp.maximum(i - 2, 0), 0, 0))
    devices = 2 * len(chips_a)
    maps = lane_maps(width // devices, devices)
    packed = jax.ShapeDtypeStruct((len(sizes), devices, LANES), BF16)
    out_shape = [half] * 4 + [packed]
    return pl.pallas_call(
        functools.partial(near_terms_kernel, sizes, chips_a, chips_b),
        grid=(4,),
        in_specs=[
            pl.BlockSpec(memory_space=pltpu.SMEM),
            whole(normed_low),
            pl.BlockSpec((None, seq_len, width), lambda i: (jnp.minimum(i, 2), 0, 0)),
            whole(mixed_low),
            whole(resid_grad),
            pl.BlockSpec((None, width, width), lambda i: (jnp.minimum(i, 2), 0, 0)),
            whole(vec),
            whole(feed_sums),
            whole(row_sums),
            *(whole(x) for x in maps),
        ],
        out_specs=[left, left, right, right, whole(packed)],
        out_shape=out_shape,
        scratch_shapes=[
            pltpu.VMEM((width, seq_len), BF16),
            pltpu.VMEM((width, width), F32),
            pltpu.VMEM((16, width), F32),
            pltpu.VMEM((8, width), F32),
        ],
        compiler_params=pltpu.CompilerParams(vmem_limit_bytes=VMEM_LIMIT),
        cost_estimate=cost(0.5),
        name="near_weight_terms",
    )(core, normed_low, qkv_grad, mixed_low, resid_grad, near, vec, feed_sums, row_sums, *maps)


def fc_terms_kernel(chips, core_ref, second_ref, pg_ref, keep_ref, send_ref, second_t):
    @pl.when(pl.program_id(0) == 0)
    def _():
        second_t[...] = second_ref[...].T

    value = dot(second_t[...], pg_ref[...])
    keep_and_send(value, core_ref[0], chips, keep_ref, send_ref, 0)


def fc_terms(core, second_low, pre_grad, chips):
    width = second_low.shape[1]
    rows, units = pre_grad.shape
    blocks = units // width
    own = width // (2 * len(chips))
    half = jax.ShapeDtypeStruct((len(chips), blocks, own, width), BF16)
    out = pl.BlockSpec((len(chips), 1, own, width), lambda j: (0, j, 0, 0))
    return pl.pallas_call(
        functools.partial(fc_terms_kernel, chips),
        grid=(blocks,),
        in_specs=[
            pl.BlockSpec(memory_space=pltpu.SMEM),
            pl.BlockSpec((rows, width), lambda j: (0, 0)),
            pl.BlockSpec((rows, width), lambda j: (0, j)),
        ],
        out_specs=[out, out],
        out_shape=[half, half],
        scratch_shapes=[pltpu.VMEM((width, rows), BF16)],
        compiler_params=pltpu.CompilerParams(vmem_limit_bytes=VMEM_LIMIT),
        cost_estimate=cost(0.5),
        name="fc_weight_terms",
    )(core, second_low, pre_grad)


def proj_terms_kernel(outer, inner, act_ref, up_ref, out_ref):
    value = dot_tn(act_ref[...], up_ref[...])
    rows, width = value.shape
    value = value.reshape(outer, inner, rows // (outer * inner), width)
    for i in range(inner):
        out_ref[i, :, 0] = value[:, i].astype(BF16)


def proj_terms(act_low, upstream_low, outer, inner):
    units = act_low.shape[1]
    rows, width = upstream_low.shape
    blocks = units // width
    shape = (inner, outer, blocks, width // (outer * inner), width)
    return pl.pallas_call(
        functools.partial(proj_terms_kernel, outer, inner),
        grid=(blocks,),
        in_specs=[
            pl.BlockSpec((rows, width), lambda j: (0, j)),
            pl.BlockSpec((rows, width), lambda j: (0, 0)),
        ],
        out_specs=pl.BlockSpec((inner, outer, 1) + shape[3:], lambda j: (0, 0, j, 0, 0)),
        out_shape=jax.ShapeDtypeStruct(shape, BF16),
        compiler_params=pltpu.CompilerParams(vmem_limit_bytes=VMEM_LIMIT),
        cost_estimate=cost(0.5),
        name="proj_weight_terms",
    )(act_low, upstream_low)


def first_kernel(
    orders, core_ref, tok_ref, left_mine, left_got, right_mine, right_got, vec_ref, qkvb_ref, qkv_ref,
    near_ref, rows_ref,
):
    width = tok_ref.shape[1]

    @pl.when(pl.program_id(0) == 0)
    def _():
        even_is_mine = core_ref[0] == 0
        own, half = left_mine.shape[2:]
        for i in range(3):
            for side, (mine, got) in enumerate([(left_mine, left_got), (right_mine, right_got)]):
                for spot, chip in enumerate(orders[side]):
                    a = mine[spot, i].astype(F32)
                    b = got[spot, i].astype(F32)
                    begin = 2 * chip * own
                    rows_ref[begin : begin + own, :] = jnp.where(even_is_mine, a, b)
                    rows_ref[begin + own : begin + 2 * own, :] = jnp.where(even_is_mine, b, a)
                near_ref[i, :, side * half : (side + 1) * half] = rows_ref[...].astype(BF16)

    first, _, _ = row_norm(tok_ref[...].astype(F32), vec_ref[0:1, :], vec_ref[1:2, :])
    first = first.astype(BF16)
    for i in range(3):
        span = slice(i * width, (i + 1) * width)
        qkv_ref[i] = (dot(first, near_ref[i]) + qkvb_ref[:, span]).astype(BF16)


def first_forward(core, tokens, pieces, orders, vec, qkv_bias):
    seq_len, width = tokens.shape
    near = jax.ShapeDtypeStruct((3, width, width), BF16)
    return pl.pallas_call(
        functools.partial(first_kernel, orders),
        grid=(seq_len // BLOCK,),
        in_specs=[
            pl.BlockSpec(memory_space=pltpu.SMEM),
            pl.BlockSpec((BLOCK, width), lambda i: (i, 0)),
            *(whole(piece) for piece in pieces),
            whole(vec),
            whole(qkv_bias),
        ],
        out_specs=[pl.BlockSpec((3, BLOCK, width), lambda i: (0, i, 0)), whole(near)],
        out_shape=[jax.ShapeDtypeStruct((3, seq_len, width), BF16), near],
        scratch_shapes=[pltpu.VMEM((width, width // 2), F32)],
        compiler_params=pltpu.CompilerParams(vmem_limit_bytes=VMEM_LIMIT),
        cost_estimate=cost(0.67),
        name="first_norm_forward",
    )(core, tokens, *pieces, vec, qkv_bias)


def group_of(blocks, own):
    each = blocks * own
    group = LANES // math.gcd(LANES, each)
    device, block, i = np.indices((group, blocks, own)).reshape(3, -1)
    swap = np.zeros((group * each, group * each), np.float32)
    swap[np.arange(group * each), block * (group * own) + device * own + i] = 1.0
    return group, jnp.asarray(swap, BF16)


def far_shard_kernel(blocks, span, fc_ref, proj_ref, out_w_ref, swap_ref, out_ref):
    own, width = out_w_ref.shape
    size = swap_ref.shape[0]
    groups = width // span
    rows = [fc_ref[:, g * size : (g + 1) * size].astype(F32) for g in range(groups)]
    swapped = dot(jnp.concatenate(rows, axis=0).astype(BF16), swap_ref[...])
    for g in range(groups):
        part = swapped[g * own : (g + 1) * own]
        for j in range(blocks):
            piece = part[:, j * span : (j + 1) * span]
            out_ref[j, :, g * span : (g + 1) * span] = piece.astype(BF16)
    for j in range(blocks):
        out_ref[blocks + j] = proj_ref[j]
    out_ref[2 * blocks] = out_w_ref[...]


def join_far(fc_shard, proj_shard, out_shard):
    own, width = out_shard.shape
    blocks = fc_shard.shape[1] // width
    group, swap = group_of(blocks, own)
    return pl.pallas_call(
        functools.partial(far_shard_kernel, blocks, group * own),
        out_shape=jax.ShapeDtypeStruct((2 * blocks + 1, own, width), BF16),
        compiler_params=pltpu.CompilerParams(vmem_limit_bytes=VMEM_LIMIT),
        name="far_shard",
    )(fc_shard, proj_shard.reshape(blocks, own, width), out_shard, swap)


def row_terms_kernel(span, index_ref, fac_ref, proj_ref, fc_ref, swap_ref, proj_out, fc_out):
    blocks, own, width = proj_ref.shape
    shape = (width, own)
    mine = lax.broadcasted_iota(jnp.int32, shape, 0) - index_ref[0] * own
    select = (mine == lax.broadcasted_iota(jnp.int32, shape, 1)).astype(BF16)

    def factor(j):
        return jnp.concatenate([fac_ref[THOUGHTS * j + i] for i in range(THOUGHTS)], axis=0)

    upstream = factor(blocks)
    terms = []
    second = dot(factor(blocks + 1), select).astype(BF16)
    for j in range(blocks):
        act = dot(factor(j), select).astype(BF16)
        proj_out[j] = proj_ref[j].astype(F32) + dot_tn(act, upstream)
        terms.append(fc_ref[j] + dot_tn(second, factor(blocks + 2 + j)))
    size = swap_ref.shape[0]
    groups = width // span
    rows = [
        jnp.concatenate([t[:, g * span : (g + 1) * span] for t in terms], axis=1)
        for g in range(groups)
    ]
    left = jnp.concatenate(rows, axis=0)
    total = sum(dot_nt(piece, swap_ref[...]) for piece in in_pieces(left))
    for g in range(groups):
        fc_out[:, g * size : (g + 1) * size] = total[g * own : (g + 1) * own]


def row_terms(index, factors, proj_sum, fc_sum):
    blocks, own, width = fc_sum.shape
    out_shape = [
        jax.ShapeDtypeStruct(proj_sum.shape, F32),
        jax.ShapeDtypeStruct((own, blocks * width), F32),
    ]
    group, swap = group_of(blocks, own)
    return pl.pallas_call(
        functools.partial(row_terms_kernel, group * own),
        grid=(1,),
        in_specs=[
            pl.BlockSpec(memory_space=pltpu.SMEM),
            whole(factors),
            whole(proj_sum),
            whole(fc_sum),
            whole(swap),
        ],
        out_specs=[whole(x) for x in out_shape],
        out_shape=out_shape,
        compiler_params=pltpu.CompilerParams(vmem_limit_bytes=VMEM_LIMIT),
        cost_estimate=cost(0.33),
        name="thought_rows_terms",
    )(index, factors, proj_sum, fc_sum, swap)


def lane_maps(own, devices):
    maps = []
    for size in (own, 2 * own):
        column = np.arange(size * devices)
        maps.append(jnp.asarray(column[None, :] % size == np.arange(size)[:, None], BF16))
        maps.append(jnp.asarray(column[None, :] // size == np.arange(devices)[:, None], F32))
    return maps


def lane_pieces(sizes, own):
    pieces = []
    for at, (name, size) in enumerate(sizes):
        wide = size == 2 * own
        step = 2 * own if wide else own
        pieces += [(at, name, begin, 2 * int(wide), step) for begin in range(0, size, step)]
    return pieces


VECTOR_ROWS = ("ln1_gain", "ln1_bias", "out_bias", "ln2_gain", "ln2_bias", "proj_bias")


def unpack_kernel(
    sizes, own, packed_ref, place_a, owner_a, place_b, owner_b, vec_ref, fcb_ref, qkvb_ref
):
    maps = (place_a, owner_a, place_b, owner_b)
    vec_ref[...] = jnp.zeros_like(vec_ref)
    width = vec_ref.shape[1]
    for at, name, begin, which, size in lane_pieces(sizes, own):
        spread = dot(packed_ref[at][:, begin : begin + size], maps[which][...])
        full = jnp.sum(spread * maps[which + 1][...], axis=0, keepdims=True)
        if name == "fc_bias":
            fcb_ref[:, begin // own * width : (begin // own + 1) * width] = full
        elif name == "qv_bias":
            qkvb_ref[:, :width] = full[:, :width]
            qkvb_ref[:, width : 2 * width] = jnp.zeros((1, width), F32)
            qkvb_ref[:, 2 * width :] = full[:, width:]
        else:
            row = VECTOR_ROWS.index(name)
            vec_ref[row : row + 1, :] = full


def unpack(packed, sizes):
    devices = packed.shape[1]
    size = dict(sizes)
    own = size["ln1_gain"]
    width = own * devices
    return pl.pallas_call(
        functools.partial(unpack_kernel, sizes, own),
        out_shape=[
            jax.ShapeDtypeStruct((8, width), F32),
            jax.ShapeDtypeStruct((1, size["fc_bias"] * devices), F32),
            jax.ShapeDtypeStruct((1, 3 * width), F32),
        ],
        compiler_params=pltpu.CompilerParams(vmem_limit_bytes=VMEM_LIMIT),
        name="vectors_unpack",
    )(packed, *lane_maps(own, devices))


def pack(rows, sizes, devices, maps, out_ref):
    out_ref[...] = jnp.zeros_like(out_ref)
    width = rows["ln1_gain"].shape[1]
    own = width // devices
    pieces = lane_pieces(sizes, own)
    for which in sorted({piece[3] for piece in pieces}):
        group = [piece for piece in pieces if piece[3] == which]
        stack = []
        for _, name, begin, _, size in group:
            span = size * devices
            first = begin // size * span
            stack.append((rows[name][:, first : first + span] * maps[which + 1][...]).astype(BF16))
        done = dot_nt(jnp.concatenate(stack, axis=0), maps[which][...]).astype(BF16)
        for i, (at, _, begin, _, size) in enumerate(group):
            out_ref[at, :, begin : begin + size] = done[i * devices : (i + 1) * devices]


def join_kernel(*refs):
    out_ref = refs[-1]
    out_ref[...] = jnp.zeros_like(out_ref)
    for at, ref in enumerate(refs[:-1]):
        out_ref[at : at + 1, : ref.shape[0]] = ref[...].astype(F32).reshape(1, ref.shape[0])


def join(vectors):
    return pl.pallas_call(
        join_kernel,
        out_shape=jax.ShapeDtypeStruct((len(vectors), LANES), F32),
        name="vectors_join",
    )(*vectors)


def part_kernel(joined_ref, *refs):
    for at, ref in enumerate(refs):
        ref[...] = joined_ref[at, : ref.shape[0]]


def part(joined, sizes):
    return pl.pallas_call(
        part_kernel,
        out_shape=[jax.ShapeDtypeStruct((size,), F32) for _, size in sizes],
        name="vectors_part",
    )(joined)


def step_on_sequence(
    near_pieces, far, vectors, tokens, cotangent, slots, count, answer_start, devices, sizes, comm
):
    vec, fc_bias, qkv_bias = vectors
    seq_len, width = tokens.shape
    info = jnp.stack([slots[0], count])

    qkv_first, near = first_forward(
        comm.core, tokens, near_pieces, comm.near_orders, vec, qkv_bias
    )
    mixed_hidden, lse_hidden = attend(info, qkv_first)
    late = QUESTION + lax.iota(jnp.int32, seq_len - QUESTION)
    upstream_low = jnp.where(
        (late >= answer_start)[:, None], cotangent[QUESTION:], jnp.zeros((), BF16)
    )
    tokens32 = tokens.astype(F32)
    weights = (near, after(far, mixed_hidden, upstream_low, tokens32))
    lse, *saved, qkv, mixed_low, hidden = thoughts_forward(
        info, tokens, tokens32, qkv_first, mixed_hidden, lse_hidden, weights, vec, fc_bias, qkv_bias
    )
    output, normed_low, second_low, act_low, pre_grad, resid_grad, mixed_grad, sums = feed(
        hidden, mixed_low, upstream_low, weights, vec, fc_bias
    )

    proj_grad = comm.proj_terms(act_low, upstream_low)
    proj_half = comm.early(proj_grad)
    halves = fc_terms(comm.core, after(second_low, proj_grad), pre_grad, comm.chips("zyxc"))
    fc_going = comm.scatter(halves, "zyxc")
    sent = go_after([fc_going])
    row_sums, factors, mixed_grad, resid_grad = thoughts_back(
        info,
        hidden,
        qkv,
        mixed_low,
        after(lse, *sent),
        saved,
        weights,
        vec,
        mixed_grad,
        resid_grad,
    )
    join_after([fc_going], row_sums)
    spread = comm.factors(factors)
    sent = go_after([fc_going, spread])
    lse, back_grad = after((lse, mixed_grad), *sent)
    qkv_grad = attend_back(qkv, mixed_low, lse, back_grad)
    join_after([fc_going, spread], qkv_grad)
    proj_half = after(proj_half, qkv_grad)
    proj_going = comm.early_end(proj_half)
    sent = (*go_after([fc_going, spread]), proj_half)
    *terms, packed = near_terms(
        comm.core,
        after(normed_low, *sent),
        qkv_grad,
        mixed_low,
        resid_grad,
        near,
        vec,
        sums,
        row_sums,
        sizes,
        comm.chips("zxyc"),
        comm.chips("zyxc"),
    )
    first = comm.scatter(terms[:2], "zxyc")
    rest = comm.scatter(terms[2:], "zyxc")
    vectors_going = comm.scatter_vectors(packed)

    join_after([fc_going, spread], packed)

    going = [first, rest, vectors_going]
    sent = go_after(going, fc_going.got, spread.buf)
    sent += go_after([fc_going, spread], *sent)
    join_after(going, *sent)
    sent = go_after(going)
    input_grad = first_back(info, hidden, after(qkv_grad, *sent), resid_grad, weights, vec)
    going += [fc_going, spread]
    join_after(going, input_grad)
    proj_g = fc_g = None
    while any(swap.todo for swap in going) or proj_g is None:
        group = [swap for swap in going if swap.todo]
        sent = go_after(group)
        done = sent
        if proj_g is None and fc_going not in group and spread not in group:
            factors, fc_sum = after((spread.finish(), fc_going.finish()), *sent)
            proj_g, fc_g = comm.terms(factors, proj_going, fc_sum)
            done = (proj_g, fc_g)
        join_after(group, *done)
    return (
        output,
        input_grad,
        first.finish(),
        rest.finish(),
        proj_g,
        fc_g,
        vectors_going.finish(),
    )


SMALL = ("ln1_gain", "ln1_bias", "qv_bias", "out_bias", "ln2_gain", "ln2_bias", "fc_bias", "proj_bias")


def on_device(
    links,
    tokens,
    ln1_gain,
    ln1_bias,
    qkv_weight,
    qv_bias,
    out_weight,
    out_bias,
    ln2_gain,
    ln2_bias,
    fc_weight,
    fc_bias,
    proj_weight,
    proj_bias,
    cotangent,
    thought_slots,
    thought_count,
    answer_start,
):
    devices = links.sizes["dp"] * links.sizes["fsdp"]
    small_shards = dict(
        ln1_gain=ln1_gain,
        ln1_bias=ln1_bias,
        qv_bias=qv_bias,
        out_bias=out_bias,
        ln2_gain=ln2_gain,
        ln2_bias=ln2_bias,
        fc_bias=fc_bias,
        proj_bias=proj_bias,
    )
    sizes = tuple((n, small_shards[n].shape[0]) for n in SMALL)
    own, width = out_weight.shape
    blocks = proj_weight.shape[0] // own
    both = ("dp", "fsdp")

    far_shard = join_far(fc_weight, proj_weight, out_weight)
    far = lax.all_gather(far_shard, both, axis=1, tiled=True)

    packed = join([small_shards[n] for n in SMALL]).astype(BF16)
    small = links.gather(packed, "zxyc", axis=0).reshape(devices, len(sizes), LANES)
    half = width // 2
    near_pieces = []
    near_texts = ("zxyc", "zyxc")
    for side, text in enumerate(near_texts):
        part_columns = [
            qkv_weight[:, i * width + side * half : i * width + (side + 1) * half] for i in range(3)
        ]
        ring = Gather(links, jnp.stack(part_columns)[None], text)
        near_pieces += ring.last()

    class Comm:
        chips = links.chips
        near_orders = [links.spots(text) for text in near_texts]
        core = (lax.axis_index("fsdp") % 2)[None].astype(jnp.int32)

        @staticmethod
        def proj_terms(act_low, upstream_low):
            return proj_terms(act_low, upstream_low, links.sizes["dp"], links.sizes["fsdp"])

        @staticmethod
        def early(value):
            return lax.psum_scatter(
                value.reshape(-1, width), "fsdp", scatter_dimension=0, tiled=True
            )

        @staticmethod
        def early_end(value):
            value = lax.psum_scatter(value, "dp", scatter_dimension=0, tiled=True)
            return value.reshape(blocks, own, width)

        @staticmethod
        def scatter(halves, text):
            return links.scatter(tuple(halves), text)

        @staticmethod
        def factors(rows):
            return Gather(links, rows, "zyxc")

        @staticmethod
        def scatter_vectors(value):
            return links.scatter(value.transpose(1, 0, 2), "zxyc")

        @staticmethod
        def terms(factors, proj_sum, fc_sum):
            index = lax.axis_index(both)[None].astype(jnp.int32)
            factors = factors.reshape(devices, FACTOR_ROWS, width).transpose(1, 0, 2)
            return row_terms(index, factors, proj_sum, fc_sum)

    output, input_grad, first, rest, proj_g, fc_g, vector_sums = step_on_sequence(
        near_pieces,
        far,
        unpack(small.transpose(1, 0, 2), sizes),
        tokens[0],
        cotangent[0],
        thought_slots[0],
        thought_count[0],
        answer_start[0],
        devices,
        sizes,
        Comm,
    )
    proj_g = proj_g.reshape(blocks * own, width)
    qkv_g = jnp.concatenate([first[0], first[1], rest[0]], axis=1)
    out_g = rest[1]
    owned = dict(zip(SMALL, part(vector_sums, sizes)))
    return (
        output[None],
        input_grad[None],
        owned["ln1_gain"],
        owned["ln1_bias"],
        qkv_g,
        owned["qv_bias"],
        out_g,
        owned["out_bias"],
        owned["ln2_gain"],
        owned["ln2_bias"],
        fc_g,
        owned["fc_bias"],
        proj_g,
        owned["proj_bias"],
    )


def solution(mesh):
    links = Links({name: mesh.shape[name] for name in ("dp", "fsdp")})
    both = ("dp", "fsdp")
    cube, matrix, vector = P(both, None, None), P(both, None), P(both)
    weight_specs = (
        vector,
        vector,
        matrix,
        vector,
        matrix,
        vector,
        vector,
        vector,
        matrix,
        vector,
        matrix,
        vector,
    )

    def per_device(*args):
        return on_device(links, *args)

    return jax.shard_map(
        per_device,
        mesh=mesh,
        in_specs=(cube,) + weight_specs + (cube, matrix, vector, vector),
        out_specs=(cube, cube) + weight_specs,
        check_vma=False,
    )
```

```python
import functools
import math

import jax
import jax.numpy as jnp
import numpy as np
from jax import lax
from jax.experimental import pallas as pl
from jax.experimental.pallas import tpu as pltpu
from jax.sharding import PartitionSpec as P

HD = 64
THOUGHTS = 2
PREFIX = 384
QUESTION = 256
SCALE = 0.125
EPSILON = 1e-05
BLOCK = 256
HEAD_ROWS = 16
WINDOW = 32
LANES = 128
FACTOR_ROWS = 24
PAIR = 2 * HD
NEG = -1e30

F32 = jnp.float32
BF16 = jnp.bfloat16
VMEM_LIMIT = 56 * 1024 * 1024


def cost(microseconds):
    return pl.CostEstimate(
        flops=int(microseconds * 1.15e9),
        bytes_accessed=int(microseconds * 3.6e6),
        transcendentals=0,
    )


def dot(a, b):
    return lax.dot_general(a, b, (((1,), (0,)), ((), ())), preferred_element_type=F32)


def dot_nt(a, b):
    return lax.dot_general(a, b, (((1,), (1,)), ((), ())), preferred_element_type=F32)


def dot_tn(a, b):
    return lax.dot_general(a, b, (((0,), (0,)), ((), ())), preferred_element_type=F32)


def bits_of(size):
    return [1 << i for i in reversed(range(int(math.log2(size))))]


class Links:
    def __init__(self, sizes):
        self.sizes = sizes
        self.canon = [("dp", b) for b in bits_of(sizes["dp"])] + [
            ("fsdp", b) for b in bits_of(sizes["fsdp"])
        ]
        dp_bits = [("dp", b) for b in bits_of(sizes["dp"])]
        f_bits = [("fsdp", b) for b in bits_of(sizes["fsdp"])]
        self.groups = {"x": dp_bits[-1:], "y": dp_bits[:-1], "z": f_bits[:-1], "c": f_bits[-1:]}

    def order(self, text):
        out = []
        for letter in text:
            out += self.groups[letter]
        return out

    def swap(self, value, stage):
        axis, bit = stage
        return lax.ppermute(value, axis, [(i, i ^ bit) for i in range(self.sizes[axis])])

    def mine(self, stage):
        axis, bit = stage
        return (lax.axis_index(axis) & bit) != 0

    def gather(self, shard, text, axis=0):
        return Gather(self, shard, text, axis).finish()

    def chips(self, text):
        stages = list(reversed(self.order(text)))[1:]
        rest = [c for c in self.canon if c in stages]
        order = []
        for spot in range(1 << len(stages)):
            chip = 0
            for at, stage in enumerate(stages):
                if spot & (1 << (len(stages) - 1 - at)):
                    chip |= 1 << (len(rest) - 1 - rest.index(stage))
            order.append(chip)
        return order

    def spots(self, text):
        stages = [c for c in reversed(self.order(text)) if c not in self.groups["c"]]
        rest = [c for c in self.canon if c in stages]
        order = []
        for spot in range(1 << len(stages)):
            chip = 0
            for at, stage in enumerate(stages):
                if spot & (1 << (len(stages) - 1 - at)):
                    chip |= 1 << (len(rest) - 1 - rest.index(stage))
            order.append(chip)
        return order

    def scatter(self, value, text):
        return Scatter(self, value, text)


class Gather:
    def __init__(self, links, shard, text, axis=0):
        self.links = links
        self.shape = shard.shape
        self.axis = axis
        self.todo = links.order(text)
        self.done = []
        self.buf = shard
        self.got = None

    def go(self):
        self.add()
        self.stage = self.todo.pop(0)
        self.got = self.links.swap(self.buf, self.stage)
        return self.buf

    def add(self):
        if self.got is not None:
            canon = self.links.canon
            place = sum(1 for d in self.done if canon.index(d) < canon.index(self.stage))
            high = self.links.mine(self.stage)
            pair = [jnp.where(high, self.got, self.buf), jnp.where(high, self.buf, self.got)]
            self.buf = jnp.stack(pair, axis=self.axis + place)
            self.done.append(self.stage)
            self.got = None
        return self.buf

    def hold(self, *deps):
        self.buf = after(self.buf, *deps)

    def join(self, *deps):
        self.got = after(self.got, *deps)
        self.add()

    def last(self):
        for stage in self.todo:
            if self.got is not None:
                high = self.links.mine(self.stage)
                pair = [jnp.where(high, self.got, self.buf), jnp.where(high, self.buf, self.got)]
                self.buf = jnp.concatenate(pair, axis=0)
            self.stage = stage
            self.got = self.links.swap(self.buf, stage)
        return [self.buf, self.got]

    def finish(self):
        while self.todo:
            self.go()
        self.add()
        shape = self.shape
        return self.buf.reshape(shape[: self.axis] + (-1,) + shape[self.axis + 1 :])


class Scatter:
    def __init__(self, links, value, text):
        self.links = links
        self.left = list(links.canon)
        self.todo = list(reversed(links.order(text)))
        self.got = None
        self.split = False
        if isinstance(value, tuple):
            self.split = True
            self.left = self.todo[1:]
            shape = (2,) * len(self.left) + value[0].shape[1:]
            self.keep, self.buf = (v.reshape(shape) for v in value)
        else:
            self.buf = value.reshape((2,) * len(self.left) + value.shape[1:])

    def go(self):
        stage = self.todo.pop(0)
        if self.split:
            self.split = False
            sent = self.buf
        else:
            place = self.left.index(stage)
            self.left.remove(stage)
            high = self.links.mine(stage).astype(jnp.int32)
            parts = [self.buf] if self.got is None else [self.keep, self.got]

            def half(side):
                cut = [lax.dynamic_index_in_dim(p, side, place, keepdims=False) for p in parts]
                return cut[0] if len(cut) == 1 else cut[0].astype(F32) + cut[1].astype(F32)

            sent = half(1 - high).astype(BF16)
            self.keep = half(high)
        self.got = self.links.swap(sent, stage)
        return sent

    def hold(self, *deps):
        if self.got is None:
            self.buf = after(self.buf, *deps)
        else:
            self.got = after(self.got, *deps)

    def join(self, *deps):
        self.got = after(self.got, *deps)

    def finish(self):
        return self.keep.astype(F32) + self.got.astype(F32)


def join_after(swaps, *deps):
    for swap in swaps:
        swap.join(*deps)


def go_after(swaps, *deps):
    for swap in swaps:
        swap.hold(*deps)
    return tuple(swap.go() for swap in swaps)


def after(value, *deps):
    return lax.optimization_barrier((value, deps))[0]


def attend_kernel(info_ref, q_ref, k_ref, v_ref, o_ref, lse_ref):
    seq_len = q_ref.shape[0]
    slot = info_ref[0]
    keys = k_ref[...]
    values_t = v_ref[...].T
    lane = lax.broadcasted_iota(jnp.int32, (BLOCK, PAIR), 1)
    key_pos = lax.broadcasted_iota(jnp.int32, (BLOCK, BLOCK), 0)
    row_pos = lax.broadcasted_iota(jnp.int32, (BLOCK, BLOCK), 1)
    causal = key_pos <= row_pos
    middle_pos = QUESTION + lax.broadcasted_iota(jnp.int32, (PREFIX - QUESTION, BLOCK), 0)
    is_slot = (middle_pos >= slot) & (middle_pos < slot + THOUGHTS)

    def hide(scores):
        if scores.shape[0] <= QUESTION:
            return scores
        middle = jnp.where(is_slot, NEG, scores[QUESTION:PREFIX])
        return jnp.concatenate([scores[:QUESTION], middle, scores[PREFIX:]], axis=0)

    for begin in range(0, seq_len, BLOCK):
        end = begin + BLOCK
        queries = q_ref[begin:end, :] * jnp.asarray(SCALE, BF16)
        parts = []
        for head in range(2):
            own = jnp.where((lane >= HD) == bool(head), queries, jnp.zeros_like(queries))
            scores = dot_nt(keys[:end], own)
            last = jnp.where(causal, scores[begin:], NEG)
            if begin:
                last = jnp.concatenate([scores[:begin], last], axis=0)
            scores = hide(last)
            peak = jnp.max(scores, axis=0, keepdims=True)
            expo = jnp.exp(scores - peak)
            total = jnp.sum(expo, axis=0, keepdims=True)
            mixed = dot(values_t[head * HD : (head + 1) * HD, :end], expo.astype(BF16))
            parts.append(mixed / total)
            lse_ref[pl.ds(2 * pl.program_id(0) + head, 1), begin:end] = peak + jnp.log(total)
        o_ref[begin:end, :] = jnp.concatenate(parts, axis=0).T.astype(BF16)


def attend(info, qkv):
    _, seq_len, width = qkv.shape
    pairs = width // PAIR

    def columns(i):
        return pl.BlockSpec((None, seq_len, PAIR), lambda g, i=i: (i, 0, g))

    return pl.pallas_call(
        attend_kernel,
        grid=(pairs,),
        in_specs=[
            pl.BlockSpec(memory_space=pltpu.SMEM),
            *(columns(i) for i in range(3)),
        ],
        out_specs=[
            pl.BlockSpec((seq_len, PAIR), lambda g: (0, g)),
            pl.BlockSpec((HEAD_ROWS, seq_len), lambda g: (0, 0)),
        ],
        out_shape=[
            jax.ShapeDtypeStruct((seq_len, width), BF16),
            jax.ShapeDtypeStruct((HEAD_ROWS, seq_len), F32),
        ],
        compiler_params=pltpu.CompilerParams(vmem_limit_bytes=VMEM_LIMIT),
        cost_estimate=cost(2.0),
        name="attention_forward",
    )(info, qkv, qkv, qkv)


def attend_back_kernel(
    q_ref, k_ref, v_ref, o_ref, lse_ref, g_ref, out_ref, dk_acc, dv_acc
):
    seq_len = q_ref.shape[0]
    pair = pl.program_id(0)
    first_row = seq_len - g_ref.shape[0]
    keys = k_ref[...]
    values = v_ref[...]
    keys_t = keys.T
    lane = lax.broadcasted_iota(jnp.int32, (BLOCK, PAIR), 1)
    key_pos = lax.broadcasted_iota(jnp.int32, (BLOCK, BLOCK), 0)
    row_pos = lax.broadcasted_iota(jnp.int32, (BLOCK, BLOCK), 1)
    causal = key_pos <= row_pos
    dk_acc[...] = jnp.zeros_like(dk_acc)
    dv_acc[...] = jnp.zeros_like(dv_acc)
    for begin in range(first_row, seq_len, BLOCK):
        end = begin + BLOCK
        local = begin - first_row
        queries = q_ref[begin:end, :] * jnp.asarray(SCALE, BF16)
        grads = g_ref[local : local + BLOCK, :]
        product_t = (grads.astype(F32) * o_ref[begin:end, :].astype(F32)).T
        owns, own_grads, probs_low, score_grads, parts = [], [], [], [], []
        for head in range(2):
            chosen = (lane >= HD) == bool(head)
            own = jnp.where(chosen, queries, jnp.zeros_like(queries))
            own_grad = jnp.where(chosen, grads, jnp.zeros_like(grads))
            rows_here = slice(head * HD, (head + 1) * HD)
            delta = jnp.sum(product_t[rows_here], axis=0, keepdims=True)
            lse = lse_ref[pl.ds(2 * pair + head, 1), begin:end]
            scores = dot_nt(keys[:end], own)
            last = jnp.where(causal, scores[begin:], NEG)
            scores = jnp.concatenate([scores[:begin], last], axis=0) if begin else last
            probs = jnp.exp(scores - lse)
            prob_grad = dot_nt(values[:end], own_grad)
            score_grad = (probs * (prob_grad - delta)).astype(BF16)
            parts.append(dot(keys_t[rows_here, :end], score_grad))
            owns.append(own)
            own_grads.append(own_grad)
            probs_low.append(probs.astype(BF16))
            score_grads.append(score_grad)
        dv_acc[:end, :] += dot(
            jnp.concatenate(probs_low, axis=1), jnp.concatenate(own_grads, axis=0)
        )
        dk_acc[:end, :] += dot(jnp.concatenate(score_grads, axis=1), jnp.concatenate(owns, axis=0))
        mine = jnp.concatenate(parts, axis=0).T * SCALE
        out_ref[0, begin:end, :] = mine.astype(BF16)
    out_ref[0, :first_row, :] = jnp.zeros((first_row, PAIR), BF16)
    out_ref[1] = dk_acc[...].astype(BF16)
    out_ref[2] = dv_acc[...].astype(BF16)


def attend_back(qkv, mixed_low, lse, mixed_grad):
    _, seq_len, width = qkv.shape
    rows = mixed_grad.shape[0]

    def columns(i):
        return pl.BlockSpec((None, seq_len, PAIR), lambda g, i=i: (i, 0, g))

    late = pl.BlockSpec((rows, PAIR), lambda g: (0, g))
    return pl.pallas_call(
        attend_back_kernel,
        grid=(width // PAIR,),
        in_specs=[
            *(columns(i) for i in range(3)),
            pl.BlockSpec((seq_len, PAIR), lambda g: (0, g)),
            pl.BlockSpec((HEAD_ROWS, seq_len), lambda g: (0, 0)),
            late,
        ],
        out_specs=pl.BlockSpec((3, seq_len, PAIR), lambda g: (0, 0, g)),
        out_shape=jax.ShapeDtypeStruct((3, seq_len, width), BF16),
        scratch_shapes=[pltpu.VMEM((seq_len, PAIR), F32), pltpu.VMEM((seq_len, PAIR), F32)],
        compiler_params=pltpu.CompilerParams(vmem_limit_bytes=VMEM_LIMIT),
        cost_estimate=cost(2.17),
        name="attention_backward",
    )(qkv, qkv, qkv, mixed_low, lse, mixed_grad)


def row_norm(row, gain, bias):
    mean = jnp.mean(row, axis=-1, keepdims=True)
    centred = row - mean
    inverse = lax.rsqrt(jnp.mean(centred * centred, axis=-1, keepdims=True) + EPSILON)
    normed = centred * inverse
    return normed * gain + bias, normed, inverse


def row_norm_back(incoming, normed, inverse, gain):
    scaled = incoming * gain
    inner = (
        scaled
        - jnp.mean(scaled, axis=-1, keepdims=True)
        - normed * jnp.mean(scaled * normed, axis=-1, keepdims=True)
    )
    return inner * inverse


GELU_A = 0.7978845608028654
GELU_B = 0.044715


def gelu(pre):
    return 0.5 * pre * (1.0 + jnp.tanh(GELU_A * (pre + GELU_B * pre * pre * pre)))


def gelu_slope(pre):
    square = pre * pre
    curve = jnp.tanh(GELU_A * pre * (1.0 + GELU_B * square))
    return 0.5 * (1.0 + curve) + 0.5 * pre * (1.0 - curve * curve) * GELU_A * (
        1.0 + 3.0 * GELU_B * square
    )


def widen(row):
    return jnp.broadcast_to(row, (8, row.shape[1])).astype(BF16)


def pick(block, index):
    rows = lax.broadcasted_iota(jnp.int32, block.shape, 0)
    return jnp.sum(jnp.where(rows == index, block.astype(F32), 0.0), axis=0, keepdims=True)


def put(block, index, row):
    rows = lax.broadcasted_iota(jnp.int32, block.shape, 0)
    return jnp.where(rows == index, row.astype(block.dtype), block)


def by_head(row, heads):
    shape = (heads, row.shape[1])
    lane_head = lax.broadcasted_iota(jnp.int32, shape, 1) // HD
    return jnp.where(lane_head == lax.broadcasted_iota(jnp.int32, shape, 0), row, 0.0)


def heads_only(block):
    lane_head = lax.broadcasted_iota(jnp.int32, block.shape, 1) // HD
    own = lane_head == lax.broadcasted_iota(jnp.int32, block.shape, 0)
    return jnp.sum(jnp.where(own, block, 0.0), axis=0, keepdims=True)


def thoughts_kernel(
    info_ref,
    tok_ref,
    lse_in_ref,
    vec_ref,
    fcb_ref,
    qkvb_ref,
    near_in,
    far_in,
    qkv_in,
    mixed_in,
    hid_in,
    lse_ref,
    pre_ref,
    prob_ref,
    res_ref,
    qkv_out,
    mixed_out,
    hid_out,
    kv_ref,
    late_q_ref,
    mixed_ref,
    hid_ref,
    near_ref,
    far_ref,
    sems,
):
    width = tok_ref.shape[1]
    blocks = (far_ref.shape[0] - 1) // 2
    rows = late_q_ref.shape[0]
    ln1_gain, ln1_bias, out_bias, ln2_gain, ln2_bias, proj_bias = (
        vec_ref[i : i + 1, :] for i in range(6)
    )
    slot = info_ref[0]
    count = info_ref[1]

    loads = [
        (qkv_in.at[:, pl.ds(0, PREFIX)], kv_ref),
        (far_in.at[pl.ds(2 * blocks, 1)], far_ref.at[pl.ds(2 * blocks, 1)]),
        (far_in.at[pl.ds(0, blocks)], far_ref.at[pl.ds(0, blocks)]),
        (far_in.at[pl.ds(blocks, blocks)], far_ref.at[pl.ds(blocks, blocks)]),
        (near_in, near_ref),
        (qkv_in.at[0, pl.ds(QUESTION, rows)], late_q_ref),
        (mixed_in.at[pl.ds(QUESTION, rows)], mixed_ref),
    ]
    loads = [pltpu.make_async_copy(a, b, sems.at[i]) for i, (a, b) in enumerate(loads)]
    for copy in loads:
        copy.start()
    hid_ref[...] = tok_ref[...].astype(F32)
    hidden_row = pick(hid_ref[...], slot - 1 - QUESTION)
    loads[0].wait()
    slot_rows = []
    slot_lse = []
    for step in range(THOUGHTS + 1):
        at = slot - 1 + step
        qkv_row = pick(kv_ref[0, QUESTION:, :], at - QUESTION)
        query = by_head(qkv_row * SCALE, HEAD_ROWS).astype(BF16)
        scores = dot_nt(query, kv_ref[1])
        key_pos = lax.broadcasted_iota(jnp.int32, scores.shape, 1)
        scores = jnp.where(key_pos <= at, scores, NEG)
        peak = jnp.max(scores, axis=1, keepdims=True)
        expo = jnp.exp(scores - peak)
        total = jnp.sum(expo, axis=1, keepdims=True)
        probs = expo / total
        mixed = heads_only(dot(probs.astype(BF16), kv_ref[2]))
        if step:
            slot_rows.append(mixed)
            slot_lse.append(peak + jnp.log(total))
        if step == THOUGHTS:
            break
        prob_ref[step * HEAD_ROWS : (step + 1) * HEAD_ROWS, :] = probs
        if not step:
            loads[1].wait()
        resid = hidden_row + dot(widen(mixed), far_ref[2 * blocks])[0:1] + out_bias
        res_ref[step : step + 1, :] = resid
        second, _, _ = row_norm(resid, ln2_gain, ln2_bias)
        second = widen(second)
        if not step:
            loads[2].wait()
        acts = []
        for j in range(blocks):
            span = slice(j * width, (j + 1) * width)
            pre = dot(second, far_ref[j])[0:1] + fcb_ref[0:1, span]
            pre_ref[step : step + 1, span] = pre
            acts.append(widen(gelu(pre)))
        if not step:
            loads[3].wait()
        fed = resid + proj_bias
        for j in range(blocks):
            fed = fed + dot(acts[j], far_ref[blocks + j])[0:1]
        first, _, _ = row_norm(fed, ln1_gain, ln1_bias)
        first = widen(first)
        hidden_row = fed
        spot = jnp.where(step < count, slot + step - QUESTION, -1)
        hid_ref[...] = put(hid_ref[...], spot, fed)
        if not step:
            loads[4].wait()
        for i in range(3):
            span = slice(i * width, (i + 1) * width)
            new_row = dot(first, near_ref[i])[0:1] + qkvb_ref[0:1, span]
            kv_ref[i, QUESTION:, :] = put(kv_ref[i, QUESTION:, :], spot, new_row)
    loads[5].wait()
    loads[6].wait()
    stores = [
        pltpu.make_async_copy(
            kv_ref.at[:, pl.ds(QUESTION, PREFIX - QUESTION)],
            qkv_out.at[:, pl.ds(QUESTION, PREFIX - QUESTION)],
            sems.at[0],
        ),
        pltpu.make_async_copy(
            hid_ref, hid_out.at[pl.ds(QUESTION, PREFIX - QUESTION)], sems.at[1]
        ),
    ]
    for copy in stores:
        copy.start()

    row_pos = QUESTION + lax.broadcasted_iota(jnp.int32, (HEAD_ROWS, rows), 1)
    late_q = late_q_ref[...]
    lse = lse_in_ref[:, QUESTION:]
    scores = []
    values = []
    top = lse
    for j in range(THOUGHTS):
        local = slot + j - QUESTION
        key = by_head(pick(kv_ref[1, QUESTION:, :], local) * SCALE, HEAD_ROWS)
        values.append(pick(kv_ref[2, QUESTION:, :], local))
        score = jnp.where(row_pos >= slot + j, dot_nt(key.astype(BF16), late_q), NEG)
        scores.append(score)
        top = jnp.maximum(top, score)
    whole_sum = jnp.exp(lse - top)
    for score in scores:
        whole_sum = whole_sum + jnp.exp(score - top)
    new_lse = top + jnp.log(whole_sum)
    ones = by_head(jnp.ones((1, width), F32), HEAD_ROWS).astype(BF16)
    share = jnp.exp(lse - new_lse)
    high = share.astype(BF16)
    low = (share - high.astype(F32)).astype(BF16)
    weights = [jnp.exp(score - new_lse).astype(BF16) for score in scores]
    step_rows = PREFIX - QUESTION
    for begin in range(0, rows, step_rows):
        span = slice(begin, begin + step_rows)
        part = mixed_ref[span, :].astype(F32) * (
            dot_tn(high[:, span], ones) + dot_tn(low[:, span], ones)
        )
        for weight, value in zip(weights, values):
            part = part + dot_tn(weight[:, span], ones) * value
        if not begin:
            for j in range(THOUGHTS):
                part = put(part, slot + j - QUESTION, slot_rows[j])
        mixed_ref[span, :] = part.astype(BF16)
    stores.append(
        pltpu.make_async_copy(mixed_ref, mixed_out.at[pl.ds(QUESTION, rows)], sems.at[2])
    )
    stores[-1].start()
    lse_ref[:, :QUESTION] = lse_in_ref[:, :QUESTION]
    column = lax.broadcasted_iota(jnp.int32, (HEAD_ROWS, step_rows), 1)
    middle = new_lse[:, :step_rows]
    for j in range(THOUGHTS):
        middle = jnp.where(column == slot + j - QUESTION, slot_lse[j], middle)
    lse_ref[:, QUESTION:PREFIX] = middle
    lse_ref[:, PREFIX:] = new_lse[:, step_rows:]
    for copy in stores:
        copy.wait()


def whole(array):
    zeros = (0,) * array.ndim
    return pl.BlockSpec(array.shape, lambda i, zeros=zeros: zeros)


def fc_spec(far):
    return pl.BlockSpec((far.shape[0] // 2,) + far.shape[1:], lambda i: (0, 0, 0))


def proj_spec(far):
    return pl.BlockSpec((far.shape[0] // 2,) + far.shape[1:], lambda i: (1, 0, 0))


def out_spec(far):
    last = far.shape[0] - 1
    return pl.BlockSpec((1,) + far.shape[1:], lambda i: (last, 0, 0))


def thoughts_forward(info, tokens, tokens32, qkv, mixed_low, lse, weights, vec, fc_bias, qkv_bias):
    near, far = weights
    seq_len, width = tokens.shape
    rows = seq_len - QUESTION
    middle = PREFIX - QUESTION
    anywhere = pl.BlockSpec(memory_space=pl.ANY)
    out_shape = [
        jax.ShapeDtypeStruct(lse.shape, F32),
        jax.ShapeDtypeStruct((8, fc_bias.shape[1]), F32),
        jax.ShapeDtypeStruct((THOUGHTS * HEAD_ROWS, PREFIX), F32),
        jax.ShapeDtypeStruct((8, width), F32),
        jax.ShapeDtypeStruct(qkv.shape, BF16),
        jax.ShapeDtypeStruct(mixed_low.shape, BF16),
        jax.ShapeDtypeStruct(tokens32.shape, F32),
    ]
    return pl.pallas_call(
        thoughts_kernel,
        grid=(1,),
        in_specs=[
            pl.BlockSpec(memory_space=pltpu.SMEM),
            pl.BlockSpec((middle, width), lambda i: (QUESTION // middle, 0)),
            whole(lse),
            whole(vec),
            whole(fc_bias),
            whole(qkv_bias),
            *[anywhere] * 5,
        ],
        out_specs=[*(whole(x) for x in out_shape[:4]), *[anywhere] * 3],
        out_shape=out_shape,
        input_output_aliases={8: 4, 9: 5, 10: 6},
        scratch_shapes=[
            pltpu.VMEM((3, PREFIX, width), BF16),
            pltpu.VMEM((rows, width), BF16),
            pltpu.VMEM((rows, width), BF16),
            pltpu.VMEM((middle, width), F32),
            pltpu.VMEM(near.shape, BF16),
            pltpu.VMEM(far.shape, BF16),
            pltpu.SemaphoreType.DMA((7,)),
        ],
        compiler_params=pltpu.CompilerParams(vmem_limit_bytes=VMEM_LIMIT),
        cost_estimate=cost(2),
        name="thought_rows_forward",
    )(info, tokens, lse, vec, fc_bias, qkv_bias, near, far, qkv, mixed_low, tokens32)


def thoughts_back_kernel(
    info_ref,
    hid_ref,
    qkv_ref,
    lse_ref,
    pre_ref,
    prob_ref,
    res_ref,
    vec_ref,
    near_in,
    far_in,
    qkv_in,
    mixed_in,
    mg_in,
    rg_in,
    sum_ref,
    fac_ref,
    mg_out,
    rg_out,
    mg_ref,
    rg_win,
    late_q_ref,
    mixed_ref,
    near_ref,
    far_ref,
    sems,
):
    width = hid_ref.shape[1]
    blocks = (far_ref.shape[0] - 1) // 2
    units = blocks * width
    rows = mg_ref.shape[0]
    ln1_gain, ln1_bias, _, ln2_gain, ln2_bias, _ = (vec_ref[i : i + 1, :] for i in range(6))
    slot = info_ref[0]
    count = info_ref[1]
    base = pl.multiple_of(((slot - 1 - QUESTION) // 16) * 16, 16)

    def window(ref):
        return ref.at[pl.ds(base, WINDOW)]

    loads = [
        (mg_in, mg_ref),
        (mixed_in.at[pl.ds(QUESTION, rows)], mixed_ref),
        (qkv_in.at[0, pl.ds(QUESTION, rows)], late_q_ref),
        (window(rg_in), rg_win),
        (near_in, near_ref),
        (far_in.at[pl.ds(blocks, blocks)], far_ref.at[pl.ds(blocks, blocks)]),
        (far_in.at[pl.ds(0, blocks)], far_ref.at[pl.ds(0, blocks)]),
        (far_in.at[pl.ds(2 * blocks, 1)], far_ref.at[pl.ds(2 * blocks, 1)]),
    ]
    loads = [pltpu.make_async_copy(a, b, sems.at[i]) for i, (a, b) in enumerate(loads)]
    for copy in loads:
        copy.start()
    for copy in loads[:4]:
        copy.wait()

    late_q = late_q_ref[...]
    mixed_grad = mg_ref[...]
    product = mixed_grad.astype(F32) * mixed_ref[...].astype(F32)
    high = product.astype(BF16)
    ones = by_head(jnp.ones((1, width), F32), HEAD_ROWS).astype(BF16)
    delta = dot_nt(ones, high) + dot_nt(ones, (product - high.astype(F32)).astype(BF16))
    lse = lse_ref[:, QUESTION:]

    def columns(block, scale):
        rows_here = [
            by_head(pick(block, slot + j - QUESTION) * scale, HEAD_ROWS) for j in range(THOUGHTS)
        ]
        return jnp.concatenate(rows_here, axis=0).astype(BF16)

    def twice(block):
        return jnp.concatenate([block] * THOUGHTS, axis=0)

    slot_pos = jnp.concatenate(
        [jnp.full((HEAD_ROWS, rows), QUESTION - j, jnp.int32) for j in range(THOUGHTS)], axis=0
    )
    seen = slot_pos + lax.broadcasted_iota(jnp.int32, slot_pos.shape, 1) >= slot
    scores = dot_nt(columns(qkv_ref[1, QUESTION:PREFIX, :], SCALE), late_q)
    probs = jnp.where(seen, jnp.exp(jnp.minimum(scores - twice(lse), 0.0)), 0.0)
    prob_grad = dot_nt(columns(qkv_ref[2, QUESTION:PREFIX, :], 1.0), mixed_grad)
    score_grad = (probs * (prob_grad - twice(delta))).astype(BF16)
    slot_keys = dot(score_grad, late_q)
    slot_values = dot(probs.astype(BF16), mixed_grad)
    slot_grads = []
    for j in range(THOUGHTS):
        span = slice(j * HEAD_ROWS, (j + 1) * HEAD_ROWS)
        slot_grads.append((heads_only(slot_keys[span]) * SCALE, heads_only(slot_values[span])))

    def through_first(at, query_grad, key_grad, value_grad):
        first_grad = (
            dot_nt(widen(query_grad), near_ref[0])
            + dot_nt(widen(key_grad), near_ref[1])
            + dot_nt(widen(value_grad), near_ref[2])
        )[0:1]
        _, normed, inverse = row_norm(hid_ref[pl.ds(at - QUESTION, 1), :], ln1_gain, ln1_bias)
        return row_norm_back(first_grad, normed, inverse, ln1_gain)

    sum_ref[...] = jnp.zeros_like(sum_ref)
    fac = {}
    loads[4].wait()
    carried = through_first(slot + 1, jnp.zeros((1, width), F32), *slot_grads[1])
    for copy in loads[5:]:
        copy.wait()
    for step in reversed(range(THOUGHTS)):
        at = slot - 1 + step
        upstream = jnp.where(step < count, carried, 0.0)
        low = widen(upstream)
        act_grad = jnp.concatenate([dot_nt(low, far_ref[blocks + j])[0:1] for j in range(blocks)], axis=1)
        pre = pre_ref[step : step + 1, :]
        pre_grad = (act_grad * gelu_slope(pre)).astype(BF16).astype(F32)
        second_grad = jnp.zeros((1, width), F32)
        for j in range(blocks):
            piece = pre_grad[:, j * width : (j + 1) * width]
            second_grad = second_grad + dot_nt(widen(piece), far_ref[j])[0:1]
        second, normed, inverse = row_norm(res_ref[step : step + 1, :], ln2_gain, ln2_bias)
        resid_grad = upstream + row_norm_back(second_grad, normed, inverse, ln2_gain)
        mixed_row = dot_nt(widen(resid_grad), far_ref[2 * blocks])[0:1]
        local = at - QUESTION
        rg_win[...] = put(rg_win[...], local - base, resid_grad)
        mg_ref[: PREFIX - QUESTION, :] = put(mg_ref[: PREFIX - QUESTION, :], local, mixed_row)
        up_low = upstream.astype(BF16).astype(F32)
        sum_ref[0:1, :units] += pre_grad
        sum_ref[1:2, :width] += second_grad * normed
        sum_ref[2:3, :width] += second_grad
        sum_ref[3:4, :width] += up_low
        sum_ref[4:5, :width] += resid_grad.astype(BF16).astype(F32)
        act = gelu(pre)
        rows_here = [act[:, j * width : (j + 1) * width] for j in range(blocks)]
        rows_here += [up_low, second]
        rows_here += [pre_grad[:, j * width : (j + 1) * width] for j in range(blocks)]
        for j, row in enumerate(rows_here):
            fac[THOUGHTS * j + step] = row
        if step:
            own_grad = by_head(mixed_row, HEAD_ROWS).astype(BF16)
            query = by_head(pick(qkv_ref[0, QUESTION:PREFIX, :], local) * SCALE, HEAD_ROWS)
            query = query.astype(BF16)
            probs = prob_ref[step * HEAD_ROWS : (step + 1) * HEAD_ROWS, :]
            prob_grad = dot_nt(own_grad, qkv_ref[2])
            own_delta = jnp.sum(prob_grad * probs, axis=1, keepdims=True)
            score_grad = (probs * (prob_grad - own_delta)).astype(BF16)
            query_grad = heads_only(dot(score_grad, qkv_ref[1])) * SCALE
            key_grad, value_grad = slot_grads[0]
            own = lax.broadcasted_iota(jnp.int32, probs.shape, 1) == at
            score_own = jnp.sum(jnp.where(own, score_grad.astype(F32), 0.0), axis=1, keepdims=True)
            prob_own = jnp.sum(jnp.where(own, probs, 0.0), axis=1, keepdims=True)
            key_grad += jnp.sum(score_own * query.astype(F32), axis=0, keepdims=True)
            value_grad += jnp.sum(prob_own * own_grad.astype(F32), axis=0, keepdims=True)
            carried = resid_grad + through_first(at, query_grad, key_grad, value_grad)
    padding = [jnp.zeros((1, width), F32)] * (fac_ref.shape[0] - len(fac))
    fac_ref[...] = jnp.concatenate([fac[i] for i in range(len(fac))] + padding, axis=0).astype(BF16)
    stores = [
        pltpu.make_async_copy(mg_ref, mg_out, sems.at[0]),
        pltpu.make_async_copy(rg_win, window(rg_out), sems.at[1]),
    ]
    for copy in stores:
        copy.start()
    for copy in stores:
        copy.wait()


SUM_ROWS = ("fc_bias", "ln2_gain", "ln2_bias", "proj_bias", "out_bias")


def thoughts_back(info, hidden, qkv, mixed_low, lse, saved, weights, vec, mixed_grad, resid_grad):
    near, far = weights
    width = hidden.shape[1]
    units = far.shape[0] // 2 * width
    middle = PREFIX - QUESTION
    anywhere = pl.BlockSpec(memory_space=pl.ANY)
    out_shape = [
        jax.ShapeDtypeStruct((8, units), F32),
        jax.ShapeDtypeStruct((FACTOR_ROWS, width), BF16),
        jax.ShapeDtypeStruct(mixed_grad.shape, BF16),
        jax.ShapeDtypeStruct(resid_grad.shape, F32),
    ]
    return pl.pallas_call(
        thoughts_back_kernel,
        grid=(1,),
        in_specs=[
            pl.BlockSpec(memory_space=pltpu.SMEM),
            pl.BlockSpec((middle, width), lambda i: (QUESTION // middle, 0)),
            pl.BlockSpec((3, PREFIX, width), lambda i: (0, 0, 0)),
            whole(lse),
            *(whole(x) for x in saved),
            whole(vec),
            *[anywhere] * 6,
        ],
        out_specs=[whole(out_shape[0]), whole(out_shape[1]), anywhere, anywhere],
        out_shape=out_shape,
        input_output_aliases={12: 2, 13: 3},
        scratch_shapes=[
            pltpu.VMEM(mixed_grad.shape, BF16),
            pltpu.VMEM((WINDOW, width), F32),
            pltpu.VMEM(mixed_grad.shape, BF16),
            pltpu.VMEM(mixed_grad.shape, BF16),
            pltpu.VMEM(near.shape, BF16),
            pltpu.VMEM(far.shape, BF16),
            pltpu.SemaphoreType.DMA((8,)),
        ],
        compiler_params=pltpu.CompilerParams(vmem_limit_bytes=VMEM_LIMIT),
        cost_estimate=cost(2.0),
        name="thought_rows_backward",
    )(
        info,
        hidden,
        qkv,
        lse,
        *saved,
        vec,
        near,
        far,
        qkv,
        mixed_low,
        mixed_grad,
        resid_grad,
    )


def feed_kernel(
    hid_ref, mixed_ref, up_ref, wout_ref, wfc_ref, wproj_ref, vec_ref, fcb_ref, out_ref, first_ref,
    second_ref, act_ref, pg_ref, rg_ref, mg_ref, sum_ref, slope_ref,
):
    width = hid_ref.shape[1]
    blocks = wfc_ref.shape[0]
    step = pl.program_id(0)
    skip = QUESTION // BLOCK
    out_bias, ln2_gain, ln2_bias, proj_bias = (vec_ref[i : i + 1, :] for i in range(2, 6))

    @pl.when(step == 0)
    def _():
        sum_ref[...] = jnp.zeros_like(sum_ref)

    hidden = hid_ref[...]
    _, first_normed, _ = row_norm(hidden, vec_ref[0:1, :], vec_ref[1:2, :])
    first_ref[...] = first_normed.astype(BF16)
    resid = hidden + dot(mixed_ref[...], wout_ref[0]) + out_bias
    second, normed, inverse = row_norm(resid, ln2_gain, ln2_bias)
    low = second.astype(BF16)
    second_ref[...] = low
    total = resid + proj_bias
    for j in range(blocks):
        span = slice(j * width, (j + 1) * width)
        pre = dot(low, wfc_ref[j]) + fcb_ref[:, span]
        square = pre * pre
        curve = jnp.tanh(GELU_A * pre * (1.0 + GELU_B * square))
        half = 0.5 + 0.5 * curve
        act = (pre * half).astype(BF16)
        rise = 0.5 * GELU_A + (1.5 * GELU_A * GELU_B) * square
        slope_ref[:, span] = (half + pre * rise * (1.0 - curve * curve)).astype(BF16)
        act_ref[:, span] = act
        total = total + dot(act, wproj_ref[j])
    out_ref[...] = total.astype(BF16)

    @pl.when(step >= skip)
    def _():
        up = up_ref[...]
        second_grad = jnp.zeros(up.shape, F32)
        for j in range(blocks):
            span = slice(j * width, (j + 1) * width)
            slope = slope_ref[:, span].astype(F32)
            pre_grad = (dot_nt(up, wproj_ref[j]) * slope).astype(BF16)
            pg_ref[:, span] = pre_grad
            sum_ref[0:1, span] += jnp.sum(pre_grad.astype(F32), axis=0, keepdims=True)
            second_grad = second_grad + dot_nt(pre_grad, wfc_ref[j])
        up32 = up.astype(F32)
        resid_grad = up32 + row_norm_back(second_grad, normed, inverse, ln2_gain)
        attn_grad = resid_grad.astype(BF16)
        rg_ref[...] = resid_grad
        mg_ref[...] = dot_nt(attn_grad, wout_ref[0]).astype(BF16)
        sum_ref[1:2, :width] += jnp.sum(second_grad * normed, axis=0, keepdims=True)
        sum_ref[2:3, :width] += jnp.sum(second_grad, axis=0, keepdims=True)
        sum_ref[3:4, :width] += jnp.sum(up32, axis=0, keepdims=True)
        sum_ref[4:5, :width] += jnp.sum(attn_grad.astype(F32), axis=0, keepdims=True)


def feed(hidden, mixed_low, upstream_low, weights, vec, fc_bias):
    far = weights[1]
    seq_len, width = hidden.shape
    late = seq_len - QUESTION
    units = fc_bias.shape[1]
    skip = QUESTION // BLOCK

    def rows(columns):
        return pl.BlockSpec((BLOCK, columns), lambda i: (i, 0))

    def late_rows(columns):
        return pl.BlockSpec((BLOCK, columns), lambda i: (jnp.maximum(i - skip, 0), 0))

    sums = jax.ShapeDtypeStruct((8, units), F32)
    return pl.pallas_call(
        feed_kernel,
        grid=(seq_len // BLOCK,),
        in_specs=[
            rows(width),
            rows(width),
            late_rows(width),
            out_spec(far),
            fc_spec(far),
            proj_spec(far),
            whole(vec),
            whole(fc_bias),
        ],
        out_specs=[
            rows(width),
            rows(width),
            late_rows(width),
            late_rows(units),
            late_rows(units),
            late_rows(width),
            late_rows(width),
            whole(sums),
        ],
        out_shape=[
            jax.ShapeDtypeStruct((seq_len, width), BF16),
            jax.ShapeDtypeStruct((seq_len, width), BF16),
            jax.ShapeDtypeStruct((late, width), BF16),
            jax.ShapeDtypeStruct((late, units), BF16),
            jax.ShapeDtypeStruct((late, units), BF16),
            jax.ShapeDtypeStruct((late, width), F32),
            jax.ShapeDtypeStruct((late, width), BF16),
            sums,
        ],
        scratch_shapes=[pltpu.VMEM((BLOCK, units), BF16)],
        compiler_params=pltpu.CompilerParams(vmem_limit_bytes=VMEM_LIMIT),
        cost_estimate=cost(3),
        name="feed_forward_and_back",
    )(hidden, mixed_low, upstream_low, far, far, far, vec, fc_bias)


def first_back_kernel(info_ref, hid_ref, grad_ref, rg_ref, near_ref, vec_ref, in_ref):
    rows, width = hid_ref.shape
    step = pl.program_id(0)
    slot = info_ref[0]
    count = info_ref[1]
    gain = vec_ref[0:1, :]
    _, normed, inverse = row_norm(hid_ref[...], gain, vec_ref[1:2, :])
    first_grad = jnp.zeros((rows, width), F32)
    for i in range(3):
        first_grad = first_grad + dot_nt(grad_ref[i], near_ref[i])
    late = (step >= QUESTION // BLOCK).astype(F32)
    grad = row_norm_back(first_grad, normed, inverse, gain) + late * rg_ref[...]
    position = step * rows + lax.broadcasted_iota(jnp.int32, (rows, 1), 0)
    replaced = (position >= slot) & (position < slot + jnp.minimum(count, THOUGHTS))
    in_ref[...] = jnp.where(replaced, 0.0, grad)


def first_back(info, hidden, qkv_grad, resid_grad, weights, vec):
    seq_len, width = hidden.shape
    skip = QUESTION // BLOCK
    rows = pl.BlockSpec((BLOCK, width), lambda i: (i, 0))
    return pl.pallas_call(
        first_back_kernel,
        grid=(seq_len // BLOCK,),
        in_specs=[
            pl.BlockSpec(memory_space=pltpu.SMEM),
            rows,
            pl.BlockSpec((3, BLOCK, width), lambda i: (0, i, 0)),
            pl.BlockSpec((BLOCK, width), lambda i: (jnp.maximum(i - skip, 0), 0)),
            whole(weights[0]),
            whole(vec),
        ],
        out_specs=rows,
        out_shape=jax.ShapeDtypeStruct((seq_len, width), F32),
        compiler_params=pltpu.CompilerParams(vmem_limit_bytes=VMEM_LIMIT),
        cost_estimate=cost(0.83),
        name="first_norm_backward",
    )(info, hidden, qkv_grad, resid_grad, weights[0], vec)


def in_pieces(value, count=3):
    pieces = []
    for _ in range(count):
        pieces.append(value.astype(BF16))
        value = value - pieces[-1].astype(F32)
    return pieces


def keep_and_send(value, core, chips, keep_ref, send_ref, at):
    own = value.shape[0] // (2 * len(chips))
    for spot, chip in enumerate(chips):
        even = value[2 * chip * own : (2 * chip + 1) * own]
        odd = value[(2 * chip + 1) * own : (2 * chip + 2) * own]
        keep_ref[spot, at] = jnp.where(core == 0, even, odd).astype(BF16)
        send_ref[spot, at] = jnp.where(core == 0, odd, even).astype(BF16)


def near_terms_kernel(
    sizes, chips_a, chips_b, core_ref, normed_ref, grad_ref, mixed_ref, rg_ref, near_ref, vec_ref,
    feed_sum_ref, row_sum_ref, place_a, owner_a, place_b, owner_b, keep_a, send_a, keep_b, send_b,
    packed_ref, normed_t, gain_ref, bias_ref, column_ref,
):
    core = core_ref[0]
    step = pl.program_id(0)
    width = normed_ref.shape[1]

    @pl.when(step == 0)
    def _():
        normed_t[...] = normed_ref[...].T
        gain_ref[...] = jnp.zeros_like(gain_ref)
        bias_ref[...] = jnp.zeros_like(bias_ref)

    def term():
        columns = vec_ref[...].T
        inner = dot(normed_t[...], grad_ref[...])
        sums = jnp.sum(grad_ref[...].astype(F32), axis=0, keepdims=True)
        gain_ref[...] += inner * near_ref[...].astype(F32)
        pieces = in_pieces(jnp.broadcast_to(sums, (8, width)), 2)
        bias_ref[...] += dot_nt(jnp.concatenate(pieces, axis=0), near_ref[...])
        column_ref[pl.ds(step, 1), :] = sums
        return inner * columns[:, 0:1] + columns[:, 1:2] * sums

    @pl.when(step < 2)
    def _():
        keep_and_send(term(), core, chips_a, keep_a, send_a, 0)

    @pl.when(step == 2)
    def _():
        keep_and_send(term(), core, chips_b, keep_b, send_b, 0)

    @pl.when(step == 3)
    def _():
        value = dot_tn(mixed_ref[QUESTION:, :], rg_ref[...].astype(BF16))
        keep_and_send(value, core, chips_b, keep_b, send_b, 0)
        ones = jnp.ones((16, width), BF16)
        totals = feed_sum_ref[...] + row_sum_ref[...]
        small = {name: totals[i : i + 1, :width] for i, name in enumerate(SUM_ROWS)}
        small["fc_bias"] = totals[0:1]
        small["ln1_gain"] = sum(dot_nt(ones, p) for p in in_pieces(gain_ref[...], 2))[0:1]
        small["ln1_bias"] = bias_ref[0:1, :] + bias_ref[8:9, :]
        small["qv_bias"] = jnp.concatenate([column_ref[0:1, :], column_ref[2:3, :]], axis=1)
        pack(small, sizes, 2 * len(chips_a), (place_a, owner_a, place_b, owner_b), packed_ref)


def near_terms(
    core, normed_low, qkv_grad, mixed_low, resid_grad, near, vec, feed_sums, row_sums, sizes, chips_a, chips_b
):
    seq_len, width = normed_low.shape
    half = jax.ShapeDtypeStruct((len(chips_a), 2, width // (2 * len(chips_a)), width), BF16)
    piece = (len(chips_a), 1) + half.shape[2:]
    left = pl.BlockSpec(piece, lambda i: (0, jnp.minimum(i, 1), 0, 0))
    right = pl.BlockSpec(piece, lambda i: (0, jnp.maximum(i - 2, 0), 0, 0))
    devices = 2 * len(chips_a)
    maps = lane_maps(width // devices, devices)
    packed = jax.ShapeDtypeStruct((len(sizes), devices, LANES), BF16)
    out_shape = [half] * 4 + [packed]
    return pl.pallas_call(
        functools.partial(near_terms_kernel, sizes, chips_a, chips_b),
        grid=(4,),
        in_specs=[
            pl.BlockSpec(memory_space=pltpu.SMEM),
            whole(normed_low),
            pl.BlockSpec((None, seq_len, width), lambda i: (jnp.minimum(i, 2), 0, 0)),
            whole(mixed_low),
            whole(resid_grad),
            pl.BlockSpec((None, width, width), lambda i: (jnp.minimum(i, 2), 0, 0)),
            whole(vec),
            whole(feed_sums),
            whole(row_sums),
            *(whole(x) for x in maps),
        ],
        out_specs=[left, left, right, right, whole(packed)],
        out_shape=out_shape,
        scratch_shapes=[
            pltpu.VMEM((width, seq_len), BF16),
            pltpu.VMEM((width, width), F32),
            pltpu.VMEM((16, width), F32),
            pltpu.VMEM((8, width), F32),
        ],
        compiler_params=pltpu.CompilerParams(vmem_limit_bytes=VMEM_LIMIT),
        cost_estimate=cost(0.5),
        name="near_weight_terms",
    )(core, normed_low, qkv_grad, mixed_low, resid_grad, near, vec, feed_sums, row_sums, *maps)


def far_terms_kernel(
    outer, inner, chips, core_ref, act_ref, up_ref, second_ref, pg_ref, proj_ref, keep_ref, send_ref,
    second_t,
):
    step = pl.program_id(0)
    blocks = pl.num_programs(0) // 2

    @pl.when(step == 0)
    def _():
        second_t[...] = second_ref[...].T

    @pl.when(step < blocks)
    def _():
        value = dot_tn(act_ref[...], up_ref[...])
        rows, width = value.shape
        value = value.reshape(outer, inner, rows // (outer * inner), width)
        for i in range(inner):
            proj_ref[i, :, 0] = value[:, i].astype(BF16)

    @pl.when(step >= blocks)
    def _():
        value = dot(second_t[...], pg_ref[...])
        keep_and_send(value, core_ref[0], chips, keep_ref, send_ref, 0)


def far_terms(core, act_low, upstream_low, second_low, pre_grad, outer, inner, chips):
    rows, units = pre_grad.shape
    width = second_low.shape[1]
    blocks = units // width
    own = width // (outer * inner)
    proj = (inner, outer, blocks, own, width)
    half = jax.ShapeDtypeStruct((len(chips), blocks, own, width), BF16)

    def early(i):
        return jnp.minimum(i, blocks - 1)

    def late(i):
        return jnp.maximum(i - blocks, 0)

    out = pl.BlockSpec((len(chips), 1, own, width), lambda i: (0, late(i), 0, 0))
    return pl.pallas_call(
        functools.partial(far_terms_kernel, outer, inner, chips),
        grid=(2 * blocks,),
        in_specs=[
            pl.BlockSpec(memory_space=pltpu.SMEM),
            pl.BlockSpec((rows, width), lambda i: (0, early(i))),
            whole(upstream_low),
            whole(second_low),
            pl.BlockSpec((rows, width), lambda i: (0, late(i))),
        ],
        out_specs=[
            pl.BlockSpec((inner, outer, 1, own, width), lambda i: (0, 0, early(i), 0, 0)),
            out,
            out,
        ],
        out_shape=[jax.ShapeDtypeStruct(proj, BF16), half, half],
        scratch_shapes=[pltpu.VMEM((width, rows), BF16)],
        compiler_params=pltpu.CompilerParams(vmem_limit_bytes=VMEM_LIMIT),
        cost_estimate=cost(1),
        name="far_weight_terms",
    )(core, act_low, upstream_low, second_low, pre_grad)


def first_kernel(
    orders, core_ref, tok_ref, left_mine, left_got, right_mine, right_got, vec_ref, qkvb_ref, qkv_ref,
    near_ref, rows_ref,
):
    width = tok_ref.shape[1]

    @pl.when(pl.program_id(0) == 0)
    def _():
        even_is_mine = core_ref[0] == 0
        own, half = left_mine.shape[2:]
        for i in range(3):
            for side, (mine, got) in enumerate([(left_mine, left_got), (right_mine, right_got)]):
                for spot, chip in enumerate(orders[side]):
                    a = mine[spot, i].astype(F32)
                    b = got[spot, i].astype(F32)
                    begin = 2 * chip * own
                    rows_ref[begin : begin + own, :] = jnp.where(even_is_mine, a, b)
                    rows_ref[begin + own : begin + 2 * own, :] = jnp.where(even_is_mine, b, a)
                near_ref[i, :, side * half : (side + 1) * half] = rows_ref[...].astype(BF16)

    first, _, _ = row_norm(tok_ref[...].astype(F32), vec_ref[0:1, :], vec_ref[1:2, :])
    first = first.astype(BF16)
    for i in range(3):
        span = slice(i * width, (i + 1) * width)
        qkv_ref[i] = (dot(first, near_ref[i]) + qkvb_ref[:, span]).astype(BF16)


def first_forward(core, tokens, pieces, orders, vec, qkv_bias):
    seq_len, width = tokens.shape
    near = jax.ShapeDtypeStruct((3, width, width), BF16)
    return pl.pallas_call(
        functools.partial(first_kernel, orders),
        grid=(seq_len // BLOCK,),
        in_specs=[
            pl.BlockSpec(memory_space=pltpu.SMEM),
            pl.BlockSpec((BLOCK, width), lambda i: (i, 0)),
            *(whole(piece) for piece in pieces),
            whole(vec),
            whole(qkv_bias),
        ],
        out_specs=[pl.BlockSpec((3, BLOCK, width), lambda i: (0, i, 0)), whole(near)],
        out_shape=[jax.ShapeDtypeStruct((3, seq_len, width), BF16), near],
        scratch_shapes=[pltpu.VMEM((width, width // 2), F32)],
        compiler_params=pltpu.CompilerParams(vmem_limit_bytes=VMEM_LIMIT),
        cost_estimate=cost(0.67),
        name="first_norm_forward",
    )(core, tokens, *pieces, vec, qkv_bias)


def group_of(blocks, own):
    each = blocks * own
    group = LANES // math.gcd(LANES, each)
    device, block, i = np.indices((group, blocks, own)).reshape(3, -1)
    swap = np.zeros((group * each, group * each), np.float32)
    swap[np.arange(group * each), block * (group * own) + device * own + i] = 1.0
    return group, jnp.asarray(swap, BF16)


def far_shard_kernel(blocks, span, fc_ref, proj_ref, out_w_ref, swap_ref, out_ref):
    own, width = out_w_ref.shape
    size = swap_ref.shape[0]
    groups = width // span
    rows = [fc_ref[:, g * size : (g + 1) * size].astype(F32) for g in range(groups)]
    swapped = dot(jnp.concatenate(rows, axis=0).astype(BF16), swap_ref[...])
    for g in range(groups):
        part = swapped[g * own : (g + 1) * own]
        for j in range(blocks):
            piece = part[:, j * span : (j + 1) * span]
            out_ref[j, :, g * span : (g + 1) * span] = piece.astype(BF16)
    for j in range(blocks):
        out_ref[blocks + j] = proj_ref[j]
    out_ref[2 * blocks] = out_w_ref[...]


def join_far(fc_shard, proj_shard, out_shard):
    own, width = out_shard.shape
    blocks = fc_shard.shape[1] // width
    group, swap = group_of(blocks, own)
    return pl.pallas_call(
        functools.partial(far_shard_kernel, blocks, group * own),
        out_shape=jax.ShapeDtypeStruct((2 * blocks + 1, own, width), BF16),
        compiler_params=pltpu.CompilerParams(vmem_limit_bytes=VMEM_LIMIT),
        name="far_shard",
    )(fc_shard, proj_shard.reshape(blocks, own, width), out_shard, swap)


def row_terms_kernel(span, index_ref, fac_ref, proj_ref, fc_ref, swap_ref, proj_out, fc_out):
    blocks, own, width = proj_ref.shape
    shape = (width, own)
    mine = lax.broadcasted_iota(jnp.int32, shape, 0) - index_ref[0] * own
    select = (mine == lax.broadcasted_iota(jnp.int32, shape, 1)).astype(BF16)

    def factor(j):
        return jnp.concatenate([fac_ref[THOUGHTS * j + i] for i in range(THOUGHTS)], axis=0)

    upstream = factor(blocks)
    terms = []
    second = dot(factor(blocks + 1), select).astype(BF16)
    for j in range(blocks):
        act = dot(factor(j), select).astype(BF16)
        proj_out[j] = proj_ref[j].astype(F32) + dot_tn(act, upstream)
        terms.append(fc_ref[j] + dot_tn(second, factor(blocks + 2 + j)))
    size = swap_ref.shape[0]
    groups = width // span
    rows = [
        jnp.concatenate([t[:, g * span : (g + 1) * span] for t in terms], axis=1)
        for g in range(groups)
    ]
    left = jnp.concatenate(rows, axis=0)
    total = sum(dot_nt(piece, swap_ref[...]) for piece in in_pieces(left))
    for g in range(groups):
        fc_out[:, g * size : (g + 1) * size] = total[g * own : (g + 1) * own]


def row_terms(index, factors, proj_sum, fc_sum):
    blocks, own, width = fc_sum.shape
    out_shape = [
        jax.ShapeDtypeStruct(proj_sum.shape, F32),
        jax.ShapeDtypeStruct((own, blocks * width), F32),
    ]
    group, swap = group_of(blocks, own)
    return pl.pallas_call(
        functools.partial(row_terms_kernel, group * own),
        grid=(1,),
        in_specs=[
            pl.BlockSpec(memory_space=pltpu.SMEM),
            whole(factors),
            whole(proj_sum),
            whole(fc_sum),
            whole(swap),
        ],
        out_specs=[whole(x) for x in out_shape],
        out_shape=out_shape,
        compiler_params=pltpu.CompilerParams(vmem_limit_bytes=VMEM_LIMIT),
        cost_estimate=cost(0.33),
        name="thought_rows_terms",
    )(index, factors, proj_sum, fc_sum, swap)


def lane_maps(own, devices):
    maps = []
    for size in (own, 2 * own):
        column = np.arange(size * devices)
        maps.append(jnp.asarray(column[None, :] % size == np.arange(size)[:, None], BF16))
        maps.append(jnp.asarray(column[None, :] // size == np.arange(devices)[:, None], F32))
    return maps


def lane_pieces(sizes, own):
    pieces = []
    for at, (name, size) in enumerate(sizes):
        wide = size == 2 * own
        step = 2 * own if wide else own
        pieces += [(at, name, begin, 2 * int(wide), step) for begin in range(0, size, step)]
    return pieces


VECTOR_ROWS = ("ln1_gain", "ln1_bias", "out_bias", "ln2_gain", "ln2_bias", "proj_bias")


def unpack_kernel(
    sizes, own, packed_ref, place_a, owner_a, place_b, owner_b, vec_ref, fcb_ref, qkvb_ref
):
    maps = (place_a, owner_a, place_b, owner_b)
    vec_ref[...] = jnp.zeros_like(vec_ref)
    width = vec_ref.shape[1]
    for at, name, begin, which, size in lane_pieces(sizes, own):
        spread = dot(packed_ref[at][:, begin : begin + size], maps[which][...])
        full = jnp.sum(spread * maps[which + 1][...], axis=0, keepdims=True)
        if name == "fc_bias":
            fcb_ref[:, begin // own * width : (begin // own + 1) * width] = full
        elif name == "qv_bias":
            qkvb_ref[:, :width] = full[:, :width]
            qkvb_ref[:, width : 2 * width] = jnp.zeros((1, width), F32)
            qkvb_ref[:, 2 * width :] = full[:, width:]
        else:
            row = VECTOR_ROWS.index(name)
            vec_ref[row : row + 1, :] = full


def unpack(packed, sizes):
    devices = packed.shape[1]
    size = dict(sizes)
    own = size["ln1_gain"]
    width = own * devices
    return pl.pallas_call(
        functools.partial(unpack_kernel, sizes, own),
        out_shape=[
            jax.ShapeDtypeStruct((8, width), F32),
            jax.ShapeDtypeStruct((1, size["fc_bias"] * devices), F32),
            jax.ShapeDtypeStruct((1, 3 * width), F32),
        ],
        compiler_params=pltpu.CompilerParams(vmem_limit_bytes=VMEM_LIMIT),
        name="vectors_unpack",
    )(packed, *lane_maps(own, devices))


def pack(rows, sizes, devices, maps, out_ref):
    out_ref[...] = jnp.zeros_like(out_ref)
    width = rows["ln1_gain"].shape[1]
    own = width // devices
    pieces = lane_pieces(sizes, own)
    for which in sorted({piece[3] for piece in pieces}):
        group = [piece for piece in pieces if piece[3] == which]
        stack = []
        for _, name, begin, _, size in group:
            span = size * devices
            first = begin // size * span
            stack.append((rows[name][:, first : first + span] * maps[which + 1][...]).astype(BF16))
        done = dot_nt(jnp.concatenate(stack, axis=0), maps[which][...]).astype(BF16)
        for i, (at, _, begin, _, size) in enumerate(group):
            out_ref[at, :, begin : begin + size] = done[i * devices : (i + 1) * devices]


def join_kernel(*refs):
    out_ref = refs[-1]
    out_ref[...] = jnp.zeros_like(out_ref)
    for at, ref in enumerate(refs[:-1]):
        out_ref[at : at + 1, : ref.shape[0]] = ref[...].astype(F32).reshape(1, ref.shape[0])


def join(vectors):
    return pl.pallas_call(
        join_kernel,
        out_shape=jax.ShapeDtypeStruct((len(vectors), LANES), F32),
        name="vectors_join",
    )(*vectors)


def part_kernel(joined_ref, *refs):
    for at, ref in enumerate(refs):
        ref[...] = joined_ref[at, : ref.shape[0]]


def part(joined, sizes):
    return pl.pallas_call(
        part_kernel,
        out_shape=[jax.ShapeDtypeStruct((size,), F32) for _, size in sizes],
        name="vectors_part",
    )(joined)


def step_on_sequence(
    near_pieces, far, vectors, tokens, cotangent, slots, count, answer_start, devices, sizes, comm
):
    vec, fc_bias, qkv_bias = vectors
    seq_len, width = tokens.shape
    info = jnp.stack([slots[0], count])

    qkv_first, near = first_forward(
        comm.core, tokens, near_pieces, comm.near_orders, vec, qkv_bias
    )
    mixed_hidden, lse_hidden = attend(info, qkv_first)
    late = QUESTION + lax.iota(jnp.int32, seq_len - QUESTION)
    upstream_low = jnp.where(
        (late >= answer_start)[:, None], cotangent[QUESTION:], jnp.zeros((), BF16)
    )
    tokens32 = tokens.astype(F32)
    weights = (near, after(far, mixed_hidden, upstream_low, tokens32))
    lse, *saved, qkv, mixed_low, hidden = thoughts_forward(
        info, tokens, tokens32, qkv_first, mixed_hidden, lse_hidden, weights, vec, fc_bias, qkv_bias
    )
    output, normed_low, second_low, act_low, pre_grad, resid_grad, mixed_grad, sums = feed(
        hidden, mixed_low, upstream_low, weights, vec, fc_bias
    )

    proj_grad, *halves = comm.far_terms(act_low, upstream_low, second_low, pre_grad)
    proj_half = comm.early(proj_grad)
    fc_going = comm.scatter(halves, "zyxc")
    sent = go_after([fc_going])
    row_sums, factors, mixed_grad, resid_grad = thoughts_back(
        info,
        hidden,
        qkv,
        mixed_low,
        after(lse, *sent),
        saved,
        weights,
        vec,
        mixed_grad,
        resid_grad,
    )
    join_after([fc_going], row_sums)
    spread = comm.factors(factors)
    sent = go_after([fc_going, spread])
    lse, back_grad = after((lse, mixed_grad), *sent)
    qkv_grad = attend_back(qkv, mixed_low, lse, back_grad)
    join_after([fc_going, spread], qkv_grad)
    proj_half = after(proj_half, qkv_grad)
    proj_going = comm.early_end(proj_half)
    sent = (*go_after([fc_going, spread]), proj_half)
    *terms, packed = near_terms(
        comm.core,
        after(normed_low, *sent),
        qkv_grad,
        mixed_low,
        resid_grad,
        near,
        vec,
        sums,
        row_sums,
        sizes,
        comm.chips("zxyc"),
        comm.chips("zyxc"),
    )
    first = comm.scatter(terms[:2], "zxyc")
    rest = comm.scatter(terms[2:], "zyxc")
    vectors_going = comm.scatter_vectors(packed)

    join_after([fc_going, spread], packed)

    going = [first, rest, vectors_going]
    sent = go_after(going, fc_going.got, spread.buf)
    sent += go_after([fc_going, spread], *sent)
    join_after(going, *sent)
    sent = go_after(going)
    input_grad = first_back(info, hidden, after(qkv_grad, *sent), resid_grad, weights, vec)
    going += [fc_going, spread]
    join_after(going, input_grad)
    proj_g = fc_g = None
    while any(swap.todo for swap in going) or proj_g is None:
        group = [swap for swap in going if swap.todo]
        sent = go_after(group)
        done = sent
        if proj_g is None and fc_going not in group and spread not in group:
            factors, fc_sum = after((spread.finish(), fc_going.finish()), *sent)
            proj_g, fc_g = comm.terms(factors, proj_going, fc_sum)
            done = (proj_g, fc_g)
        join_after(group, *done)
    return (
        output,
        input_grad,
        first.finish(),
        rest.finish(),
        proj_g,
        fc_g,
        vectors_going.finish(),
    )


SMALL = ("ln1_gain", "ln1_bias", "qv_bias", "out_bias", "ln2_gain", "ln2_bias", "fc_bias", "proj_bias")


def on_device(
    links,
    tokens,
    ln1_gain,
    ln1_bias,
    qkv_weight,
    qv_bias,
    out_weight,
    out_bias,
    ln2_gain,
    ln2_bias,
    fc_weight,
    fc_bias,
    proj_weight,
    proj_bias,
    cotangent,
    thought_slots,
    thought_count,
    answer_start,
):
    devices = links.sizes["dp"] * links.sizes["fsdp"]
    small_shards = dict(
        ln1_gain=ln1_gain,
        ln1_bias=ln1_bias,
        qv_bias=qv_bias,
        out_bias=out_bias,
        ln2_gain=ln2_gain,
        ln2_bias=ln2_bias,
        fc_bias=fc_bias,
        proj_bias=proj_bias,
    )
    sizes = tuple((n, small_shards[n].shape[0]) for n in SMALL)
    own, width = out_weight.shape
    blocks = proj_weight.shape[0] // own
    both = ("dp", "fsdp")

    far_shard = join_far(fc_weight, proj_weight, out_weight)
    far = lax.all_gather(far_shard, both, axis=1, tiled=True)

    packed = join([small_shards[n] for n in SMALL]).astype(BF16)
    small = links.gather(packed, "zxyc", axis=0).reshape(devices, len(sizes), LANES)
    half = width // 2
    near_pieces = []
    near_texts = ("zxyc", "zyxc")
    for side, text in enumerate(near_texts):
        part_columns = [
            qkv_weight[:, i * width + side * half : i * width + (side + 1) * half] for i in range(3)
        ]
        ring = Gather(links, jnp.stack(part_columns)[None], text)
        near_pieces += ring.last()

    class Comm:
        chips = links.chips
        near_orders = [links.spots(text) for text in near_texts]
        core = (lax.axis_index("fsdp") % 2)[None].astype(jnp.int32)

        @staticmethod
        def far_terms(act_low, upstream_low, second_low, pre_grad):
            sizes_here = links.sizes["dp"], links.sizes["fsdp"]
            return far_terms(
                Comm.core,
                act_low,
                upstream_low,
                second_low,
                pre_grad,
                *sizes_here,
                links.chips("zyxc"),
            )

        @staticmethod
        def early(value):
            return lax.psum_scatter(
                value.reshape(-1, width), "fsdp", scatter_dimension=0, tiled=True
            )

        @staticmethod
        def early_end(value):
            value = lax.psum_scatter(value, "dp", scatter_dimension=0, tiled=True)
            return value.reshape(blocks, own, width)

        @staticmethod
        def scatter(halves, text):
            return links.scatter(tuple(halves), text)

        @staticmethod
        def factors(rows):
            return Gather(links, rows, "zyxc")

        @staticmethod
        def scatter_vectors(value):
            return links.scatter(value.transpose(1, 0, 2), "zxyc")

        @staticmethod
        def terms(factors, proj_sum, fc_sum):
            index = lax.axis_index(both)[None].astype(jnp.int32)
            factors = factors.reshape(devices, FACTOR_ROWS, width).transpose(1, 0, 2)
            return row_terms(index, factors, proj_sum, fc_sum)

    output, input_grad, first, rest, proj_g, fc_g, vector_sums = step_on_sequence(
        near_pieces,
        far,
        unpack(small.transpose(1, 0, 2), sizes),
        tokens[0],
        cotangent[0],
        thought_slots[0],
        thought_count[0],
        answer_start[0],
        devices,
        sizes,
        Comm,
    )
    proj_g = proj_g.reshape(blocks * own, width)
    qkv_g = jnp.concatenate([first[0], first[1], rest[0]], axis=1)
    out_g = rest[1]
    owned = dict(zip(SMALL, part(vector_sums, sizes)))
    return (
        output[None],
        input_grad[None],
        owned["ln1_gain"],
        owned["ln1_bias"],
        qkv_g,
        owned["qv_bias"],
        out_g,
        owned["out_bias"],
        owned["ln2_gain"],
        owned["ln2_bias"],
        fc_g,
        owned["fc_bias"],
        proj_g,
        owned["proj_bias"],
    )


def solution(mesh):
    links = Links({name: mesh.shape[name] for name in ("dp", "fsdp")})
    both = ("dp", "fsdp")
    cube, matrix, vector = P(both, None, None), P(both, None), P(both)
    weight_specs = (
        vector,
        vector,
        matrix,
        vector,
        matrix,
        vector,
        vector,
        vector,
        matrix,
        vector,
        matrix,
        vector,
    )

    def per_device(*args):
        return on_device(links, *args)

    return jax.shard_map(
        per_device,
        mesh=mesh,
        in_specs=(cube,) + weight_specs + (cube, matrix, vector, vector),
        out_specs=(cube, cube) + weight_specs,
        check_vma=False,
    )
```

```python
import functools
import math

import jax
import jax.numpy as jnp
import numpy as np
from jax import lax
from jax.experimental import pallas as pl
from jax.experimental.pallas import tpu as pltpu
from jax.sharding import PartitionSpec as P

HD = 64
THOUGHTS = 2
PREFIX = 384
QUESTION = 256
SCALE = 0.125
EPSILON = 1e-05
BLOCK = 256
HEAD_ROWS = 16
WINDOW = 32
LANES = 128
FACTOR_ROWS = 24
PAIR = 2 * HD
NEG = -1e30

F32 = jnp.float32
BF16 = jnp.bfloat16
VMEM_LIMIT = 56 * 1024 * 1024


def cost(microseconds):
    return pl.CostEstimate(
        flops=int(microseconds * 1.15e9),
        bytes_accessed=int(microseconds * 3.6e6),
        transcendentals=0,
    )


def dot(a, b):
    return lax.dot_general(a, b, (((1,), (0,)), ((), ())), preferred_element_type=F32)


def dot_nt(a, b):
    return lax.dot_general(a, b, (((1,), (1,)), ((), ())), preferred_element_type=F32)


def dot_tn(a, b):
    return lax.dot_general(a, b, (((0,), (0,)), ((), ())), preferred_element_type=F32)


def bits_of(size):
    return [1 << i for i in reversed(range(int(math.log2(size))))]


class Links:
    def __init__(self, sizes):
        self.sizes = sizes
        self.canon = [("dp", b) for b in bits_of(sizes["dp"])] + [
            ("fsdp", b) for b in bits_of(sizes["fsdp"])
        ]
        dp_bits = [("dp", b) for b in bits_of(sizes["dp"])]
        f_bits = [("fsdp", b) for b in bits_of(sizes["fsdp"])]
        self.groups = {"x": dp_bits[-1:], "y": dp_bits[:-1], "z": f_bits[:-1], "c": f_bits[-1:]}

    def order(self, text):
        out = []
        for letter in text:
            out += self.groups[letter]
        return out

    def swap(self, value, stage):
        axis, bit = stage
        return lax.ppermute(value, axis, [(i, i ^ bit) for i in range(self.sizes[axis])])

    def mine(self, stage):
        axis, bit = stage
        return (lax.axis_index(axis) & bit) != 0

    def gather(self, shard, text, axis=0):
        return Gather(self, shard, text, axis).finish()

    def chips(self, text):
        stages = list(reversed(self.order(text)))[1:]
        rest = [c for c in self.canon if c in stages]
        order = []
        for spot in range(1 << len(stages)):
            chip = 0
            for at, stage in enumerate(stages):
                if spot & (1 << (len(stages) - 1 - at)):
                    chip |= 1 << (len(rest) - 1 - rest.index(stage))
            order.append(chip)
        return order

    def spots(self, text):
        stages = [c for c in reversed(self.order(text)) if c not in self.groups["c"]]
        rest = [c for c in self.canon if c in stages]
        order = []
        for spot in range(1 << len(stages)):
            chip = 0
            for at, stage in enumerate(stages):
                if spot & (1 << (len(stages) - 1 - at)):
                    chip |= 1 << (len(rest) - 1 - rest.index(stage))
            order.append(chip)
        return order

    def scatter(self, value, text):
        return Scatter(self, value, text)


class Gather:
    def __init__(self, links, shard, text, axis=0):
        self.links = links
        self.shape = shard.shape
        self.axis = axis
        self.todo = links.order(text)
        self.done = []
        self.buf = shard
        self.got = None

    def go(self):
        self.add()
        self.stage = self.todo.pop(0)
        self.got = self.links.swap(self.buf, self.stage)
        return self.buf

    def add(self):
        if self.got is not None:
            canon = self.links.canon
            place = sum(1 for d in self.done if canon.index(d) < canon.index(self.stage))
            high = self.links.mine(self.stage)
            pair = [jnp.where(high, self.got, self.buf), jnp.where(high, self.buf, self.got)]
            self.buf = jnp.stack(pair, axis=self.axis + place)
            self.done.append(self.stage)
            self.got = None
        return self.buf

    def hold(self, *deps):
        self.buf = after(self.buf, *deps)

    def join(self, *deps):
        self.got = after(self.got, *deps)
        self.add()

    def last(self):
        for stage in self.todo:
            if self.got is not None:
                high = self.links.mine(self.stage)
                pair = [jnp.where(high, self.got, self.buf), jnp.where(high, self.buf, self.got)]
                self.buf = jnp.concatenate(pair, axis=0)
            self.stage = stage
            self.got = self.links.swap(self.buf, stage)
        return [self.buf, self.got]

    def finish(self):
        while self.todo:
            self.go()
        self.add()
        shape = self.shape
        return self.buf.reshape(shape[: self.axis] + (-1,) + shape[self.axis + 1 :])


class Scatter:
    def __init__(self, links, value, text):
        self.links = links
        self.left = list(links.canon)
        self.todo = list(reversed(links.order(text)))
        self.got = None
        self.split = False
        if isinstance(value, tuple):
            self.split = True
            self.left = self.todo[1:]
            shape = (2,) * len(self.left) + value[0].shape[1:]
            self.keep, self.buf = (v.reshape(shape) for v in value)
        else:
            self.buf = value.reshape((2,) * len(self.left) + value.shape[1:])

    def go(self):
        stage = self.todo.pop(0)
        if self.split:
            self.split = False
            sent = self.buf
        else:
            place = self.left.index(stage)
            self.left.remove(stage)
            high = self.links.mine(stage).astype(jnp.int32)
            parts = [self.buf] if self.got is None else [self.keep, self.got]

            def half(side):
                cut = [lax.dynamic_index_in_dim(p, side, place, keepdims=False) for p in parts]
                return cut[0] if len(cut) == 1 else cut[0].astype(F32) + cut[1].astype(F32)

            sent = half(1 - high).astype(BF16)
            self.keep = half(high)
        self.got = self.links.swap(sent, stage)
        return sent

    def hold(self, *deps):
        if self.got is None:
            self.buf = after(self.buf, *deps)
        else:
            self.got = after(self.got, *deps)

    def join(self, *deps):
        self.got = after(self.got, *deps)

    def finish(self):
        return self.keep.astype(F32) + self.got.astype(F32)


def join_after(swaps, *deps):
    for swap in swaps:
        swap.join(*deps)


def go_after(swaps, *deps):
    for swap in swaps:
        swap.hold(*deps)
    return tuple(swap.go() for swap in swaps)


def after(value, *deps):
    return lax.optimization_barrier((value, deps))[0]


def attend_kernel(info_ref, q_ref, k_ref, v_ref, o_ref, lse_ref):
    seq_len = q_ref.shape[0]
    slot = info_ref[0]
    keys = k_ref[...]
    values_t = v_ref[...].T
    lane = lax.broadcasted_iota(jnp.int32, (BLOCK, PAIR), 1)
    key_pos = lax.broadcasted_iota(jnp.int32, (BLOCK, BLOCK), 0)
    row_pos = lax.broadcasted_iota(jnp.int32, (BLOCK, BLOCK), 1)
    causal = key_pos <= row_pos
    middle_pos = QUESTION + lax.broadcasted_iota(jnp.int32, (PREFIX - QUESTION, BLOCK), 0)
    is_slot = (middle_pos >= slot) & (middle_pos < slot + THOUGHTS)

    def hide(scores):
        if scores.shape[0] <= QUESTION:
            return scores
        middle = jnp.where(is_slot, NEG, scores[QUESTION:PREFIX])
        return jnp.concatenate([scores[:QUESTION], middle, scores[PREFIX:]], axis=0)

    for begin in range(0, seq_len, BLOCK):
        end = begin + BLOCK
        queries = q_ref[begin:end, :] * jnp.asarray(SCALE, BF16)
        parts = []
        for head in range(2):
            own = jnp.where((lane >= HD) == bool(head), queries, jnp.zeros_like(queries))
            scores = dot_nt(keys[:end], own)
            last = jnp.where(causal, scores[begin:], NEG)
            if begin:
                last = jnp.concatenate([scores[:begin], last], axis=0)
            scores = hide(last)
            peak = jnp.max(scores, axis=0, keepdims=True)
            expo = jnp.exp(scores - peak)
            total = jnp.sum(expo, axis=0, keepdims=True)
            mixed = dot(values_t[head * HD : (head + 1) * HD, :end], expo.astype(BF16))
            parts.append(mixed / total)
            lse_ref[pl.ds(2 * pl.program_id(0) + head, 1), begin:end] = peak + jnp.log(total)
        o_ref[begin:end, :] = jnp.concatenate(parts, axis=0).T.astype(BF16)


def attend(info, qkv):
    _, seq_len, width = qkv.shape
    pairs = width // PAIR

    def columns(i):
        return pl.BlockSpec((None, seq_len, PAIR), lambda g, i=i: (i, 0, g))

    return pl.pallas_call(
        attend_kernel,
        grid=(pairs,),
        in_specs=[
            pl.BlockSpec(memory_space=pltpu.SMEM),
            *(columns(i) for i in range(3)),
        ],
        out_specs=[
            pl.BlockSpec((seq_len, PAIR), lambda g: (0, g)),
            pl.BlockSpec((HEAD_ROWS, seq_len), lambda g: (0, 0)),
        ],
        out_shape=[
            jax.ShapeDtypeStruct((seq_len, width), BF16),
            jax.ShapeDtypeStruct((HEAD_ROWS, seq_len), F32),
        ],
        compiler_params=pltpu.CompilerParams(vmem_limit_bytes=VMEM_LIMIT),
        cost_estimate=cost(2.0),
        name="attention_forward",
    )(info, qkv, qkv, qkv)


def attend_back_kernel(
    q_ref, k_ref, v_ref, o_ref, lse_ref, g_ref, out_ref, dk_acc, dv_acc
):
    seq_len = q_ref.shape[0]
    pair = pl.program_id(0)
    first_row = seq_len - g_ref.shape[0]
    keys = k_ref[...]
    values = v_ref[...]
    keys_t = keys.T
    lane = lax.broadcasted_iota(jnp.int32, (BLOCK, PAIR), 1)
    key_pos = lax.broadcasted_iota(jnp.int32, (BLOCK, BLOCK), 0)
    row_pos = lax.broadcasted_iota(jnp.int32, (BLOCK, BLOCK), 1)
    causal = key_pos <= row_pos
    dk_acc[...] = jnp.zeros_like(dk_acc)
    dv_acc[...] = jnp.zeros_like(dv_acc)
    for begin in range(first_row, seq_len, BLOCK):
        end = begin + BLOCK
        local = begin - first_row
        queries = q_ref[begin:end, :] * jnp.asarray(SCALE, BF16)
        grads = g_ref[local : local + BLOCK, :]
        product_t = (grads.astype(F32) * o_ref[begin:end, :].astype(F32)).T
        owns, own_grads, probs_low, score_grads, parts = [], [], [], [], []
        for head in range(2):
            chosen = (lane >= HD) == bool(head)
            own = jnp.where(chosen, queries, jnp.zeros_like(queries))
            own_grad = jnp.where(chosen, grads, jnp.zeros_like(grads))
            rows_here = slice(head * HD, (head + 1) * HD)
            delta = jnp.sum(product_t[rows_here], axis=0, keepdims=True)
            lse = lse_ref[pl.ds(2 * pair + head, 1), begin:end]
            scores = dot_nt(keys[:end], own)
            last = jnp.where(causal, scores[begin:], NEG)
            scores = jnp.concatenate([scores[:begin], last], axis=0) if begin else last
            probs = jnp.exp(scores - lse)
            prob_grad = dot_nt(values[:end], own_grad)
            score_grad = (probs * (prob_grad - delta)).astype(BF16)
            parts.append(dot(keys_t[rows_here, :end], score_grad))
            owns.append(own)
            own_grads.append(own_grad)
            probs_low.append(probs.astype(BF16))
            score_grads.append(score_grad)
        dv_acc[:end, :] += dot(
            jnp.concatenate(probs_low, axis=1), jnp.concatenate(own_grads, axis=0)
        )
        dk_acc[:end, :] += dot(jnp.concatenate(score_grads, axis=1), jnp.concatenate(owns, axis=0))
        mine = jnp.concatenate(parts, axis=0).T * SCALE
        out_ref[0, begin:end, :] = mine.astype(BF16)
    out_ref[0, :first_row, :] = jnp.zeros((first_row, PAIR), BF16)
    out_ref[1] = dk_acc[...].astype(BF16)
    out_ref[2] = dv_acc[...].astype(BF16)


def attend_back(qkv, mixed_low, lse, mixed_grad):
    _, seq_len, width = qkv.shape
    rows = mixed_grad.shape[0]

    def columns(i):
        return pl.BlockSpec((None, seq_len, PAIR), lambda g, i=i: (i, 0, g))

    late = pl.BlockSpec((rows, PAIR), lambda g: (0, g))
    return pl.pallas_call(
        attend_back_kernel,
        grid=(width // PAIR,),
        in_specs=[
            *(columns(i) for i in range(3)),
            pl.BlockSpec((seq_len, PAIR), lambda g: (0, g)),
            pl.BlockSpec((HEAD_ROWS, seq_len), lambda g: (0, 0)),
            late,
        ],
        out_specs=pl.BlockSpec((3, seq_len, PAIR), lambda g: (0, 0, g)),
        out_shape=jax.ShapeDtypeStruct((3, seq_len, width), BF16),
        scratch_shapes=[pltpu.VMEM((seq_len, PAIR), F32), pltpu.VMEM((seq_len, PAIR), F32)],
        compiler_params=pltpu.CompilerParams(vmem_limit_bytes=VMEM_LIMIT),
        cost_estimate=cost(2.17),
        name="attention_backward",
    )(qkv, qkv, qkv, mixed_low, lse, mixed_grad)


def row_norm(row, gain, bias):
    mean = jnp.mean(row, axis=-1, keepdims=True)
    centred = row - mean
    inverse = lax.rsqrt(jnp.mean(centred * centred, axis=-1, keepdims=True) + EPSILON)
    normed = centred * inverse
    return normed * gain + bias, normed, inverse


def row_norm_back(incoming, normed, inverse, gain):
    scaled = incoming * gain
    inner = (
        scaled
        - jnp.mean(scaled, axis=-1, keepdims=True)
        - normed * jnp.mean(scaled * normed, axis=-1, keepdims=True)
    )
    return inner * inverse


GELU_A = 0.7978845608028654
GELU_B = 0.044715


def gelu(pre):
    return 0.5 * pre * (1.0 + jnp.tanh(GELU_A * (pre + GELU_B * pre * pre * pre)))


def gelu_slope(pre):
    square = pre * pre
    curve = jnp.tanh(GELU_A * pre * (1.0 + GELU_B * square))
    return 0.5 * (1.0 + curve) + 0.5 * pre * (1.0 - curve * curve) * GELU_A * (
        1.0 + 3.0 * GELU_B * square
    )


def widen(row):
    return jnp.broadcast_to(row, (8, row.shape[1])).astype(BF16)


def pick(block, index):
    rows = lax.broadcasted_iota(jnp.int32, block.shape, 0)
    return jnp.sum(jnp.where(rows == index, block.astype(F32), 0.0), axis=0, keepdims=True)


def put(block, index, row):
    rows = lax.broadcasted_iota(jnp.int32, block.shape, 0)
    return jnp.where(rows == index, row.astype(block.dtype), block)


def by_head(row, heads):
    shape = (heads, row.shape[1])
    lane_head = lax.broadcasted_iota(jnp.int32, shape, 1) // HD
    return jnp.where(lane_head == lax.broadcasted_iota(jnp.int32, shape, 0), row, 0.0)


def heads_only(block):
    lane_head = lax.broadcasted_iota(jnp.int32, block.shape, 1) // HD
    own = lane_head == lax.broadcasted_iota(jnp.int32, block.shape, 0)
    return jnp.sum(jnp.where(own, block, 0.0), axis=0, keepdims=True)


def thoughts_kernel(
    info_ref,
    tok_ref,
    lse_in_ref,
    vec_ref,
    fcb_ref,
    qkvb_ref,
    near_in,
    far_in,
    qkv_in,
    mixed_in,
    hid_in,
    lse_ref,
    pre_ref,
    prob_ref,
    res_ref,
    qkv_out,
    mixed_out,
    hid_out,
    kv_ref,
    late_q_ref,
    mixed_ref,
    hid_ref,
    near_ref,
    far_ref,
    sems,
):
    width = tok_ref.shape[1]
    blocks = (far_ref.shape[0] - 1) // 2
    rows = late_q_ref.shape[0]
    ln1_gain, ln1_bias, out_bias, ln2_gain, ln2_bias, proj_bias = (
        vec_ref[i : i + 1, :] for i in range(6)
    )
    slot = info_ref[0]
    count = info_ref[1]

    loads = [
        (qkv_in.at[:, pl.ds(0, PREFIX)], kv_ref),
        (far_in.at[pl.ds(2 * blocks, 1)], far_ref.at[pl.ds(2 * blocks, 1)]),
        (far_in.at[pl.ds(0, blocks)], far_ref.at[pl.ds(0, blocks)]),
        (far_in.at[pl.ds(blocks, blocks)], far_ref.at[pl.ds(blocks, blocks)]),
        (near_in, near_ref),
        (qkv_in.at[0, pl.ds(QUESTION, rows)], late_q_ref),
        (mixed_in.at[pl.ds(QUESTION, rows)], mixed_ref),
    ]
    loads = [pltpu.make_async_copy(a, b, sems.at[i]) for i, (a, b) in enumerate(loads)]
    for copy in loads:
        copy.start()
    hid_ref[...] = tok_ref[...].astype(F32)
    hidden_row = pick(hid_ref[...], slot - 1 - QUESTION)
    loads[0].wait()
    slot_rows = []
    slot_lse = []
    for step in range(THOUGHTS + 1):
        at = slot - 1 + step
        qkv_row = pick(kv_ref[0, QUESTION:, :], at - QUESTION)
        query = by_head(qkv_row * SCALE, HEAD_ROWS).astype(BF16)
        scores = dot_nt(query, kv_ref[1])
        key_pos = lax.broadcasted_iota(jnp.int32, scores.shape, 1)
        scores = jnp.where(key_pos <= at, scores, NEG)
        peak = jnp.max(scores, axis=1, keepdims=True)
        expo = jnp.exp(scores - peak)
        total = jnp.sum(expo, axis=1, keepdims=True)
        probs = expo / total
        mixed = heads_only(dot(probs.astype(BF16), kv_ref[2]))
        if step:
            slot_rows.append(mixed)
            slot_lse.append(peak + jnp.log(total))
        if step == THOUGHTS:
            break
        prob_ref[step * HEAD_ROWS : (step + 1) * HEAD_ROWS, :] = probs
        if not step:
            loads[1].wait()
        resid = hidden_row + dot(widen(mixed), far_ref[2 * blocks])[0:1] + out_bias
        res_ref[step : step + 1, :] = resid
        second, _, _ = row_norm(resid, ln2_gain, ln2_bias)
        second = widen(second)
        if not step:
            loads[2].wait()
        acts = []
        for j in range(blocks):
            span = slice(j * width, (j + 1) * width)
            pre = dot(second, far_ref[j])[0:1] + fcb_ref[0:1, span]
            pre_ref[step : step + 1, span] = pre
            acts.append(widen(gelu(pre)))
        if not step:
            loads[3].wait()
        fed = resid + proj_bias
        for j in range(blocks):
            fed = fed + dot(acts[j], far_ref[blocks + j])[0:1]
        first, _, _ = row_norm(fed, ln1_gain, ln1_bias)
        first = widen(first)
        hidden_row = fed
        spot = jnp.where(step < count, slot + step - QUESTION, -1)
        hid_ref[...] = put(hid_ref[...], spot, fed)
        if not step:
            loads[4].wait()
        for i in range(3):
            span = slice(i * width, (i + 1) * width)
            new_row = dot(first, near_ref[i])[0:1] + qkvb_ref[0:1, span]
            kv_ref[i, QUESTION:, :] = put(kv_ref[i, QUESTION:, :], spot, new_row)
    loads[5].wait()
    loads[6].wait()
    stores = [
        pltpu.make_async_copy(
            kv_ref.at[:, pl.ds(QUESTION, PREFIX - QUESTION)],
            qkv_out.at[:, pl.ds(QUESTION, PREFIX - QUESTION)],
            sems.at[0],
        ),
        pltpu.make_async_copy(
            hid_ref, hid_out.at[pl.ds(QUESTION, PREFIX - QUESTION)], sems.at[1]
        ),
    ]
    for copy in stores:
        copy.start()

    row_pos = QUESTION + lax.broadcasted_iota(jnp.int32, (HEAD_ROWS, rows), 1)
    late_q = late_q_ref[...]
    lse = lse_in_ref[:, QUESTION:]
    scores = []
    values = []
    top = lse
    for j in range(THOUGHTS):
        local = slot + j - QUESTION
        key = by_head(pick(kv_ref[1, QUESTION:, :], local) * SCALE, HEAD_ROWS)
        values.append(pick(kv_ref[2, QUESTION:, :], local))
        score = jnp.where(row_pos >= slot + j, dot_nt(key.astype(BF16), late_q), NEG)
        scores.append(score)
        top = jnp.maximum(top, score)
    whole_sum = jnp.exp(lse - top)
    for score in scores:
        whole_sum = whole_sum + jnp.exp(score - top)
    new_lse = top + jnp.log(whole_sum)
    ones = by_head(jnp.ones((1, width), F32), HEAD_ROWS).astype(BF16)
    share = jnp.exp(lse - new_lse)
    high = share.astype(BF16)
    low = (share - high.astype(F32)).astype(BF16)
    weights = [jnp.exp(score - new_lse).astype(BF16) for score in scores]
    step_rows = PREFIX - QUESTION
    for begin in range(0, rows, step_rows):
        span = slice(begin, begin + step_rows)
        part = mixed_ref[span, :].astype(F32) * (
            dot_tn(high[:, span], ones) + dot_tn(low[:, span], ones)
        )
        for weight, value in zip(weights, values):
            part = part + dot_tn(weight[:, span], ones) * value
        if not begin:
            for j in range(THOUGHTS):
                part = put(part, slot + j - QUESTION, slot_rows[j])
        mixed_ref[span, :] = part.astype(BF16)
    stores.append(
        pltpu.make_async_copy(mixed_ref, mixed_out.at[pl.ds(QUESTION, rows)], sems.at[2])
    )
    stores[-1].start()
    lse_ref[:, :QUESTION] = lse_in_ref[:, :QUESTION]
    column = lax.broadcasted_iota(jnp.int32, (HEAD_ROWS, step_rows), 1)
    middle = new_lse[:, :step_rows]
    for j in range(THOUGHTS):
        middle = jnp.where(column == slot + j - QUESTION, slot_lse[j], middle)
    lse_ref[:, QUESTION:PREFIX] = middle
    lse_ref[:, PREFIX:] = new_lse[:, step_rows:]
    for copy in stores:
        copy.wait()


def whole(array):
    zeros = (0,) * array.ndim
    return pl.BlockSpec(array.shape, lambda i, zeros=zeros: zeros)


def fc_spec(far):
    return pl.BlockSpec((far.shape[0] // 2,) + far.shape[1:], lambda i: (0, 0, 0))


def proj_spec(far):
    return pl.BlockSpec((far.shape[0] // 2,) + far.shape[1:], lambda i: (1, 0, 0))


def out_spec(far):
    last = far.shape[0] - 1
    return pl.BlockSpec((1,) + far.shape[1:], lambda i: (last, 0, 0))


def thoughts_forward(info, tokens, tokens32, qkv, mixed_low, lse, weights, vec, fc_bias, qkv_bias):
    near, far = weights
    seq_len, width = tokens.shape
    rows = seq_len - QUESTION
    middle = PREFIX - QUESTION
    anywhere = pl.BlockSpec(memory_space=pl.ANY)
    out_shape = [
        jax.ShapeDtypeStruct(lse.shape, F32),
        jax.ShapeDtypeStruct((8, fc_bias.shape[1]), F32),
        jax.ShapeDtypeStruct((THOUGHTS * HEAD_ROWS, PREFIX), F32),
        jax.ShapeDtypeStruct((8, width), F32),
        jax.ShapeDtypeStruct(qkv.shape, BF16),
        jax.ShapeDtypeStruct(mixed_low.shape, BF16),
        jax.ShapeDtypeStruct(tokens32.shape, F32),
    ]
    return pl.pallas_call(
        thoughts_kernel,
        grid=(1,),
        in_specs=[
            pl.BlockSpec(memory_space=pltpu.SMEM),
            pl.BlockSpec((middle, width), lambda i: (QUESTION // middle, 0)),
            whole(lse),
            whole(vec),
            whole(fc_bias),
            whole(qkv_bias),
            *[anywhere] * 5,
        ],
        out_specs=[*(whole(x) for x in out_shape[:4]), *[anywhere] * 3],
        out_shape=out_shape,
        input_output_aliases={8: 4, 9: 5, 10: 6},
        scratch_shapes=[
            pltpu.VMEM((3, PREFIX, width), BF16),
            pltpu.VMEM((rows, width), BF16),
            pltpu.VMEM((rows, width), BF16),
            pltpu.VMEM((middle, width), F32),
            pltpu.VMEM(near.shape, BF16),
            pltpu.VMEM(far.shape, BF16),
            pltpu.SemaphoreType.DMA((7,)),
        ],
        compiler_params=pltpu.CompilerParams(vmem_limit_bytes=VMEM_LIMIT),
        cost_estimate=cost(2),
        name="thought_rows_forward",
    )(info, tokens, lse, vec, fc_bias, qkv_bias, near, far, qkv, mixed_low, tokens32)


def thoughts_back_kernel(
    info_ref,
    hid_ref,
    qkv_ref,
    lse_ref,
    pre_ref,
    prob_ref,
    res_ref,
    vec_ref,
    near_in,
    far_in,
    qkv_in,
    mixed_in,
    mg_in,
    rg_in,
    sum_ref,
    fac_ref,
    mg_out,
    rg_out,
    mg_ref,
    rg_win,
    late_q_ref,
    mixed_ref,
    near_ref,
    far_ref,
    sems,
):
    width = hid_ref.shape[1]
    blocks = (far_ref.shape[0] - 1) // 2
    units = blocks * width
    rows = mg_ref.shape[0]
    ln1_gain, ln1_bias, _, ln2_gain, ln2_bias, _ = (vec_ref[i : i + 1, :] for i in range(6))
    slot = info_ref[0]
    count = info_ref[1]
    base = pl.multiple_of(((slot - 1 - QUESTION) // 16) * 16, 16)

    def window(ref):
        return ref.at[pl.ds(base, WINDOW)]

    loads = [
        (mg_in, mg_ref),
        (mixed_in.at[pl.ds(QUESTION, rows)], mixed_ref),
        (qkv_in.at[0, pl.ds(QUESTION, rows)], late_q_ref),
        (window(rg_in), rg_win),
        (near_in, near_ref),
        (far_in.at[pl.ds(blocks, blocks)], far_ref.at[pl.ds(blocks, blocks)]),
        (far_in.at[pl.ds(0, blocks)], far_ref.at[pl.ds(0, blocks)]),
        (far_in.at[pl.ds(2 * blocks, 1)], far_ref.at[pl.ds(2 * blocks, 1)]),
    ]
    loads = [pltpu.make_async_copy(a, b, sems.at[i]) for i, (a, b) in enumerate(loads)]
    for copy in loads:
        copy.start()
    for copy in loads[:4]:
        copy.wait()

    late_q = late_q_ref[...]
    mixed_grad = mg_ref[...]
    product = mixed_grad.astype(F32) * mixed_ref[...].astype(F32)
    high = product.astype(BF16)
    ones = by_head(jnp.ones((1, width), F32), HEAD_ROWS).astype(BF16)
    delta = dot_nt(ones, high) + dot_nt(ones, (product - high.astype(F32)).astype(BF16))
    lse = lse_ref[:, QUESTION:]

    def columns(block, scale):
        rows_here = [
            by_head(pick(block, slot + j - QUESTION) * scale, HEAD_ROWS) for j in range(THOUGHTS)
        ]
        return jnp.concatenate(rows_here, axis=0).astype(BF16)

    def twice(block):
        return jnp.concatenate([block] * THOUGHTS, axis=0)

    slot_pos = jnp.concatenate(
        [jnp.full((HEAD_ROWS, rows), QUESTION - j, jnp.int32) for j in range(THOUGHTS)], axis=0
    )
    seen = slot_pos + lax.broadcasted_iota(jnp.int32, slot_pos.shape, 1) >= slot
    scores = dot_nt(columns(qkv_ref[1, QUESTION:PREFIX, :], SCALE), late_q)
    probs = jnp.where(seen, jnp.exp(jnp.minimum(scores - twice(lse), 0.0)), 0.0)
    prob_grad = dot_nt(columns(qkv_ref[2, QUESTION:PREFIX, :], 1.0), mixed_grad)
    score_grad = (probs * (prob_grad - twice(delta))).astype(BF16)
    slot_keys = dot(score_grad, late_q)
    slot_values = dot(probs.astype(BF16), mixed_grad)
    slot_grads = []
    for j in range(THOUGHTS):
        span = slice(j * HEAD_ROWS, (j + 1) * HEAD_ROWS)
        slot_grads.append((heads_only(slot_keys[span]) * SCALE, heads_only(slot_values[span])))

    def through_first(at, query_grad, key_grad, value_grad):
        first_grad = (
            dot_nt(widen(query_grad), near_ref[0])
            + dot_nt(widen(key_grad), near_ref[1])
            + dot_nt(widen(value_grad), near_ref[2])
        )[0:1]
        _, normed, inverse = row_norm(hid_ref[pl.ds(at - QUESTION, 1), :], ln1_gain, ln1_bias)
        return row_norm_back(first_grad, normed, inverse, ln1_gain)

    sum_ref[...] = jnp.zeros_like(sum_ref)
    fac = {}
    loads[4].wait()
    carried = through_first(slot + 1, jnp.zeros((1, width), F32), *slot_grads[1])
    for copy in loads[5:]:
        copy.wait()
    for step in reversed(range(THOUGHTS)):
        at = slot - 1 + step
        upstream = jnp.where(step < count, carried, 0.0)
        low = widen(upstream)
        act_grad = jnp.concatenate([dot_nt(low, far_ref[blocks + j])[0:1] for j in range(blocks)], axis=1)
        pre = pre_ref[step : step + 1, :]
        pre_grad = (act_grad * gelu_slope(pre)).astype(BF16).astype(F32)
        second_grad = jnp.zeros((1, width), F32)
        for j in range(blocks):
            piece = pre_grad[:, j * width : (j + 1) * width]
            second_grad = second_grad + dot_nt(widen(piece), far_ref[j])[0:1]
        second, normed, inverse = row_norm(res_ref[step : step + 1, :], ln2_gain, ln2_bias)
        resid_grad = upstream + row_norm_back(second_grad, normed, inverse, ln2_gain)
        mixed_row = dot_nt(widen(resid_grad), far_ref[2 * blocks])[0:1]
        local = at - QUESTION
        rg_win[...] = put(rg_win[...], local - base, resid_grad)
        mg_ref[: PREFIX - QUESTION, :] = put(mg_ref[: PREFIX - QUESTION, :], local, mixed_row)
        up_low = upstream.astype(BF16).astype(F32)
        sum_ref[0:1, :units] += pre_grad
        sum_ref[1:2, :width] += second_grad * normed
        sum_ref[2:3, :width] += second_grad
        sum_ref[3:4, :width] += up_low
        sum_ref[4:5, :width] += resid_grad.astype(BF16).astype(F32)
        act = gelu(pre)
        rows_here = [act[:, j * width : (j + 1) * width] for j in range(blocks)]
        rows_here += [up_low, second]
        rows_here += [pre_grad[:, j * width : (j + 1) * width] for j in range(blocks)]
        for j, row in enumerate(rows_here):
            fac[THOUGHTS * j + step] = row
        if step:
            own_grad = by_head(mixed_row, HEAD_ROWS).astype(BF16)
            query = by_head(pick(qkv_ref[0, QUESTION:PREFIX, :], local) * SCALE, HEAD_ROWS)
            query = query.astype(BF16)
            probs = prob_ref[step * HEAD_ROWS : (step + 1) * HEAD_ROWS, :]
            prob_grad = dot_nt(own_grad, qkv_ref[2])
            own_delta = jnp.sum(prob_grad * probs, axis=1, keepdims=True)
            score_grad = (probs * (prob_grad - own_delta)).astype(BF16)
            query_grad = heads_only(dot(score_grad, qkv_ref[1])) * SCALE
            key_grad, value_grad = slot_grads[0]
            own = lax.broadcasted_iota(jnp.int32, probs.shape, 1) == at
            score_own = jnp.sum(jnp.where(own, score_grad.astype(F32), 0.0), axis=1, keepdims=True)
            prob_own = jnp.sum(jnp.where(own, probs, 0.0), axis=1, keepdims=True)
            key_grad += jnp.sum(score_own * query.astype(F32), axis=0, keepdims=True)
            value_grad += jnp.sum(prob_own * own_grad.astype(F32), axis=0, keepdims=True)
            carried = resid_grad + through_first(at, query_grad, key_grad, value_grad)
    padding = [jnp.zeros((1, width), F32)] * (fac_ref.shape[0] - len(fac))
    fac_ref[...] = jnp.concatenate([fac[i] for i in range(len(fac))] + padding, axis=0).astype(BF16)
    stores = [
        pltpu.make_async_copy(mg_ref, mg_out, sems.at[0]),
        pltpu.make_async_copy(rg_win, window(rg_out), sems.at[1]),
    ]
    for copy in stores:
        copy.start()
    for copy in stores:
        copy.wait()


SUM_ROWS = ("fc_bias", "ln2_gain", "ln2_bias", "proj_bias", "out_bias")


def thoughts_back(info, hidden, qkv, mixed_low, lse, saved, weights, vec, mixed_grad, resid_grad):
    near, far = weights
    width = hidden.shape[1]
    units = far.shape[0] // 2 * width
    middle = PREFIX - QUESTION
    anywhere = pl.BlockSpec(memory_space=pl.ANY)
    out_shape = [
        jax.ShapeDtypeStruct((8, units), F32),
        jax.ShapeDtypeStruct((FACTOR_ROWS, width), BF16),
        jax.ShapeDtypeStruct(mixed_grad.shape, BF16),
        jax.ShapeDtypeStruct(resid_grad.shape, F32),
    ]
    return pl.pallas_call(
        thoughts_back_kernel,
        grid=(1,),
        in_specs=[
            pl.BlockSpec(memory_space=pltpu.SMEM),
            pl.BlockSpec((middle, width), lambda i: (QUESTION // middle, 0)),
            pl.BlockSpec((3, PREFIX, width), lambda i: (0, 0, 0)),
            whole(lse),
            *(whole(x) for x in saved),
            whole(vec),
            *[anywhere] * 6,
        ],
        out_specs=[whole(out_shape[0]), whole(out_shape[1]), anywhere, anywhere],
        out_shape=out_shape,
        input_output_aliases={12: 2, 13: 3},
        scratch_shapes=[
            pltpu.VMEM(mixed_grad.shape, BF16),
            pltpu.VMEM((WINDOW, width), F32),
            pltpu.VMEM(mixed_grad.shape, BF16),
            pltpu.VMEM(mixed_grad.shape, BF16),
            pltpu.VMEM(near.shape, BF16),
            pltpu.VMEM(far.shape, BF16),
            pltpu.SemaphoreType.DMA((8,)),
        ],
        compiler_params=pltpu.CompilerParams(vmem_limit_bytes=VMEM_LIMIT),
        cost_estimate=cost(2.0),
        name="thought_rows_backward",
    )(
        info,
        hidden,
        qkv,
        lse,
        *saved,
        vec,
        near,
        far,
        qkv,
        mixed_low,
        mixed_grad,
        resid_grad,
    )


def feed_kernel(
    hid_ref, mixed_ref, up_ref, wout_ref, wfc_ref, wproj_ref, vec_ref, fcb_ref, out_ref, first_ref,
    second_ref, act_ref, pg_ref, rg_ref, mg_ref, sum_ref, slope_ref,
):
    width = hid_ref.shape[1]
    blocks = wfc_ref.shape[0]
    step = pl.program_id(0)
    skip = QUESTION // BLOCK
    out_bias, ln2_gain, ln2_bias, proj_bias = (vec_ref[i : i + 1, :] for i in range(2, 6))

    @pl.when(step == 0)
    def _():
        sum_ref[...] = jnp.zeros_like(sum_ref)

    hidden = hid_ref[...]
    _, first_normed, _ = row_norm(hidden, vec_ref[0:1, :], vec_ref[1:2, :])
    first_ref[...] = first_normed.astype(BF16)
    resid = hidden + dot(mixed_ref[...], wout_ref[0]) + out_bias
    second, normed, inverse = row_norm(resid, ln2_gain, ln2_bias)
    low = second.astype(BF16)
    second_ref[...] = low
    total = resid + proj_bias
    for j in range(blocks):
        span = slice(j * width, (j + 1) * width)
        pre = dot(low, wfc_ref[j]) + fcb_ref[:, span]
        square = pre * pre
        curve = jnp.tanh(GELU_A * pre * (1.0 + GELU_B * square))
        half = 0.5 + 0.5 * curve
        act = (pre * half).astype(BF16)
        rise = 0.5 * GELU_A + (1.5 * GELU_A * GELU_B) * square
        slope_ref[:, span] = (half + pre * rise * (1.0 - curve * curve)).astype(BF16)
        act_ref[:, span] = act
        total = total + dot(act, wproj_ref[j])
    out_ref[...] = total.astype(BF16)

    @pl.when(step >= skip)
    def _():
        up = up_ref[...]
        second_grad = jnp.zeros(up.shape, F32)
        for j in range(blocks):
            span = slice(j * width, (j + 1) * width)
            slope = slope_ref[:, span].astype(F32)
            pre_grad = (dot_nt(up, wproj_ref[j]) * slope).astype(BF16)
            pg_ref[:, span] = pre_grad
            sum_ref[0:1, span] += jnp.sum(pre_grad.astype(F32), axis=0, keepdims=True)
            second_grad = second_grad + dot_nt(pre_grad, wfc_ref[j])
        up32 = up.astype(F32)
        resid_grad = up32 + row_norm_back(second_grad, normed, inverse, ln2_gain)
        attn_grad = resid_grad.astype(BF16)
        rg_ref[...] = resid_grad
        mg_ref[...] = dot_nt(attn_grad, wout_ref[0]).astype(BF16)
        sum_ref[1:2, :width] += jnp.sum(second_grad * normed, axis=0, keepdims=True)
        sum_ref[2:3, :width] += jnp.sum(second_grad, axis=0, keepdims=True)
        sum_ref[3:4, :width] += jnp.sum(up32, axis=0, keepdims=True)
        sum_ref[4:5, :width] += jnp.sum(attn_grad.astype(F32), axis=0, keepdims=True)


def feed(hidden, mixed_low, upstream_low, weights, vec, fc_bias):
    far = weights[1]
    seq_len, width = hidden.shape
    late = seq_len - QUESTION
    units = fc_bias.shape[1]
    skip = QUESTION // BLOCK

    def rows(columns):
        return pl.BlockSpec((BLOCK, columns), lambda i: (i, 0))

    def late_rows(columns):
        return pl.BlockSpec((BLOCK, columns), lambda i: (jnp.maximum(i - skip, 0), 0))

    sums = jax.ShapeDtypeStruct((8, units), F32)
    return pl.pallas_call(
        feed_kernel,
        grid=(seq_len // BLOCK,),
        in_specs=[
            rows(width),
            rows(width),
            late_rows(width),
            out_spec(far),
            fc_spec(far),
            proj_spec(far),
            whole(vec),
            whole(fc_bias),
        ],
        out_specs=[
            rows(width),
            rows(width),
            late_rows(width),
            late_rows(units),
            late_rows(units),
            late_rows(width),
            late_rows(width),
            whole(sums),
        ],
        out_shape=[
            jax.ShapeDtypeStruct((seq_len, width), BF16),
            jax.ShapeDtypeStruct((seq_len, width), BF16),
            jax.ShapeDtypeStruct((late, width), BF16),
            jax.ShapeDtypeStruct((late, units), BF16),
            jax.ShapeDtypeStruct((late, units), BF16),
            jax.ShapeDtypeStruct((late, width), F32),
            jax.ShapeDtypeStruct((late, width), BF16),
            sums,
        ],
        scratch_shapes=[pltpu.VMEM((BLOCK, units), BF16)],
        compiler_params=pltpu.CompilerParams(vmem_limit_bytes=VMEM_LIMIT),
        cost_estimate=cost(3),
        name="feed_forward_and_back",
    )(hidden, mixed_low, upstream_low, far, far, far, vec, fc_bias)


def first_back_kernel(info_ref, hid_ref, grad_ref, rg_ref, near_ref, vec_ref, in_ref):
    rows, width = hid_ref.shape
    step = pl.program_id(0)
    slot = info_ref[0]
    count = info_ref[1]
    gain = vec_ref[0:1, :]
    _, normed, inverse = row_norm(hid_ref[...], gain, vec_ref[1:2, :])
    first_grad = jnp.zeros((rows, width), F32)
    for i in range(3):
        first_grad = first_grad + dot_nt(grad_ref[i], near_ref[i])
    late = (step >= QUESTION // BLOCK).astype(F32)
    grad = row_norm_back(first_grad, normed, inverse, gain) + late * rg_ref[...]
    position = step * rows + lax.broadcasted_iota(jnp.int32, (rows, 1), 0)
    replaced = (position >= slot) & (position < slot + jnp.minimum(count, THOUGHTS))
    in_ref[...] = jnp.where(replaced, 0.0, grad)


def first_back(info, hidden, qkv_grad, resid_grad, weights, vec):
    seq_len, width = hidden.shape
    skip = QUESTION // BLOCK
    rows = pl.BlockSpec((BLOCK, width), lambda i: (i, 0))
    return pl.pallas_call(
        first_back_kernel,
        grid=(seq_len // BLOCK,),
        in_specs=[
            pl.BlockSpec(memory_space=pltpu.SMEM),
            rows,
            pl.BlockSpec((3, BLOCK, width), lambda i: (0, i, 0)),
            pl.BlockSpec((BLOCK, width), lambda i: (jnp.maximum(i - skip, 0), 0)),
            whole(weights[0]),
            whole(vec),
        ],
        out_specs=rows,
        out_shape=jax.ShapeDtypeStruct((seq_len, width), F32),
        compiler_params=pltpu.CompilerParams(vmem_limit_bytes=VMEM_LIMIT),
        cost_estimate=cost(0.83),
        name="first_norm_backward",
    )(info, hidden, qkv_grad, resid_grad, weights[0], vec)


def in_pieces(value, count=3):
    pieces = []
    for _ in range(count):
        pieces.append(value.astype(BF16))
        value = value - pieces[-1].astype(F32)
    return pieces


def keep_and_send(value, core, chips, keep_ref, send_ref, at):
    own = value.shape[0] // (2 * len(chips))
    for spot, chip in enumerate(chips):
        even = value[2 * chip * own : (2 * chip + 1) * own]
        odd = value[(2 * chip + 1) * own : (2 * chip + 2) * own]
        keep_ref[spot, at] = jnp.where(core == 0, even, odd).astype(BF16)
        send_ref[spot, at] = jnp.where(core == 0, odd, even).astype(BF16)


def near_terms_kernel(
    sizes, chips_a, chips_b, core_ref, normed_ref, grad_ref, mixed_ref, rg_ref, near_ref, vec_ref,
    feed_sum_ref, row_sum_ref, place_a, owner_a, place_b, owner_b, keep_a, send_a, keep_b, send_b,
    packed_ref, normed_t, gain_ref, bias_ref, column_ref,
):
    core = core_ref[0]
    step = pl.program_id(0)
    width = normed_ref.shape[1]

    @pl.when(step == 0)
    def _():
        normed_t[...] = normed_ref[...].T
        gain_ref[...] = jnp.zeros_like(gain_ref)
        bias_ref[...] = jnp.zeros_like(bias_ref)

    def term():
        columns = vec_ref[...].T
        inner = dot(normed_t[...], grad_ref[...])
        sums = jnp.sum(grad_ref[...].astype(F32), axis=0, keepdims=True)
        gain_ref[...] += inner * near_ref[...].astype(F32)
        pieces = in_pieces(jnp.broadcast_to(sums, (8, width)), 2)
        bias_ref[...] += dot_nt(jnp.concatenate(pieces, axis=0), near_ref[...])
        column_ref[pl.ds(step, 1), :] = sums
        return inner * columns[:, 0:1] + columns[:, 1:2] * sums

    @pl.when(step < 2)
    def _():
        keep_and_send(term(), core, chips_a, keep_a, send_a, 0)

    @pl.when(step == 2)
    def _():
        keep_and_send(term(), core, chips_b, keep_b, send_b, 0)

    @pl.when(step == 3)
    def _():
        value = dot_tn(mixed_ref[QUESTION:, :], rg_ref[...].astype(BF16))
        keep_and_send(value, core, chips_b, keep_b, send_b, 0)
        ones = jnp.ones((16, width), BF16)
        totals = feed_sum_ref[...] + row_sum_ref[...]
        small = {name: totals[i : i + 1, :width] for i, name in enumerate(SUM_ROWS)}
        small["fc_bias"] = totals[0:1]
        small["ln1_gain"] = sum(dot_nt(ones, p) for p in in_pieces(gain_ref[...], 2))[0:1]
        small["ln1_bias"] = bias_ref[0:1, :] + bias_ref[8:9, :]
        small["qv_bias"] = jnp.concatenate([column_ref[0:1, :], column_ref[2:3, :]], axis=1)
        pack(small, sizes, 2 * len(chips_a), (place_a, owner_a, place_b, owner_b), packed_ref)


def near_terms(
    core, normed_low, qkv_grad, mixed_low, resid_grad, near, vec, feed_sums, row_sums, sizes, chips_a, chips_b
):
    seq_len, width = normed_low.shape
    half = jax.ShapeDtypeStruct((len(chips_a), 2, width // (2 * len(chips_a)), width), BF16)
    piece = (len(chips_a), 1) + half.shape[2:]
    left = pl.BlockSpec(piece, lambda i: (0, jnp.minimum(i, 1), 0, 0))
    right = pl.BlockSpec(piece, lambda i: (0, jnp.maximum(i - 2, 0), 0, 0))
    devices = 2 * len(chips_a)
    maps = lane_maps(width // devices, devices)
    packed = jax.ShapeDtypeStruct((len(sizes), devices, LANES), BF16)
    out_shape = [half] * 4 + [packed]
    return pl.pallas_call(
        functools.partial(near_terms_kernel, sizes, chips_a, chips_b),
        grid=(4,),
        in_specs=[
            pl.BlockSpec(memory_space=pltpu.SMEM),
            whole(normed_low),
            pl.BlockSpec((None, seq_len, width), lambda i: (jnp.minimum(i, 2), 0, 0)),
            whole(mixed_low),
            whole(resid_grad),
            pl.BlockSpec((None, width, width), lambda i: (jnp.minimum(i, 2), 0, 0)),
            whole(vec),
            whole(feed_sums),
            whole(row_sums),
            *(whole(x) for x in maps),
        ],
        out_specs=[left, left, right, right, whole(packed)],
        out_shape=out_shape,
        scratch_shapes=[
            pltpu.VMEM((width, seq_len), BF16),
            pltpu.VMEM((width, width), F32),
            pltpu.VMEM((16, width), F32),
            pltpu.VMEM((8, width), F32),
        ],
        compiler_params=pltpu.CompilerParams(vmem_limit_bytes=VMEM_LIMIT),
        cost_estimate=cost(0.5),
        name="near_weight_terms",
    )(core, normed_low, qkv_grad, mixed_low, resid_grad, near, vec, feed_sums, row_sums, *maps)


def far_terms_kernel(
    outer, inner, chips, core_ref, act_ref, up_ref, second_ref, pg_ref, proj_ref, keep_ref, send_ref,
    second_t,
):
    step = pl.program_id(0)
    blocks = pl.num_programs(0) // 2

    @pl.when(step == 0)
    def _():
        second_t[...] = second_ref[...].T

    @pl.when(step < blocks)
    def _():
        value = dot_tn(act_ref[...], up_ref[...])
        rows, width = value.shape
        value = value.reshape(outer, inner, rows // (outer * inner), width)
        for i in range(inner):
            proj_ref[i, :, 0] = value[:, i].astype(BF16)

    @pl.when(step >= blocks)
    def _():
        value = dot(second_t[...], pg_ref[...])
        keep_and_send(value, core_ref[0], chips, keep_ref, send_ref, 0)


def far_terms(core, act_low, upstream_low, second_low, pre_grad, outer, inner, chips):
    rows, units = pre_grad.shape
    width = second_low.shape[1]
    blocks = units // width
    own = width // (outer * inner)
    proj = (inner, outer, blocks, own, width)
    half = jax.ShapeDtypeStruct((len(chips), blocks, own, width), BF16)

    def early(i):
        return jnp.minimum(i, blocks - 1)

    def late(i):
        return jnp.maximum(i - blocks, 0)

    out = pl.BlockSpec((len(chips), 1, own, width), lambda i: (0, late(i), 0, 0))
    return pl.pallas_call(
        functools.partial(far_terms_kernel, outer, inner, chips),
        grid=(2 * blocks,),
        in_specs=[
            pl.BlockSpec(memory_space=pltpu.SMEM),
            pl.BlockSpec((rows, width), lambda i: (0, early(i))),
            whole(upstream_low),
            whole(second_low),
            pl.BlockSpec((rows, width), lambda i: (0, late(i))),
        ],
        out_specs=[
            pl.BlockSpec((inner, outer, 1, own, width), lambda i: (0, 0, early(i), 0, 0)),
            out,
            out,
        ],
        out_shape=[jax.ShapeDtypeStruct(proj, BF16), half, half],
        scratch_shapes=[pltpu.VMEM((width, rows), BF16)],
        compiler_params=pltpu.CompilerParams(vmem_limit_bytes=VMEM_LIMIT),
        cost_estimate=cost(1),
        name="far_weight_terms",
    )(core, act_low, upstream_low, second_low, pre_grad)


def first_kernel(
    orders, core_ref, tok_ref, left_mine, left_got, right_mine, right_got, vec_ref, qkvb_ref, qkv_ref,
    near_ref, rows_ref,
):
    width = tok_ref.shape[1]

    @pl.when(pl.program_id(0) == 0)
    def _():
        even_is_mine = core_ref[0] == 0
        own, half = left_mine.shape[2:]
        for i in range(3):
            for side, (mine, got) in enumerate([(left_mine, left_got), (right_mine, right_got)]):
                for spot, chip in enumerate(orders[side]):
                    a = mine[spot, i].astype(F32)
                    b = got[spot, i].astype(F32)
                    begin = 2 * chip * own
                    rows_ref[begin : begin + own, :] = jnp.where(even_is_mine, a, b)
                    rows_ref[begin + own : begin + 2 * own, :] = jnp.where(even_is_mine, b, a)
                near_ref[i, :, side * half : (side + 1) * half] = rows_ref[...].astype(BF16)

    first, _, _ = row_norm(tok_ref[...].astype(F32), vec_ref[0:1, :], vec_ref[1:2, :])
    first = first.astype(BF16)
    for i in range(3):
        span = slice(i * width, (i + 1) * width)
        qkv_ref[i] = (dot(first, near_ref[i]) + qkvb_ref[:, span]).astype(BF16)


def first_forward(core, tokens, pieces, orders, vec, qkv_bias):
    seq_len, width = tokens.shape
    near = jax.ShapeDtypeStruct((3, width, width), BF16)
    return pl.pallas_call(
        functools.partial(first_kernel, orders),
        grid=(seq_len // BLOCK,),
        in_specs=[
            pl.BlockSpec(memory_space=pltpu.SMEM),
            pl.BlockSpec((BLOCK, width), lambda i: (i, 0)),
            *(whole(piece) for piece in pieces),
            whole(vec),
            whole(qkv_bias),
        ],
        out_specs=[pl.BlockSpec((3, BLOCK, width), lambda i: (0, i, 0)), whole(near)],
        out_shape=[jax.ShapeDtypeStruct((3, seq_len, width), BF16), near],
        scratch_shapes=[pltpu.VMEM((width, width // 2), F32)],
        compiler_params=pltpu.CompilerParams(vmem_limit_bytes=VMEM_LIMIT),
        cost_estimate=cost(0.67),
        name="first_norm_forward",
    )(core, tokens, *pieces, vec, qkv_bias)


def group_of(blocks, own):
    each = blocks * own
    group = LANES // math.gcd(LANES, each)
    device, block, i = np.indices((group, blocks, own)).reshape(3, -1)
    swap = np.zeros((group * each, group * each), np.float32)
    swap[np.arange(group * each), block * (group * own) + device * own + i] = 1.0
    return group, jnp.asarray(swap, BF16)


def far_shard_kernel(blocks, span, fc_ref, proj_ref, out_w_ref, swap_ref, out_ref):
    own, width = out_w_ref.shape
    size = swap_ref.shape[0]
    groups = width // span
    rows = [fc_ref[:, g * size : (g + 1) * size].astype(F32) for g in range(groups)]
    swapped = dot(jnp.concatenate(rows, axis=0).astype(BF16), swap_ref[...])
    for g in range(groups):
        part = swapped[g * own : (g + 1) * own]
        for j in range(blocks):
            piece = part[:, j * span : (j + 1) * span]
            out_ref[j, :, g * span : (g + 1) * span] = piece.astype(BF16)
    for j in range(blocks):
        out_ref[blocks + j] = proj_ref[j]
    out_ref[2 * blocks] = out_w_ref[...]


def join_far(fc_shard, proj_shard, out_shard):
    own, width = out_shard.shape
    blocks = fc_shard.shape[1] // width
    group, swap = group_of(blocks, own)
    return pl.pallas_call(
        functools.partial(far_shard_kernel, blocks, group * own),
        out_shape=jax.ShapeDtypeStruct((2 * blocks + 1, own, width), BF16),
        compiler_params=pltpu.CompilerParams(vmem_limit_bytes=VMEM_LIMIT),
        name="far_shard",
    )(fc_shard, proj_shard.reshape(blocks, own, width), out_shard, swap)


def row_terms_kernel(span, index_ref, fac_ref, proj_ref, fc_ref, swap_ref, proj_out, fc_out):
    blocks, own, width = proj_ref.shape
    shape = (width, own)
    mine = lax.broadcasted_iota(jnp.int32, shape, 0) - index_ref[0] * own
    select = (mine == lax.broadcasted_iota(jnp.int32, shape, 1)).astype(BF16)

    def factor(j):
        return jnp.concatenate([fac_ref[THOUGHTS * j + i] for i in range(THOUGHTS)], axis=0)

    upstream = factor(blocks)
    terms = []
    second = dot(factor(blocks + 1), select).astype(BF16)
    for j in range(blocks):
        act = dot(factor(j), select).astype(BF16)
        proj_out[j] = proj_ref[j].astype(F32) + dot_tn(act, upstream)
        terms.append(fc_ref[j] + dot_tn(second, factor(blocks + 2 + j)))
    size = swap_ref.shape[0]
    groups = width // span
    rows = [
        jnp.concatenate([t[:, g * span : (g + 1) * span] for t in terms], axis=1)
        for g in range(groups)
    ]
    left = jnp.concatenate(rows, axis=0)
    total = sum(dot_nt(piece, swap_ref[...]) for piece in in_pieces(left))
    for g in range(groups):
        fc_out[:, g * size : (g + 1) * size] = total[g * own : (g + 1) * own]


def row_terms(index, factors, proj_sum, fc_sum):
    blocks, own, width = fc_sum.shape
    out_shape = [
        jax.ShapeDtypeStruct(proj_sum.shape, F32),
        jax.ShapeDtypeStruct((own, blocks * width), F32),
    ]
    group, swap = group_of(blocks, own)
    return pl.pallas_call(
        functools.partial(row_terms_kernel, group * own),
        grid=(1,),
        in_specs=[
            pl.BlockSpec(memory_space=pltpu.SMEM),
            whole(factors),
            whole(proj_sum),
            whole(fc_sum),
            whole(swap),
        ],
        out_specs=[whole(x) for x in out_shape],
        out_shape=out_shape,
        compiler_params=pltpu.CompilerParams(vmem_limit_bytes=VMEM_LIMIT),
        cost_estimate=cost(0.33),
        name="thought_rows_terms",
    )(index, factors, proj_sum, fc_sum, swap)


def lane_maps(own, devices):
    maps = []
    for size in (own, 2 * own):
        column = np.arange(size * devices)
        maps.append(jnp.asarray(column[None, :] % size == np.arange(size)[:, None], BF16))
        maps.append(jnp.asarray(column[None, :] // size == np.arange(devices)[:, None], F32))
    return maps


def lane_pieces(sizes, own):
    pieces = []
    for at, (name, size) in enumerate(sizes):
        wide = size == 2 * own
        step = 2 * own if wide else own
        pieces += [(at, name, begin, 2 * int(wide), step) for begin in range(0, size, step)]
    return pieces


VECTOR_ROWS = ("ln1_gain", "ln1_bias", "out_bias", "ln2_gain", "ln2_bias", "proj_bias")


def unpack_kernel(
    sizes, own, packed_ref, place_a, owner_a, place_b, owner_b, vec_ref, fcb_ref, qkvb_ref
):
    maps = (place_a, owner_a, place_b, owner_b)
    vec_ref[...] = jnp.zeros_like(vec_ref)
    width = vec_ref.shape[1]
    for at, name, begin, which, size in lane_pieces(sizes, own):
        spread = dot(packed_ref[at][:, begin : begin + size], maps[which][...])
        full = jnp.sum(spread * maps[which + 1][...], axis=0, keepdims=True)
        if name == "fc_bias":
            fcb_ref[:, begin // own * width : (begin // own + 1) * width] = full
        elif name == "qv_bias":
            qkvb_ref[:, :width] = full[:, :width]
            qkvb_ref[:, width : 2 * width] = jnp.zeros((1, width), F32)
            qkvb_ref[:, 2 * width :] = full[:, width:]
        else:
            row = VECTOR_ROWS.index(name)
            vec_ref[row : row + 1, :] = full


def unpack(packed, sizes):
    devices = packed.shape[1]
    size = dict(sizes)
    own = size["ln1_gain"]
    width = own * devices
    return pl.pallas_call(
        functools.partial(unpack_kernel, sizes, own),
        out_shape=[
            jax.ShapeDtypeStruct((8, width), F32),
            jax.ShapeDtypeStruct((1, size["fc_bias"] * devices), F32),
            jax.ShapeDtypeStruct((1, 3 * width), F32),
        ],
        compiler_params=pltpu.CompilerParams(vmem_limit_bytes=VMEM_LIMIT),
        name="vectors_unpack",
    )(packed, *lane_maps(own, devices))


def pack(rows, sizes, devices, maps, out_ref):
    out_ref[...] = jnp.zeros_like(out_ref)
    width = rows["ln1_gain"].shape[1]
    own = width // devices
    pieces = lane_pieces(sizes, own)
    for which in sorted({piece[3] for piece in pieces}):
        group = [piece for piece in pieces if piece[3] == which]
        stack = []
        for _, name, begin, _, size in group:
            span = size * devices
            first = begin // size * span
            stack.append((rows[name][:, first : first + span] * maps[which + 1][...]).astype(BF16))
        done = dot_nt(jnp.concatenate(stack, axis=0), maps[which][...]).astype(BF16)
        for i, (at, _, begin, _, size) in enumerate(group):
            out_ref[at, :, begin : begin + size] = done[i * devices : (i + 1) * devices]


def join_kernel(*refs):
    out_ref = refs[-1]
    out_ref[...] = jnp.zeros_like(out_ref)
    for at, ref in enumerate(refs[:-1]):
        out_ref[at : at + 1, : ref.shape[0]] = ref[...].astype(F32).reshape(1, ref.shape[0])


def join(vectors):
    return pl.pallas_call(
        join_kernel,
        out_shape=jax.ShapeDtypeStruct((len(vectors), LANES), F32),
        name="vectors_join",
    )(*vectors)


def part_kernel(joined_ref, *refs):
    for at, ref in enumerate(refs):
        ref[...] = joined_ref[at, : ref.shape[0]]


def part(joined, sizes):
    return pl.pallas_call(
        part_kernel,
        out_shape=[jax.ShapeDtypeStruct((size,), F32) for _, size in sizes],
        name="vectors_part",
    )(joined)


def step_on_sequence(
    near_pieces, far, vectors, tokens, cotangent, slots, count, answer_start, devices, sizes, comm
):
    vec, fc_bias, qkv_bias = vectors
    seq_len, width = tokens.shape
    info = jnp.stack([slots[0], count])

    qkv_first, near = first_forward(
        comm.core, tokens, near_pieces, comm.near_orders, vec, qkv_bias
    )
    mixed_hidden, lse_hidden = attend(info, qkv_first)
    late = QUESTION + lax.iota(jnp.int32, seq_len - QUESTION)
    upstream_low = jnp.where(
        (late >= answer_start)[:, None], cotangent[QUESTION:], jnp.zeros((), BF16)
    )
    tokens32 = tokens.astype(F32)
    weights = (near, after(far, mixed_hidden, upstream_low, tokens32))
    lse, *saved, qkv, mixed_low, hidden = thoughts_forward(
        info, tokens, tokens32, qkv_first, mixed_hidden, lse_hidden, weights, vec, fc_bias, qkv_bias
    )
    output, normed_low, second_low, act_low, pre_grad, resid_grad, mixed_grad, sums = feed(
        hidden, mixed_low, upstream_low, weights, vec, fc_bias
    )

    proj_grad, *halves = comm.far_terms(act_low, upstream_low, second_low, pre_grad)
    proj_half = comm.early(proj_grad)
    fc_going = comm.scatter(halves, "zxyc")
    sent = go_after([fc_going])
    row_sums, factors, mixed_grad, resid_grad = thoughts_back(
        info,
        hidden,
        qkv,
        mixed_low,
        after(lse, *sent),
        saved,
        weights,
        vec,
        mixed_grad,
        resid_grad,
    )
    join_after([fc_going], row_sums)
    spread = comm.factors(factors)
    sent = go_after([fc_going, spread])
    lse, back_grad = after((lse, mixed_grad), *sent)
    qkv_grad = attend_back(qkv, mixed_low, lse, back_grad)
    join_after([fc_going, spread], qkv_grad)
    proj_half = after(proj_half, qkv_grad)
    proj_going = comm.early_end(proj_half)
    sent = (*go_after([fc_going, spread]), proj_half)
    *terms, packed = near_terms(
        comm.core,
        after(normed_low, *sent),
        qkv_grad,
        mixed_low,
        resid_grad,
        near,
        vec,
        sums,
        row_sums,
        sizes,
        comm.chips("zxyc"),
        comm.chips("zyxc"),
    )
    first = comm.scatter(terms[:2], "zxyc")
    rest = comm.scatter(terms[2:], "zyxc")
    vectors_going = comm.scatter_vectors(packed)

    join_after([fc_going, spread], packed)

    going = [first, rest, vectors_going]
    sent = go_after(going, fc_going.got, spread.buf)
    sent += go_after([fc_going, spread], *sent)
    join_after(going, *sent)
    sent = go_after(going)
    input_grad = first_back(info, hidden, after(qkv_grad, *sent), resid_grad, weights, vec)
    going += [fc_going, spread]
    join_after(going, input_grad)
    proj_g = fc_g = None
    while any(swap.todo for swap in going) or proj_g is None:
        group = [swap for swap in going if swap.todo]
        sent = go_after(group)
        done = sent
        if proj_g is None and fc_going not in group and spread not in group:
            factors, fc_sum = after((spread.finish(), fc_going.finish()), *sent)
            proj_g, fc_g = comm.terms(factors, proj_going, fc_sum)
            done = (proj_g, fc_g)
        join_after(group, *done)
    return (
        output,
        input_grad,
        first.finish(),
        rest.finish(),
        proj_g,
        fc_g,
        vectors_going.finish(),
    )


SMALL = ("ln1_gain", "ln1_bias", "qv_bias", "out_bias", "ln2_gain", "ln2_bias", "fc_bias", "proj_bias")


def on_device(
    links,
    tokens,
    ln1_gain,
    ln1_bias,
    qkv_weight,
    qv_bias,
    out_weight,
    out_bias,
    ln2_gain,
    ln2_bias,
    fc_weight,
    fc_bias,
    proj_weight,
    proj_bias,
    cotangent,
    thought_slots,
    thought_count,
    answer_start,
):
    devices = links.sizes["dp"] * links.sizes["fsdp"]
    small_shards = dict(
        ln1_gain=ln1_gain,
        ln1_bias=ln1_bias,
        qv_bias=qv_bias,
        out_bias=out_bias,
        ln2_gain=ln2_gain,
        ln2_bias=ln2_bias,
        fc_bias=fc_bias,
        proj_bias=proj_bias,
    )
    sizes = tuple((n, small_shards[n].shape[0]) for n in SMALL)
    own, width = out_weight.shape
    blocks = proj_weight.shape[0] // own
    both = ("dp", "fsdp")

    far_shard = join_far(fc_weight, proj_weight, out_weight)
    far = lax.all_gather(far_shard, both, axis=1, tiled=True)

    packed = join([small_shards[n] for n in SMALL]).astype(BF16)
    small = links.gather(packed, "zxyc", axis=0).reshape(devices, len(sizes), LANES)
    half = width // 2
    near_pieces = []
    near_texts = ("zxyc", "zyxc")
    for side, text in enumerate(near_texts):
        part_columns = [
            qkv_weight[:, i * width + side * half : i * width + (side + 1) * half] for i in range(3)
        ]
        ring = Gather(links, jnp.stack(part_columns)[None], text)
        near_pieces += ring.last()

    class Comm:
        chips = links.chips
        near_orders = [links.spots(text) for text in near_texts]
        core = (lax.axis_index("fsdp") % 2)[None].astype(jnp.int32)

        @staticmethod
        def far_terms(act_low, upstream_low, second_low, pre_grad):
            sizes_here = links.sizes["dp"], links.sizes["fsdp"]
            return far_terms(
                Comm.core,
                act_low,
                upstream_low,
                second_low,
                pre_grad,
                *sizes_here,
                links.chips("zxyc"),
            )

        @staticmethod
        def early(value):
            return lax.psum_scatter(
                value.reshape(-1, width), "fsdp", scatter_dimension=0, tiled=True
            )

        @staticmethod
        def early_end(value):
            value = lax.psum_scatter(value, "dp", scatter_dimension=0, tiled=True)
            return value.reshape(blocks, own, width)

        @staticmethod
        def scatter(halves, text):
            return links.scatter(tuple(halves), text)

        @staticmethod
        def factors(rows):
            return Gather(links, rows, "zyxc")

        @staticmethod
        def scatter_vectors(value):
            return links.scatter(value.transpose(1, 0, 2), "zxyc")

        @staticmethod
        def terms(factors, proj_sum, fc_sum):
            index = lax.axis_index(both)[None].astype(jnp.int32)
            factors = factors.reshape(devices, FACTOR_ROWS, width).transpose(1, 0, 2)
            return row_terms(index, factors, proj_sum, fc_sum)

    output, input_grad, first, rest, proj_g, fc_g, vector_sums = step_on_sequence(
        near_pieces,
        far,
        unpack(small.transpose(1, 0, 2), sizes),
        tokens[0],
        cotangent[0],
        thought_slots[0],
        thought_count[0],
        answer_start[0],
        devices,
        sizes,
        Comm,
    )
    proj_g = proj_g.reshape(blocks * own, width)
    qkv_g = jnp.concatenate([first[0], first[1], rest[0]], axis=1)
    out_g = rest[1]
    owned = dict(zip(SMALL, part(vector_sums, sizes)))
    return (
        output[None],
        input_grad[None],
        owned["ln1_gain"],
        owned["ln1_bias"],
        qkv_g,
        owned["qv_bias"],
        out_g,
        owned["out_bias"],
        owned["ln2_gain"],
        owned["ln2_bias"],
        fc_g,
        owned["fc_bias"],
        proj_g,
        owned["proj_bias"],
    )


def solution(mesh):
    links = Links({name: mesh.shape[name] for name in ("dp", "fsdp")})
    both = ("dp", "fsdp")
    cube, matrix, vector = P(both, None, None), P(both, None), P(both)
    weight_specs = (
        vector,
        vector,
        matrix,
        vector,
        matrix,
        vector,
        vector,
        vector,
        matrix,
        vector,
        matrix,
        vector,
    )

    def per_device(*args):
        return on_device(links, *args)

    return jax.shard_map(
        per_device,
        mesh=mesh,
        in_specs=(cube,) + weight_specs + (cube, matrix, vector, vector),
        out_specs=(cube, cube) + weight_specs,
        check_vma=False,
    )
```
